32 devices in a mesh: replica: 2 (over y), branch: 4 (over z), tensor: 4 (over x, core).
Axes of the slice: x: 2, y: 2, z: 4, core: 2. Of those that a mesh axis runs over, the one named last changes fastest.
Arguments:
- prompt_ssm: float32 [8, 16, 4096], P(('replica', 'branch'), None, 'tensor'), parts along dimension 0, may hold values from -6 to 6
- prompt_conv: bfloat16 [8, 3, 4096], P(('replica', 'branch'), None, 'tensor'), parts along dimension 0, may hold values from -6 to 6
- prompt_of: int32 [128], P(('replica', 'branch')), parts along dimension 0, may hold values from 0 to 3
- step_in: bfloat16 [128, 4, 2, 4096], P(('replica', 'branch'), None, None, 'tensor'), parts along dimension 0, may hold values from -6 to 6
- conv_weight: float32 [4, 4096], P(None, 'tensor'), may hold values from -3 to 3
- conv_bias: float32 [4096], P('tensor'), may hold values from -3 to 3
- x_weight: bfloat16 [4096, 288], P('tensor'), may hold values from -0.09375 to 0.09375
- dt_weight: bfloat16 [256, 4096], P(None, 'tensor'), may hold values from -0.375 to 0.375
- dt_bias: float32 [4096], P('tensor'), may hold values from -4 to -1
- a_log: float32 [16, 4096], P(None, 'tensor'), may hold values from 0 to 2.77
- skip: float32 [4096], P('tensor'), may hold values from 0.5 to 1.5
- send_rows: int32 [8, 4, 1], P(('replica', 'branch')), parts along dimension 0, may hold values from -1 to 15, as said below
- child_slot: int32 [128], P(('replica', 'branch')), parts along dimension 0, may hold values from 0 to 3, as said below
Outputs:
- decoded: bfloat16 [128, 4, 4096], P(('replica', 'branch'), None, 'tensor'), parts along dimension 0
- child_ssm: float32 [128, 16, 4096], P(('replica', 'branch'), None, 'tensor'), parts along dimension 0
- child_conv: bfloat16 [128, 3, 4096], P(('replica', 'branch'), None, 'tensor'), parts along dimension 0
The draws below stay inside these ranges and needn't reach their ends.
There are 2 independent parts, one for each index of `replica`. The reference program is written for one: setup_inputs(seed, part) draws one part's arguments, and reference() takes and returns one part's arrays. A program takes and returns all parts, laid end to end along the dimension named above; an argument that names none is the same for every part. Nothing has to cross between parts.
Inputs may be any that keep to these rules, and one draw needn't show every extreme that they name: send_rows[s, d, c] is a branch of owner s (its row among the 16 branches of s) carried in slot c to owner d, or -1 for an empty slot; in each block the full slots come first. child_slot[j] = s * 1 + c names a full slot that owner j // 16 receives from owner s; each full slot that an owner receives is named by at least one of its children.
All inputs are finite; a program needn't handle non-finite values.
Results may differ from the reference program's by a relative error of at most 0.0061.
Values may be sent and summed in bfloat16 or wider, within the bound.
No kernel may reach another device: no remote copies, remote signals or barrier semaphores. Data moves between devices by JAX's collectives and lax.ppermute only.
A program may use at most 64 MiB of HBM per device.

```python
import jax
import jax.numpy as jnp

E = 4096
STATE = 16
DTR = 256
KCONV = 4
STEPS = 4
RB = 16
CAP = 1
OWNERS = 4
XW = 288
BRANCHES = 64
PROMPTS = 4


def routing_plan(key):
    owners = OWNERS
    active_n = min(RB // CAP, owners)
    key_offset, key_full, key_order, key_slots, key_extra, key_child = jax.random.split(key, 6)
    offset = jax.random.randint(key_offset, (owners,), 0, owners)
    source = jnp.arange(owners, dtype=jnp.int32)[:, None]
    relative = (source - offset[None, :]) % owners
    active = relative < active_n
    fuller = (jax.random.randint(key_full, (owners, owners), 0, 4) > 0) | (relative == 0)
    counts = jnp.where(active, jnp.where(fuller, CAP, 1), 0)
    slot_ids = jnp.arange(CAP, dtype=jnp.int32)
    valid = slot_ids[None, None, :] < counts[:, :, None]
    flat_valid = valid.reshape(owners, owners * CAP).astype(jnp.int32)
    counter = jnp.cumsum(flat_valid, axis=1) - flat_valid
    scores = jax.random.randint(key_order, (owners, RB), 0, 2 ** 20) * RB + jnp.arange(RB, dtype=jnp.int32)[None, :]
    shuffle = jnp.argsort(scores, axis=1).astype(jnp.int32)
    chosen = jnp.take_along_axis(shuffle, counter % RB, axis=1)
    sent = jnp.where(flat_valid > 0, chosen, -1).reshape(owners, owners, CAP)
    received = jnp.transpose(valid, (1, 0, 2)).reshape(owners, owners * CAP).astype(jnp.int32)
    full_count = jnp.sum(received, axis=1)
    slot_scores = (1 - received) * 2 ** 28 + jax.random.randint(key_slots, (owners, owners * CAP), 0, 2 ** 20) * (owners * CAP) + jnp.arange(owners * CAP, dtype=jnp.int32)[None, :]
    ordered = jnp.argsort(slot_scores, axis=1).astype(jnp.int32)
    extras = jax.random.randint(key_extra, (owners, RB), 0, 2 ** 20) % full_count[:, None]
    position = jnp.arange(RB, dtype=jnp.int32)[None, :]
    index = jnp.where(position < full_count[:, None], position, extras)
    children = jnp.take_along_axis(ordered, index, axis=1)
    child_scores = jax.random.randint(key_child, (owners, RB), 0, 2 ** 20) * RB + jnp.arange(RB, dtype=jnp.int32)[None, :]
    child_order = jnp.argsort(child_scores, axis=1).astype(jnp.int32)
    children = jnp.take_along_axis(children, child_order, axis=1)
    return (sent.astype(jnp.int32), children.reshape(-1).astype(jnp.int32))


def draw_send_rows(key, part):
    sent, children = routing_plan(key)
    return sent


def draw_child_slot(key, part):
    sent, children = routing_plan(key)
    return children


def place_ends(drawn, key, low, high):
    place = [jax.random.randint(jax.random.fold_in(key, axis), (), 0, length) for axis, length in enumerate(drawn.shape)]
    main_axis = drawn.shape.index(max(drawn.shape))
    next_to = place[:main_axis] + [(place[main_axis] + 1) % drawn.shape[main_axis]] + place[main_axis + 1:]
    return drawn.at[tuple(place)].set(low).at[tuple(next_to)].set(high)


def level_of(own_key, shape, cuts, low, largest):
    loudness = 1.0
    for axis_at, blocks in cuts:
        heights = jax.random.uniform(jax.random.fold_in(jax.random.fold_in(own_key, 6), axis_at), (blocks,), jnp.float32, low / len(cuts), largest / len(cuts))
        loudness = loudness * jnp.repeat(jnp.exp(heights), shape[axis_at] // blocks).reshape((-1,) + (1,) * (len(shape) - 1 - axis_at))
    return loudness


def normal_values(key, shape, deviation, reach, shards=(), kind=jnp.bfloat16):
    loudness = level_of(key, shape, shards, -0.22, 0.18) if shards else 1.0
    entries = jax.random.normal(key, shape, jnp.float32) * deviation * loudness
    return jnp.minimum(jnp.maximum(entries, -reach), reach).astype(kind)


def setup_inputs(seed: int = 0, part: int = 0) -> dict:
    arg_keys = jax.random.split(jax.random.key(seed), 14)
    own_keys = jax.random.split(jax.random.fold_in(arg_keys[13], part), 14)
    return {
        "prompt_ssm": normal_values(own_keys[0], (PROMPTS, STATE, E), 1.0, 6.0, ((0, 4), (2, 4)), jnp.float32),
        "prompt_conv": normal_values(own_keys[1], (PROMPTS, KCONV - 1, E), 1.0, 6.0, ((0, 4), (2, 4))),
        "prompt_of": place_ends(jax.random.randint(own_keys[2], (BRANCHES,), 0, PROMPTS), jax.random.fold_in(own_keys[2], 1), 0, PROMPTS - 1).astype(jnp.int32),
        "step_in": normal_values(own_keys[3], (BRANCHES, STEPS, 2, E), 1.0, 6.0, ((0, 4), (3, 4))),
        "conv_weight": normal_values(arg_keys[4], (KCONV, E), 0.5, 3.0, ((1, 4),), jnp.float32),
        "conv_bias": normal_values(arg_keys[5], (E,), 0.5, 3.0, ((0, 4),), jnp.float32),
        "x_weight": normal_values(arg_keys[6], (E, XW), E ** -0.5, 0.09375, ((0, 4),)),
        "dt_weight": normal_values(arg_keys[7], (DTR, E), DTR ** -0.5, 0.375, ((1, 4),)),
        "dt_bias": jnp.clip(-4.0 + 3.0 * jax.random.uniform(arg_keys[8], (E,), jnp.float32) ** level_of(arg_keys[8], (E,), ((0, 4),), -0.2, 0.2), -4.0, -1.0),
        "a_log": jnp.clip(2.77 * jax.random.uniform(arg_keys[9], (STATE, E), jnp.float32) ** level_of(arg_keys[9], (STATE, E), ((1, 4),), -0.2, 0.2), 0.0, 2.77),
        "skip": jnp.clip(0.5 + 1.0 * jax.random.uniform(arg_keys[10], (E,), jnp.float32) ** level_of(arg_keys[10], (E,), ((0, 4),), -0.2, 0.2), 0.5, 1.5),
        "send_rows": draw_send_rows(jax.random.fold_in(jax.random.fold_in(arg_keys[13], part), 71), part),
        "child_slot": draw_child_slot(jax.random.fold_in(jax.random.fold_in(arg_keys[13], part), 71), part),
    }


def decode_steps(states, windows, step_in, conv_weight, conv_bias, x_weight, dt_weight, dt_bias, a_log, skip):
    kernel_len = conv_weight.shape[0]
    rank_size = dt_weight.shape[0]
    state_size = a_log.shape[0]
    decay_rate = -jnp.exp(a_log)
    outputs = []
    for position in range(step_in.shape[1]):
        x_now = step_in[:, position, 0]
        z_now = step_in[:, position, 1]
        conv_sum = conv_weight[kernel_len - 1] * x_now.astype(jnp.float32) + conv_bias
        for offset in range(kernel_len - 1):
            conv_sum = conv_sum + conv_weight[offset] * windows[:, offset].astype(jnp.float32)
        activated = jax.nn.silu(conv_sum)
        x_proj = jnp.dot(activated.astype(jnp.bfloat16), x_weight, preferred_element_type=jnp.float32)
        delta_in = x_proj[:, :rank_size].astype(jnp.bfloat16)
        b_proj = x_proj[:, rank_size:rank_size + state_size]
        c_proj = x_proj[:, rank_size + state_size:]
        delta = jax.nn.softplus(jnp.dot(delta_in, dt_weight, preferred_element_type=jnp.float32) + dt_bias)
        states = jnp.exp(delta[:, None, :] * decay_rate[None]) * states + (delta * activated)[:, None, :] * b_proj[:, :, None]
        output = jnp.sum(c_proj[:, :, None] * states, axis=1) + skip * activated
        outputs.append((output * jax.nn.silu(z_now.astype(jnp.float32))).astype(jnp.bfloat16))
        windows = jnp.concatenate([windows[:, 1:], x_now[:, None]], axis=1)
    return states, windows, jnp.stack(outputs, axis=1)


def reference(prompt_ssm, prompt_conv, prompt_of, step_in, conv_weight, conv_bias, x_weight, dt_weight, dt_bias, a_log, skip, send_rows, child_slot):
    start_ssm = prompt_ssm[prompt_of]
    start_conv = prompt_conv[prompt_of]
    states, windows, decoded = decode_steps(start_ssm, start_conv, step_in, conv_weight, conv_bias, x_weight, dt_weight, dt_bias, a_log, skip)
    target = (jnp.arange(BRANCHES) // RB).astype(jnp.int32)
    source = (child_slot // CAP).astype(jnp.int32)
    slot_in = (child_slot % CAP).astype(jnp.int32)
    parent = source * RB + send_rows[source, target, slot_in]
    return decoded, states[parent], windows[parent]
```

```python
import functools
import math

import jax
import jax.numpy as jnp
from jax import lax
from jax.experimental import pallas as pl
from jax.experimental.pallas import tpu as pltpu
from jax.sharding import PartitionSpec as P

F32 = jnp.float32
BF16 = jnp.bfloat16
LANES = 128
VMEM_LIMIT = 48 * 2**20
DIRECT_MOST = 4


def vmem():
    return pl.BlockSpec(memory_space=pltpu.VMEM)


def smem():
    return pl.BlockSpec(memory_space=pltpu.SMEM)


def call(kernel, outs, in_specs, out_specs, scratch=(), flops=0, nbytes=0, trans=0):
    return pl.pallas_call(
        kernel,
        out_shape=outs,
        in_specs=in_specs,
        out_specs=out_specs,
        scratch_shapes=list(scratch),
        compiler_params=pltpu.CompilerParams(vmem_limit_bytes=VMEM_LIMIT),
        cost_estimate=pl.CostEstimate(flops=flops, bytes_accessed=nbytes, transcendentals=trans),
    )


def shift_exchange(parts, axis):
    size = lax.axis_size(axis)
    got = [parts[0]]
    for shift in range(1, size):
        pairs = [(i, (i + shift) % size) for i in range(size)]
        got.append(lax.ppermute(parts[shift], axis, pairs))
    return got


def read_rows(refs, row):
    rows = [
        ref[i, row : row + 1, :].astype(F32) for ref in refs for i in range(ref.shape[0])
    ]
    return rows[0] if len(rows) == 1 else jnp.concatenate(rows, axis=0)


def pack_kernel(kernel_len, capacity, me_ref, rows_ref, prompt_ref, step_hbm, conv_ref, *rest):
    outs, (held, sems) = rest[:-2], rest[-2:]
    owners = rows_ref.shape[0]
    channels = conv_ref.shape[2]
    me = me_ref[0]
    copies, rows = [], []
    for shift in range(owners):
        target = lax.rem(me + shift, owners)
        for c in range(capacity):
            row = jnp.maximum(rows_ref[target, c], 0)
            slot = shift * capacity + c
            copy = pltpu.make_async_copy(step_hbm.at[row], held.at[slot], sems.at[slot])
            copy.start()
            copies.append(copy)
            rows.append(row)
    conv = conv_ref[0].astype(F32)
    for shift in range(owners):
        pieces = [conv]
        for c in range(capacity):
            slot = shift * capacity + c
            copies[slot].wait()
            pieces.append(held[slot, :, 0, :].astype(F32))
        for c in range(capacity):
            number = prompt_ref[rows[shift * capacity + c]].astype(F32)
            pieces.append(jnp.full((1, channels), number, F32))
        message = jnp.concatenate(pieces, axis=0).astype(BF16)
        ref = outs[shift] if len(outs) > 1 else outs[0]
        ref[shift if len(outs) == 1 else 0] = message


def own_onehot(prompt_ref, me, owners):
    rows = prompt_ref.shape[0]
    row_of = lax.broadcasted_iota(jnp.int32, (rows, owners), 0)
    column = lax.broadcasted_iota(jnp.int32, (rows, owners), 1)
    wanted = jnp.zeros((rows, owners), jnp.int32)
    for b in range(rows):
        wanted = jnp.where(row_of == b, lax.rem(me - prompt_ref[b] + owners, owners), wanted)
    return (wanted == column).astype(F32)


def slot_onehot(numbers, me, owners):
    column = lax.broadcasted_iota(jnp.int32, (numbers.shape[0], owners), 1)
    held_by = lax.rem(me - column + owners, owners)
    return (numbers[:, :owners].astype(jnp.int32) == held_by).astype(F32)


def silu(v):
    return v / (1.0 + jnp.exp(-v))


def project_kernel(
    n_msgs, steps, me_ref, prompt_ref, x_ref, cw_ref, cb_ref, xw_ref, *rest
):
    msgs, (act_ref, part_ref) = rest[:n_msgs], rest[n_msgs:]
    owners = sum(m.shape[0] for m in msgs)
    taps = cw_ref.shape[0]
    me = me_ref[0]
    rb = x_ref.shape[1]
    windows = [read_rows(msgs, k) for k in range(taps - 1)]
    slot_x = [read_rows(msgs, taps - 1 + t) for t in range(steps)]
    numbers = read_rows(msgs, taps - 1 + steps)
    own_pick = own_onehot(prompt_ref, me, owners).astype(BF16)
    slot_pick = slot_onehot(numbers, me, owners).astype(BF16)

    def pick(onehot, table):
        return jnp.dot(onehot, table.astype(BF16), preferred_element_type=F32)

    row = 0
    for onehot, xs in (
        (own_pick, [x_ref[t].astype(F32) for t in range(steps)]),
        (slot_pick, slot_x),
    ):
        count = onehot.shape[0]
        line = [pick(onehot, w) for w in windows] + xs
        for t in range(steps):
            conv = cw_ref[taps - 1 : taps, :] * line[t + taps - 1] + cb_ref[...]
            for k in range(taps - 1):
                conv = conv + cw_ref[k : k + 1, :] * line[t + k]
            act_ref[row : row + count, :] = silu(conv)
            row += count
    part_ref[...] = jnp.dot(
        act_ref[...].astype(BF16), xw_ref[...], preferred_element_type=F32
    )


def windows_kernel(n_msgs, taps, steps, me_ref, child_ref, *rest):
    msgs, (out_ref, held) = rest[:n_msgs], rest[n_msgs:]
    owners = sum(m.shape[0] for m in msgs)
    me = me_ref[0]
    first = taps - 1 + steps - (taps - 1)
    slot = 0
    for ref in msgs:
        for i in range(ref.shape[0]):
            held[slot] = ref[i].astype(F32)[first : first + taps - 1, :]
            slot += 1
    for j in range(out_ref.shape[0]):
        at = lax.rem(me - child_ref[j] + owners, owners)
        out_ref[j] = held[at].astype(BF16)


def decode_kernel(
    n_parts,
    n_msgs,
    n_ssm,
    steps,
    taps,
    me_ref,
    prompt_ref,
    child_ref,
    act_ref,
    z_ref,
    dtw_ref,
    dtb_ref,
    alog_ref,
    skip_ref,
    *rest,
):
    parts, rest = rest[:n_parts], rest[n_parts:]
    msgs, rest = rest[:n_msgs], rest[n_msgs:]
    ssms, rest = rest[:n_ssm], rest[n_ssm:]
    dec_ref, child_ssm, delta_s, gain_s, rate_s, b_s, c_s, slots_s, sems = rest
    owners = sum(m.shape[0] for m in msgs)
    me = me_ref[0]
    rb = dec_ref.shape[0]
    rank = dtw_ref.shape[0]
    n_state, channels = alog_ref.shape
    own_rows = steps * rb
    chunks = channels // LANES

    proj = parts[0][...]
    for ref in parts[1:]:
        proj = proj + ref[...]
    delta_in = proj[:, :rank].astype(BF16)
    delta = jnp.dot(delta_in, dtw_ref[...], preferred_element_type=F32) + dtb_ref[...]
    delta = jnp.maximum(delta, 0.0) + jnp.log1p(jnp.exp(-jnp.abs(delta)))
    delta_s[...] = delta
    gain_s[...] = delta * act_ref[...]
    rate_s[...] = jnp.exp(alog_ref[...]) * (-math.log2(math.e))
    rows = proj.shape[0]
    for n in range(n_state):
        b_s[n] = jnp.broadcast_to(proj[:, rank + n : rank + n + 1], (rows, LANES))
        c_s[n] = jnp.broadcast_to(
            proj[:own_rows, rank + n_state + n : rank + n_state + n + 1], (own_rows, LANES)
        )
    own_pick = own_onehot(prompt_ref, me, owners)
    numbers = read_rows(msgs, taps - 1 + steps)
    slot_pick = slot_onehot(numbers, me, owners)
    n_slots = slot_pick.shape[0]

    def start(pick, n, columns):
        total, k = None, 0
        for ref in ssms:
            for i in range(ref.shape[0]):
                row = ref[i, n : n + 1, columns]
                term = pick[:, k : k + 1] * row
                total = term if total is None else total + term
                k += 1
        return total

    def slot_chunk(chunk, carry):
        columns = pl.ds(pl.multiple_of(chunk * LANES, LANES), LANES)
        for n in range(n_state):
            rate = rate_s[n : n + 1, columns]
            state = start(slot_pick, n, columns)
            for t in range(steps):
                at = pl.ds(own_rows + t * n_slots, n_slots)
                state = (
                    jnp.exp2(delta_s[at, columns] * rate) * state
                    + gain_s[at, columns] * b_s[n, at, :]
                )
            slots_s[:, n, columns] = state
        return carry

    lax.fori_loop(0, chunks, slot_chunk, 0)
    copies = []
    for j in range(rb):
        at = lax.rem(me - child_ref[j] + owners, owners)
        copy = pltpu.make_async_copy(slots_s.at[at], child_ssm.at[j], sems.at[j])
        copy.start()
        copies.append(copy)

    def own_chunk(chunk, carry):
        columns = pl.ds(pl.multiple_of(chunk * LANES, LANES), LANES)
        sums = [None] * steps
        for n in range(n_state):
            rate = rate_s[n : n + 1, columns]
            state = start(own_pick, n, columns)
            for t in range(steps):
                at = pl.ds(t * rb, rb)
                state = (
                    jnp.exp2(delta_s[at, columns] * rate) * state
                    + gain_s[at, columns] * b_s[n, at, :]
                )
                term = c_s[n, at, :] * state
                sums[t] = term if sums[t] is None else sums[t] + term
        for t in range(steps):
            at = pl.ds(t * rb, rb)
            out = sums[t] + skip_ref[:, columns] * act_ref[at, columns]
            out = out * silu(z_ref[t, :, columns].astype(F32))
            dec_ref[:, t, columns] = out.astype(BF16)
        return carry

    lax.fori_loop(0, chunks, own_chunk, 0)
    for copy in copies:
        copy.wait()


def on_device(
    prompt_ssm,
    prompt_conv,
    prompt_of,
    step_in,
    conv_weight,
    conv_bias,
    x_weight,
    dt_weight,
    dt_bias,
    a_log,
    skip,
    send_rows,
    child_slot,
):
    owners = lax.axis_size("branch")
    capacity = send_rows.shape[2]
    assert prompt_ssm.shape[0] == 1 and capacity == 1
    rb, steps, _, channels = step_in.shape
    taps = conv_weight.shape[0]
    width = x_weight.shape[1]
    n_state = a_log.shape[0]
    n_slots = owners * capacity
    rows = steps * (rb + n_slots)
    depth = taps - 1 + capacity * (steps + 1)
    direct = owners <= DIRECT_MOST
    me = lax.axis_index("branch").astype(jnp.int32).reshape(1)

    if direct:
        msg_shapes = [jax.ShapeDtypeStruct((1, depth, channels), BF16)] * owners
    else:
        msg_shapes = [jax.ShapeDtypeStruct((owners, depth, channels), BF16)]
    msgs = call(
        functools.partial(pack_kernel, taps, capacity),
        msg_shapes,
        [smem(), smem(), smem(), pl.BlockSpec(memory_space=pl.ANY), vmem()],
        [vmem()] * len(msg_shapes),
        [
            pltpu.VMEM((n_slots,) + step_in.shape[1:], BF16),
            pltpu.SemaphoreType.DMA((n_slots,)),
        ],
        nbytes=n_slots * steps * channels * 4,
    )(me, send_rows[0], prompt_of, step_in, prompt_conv)
    x_own = jnp.transpose(step_in[:, :, 0], (1, 0, 2))
    z_own = jnp.transpose(step_in[:, :, 1], (1, 0, 2))

    if direct:
        msgs = shift_exchange(msgs, "branch")
        (prompt_later, msgs) = lax.optimization_barrier((prompt_ssm, msgs))
        ssms = shift_exchange([prompt_later] * owners, "branch")
    else:
        by_owner = jnp.roll(msgs[0], me[0], axis=0)
        came = lax.all_to_all(by_owner, "branch", split_axis=0, concat_axis=0, tiled=True)
        msgs = [jnp.roll(came[::-1], me[0] + 1, axis=0)]
        every = lax.all_gather(prompt_ssm, "branch", axis=0, tiled=True)
        ssms = [jnp.roll(every[::-1], me[0] + 1, axis=0)]

    n_msgs = len(msgs)
    act, part = call(
        functools.partial(project_kernel, n_msgs, steps),
        [
            jax.ShapeDtypeStruct((rows, channels), F32),
            jax.ShapeDtypeStruct((rows, width), F32),
        ],
        [smem(), smem()] + [vmem()] * (4 + n_msgs),
        [vmem()] * 2,
        flops=2 * rows * channels * width,
        nbytes=channels * width * 2 + rows * (channels + width) * 4,
        trans=rows * channels,
    )(me, prompt_of, x_own, conv_weight, conv_bias[None], x_weight, *msgs)
    parts = shift_exchange([part] * lax.axis_size("tensor"), "tensor")

    child_conv = call(
        functools.partial(windows_kernel, n_msgs, taps, steps),
        jax.ShapeDtypeStruct((rb, taps - 1, channels), BF16),
        [smem(), smem()] + [vmem()] * n_msgs,
        vmem(),
        [pltpu.VMEM((n_slots, taps - 1, channels), F32)],
        nbytes=rb * taps * channels * 2,
    )(me, child_slot, *msgs)

    decoded, child_ssm = call(
        functools.partial(decode_kernel, len(parts), n_msgs, len(ssms), steps, taps),
        [
            jax.ShapeDtypeStruct((rb, steps, channels), BF16),
            jax.ShapeDtypeStruct((rb, n_state, channels), F32),
        ],
        [smem()] * 3 + [vmem()] * (6 + len(parts) + n_msgs + len(ssms)),
        [vmem(), pl.BlockSpec(memory_space=pl.ANY)],
        [
            pltpu.VMEM((rows, channels), F32),
            pltpu.VMEM((rows, channels), F32),
            pltpu.VMEM((n_state, channels), F32),
            pltpu.VMEM((n_state, rows, LANES), F32),
            pltpu.VMEM((n_state, steps * rb, LANES), F32),
            pltpu.VMEM((n_slots, n_state, channels), F32),
            pltpu.SemaphoreType.DMA((rb,)),
        ],
        flops=8 * rows * n_state * channels,
        nbytes=(rb + owners) * n_state * channels * 4,
        trans=rows * n_state * channels,
    )(
        me,
        prompt_of,
        child_slot,
        act,
        z_own,
        dt_weight,
        dt_bias[None],
        a_log,
        skip[None],
        *parts,
        *msgs,
        *ssms,
    )
    return (decoded, child_ssm, child_conv)


def solution(mesh):
    placed = (
        P(("replica", "branch"), None, "tensor"),
        P(("replica", "branch"), None, "tensor"),
        P(("replica", "branch")),
        P(("replica", "branch"), None, None, "tensor"),
        P(None, "tensor"),
        P("tensor"),
        P("tensor", None),
        P(None, "tensor"),
        P("tensor"),
        P(None, "tensor"),
        P("tensor"),
        P(("replica", "branch"), None, None),
        P(("replica", "branch")),
    )
    return jax.shard_map(
        on_device,
        mesh=mesh,
        in_specs=placed,
        out_specs=(
            P(("replica", "branch"), None, "tensor"),
            P(("replica", "branch"), None, "tensor"),
            P(("replica", "branch"), None, "tensor"),
        ),
        check_vma=False,
    )
```

```python
import functools
import math

import jax
import jax.numpy as jnp
from jax import lax
from jax.experimental import pallas as pl
from jax.experimental.pallas import tpu as pltpu
from jax.sharding import PartitionSpec as P

F32 = jnp.float32
BF16 = jnp.bfloat16
LANES = 128
VMEM_LIMIT = 48 * 2**20
DIRECT_MOST = 4


def vmem():
    return pl.BlockSpec(memory_space=pltpu.VMEM)


def smem():
    return pl.BlockSpec(memory_space=pltpu.SMEM)


def hbm():
    return pl.BlockSpec(memory_space=pltpu.HBM)


def anywhere():
    return pl.BlockSpec(memory_space=pl.ANY)


def shaped(shape, dtype):
    return jax.ShapeDtypeStruct(shape, dtype)


def call(kernel, outs, in_specs, out_specs, scratch=(), flops=0, nbytes=0, trans=0):
    return pl.pallas_call(
        kernel,
        out_shape=outs,
        in_specs=in_specs,
        out_specs=out_specs,
        scratch_shapes=list(scratch),
        compiler_params=pltpu.CompilerParams(vmem_limit_bytes=VMEM_LIMIT),
        cost_estimate=pl.CostEstimate(flops=flops, bytes_accessed=nbytes, transcendentals=trans),
    )


def swap(value, axis, distance):
    size = lax.axis_size(axis)
    return lax.ppermute(value, axis, [(i, i ^ distance) for i in range(size)])


def blocks(refs):
    return [(ref, i) for ref in refs for i in range(ref.shape[0])]


def read_rows(refs, row):
    return jnp.concatenate(
        [ref[i, row : row + 1, :].astype(F32) for ref, i in blocks(refs)], axis=0
    )


def pick_rows(pick, rows):
    if len(rows) > DIRECT_MOST:
        table = jnp.concatenate(rows, axis=0).astype(BF16)
        return jnp.dot(pick.astype(BF16), table, preferred_element_type=F32)
    total = pick[:, 0:1] * rows[0]
    for k in range(1, len(rows)):
        total = total + pick[:, k : k + 1] * rows[k]
    return total


def pack_kernel(key_ref, rows_hbm, prompt_hbm, step_hbm, conv_hbm, ssm_hbm, *rest):
    outs, (rows_s, prompt_s, held, conv, ssm, sems, row_sems) = rest[:-7], rest[-7:]
    owners = rows_hbm.shape[0]
    channels = conv_hbm.shape[2]
    first = pltpu.make_async_copy(rows_hbm, rows_s, sems.at[0])
    others = [
        pltpu.make_async_copy(prompt_hbm, prompt_s, sems.at[1]),
        pltpu.make_async_copy(conv_hbm, conv, sems.at[2]),
        pltpu.make_async_copy(ssm_hbm, ssm, sems.at[3]),
    ]
    first.start()
    for copy in others:
        copy.start()
    first.wait()
    key = key_ref[0]
    copies, rows = [], []
    for k in range(owners):
        row = jnp.maximum(rows_s[jnp.bitwise_xor(key, k)], 0)
        copy = pltpu.make_async_copy(step_hbm.at[row], held.at[k], row_sems.at[k])
        copy.start()
        copies.append(copy)
        rows.append(row)
    for copy in others:
        copy.wait()
    fixed = [ssm[0], conv[0].astype(F32)]
    for k, (ref, i) in enumerate(blocks(outs)):
        copies[k].wait()
        xs = held[k, :, 0, :].astype(F32)
        number = jnp.full((1, channels), prompt_s[rows[k]].astype(F32), F32)
        ref[i] = jnp.concatenate(fixed + [xs, number], axis=0).astype(BF16)


def own_onehot(prompt_ref, key, owners):
    shape = (prompt_ref.shape[0], owners)
    row_of = lax.broadcasted_iota(jnp.int32, shape, 0)
    wanted = jnp.zeros(shape, jnp.int32)
    for b in range(shape[0]):
        wanted = jnp.where(row_of == b, jnp.bitwise_xor(prompt_ref[b], key), wanted)
    return (wanted == lax.broadcasted_iota(jnp.int32, shape, 1)).astype(F32)


def slot_onehot(numbers, key, owners):
    column = lax.broadcasted_iota(jnp.int32, (numbers.shape[0], owners), 1)
    held_by = jnp.bitwise_xor(column, key)
    return (numbers[:, :owners].astype(jnp.int32) == held_by).astype(F32)


def silu(v):
    return v / (1.0 + jnp.exp(-v))


def prepare_kernel(step_ref, cw_ref, cb_ref, after_ref, base_ref, gate_ref):
    del after_ref
    steps = step_ref.shape[1]
    taps = cw_ref.shape[0]
    xs = [step_ref[:, t, 0, :].astype(F32) for t in range(steps)]
    for t in range(steps):
        total = cw_ref[taps - 1 : taps, :] * xs[t] + cb_ref[...]
        for k in range(max(0, taps - 1 - t), taps - 1):
            total = total + cw_ref[k : k + 1, :] * xs[t + k - taps + 1]
        base_ref[t] = total
        gate_ref[t] = silu(step_ref[:, t, 1, :].astype(F32))


def project_kernel(n_msgs, n_state, key_ref, prompt_ref, base_ref, cw_ref, cb_ref, xwt_ref, *rest):
    msgs, (act_ref, part_ref, short_ref) = rest[:n_msgs], rest[n_msgs:]
    owners = sum(m.shape[0] for m in msgs)
    taps = cw_ref.shape[0]
    steps, rb, _ = base_ref.shape
    key = key_ref[0]
    past = taps - 1
    at_x = n_state + past
    windows = [
        [ref[i, n_state + k : n_state + k + 1, :].astype(F32) for ref, i in blocks(msgs)]
        for k in range(past)
    ]
    numbers = read_rows(msgs, at_x + steps)
    own = own_onehot(prompt_ref, key, owners)
    own_windows = [pick_rows(own, w) for w in windows]
    for t in range(steps):
        conv = base_ref[t]
        for k in range(past - t):
            conv = conv + cw_ref[k : k + 1, :] * own_windows[t + k]
        act_ref[t * rb : (t + 1) * rb, :] = silu(conv)
    slot = slot_onehot(numbers, key, owners)
    line = [pick_rows(slot, w) for w in windows]
    line += [read_rows(msgs, at_x + t) for t in range(steps)]
    row = steps * rb
    for t in range(steps):
        conv = cw_ref[past:taps, :] * line[t + past] + cb_ref[...]
        for k in range(past):
            conv = conv + cw_ref[k : k + 1, :] * line[t + k]
        act_ref[row : row + owners, :] = silu(conv)
        row += owners
    part = lax.dot_general(
        act_ref[...].astype(BF16),
        xwt_ref[...],
        (((1,), (1,)), ((), ())),
        preferred_element_type=F32,
    )
    part_ref[...] = part
    short_ref[...] = part.astype(BF16)


def start_kernel(
    n_msgs, taps, steps, key_ref, prompt_ref, child_ref, alog_ref, after_ref, *rest
):
    del after_ref
    msgs, (own_ref, slot_ref, rate_ref, conv_ref, held) = rest[:n_msgs], rest[n_msgs:]
    owners = sum(m.shape[0] for m in msgs)
    key = key_ref[0]
    n_state = own_ref.shape[0]
    past = taps - 1
    rate_ref[...] = jnp.exp(alog_ref[...]) * (-math.log2(math.e))
    own = own_onehot(prompt_ref, key, owners)
    slot = slot_onehot(read_rows(msgs, n_state + past + steps), key, owners)
    for n in range(n_state):
        rows = [ref[i, n : n + 1, :].astype(F32) for ref, i in blocks(msgs)]
        own_ref[n] = pick_rows(own, rows)
        slot_ref[n] = pick_rows(slot, rows)
    first = n_state + past + steps - past
    for k, (ref, i) in enumerate(blocks(msgs)):
        held[k] = ref[i].astype(F32)[first : first + past, :]
    for j in range(child_ref.shape[0]):
        window = held[jnp.bitwise_xor(child_ref[j], key)].astype(BF16)
        for k in range(past):
            conv_ref[k, j : j + 1, :] = window[k : k + 1, :]


def decode_kernel(
    n_parts,
    key_ref,
    child_ref,
    act_ref,
    gate_ref,
    own_ref,
    slot_ref,
    rate_ref,
    dtw_ref,
    dtb_ref,
    skip_ref,
    *rest,
):
    parts, rest = rest[:n_parts], rest[n_parts:]
    dec_ref, child_ssm, delta_s, gain_s, b_s, c_s, slots_s, line_s, sems = rest
    key = key_ref[0]
    rb, steps, channels = dec_ref.shape
    rank = dtw_ref.shape[0]
    n_state, n_slots, _ = slot_ref.shape
    own_rows = steps * rb
    chunks = channels // LANES

    proj = parts[0][...]
    for ref in parts[1:]:
        proj = proj + ref[...].astype(F32)
    delta_in = proj[:, :rank].astype(BF16)
    delta = jnp.dot(delta_in, dtw_ref[...], preferred_element_type=F32) + dtb_ref[...]
    delta = jnp.maximum(delta, 0.0) + jnp.log1p(jnp.exp(-jnp.abs(delta)))
    delta_s[...] = delta
    gain_s[...] = delta * act_ref[...]
    rows = proj.shape[0]
    for n in range(n_state):
        b_s[n] = jnp.broadcast_to(proj[:, rank + n : rank + n + 1], (rows, LANES))
        c_s[n] = jnp.broadcast_to(
            proj[:own_rows, rank + n_state + n : rank + n_state + n + 1], (own_rows, LANES)
        )

    def step(state, rate, n, at, columns):
        decay = jnp.exp2(delta_s[at, columns] * rate)
        return decay * state + gain_s[at, columns] * b_s[n, at, :]

    def slot_chunk(chunk, carry):
        columns = pl.ds(pl.multiple_of(chunk * LANES, LANES), LANES)
        for n in range(n_state):
            rate = rate_ref[n : n + 1, columns]
            state = slot_ref[n, :, columns]
            for t in range(steps):
                state = step(state, rate, n, pl.ds(own_rows + t * n_slots, n_slots), columns)
            slots_s[:, n, columns] = state
        return carry

    lax.fori_loop(0, chunks, slot_chunk, 0)
    copies = []
    for j in range(rb):
        at = jnp.bitwise_xor(child_ref[j], key)
        copy = pltpu.make_async_copy(slots_s.at[at], child_ssm.at[j], sems.at[j])
        copy.start()
        copies.append(copy)

    def own_chunk(chunk, carry):
        columns = pl.ds(pl.multiple_of(chunk * LANES, LANES), LANES)
        sums = [None] * steps
        for n in range(n_state):
            rate = rate_ref[n : n + 1, columns]
            state = own_ref[n, :, columns]
            for t in range(steps):
                at = pl.ds(t * rb, rb)
                state = step(state, rate, n, at, columns)
                term = c_s[n, at, :] * state
                sums[t] = term if sums[t] is None else sums[t] + term
        for t in range(steps):
            out = sums[t] + skip_ref[:, columns] * act_ref[pl.ds(t * rb, rb), columns]
            line_s[pl.ds(t, rb, stride=steps), :] = out * gate_ref[t, :, columns]
        dec_ref[:, :, columns] = line_s[...].reshape(rb, steps, LANES).astype(BF16)
        return carry

    lax.fori_loop(0, chunks, own_chunk, 0)
    for copy in copies:
        copy.wait()


def on_device(
    prompt_ssm,
    prompt_conv,
    prompt_of,
    step_in,
    conv_weight,
    conv_bias,
    x_weight,
    dt_weight,
    dt_bias,
    a_log,
    skip,
    send_rows,
    child_slot,
):
    owners = lax.axis_size("branch")
    tensors = lax.axis_size("tensor")
    assert owners & (owners - 1) == 0 and tensors & (tensors - 1) == 0
    assert prompt_ssm.shape[0] == 1 and send_rows.shape[2] == 1
    rb, steps, _, channels = step_in.shape
    taps = conv_weight.shape[0]
    width = x_weight.shape[1]
    n_state = a_log.shape[0]
    rows = steps * (rb + owners)
    depth = n_state + taps - 1 + steps + 1
    direct = owners <= DIRECT_MOST
    me = lax.axis_index("branch").astype(jnp.int32).reshape(1)
    key = me if direct else jnp.zeros((1,), jnp.int32)
    conv_bias, dt_bias, skip = conv_bias[None], dt_bias[None], skip[None]

    msg_shapes = [(1, depth, channels)] * owners if direct else [(owners, depth, channels)]
    msgs = call(
        pack_kernel,
        [shaped(s, BF16) for s in msg_shapes],
        [smem()] + [hbm()] * 5,
        [vmem()] * len(msg_shapes),
        [
            pltpu.SMEM((owners,), jnp.int32),
            pltpu.SMEM((rb,), jnp.int32),
            pltpu.VMEM((owners,) + step_in.shape[1:], BF16),
            pltpu.VMEM(prompt_conv.shape, BF16),
            pltpu.VMEM(prompt_ssm.shape, F32),
            pltpu.SemaphoreType.DMA((4,)),
            pltpu.SemaphoreType.DMA((owners,)),
        ],
        nbytes=owners * depth * channels * 2,
    )(key, send_rows.reshape(owners), prompt_of, step_in, prompt_conv, prompt_ssm)
    base, gate = call(
        prepare_kernel,
        [shaped((steps, rb, channels), F32)] * 2,
        [vmem()] * 3 + [anywhere()],
        [vmem()] * 2,
        flops=10 * steps * rb * channels,
        nbytes=12 * steps * rb * channels,
        trans=steps * rb * channels,
    )(step_in, conv_weight, conv_bias, msgs[0])
    if direct:
        msgs = [msgs[0]] + [swap(msgs[k], "branch", k) for k in range(1, owners)]
    else:
        msgs = [lax.all_to_all(msgs[0], "branch", split_axis=0, concat_axis=0, tiled=True)]

    n_msgs = len(msgs)
    act, part, short = call(
        functools.partial(project_kernel, n_msgs, n_state),
        [
            shaped((rows, channels), F32),
            shaped((rows, width), F32),
            shaped((rows, width), BF16),
        ],
        [smem(), smem()] + [vmem()] * (4 + n_msgs),
        [vmem()] * 3,
        flops=2 * rows * channels * width,
        nbytes=channels * width * 2 + rows * (channels + width) * 4,
        trans=rows * channels,
    )(key, prompt_of, base, conv_weight, conv_bias, x_weight.T, *msgs)
    parts = [part, swap(part, "tensor", 1)]
    parts += [swap(short, "tensor", k) for k in range(2, tensors)]

    own_start, slot_start, rate, child_conv = call(
        functools.partial(start_kernel, n_msgs, taps, steps),
        [
            shaped((n_state, rb, channels), F32),
            shaped((n_state, owners, channels), F32),
            shaped((n_state, channels), F32),
            shaped((taps - 1, rb, channels), BF16),
        ],
        [smem()] * 3 + [vmem(), anywhere()] + [vmem()] * n_msgs,
        [vmem()] * 4,
        [pltpu.VMEM((owners, taps - 1, channels), F32)],
        flops=6 * n_state * (rb + owners) * channels,
        nbytes=4 * n_state * (rb + owners) * channels,
    )(key, prompt_of, child_slot, a_log, act, *msgs)

    decoded, child_ssm = call(
        functools.partial(decode_kernel, len(parts)),
        [
            shaped((rb, steps, channels), BF16),
            shaped((rb, n_state, channels), F32),
        ],
        [smem()] * 2 + [vmem()] * (8 + len(parts)),
        [vmem(), anywhere()],
        [
            pltpu.VMEM((rows, channels), F32),
            pltpu.VMEM((rows, channels), F32),
            pltpu.VMEM((n_state, rows, LANES), F32),
            pltpu.VMEM((n_state, steps * rb, LANES), F32),
            pltpu.VMEM((owners, n_state, channels), F32),
            pltpu.VMEM((steps * rb, LANES), F32),
            pltpu.SemaphoreType.DMA((rb,)),
        ],
        flops=8 * rows * n_state * channels,
        nbytes=(rb + owners) * n_state * channels * 4,
        trans=rows * n_state * channels,
    )(
        key,
        child_slot,
        act,
        gate,
        own_start,
        slot_start,
        rate,
        dt_weight,
        dt_bias,
        skip,
        *parts,
    )
    return (decoded, child_ssm, jnp.transpose(child_conv, (1, 0, 2)))


def solution(mesh):
    placed = (
        P(("replica", "branch"), None, "tensor"),
        P(("replica", "branch"), None, "tensor"),
        P(("replica", "branch")),
        P(("replica", "branch"), None, None, "tensor"),
        P(None, "tensor"),
        P("tensor"),
        P("tensor", None),
        P(None, "tensor"),
        P("tensor"),
        P(None, "tensor"),
        P("tensor"),
        P(("replica", "branch"), None, None),
        P(("replica", "branch")),
    )
    return jax.shard_map(
        on_device,
        mesh=mesh,
        in_specs=placed,
        out_specs=(
            P(("replica", "branch"), None, "tensor"),
            P(("replica", "branch"), None, "tensor"),
            P(("replica", "branch"), None, "tensor"),
        ),
        check_vma=False,
    )
```

```python
import functools
import math

import jax
import jax.numpy as jnp
from jax import lax
from jax.experimental import pallas as pl
from jax.experimental.pallas import tpu as pltpu
from jax.sharding import PartitionSpec as P

F32 = jnp.float32
BF16 = jnp.bfloat16
LANES = 128
VMEM_LIMIT = 48 * 2**20
DIRECT = 4


def vmem():
    return pl.BlockSpec(memory_space=pltpu.VMEM)


def smem():
    return pl.BlockSpec(memory_space=pltpu.SMEM)


def hbm():
    return pl.BlockSpec(memory_space=pltpu.HBM)


def anywhere():
    return pl.BlockSpec(memory_space=pl.ANY)


def pinned(array):
    return pltpu.with_memory_space_constraint(array, pltpu.HBM)


def shaped(shape, dtype):
    return jax.ShapeDtypeStruct(shape, dtype)


def call(kernel, outs, in_specs, out_specs, scratch=(), flops=0, nbytes=0, trans=0):
    return pl.pallas_call(
        kernel,
        out_shape=outs,
        in_specs=in_specs,
        out_specs=out_specs,
        scratch_shapes=list(scratch),
        compiler_params=pltpu.CompilerParams(vmem_limit_bytes=VMEM_LIMIT),
        cost_estimate=pl.CostEstimate(flops=flops, bytes_accessed=nbytes, transcendentals=trans),
    )


def swap(value, axis, distance):
    size = lax.axis_size(axis)
    return lax.ppermute(value, axis, [(i, i ^ distance) for i in range(size)])


def all_of(copies):
    for copy in copies:
        copy.start()
    for copy in copies:
        copy.wait()


def blocks(refs):
    return [(ref, i) for ref in refs for i in range(ref.shape[0])]


def pick_rows(pick, rows):
    total = pick[:, 0:1] * rows[0]
    for k in range(1, len(rows)):
        total = total + pick[:, k : k + 1] * rows[k]
    return total


def pack_kernel(direct, key_ref, rows_hbm, prompt_hbm, step_hbm, conv_hbm, ssm_hbm, *rest):
    outs, (rows_s, prompt_s, step, conv, ssm, sems) = rest[:-6], rest[-6:]
    owners = rows_hbm.shape[0]
    rb, _, _, channels = step_hbm.shape
    part = rb // 4
    copies = [
        pltpu.make_async_copy(rows_hbm, rows_s, sems.at[0]),
        pltpu.make_async_copy(prompt_hbm, prompt_s, sems.at[1]),
        pltpu.make_async_copy(conv_hbm, conv, sems.at[2]),
        pltpu.make_async_copy(ssm_hbm, ssm, sems.at[3]),
    ]
    for i in range(4):
        some = pl.ds(i * part, part)
        copies.append(pltpu.make_async_copy(step_hbm.at[some], step.at[some], sems.at[4 + i]))
    all_of(copies)
    key = key_ref[0]
    window = conv[0].astype(F32)
    for k, (ref, i) in enumerate(blocks(outs)):
        target = jnp.bitwise_xor(key, k)
        row = jnp.maximum(rows_s[target], 0)
        xs = step[row, :, 0, :].astype(F32)
        told = jnp.bitwise_xor(prompt_s[row], target) if direct else prompt_s[row]
        pieces = [window, xs, jnp.full((1, channels), told.astype(F32), F32)]
        if ref.shape[1] > sum(p.shape[0] for p in pieces):
            pieces.append(ssm[0])
        ref[i] = jnp.concatenate(pieces, axis=0).astype(BF16)


def silu(v):
    return v / (1.0 + jnp.exp(-v))


def prepare_kernel(
    key_ref, prompt_ref, step_ref, cw_hbm, cb_hbm, xwt_hbm, after_ref, *rest
):
    del after_ref
    base_ref, gate_ref, pick_ref, cw_ref, cb_ref, xwt_ref, sems = rest
    copies = [
        pltpu.make_async_copy(cw_hbm, cw_ref, sems.at[0]),
        pltpu.make_async_copy(cb_hbm, cb_ref, sems.at[1]),
        pltpu.make_async_copy(xwt_hbm, xwt_ref, sems.at[2]),
    ]
    for copy in copies:
        copy.start()
    steps = step_ref.shape[1]
    taps = cw_hbm.shape[0]
    shape = pick_ref.shape
    row_of = lax.broadcasted_iota(jnp.int32, shape, 0)
    wanted = jnp.zeros(shape, jnp.int32)
    for b in range(shape[0]):
        wanted = jnp.where(row_of == b, jnp.bitwise_xor(prompt_ref[b], key_ref[0]), wanted)
    pick_ref[...] = (wanted == lax.broadcasted_iota(jnp.int32, shape, 1)).astype(F32)
    xs = [step_ref[:, t, 0, :].astype(F32) for t in range(steps)]
    for t in range(steps):
        gate_ref[t] = silu(step_ref[:, t, 1, :].astype(F32))
    copies[0].wait()
    copies[1].wait()
    for t in range(steps):
        total = cw_ref[taps - 1 : taps, :] * xs[t] + cb_ref[...]
        for k in range(max(0, taps - 1 - t), taps - 1):
            total = total + cw_ref[k : k + 1, :] * xs[t + k - taps + 1]
        base_ref[t] = total
    copies[2].wait()


def slot_onehot(numbers, owners):
    column = lax.broadcasted_iota(jnp.int32, (numbers.shape[0], owners), 1)
    return (numbers[:, :owners].astype(jnp.int32) == column).astype(F32)


def project_kernel(n_msgs, pick_ref, base_ref, cw_ref, cb_ref, xwt_ref, *rest):
    msgs, outs = rest[:n_msgs], rest[n_msgs:]
    act_ref, part_ref = outs[:2]
    taps = cw_ref.shape[0]
    steps, rb, _ = base_ref.shape
    past = taps - 1
    text = past + steps + 1
    held = [ref[i].astype(F32) for ref, i in blocks(msgs)]
    owners = len(held)
    windows = [[h[k : k + 1, :] for h in held] for k in range(past)]
    own = pick_ref[...]
    own_windows = [pick_rows(own, w) for w in windows]
    for t in range(steps):
        conv = base_ref[t]
        for k in range(past - t):
            conv = conv + cw_ref[k : k + 1, :] * own_windows[t + k]
        act_ref[t * rb : (t + 1) * rb, :] = silu(conv)

    def line_of(row):
        return jnp.concatenate([h[row : row + 1, :] for h in held], axis=0)

    slot = slot_onehot(line_of(past + steps), owners)
    line = [pick_rows(slot, w) for w in windows]
    line += [line_of(past + t) for t in range(steps)]
    row = steps * rb
    for t in range(steps):
        conv = cw_ref[past:taps, :] * line[t + past] + cb_ref[...]
        for k in range(past):
            conv = conv + cw_ref[k : k + 1, :] * line[t + k]
        act_ref[row : row + owners, :] = silu(conv)
        row += owners
    part_ref[...] = lax.dot_general(
        act_ref[...].astype(BF16),
        xwt_ref[...],
        (((1,), (1,)), ((), ())),
        preferred_element_type=F32,
    )
    for pair_ref in outs[2:]:
        states = [held[0][text:, :], held[1][text:, :]]
        pair_ref[0] = jnp.concatenate(states, axis=0).astype(BF16)


def add_kernel(a_ref, b_ref, sum_ref, short_ref):
    total = a_ref[...] + b_ref[...].astype(F32)
    sum_ref[...] = total
    short_ref[...] = total.astype(BF16)


def late_kernel(
    n_msgs, taps, key_ref, child_ref, alog_ref, dtw_hbm, dtb_hbm, skip_hbm, after_ref, *rest
):
    del after_ref
    msgs, rest = rest[:n_msgs], rest[n_msgs:]
    rate_ref, conv_ref, dtw_ref, dtb_ref, skip_ref, held, sems = rest
    copies = [
        pltpu.make_async_copy(dtw_hbm, dtw_ref, sems.at[0]),
        pltpu.make_async_copy(dtb_hbm, dtb_ref, sems.at[1]),
        pltpu.make_async_copy(skip_hbm, skip_ref, sems.at[2]),
    ]
    for copy in copies:
        copy.start()
    rate_ref[...] = jnp.exp(alog_ref[...]) * (-math.log2(math.e))
    past, rb, _ = conv_ref.shape
    steps = held.shape[1]
    for k, (ref, i) in enumerate(blocks(msgs)):
        held[k] = ref[i].astype(F32)[past : past + steps, :]
    for j in range(rb):
        window = held[jnp.bitwise_xor(child_ref[j], key_ref[0])].astype(BF16)
        for k in range(past):
            at = steps - past + k
            conv_ref[k, j : j + 1, :] = window[at : at + 1, :]
    for copy in copies:
        copy.wait()


def decode_kernel(
    n_msgs,
    pair,
    taps,
    key_ref,
    child_ref,
    pick_ref,
    act_ref,
    gate_ref,
    rate_ref,
    dtw_ref,
    dtb_ref,
    skip_ref,
    part_ref,
    other_ref,
    *rest,
):
    msgs, rest = rest[:n_msgs], rest[n_msgs:]
    pairs, rest = rest[:pair], rest[pair:]
    dec_ref, child_ssm, delta_s, gain_s, b_s, c_s, start_s, slots_s, line_s, sems = rest
    key = key_ref[0]
    rb, steps, channels = dec_ref.shape
    rank = dtw_ref.shape[0]
    n_state = rate_ref.shape[0]
    n_slots = slots_s.shape[0]
    own_rows = steps * rb
    rows = own_rows + steps * n_slots
    chunks = channels // LANES
    past = taps - 1
    text = past + steps + 1

    proj = part_ref[...] + other_ref[...].astype(F32)
    delta_in = proj[:, :rank].astype(BF16)
    delta = jnp.dot(delta_in, dtw_ref[...], preferred_element_type=F32) + dtb_ref[...]
    delta = jnp.maximum(delta, 0.0) + jnp.log1p(jnp.exp(-jnp.abs(delta)))
    delta_s[...] = delta
    gain_s[...] = delta * act_ref[...]
    for n in range(n_state):
        b_s[n] = jnp.broadcast_to(proj[:, rank + n : rank + n + 1], (rows, LANES))
        c_s[n] = jnp.broadcast_to(
            proj[:own_rows, rank + n_state + n : rank + n_state + n + 1], (own_rows, LANES)
        )

    held = [ref[i].astype(F32) for ref, i in blocks(msgs)]
    numbers = jnp.concatenate([h[text - 1 : text, :] for h in held], axis=0)
    states = [h[text:, :] for h in held if h.shape[0] > text]
    for ref in pairs:
        both = ref[0].astype(F32)
        states += [both[:n_state, :], both[n_state:, :]]
    for k, state in enumerate(states):
        start_s[k] = state

    def masks(pick):
        wide = (pick.shape[0], LANES)
        return [jnp.broadcast_to(pick[:, k : k + 1], wide) for k in range(n_slots)]

    own_masks = masks(pick_ref[...])
    slot_masks = masks(slot_onehot(numbers, n_slots))

    def start(mask, n, columns):
        total = mask[0] * start_s[0, n : n + 1, columns]
        for k in range(1, n_slots):
            total = total + mask[k] * start_s[k, n : n + 1, columns]
        return total

    def slot_chunk(chunk, carry):
        columns = pl.ds(pl.multiple_of(chunk * LANES, LANES), LANES)
        at = [pl.ds(own_rows + t * n_slots, n_slots) for t in range(steps)]
        delta = [delta_s[a, columns] for a in at]
        gain = [gain_s[a, columns] for a in at]
        for n in range(n_state):
            rate = rate_ref[n : n + 1, columns]
            state = start(slot_masks, n, columns)
            for t in range(steps):
                state = jnp.exp2(delta[t] * rate) * state + gain[t] * b_s[n, at[t], :]
            slots_s[:, n, columns] = state
        return carry

    lax.fori_loop(0, chunks, slot_chunk, 0)
    copies = []
    for j in range(rb):
        at = jnp.bitwise_xor(child_ref[j], key)
        copy = pltpu.make_async_copy(slots_s.at[at], child_ssm.at[j], sems.at[j])
        copy.start()
        copies.append(copy)

    def own_chunk(chunk, carry):
        columns = pl.ds(pl.multiple_of(chunk * LANES, LANES), LANES)
        at = [pl.ds(t * rb, rb) for t in range(steps)]
        delta = [delta_s[a, columns] for a in at]
        gain = [gain_s[a, columns] for a in at]
        sums = [skip_ref[:, columns] * act_ref[a, columns] for a in at]
        for n in range(n_state):
            rate = rate_ref[n : n + 1, columns]
            state = start(own_masks, n, columns)
            for t in range(steps):
                state = jnp.exp2(delta[t] * rate) * state + gain[t] * b_s[n, at[t], :]
                sums[t] = sums[t] + c_s[n, at[t], :] * state
        for t in range(steps):
            line_s[pl.ds(t, rb, stride=steps), :] = sums[t] * gate_ref[t, :, columns]
        dec_ref[:, :, columns] = line_s[...].reshape(rb, steps, LANES).astype(BF16)
        return carry

    lax.fori_loop(0, chunks, own_chunk, 0)
    for copy in copies:
        copy.wait()


def on_device(
    prompt_ssm,
    prompt_conv,
    prompt_of,
    step_in,
    conv_weight,
    conv_bias,
    x_weight,
    dt_weight,
    dt_bias,
    a_log,
    skip,
    send_rows,
    child_slot,
):
    owners = lax.axis_size("branch")
    tensors = lax.axis_size("tensor")
    assert owners & (owners - 1) == 0 and tensors & (tensors - 1) == 0
    assert prompt_ssm.shape[0] == 1 and send_rows.shape[2] == 1
    rb, steps, _, channels = step_in.shape
    taps = conv_weight.shape[0]
    width = x_weight.shape[1]
    n_state = a_log.shape[0]
    rows = steps * (rb + owners)
    short = taps - 1 + steps + 1
    depth = short + n_state
    direct = owners == DIRECT
    me = lax.axis_index("branch").astype(jnp.int32).reshape(1)
    key = me if direct else jnp.zeros((1,), jnp.int32)

    if direct:
        msg_shapes = [(1, d, channels) for d in (depth, depth, short, short)]
    else:
        msg_shapes = [(owners, depth, channels)]
    msgs = call(
        functools.partial(pack_kernel, direct),
        [shaped(s, BF16) for s in msg_shapes],
        [smem()] + [hbm()] * 5,
        [vmem()] * len(msg_shapes),
        [
            pltpu.SMEM((owners,), jnp.int32),
            pltpu.SMEM((rb,), jnp.int32),
            pltpu.VMEM(step_in.shape, BF16),
            pltpu.VMEM(prompt_conv.shape, BF16),
            pltpu.VMEM(prompt_ssm.shape, F32),
            pltpu.SemaphoreType.DMA((8,)),
        ],
        nbytes=owners * depth * channels * 2,
    )(
        key,
        pinned(send_rows.reshape(owners)),
        pinned(prompt_of),
        pinned(step_in),
        pinned(prompt_conv),
        pinned(prompt_ssm),
    )
    base, gate, pick, taps_near, bias_near, weight_near = call(
        prepare_kernel,
        [
            shaped((steps, rb, channels), F32),
            shaped((steps, rb, channels), F32),
            shaped((rb, owners), F32),
            shaped((taps, channels), F32),
            shaped((1, channels), F32),
            shaped((width, channels), BF16),
        ],
        [smem(), smem(), vmem(), hbm(), hbm(), hbm(), anywhere()],
        [vmem()] * 6,
        [pltpu.SemaphoreType.DMA((3,))],
        flops=10 * steps * rb * channels,
        nbytes=12 * steps * rb * channels,
        trans=steps * rb * channels,
    )(
        key,
        prompt_of,
        step_in,
        pinned(conv_weight),
        pinned(conv_bias[None]),
        pinned(x_weight.T),
        msgs[0],
    )
    if direct:
        msgs = [msgs[0]] + [swap(msgs[k], "branch", k) for k in range(1, owners)]
    else:
        msgs = [lax.all_to_all(msgs[0], "branch", split_axis=0, concat_axis=0, tiled=True)]

    n_msgs = len(msgs)
    pair_shapes = [(1, 2 * n_state, channels)] if direct else []
    act, part, *pairs = call(
        functools.partial(project_kernel, n_msgs),
        [
            shaped((rows, channels), F32),
            shaped((rows, width), F32),
        ]
        + [shaped(s, BF16) for s in pair_shapes],
        [vmem()] * (5 + n_msgs),
        [vmem()] * (2 + len(pair_shapes)),
        flops=2 * rows * channels * width,
        nbytes=channels * width * 2 + rows * (channels + width) * 4,
        trans=rows * channels,
    )(pick, base, taps_near, bias_near, weight_near, *msgs)
    other = swap(part, "tensor", 1)
    pairs = [swap(p, "branch", 2) for p in pairs]
    distance = 2
    while distance < tensors:
        part, brief = call(
            add_kernel,
            [shaped((rows, width), F32), shaped((rows, width), BF16)],
            [vmem()] * 2,
            [vmem()] * 2,
            flops=rows * width,
            nbytes=rows * width * 14,
        )(part, other)
        other = swap(brief, "tensor", distance)
        distance *= 2

    rate, child_conv, dtw_near, dtb_near, skip_near = call(
        functools.partial(late_kernel, n_msgs, taps),
        [
            shaped((n_state, channels), F32),
            shaped((taps - 1, rb, channels), BF16),
            shaped(dt_weight.shape, BF16),
            shaped((1, channels), F32),
            shaped((1, channels), F32),
        ],
        [smem()] * 2 + [vmem()] + [hbm()] * 3 + [anywhere()] + [vmem()] * n_msgs,
        [vmem()] * 5,
        [
            pltpu.VMEM((owners, steps, channels), F32),
            pltpu.SemaphoreType.DMA((3,)),
        ],
        flops=4 * n_state * channels,
        nbytes=4 * n_state * (rb + owners) * channels,
    )(
        key,
        child_slot,
        a_log,
        pinned(dt_weight),
        pinned(dt_bias[None]),
        pinned(skip[None]),
        part,
        *msgs,
    )

    decoded, child_ssm = call(
        functools.partial(decode_kernel, n_msgs, len(pairs), taps),
        [
            shaped((rb, steps, channels), BF16),
            shaped((rb, n_state, channels), F32),
        ],
        [smem()] * 2 + [vmem()] * (9 + n_msgs + len(pairs)),
        [vmem(), anywhere()],
        [
            pltpu.VMEM((rows, channels), F32),
            pltpu.VMEM((rows, channels), F32),
            pltpu.VMEM((n_state, rows, LANES), F32),
            pltpu.VMEM((n_state, steps * rb, LANES), F32),
            pltpu.VMEM((owners, n_state, channels), F32),
            pltpu.VMEM((owners, n_state, channels), F32),
            pltpu.VMEM((steps * rb, LANES), F32),
            pltpu.SemaphoreType.DMA((rb,)),
        ],
        flops=8 * rows * n_state * channels,
        nbytes=(rb + owners) * n_state * channels * 4,
        trans=rows * n_state * channels,
    )(
        key,
        child_slot,
        pick,
        act,
        gate,
        rate,
        dtw_near,
        dtb_near,
        skip_near,
        part,
        other,
        *msgs,
        *pairs,
    )
    return (decoded, child_ssm, jnp.transpose(child_conv, (1, 0, 2)))


def solution(mesh):
    placed = (
        P(("replica", "branch"), None, "tensor"),
        P(("replica", "branch"), None, "tensor"),
        P(("replica", "branch")),
        P(("replica", "branch"), None, None, "tensor"),
        P(None, "tensor"),
        P("tensor"),
        P("tensor", None),
        P(None, "tensor"),
        P("tensor"),
        P(None, "tensor"),
        P("tensor"),
        P(("replica", "branch"), None, None),
        P(("replica", "branch")),
    )
    return jax.shard_map(
        on_device,
        mesh=mesh,
        in_specs=placed,
        out_specs=(
            P(("replica", "branch"), None, "tensor"),
            P(("replica", "branch"), None, "tensor"),
            P(("replica", "branch"), None, "tensor"),
        ),
        check_vma=False,
    )
```

```python
import functools
import math

import jax
import jax.numpy as jnp
from jax import lax
from jax.experimental import pallas as pl
from jax.experimental.pallas import tpu as pltpu
from jax.sharding import PartitionSpec as P

F32 = jnp.float32
BF16 = jnp.bfloat16
LANES = 128
VMEM_LIMIT = 48 * 2**20
WEIGHT_PARTS = 6
DT_PARTS = 4
DIRECT = 4


def vmem():
    return pl.BlockSpec(memory_space=pltpu.VMEM)


def hbm():
    return pl.BlockSpec(memory_space=pltpu.HBM)


def anywhere():
    return pl.BlockSpec(memory_space=pl.ANY)


def pinned(array):
    return pltpu.with_memory_space_constraint(array, pltpu.HBM)


def shaped(shape, dtype):
    return jax.ShapeDtypeStruct(shape, dtype)


def call(kernel, outs, in_specs, out_specs, scratch=(), flops=0, nbytes=0, trans=0):
    return pl.pallas_call(
        kernel,
        out_shape=outs,
        in_specs=in_specs,
        out_specs=out_specs,
        scratch_shapes=list(scratch),
        compiler_params=pltpu.CompilerParams(vmem_limit_bytes=VMEM_LIMIT),
        cost_estimate=pl.CostEstimate(flops=flops, bytes_accessed=nbytes, transcendentals=trans),
    )


def swap(value, axis, distance):
    size = lax.axis_size(axis)
    return lax.ppermute(value, axis, [(i, i ^ distance) for i in range(size)])


def all_of(copies):
    for copy in copies:
        copy.start()
    for copy in copies:
        copy.wait()


def blocks(refs):
    return [(ref, i) for ref in refs for i in range(ref.shape[0])]


def in_parts(source, target, sems, first, count):
    rows = source.shape[0] // count
    at = [pl.ds(i * rows, rows) for i in range(count)]
    return [
        pltpu.make_async_copy(source.at[a], target.at[a], sems.at[first + i])
        for i, a in enumerate(at)
    ]


def scalar_onehot(numbers_s, key, shape):
    row_of = lax.broadcasted_iota(jnp.int32, shape, 0)
    wanted = jnp.zeros(shape, jnp.int32)
    for b in range(shape[0]):
        wanted = jnp.where(row_of == b, jnp.bitwise_xor(numbers_s[b], key), wanted)
    return (wanted == lax.broadcasted_iota(jnp.int32, shape, 1)).astype(F32)


def pick_rows(pick, rows):
    total = pick[:, 0:1] * rows[0]
    for k in range(1, len(rows)):
        total = total + pick[:, k : k + 1] * rows[k]
    return total


def pack_kernel(direct, key_hbm, rows_hbm, prompt_hbm, step_hbm, conv_hbm, ssm_hbm, *rest):
    outs, (key_s, rows_s, prompt_s, step, conv, ssm, sems) = rest[:-7], rest[-7:]
    owners = rows_hbm.shape[0]
    channels = step_hbm.shape[3]
    copies = [
        pltpu.make_async_copy(key_hbm, key_s, sems.at[4]),
        pltpu.make_async_copy(rows_hbm, rows_s, sems.at[0]),
        pltpu.make_async_copy(prompt_hbm, prompt_s, sems.at[1]),
        pltpu.make_async_copy(conv_hbm, conv, sems.at[2]),
        pltpu.make_async_copy(ssm_hbm, ssm, sems.at[3]),
    ]
    all_of(copies + in_parts(step_hbm, step, sems, 5, 4))
    key = key_s[0]
    window = conv[0].astype(F32)
    for k, (ref, i) in enumerate(blocks(outs)):
        target = jnp.bitwise_xor(key, k)
        row = jnp.maximum(rows_s[target], 0)
        xs = step[row, :, 0, :].astype(F32)
        told = jnp.bitwise_xor(prompt_s[row], target) if direct else prompt_s[row]
        pieces = [window, xs, jnp.full((1, channels), told.astype(F32), F32)]
        if ref.shape[1] > sum(p.shape[0] for p in pieces):
            pieces.append(ssm[0])
        ref[i] = jnp.concatenate(pieces, axis=0).astype(BF16)


def silu(v):
    return v / (1.0 + jnp.exp(-v))


def pair_kernel(text, own_ref, other_ref, pair_ref):
    states = [ref[0].astype(F32)[text:, :] for ref in (own_ref, other_ref)]
    pair_ref[0] = jnp.concatenate(states, axis=0).astype(BF16)


def prepare_kernel(
    key_hbm, prompt_hbm, step_ref, cw_hbm, cb_hbm, xwt_hbm, after_ref, *rest
):
    del after_ref
    base_ref, gate_ref, pick_ref, cw_ref, cb_ref, xwt_ref, key_s, prompt_s, sems = rest
    small = [
        pltpu.make_async_copy(cw_hbm, cw_ref, sems.at[0]),
        pltpu.make_async_copy(cb_hbm, cb_ref, sems.at[1]),
        pltpu.make_async_copy(key_hbm, key_s, sems.at[2]),
        pltpu.make_async_copy(prompt_hbm, prompt_s, sems.at[3]),
    ]
    large = in_parts(xwt_hbm, xwt_ref, sems, 4, WEIGHT_PARTS)
    for copy in small + large:
        copy.start()
    steps = step_ref.shape[1]
    taps = cw_hbm.shape[0]
    xs = [step_ref[:, t, 0, :].astype(F32) for t in range(steps)]
    for t in range(steps):
        gate_ref[t] = silu(step_ref[:, t, 1, :].astype(F32))
    for copy in small:
        copy.wait()
    for t in range(steps):
        total = cw_ref[taps - 1 : taps, :] * xs[t] + cb_ref[...]
        for k in range(max(0, taps - 1 - t), taps - 1):
            total = total + cw_ref[k : k + 1, :] * xs[t + k - taps + 1]
        base_ref[t] = total
    pick_ref[...] = scalar_onehot(prompt_s, key_s[0], pick_ref.shape)
    for copy in large:
        copy.wait()


def slot_onehot(numbers, owners):
    column = lax.broadcasted_iota(jnp.int32, (numbers.shape[0], owners), 1)
    return (numbers[:, :owners].astype(jnp.int32) == column).astype(F32)


def project_kernel(n_msgs, pick_ref, base_ref, cw_ref, cb_ref, xwt_ref, *rest):
    msgs, (act_ref, part_ref) = rest[:n_msgs], rest[n_msgs:]
    taps = cw_ref.shape[0]
    steps, rb, _ = base_ref.shape
    past = taps - 1
    held = [ref[i].astype(F32) for ref, i in blocks(msgs)]
    owners = len(held)
    windows = [[h[k : k + 1, :] for h in held] for k in range(past)]
    own = pick_ref[...]
    own_windows = [pick_rows(own, w) for w in windows]
    for t in range(steps):
        conv = base_ref[t]
        for k in range(past - t):
            conv = conv + cw_ref[k : k + 1, :] * own_windows[t + k]
        act_ref[t * rb : (t + 1) * rb, :] = silu(conv)

    def line_of(row):
        return jnp.concatenate([h[row : row + 1, :] for h in held], axis=0)

    slot = slot_onehot(line_of(past + steps), owners)
    line = [pick_rows(slot, w) for w in windows]
    line += [line_of(past + t) for t in range(steps)]
    row = steps * rb
    for t in range(steps):
        conv = cw_ref[past:taps, :] * line[t + past] + cb_ref[...]
        for k in range(past):
            conv = conv + cw_ref[k : k + 1, :] * line[t + k]
        act_ref[row : row + owners, :] = silu(conv)
        row += owners
    part_ref[...] = lax.dot_general(
        act_ref[...].astype(BF16),
        xwt_ref[...],
        (((1,), (1,)), ((), ())),
        preferred_element_type=F32,
    )


def fetch_kernel(
    n_msgs, steps, key_hbm, child_hbm, alog_hbm, dtw_hbm, dtb_hbm, skip_hbm, after_ref, *rest
):
    del after_ref
    msgs, rest = rest[:n_msgs], rest[n_msgs:]
    rate_ref, twin_ref, conv_ref, dtw_ref, dtb_ref, skip_ref, key_s, child_s, alog, sems = rest
    small = [
        pltpu.make_async_copy(key_hbm, key_s, sems.at[0]),
        pltpu.make_async_copy(child_hbm, child_s, sems.at[1]),
        pltpu.make_async_copy(alog_hbm, alog, sems.at[2]),
        pltpu.make_async_copy(dtb_hbm, dtb_ref, sems.at[3]),
        pltpu.make_async_copy(skip_hbm, skip_ref, sems.at[4]),
    ]
    large = in_parts(dtw_hbm, dtw_ref, sems, 5, DT_PARTS)
    for copy in small + large:
        copy.start()
    past, rb, channels = conv_ref.shape
    held = [ref[i].astype(F32) for ref, i in blocks(msgs)]
    for copy in small:
        copy.wait()
    owners = len(held)
    rate = jnp.exp(alog[...]) * (-math.log2(math.e))
    rate_ref[...] = rate
    half = (owners, channels)
    for m in range(rate.shape[0] // 2):
        two = [jnp.broadcast_to(rate[n : n + 1, :], half) for n in (2 * m, 2 * m + 1)]
        twin_ref[m] = jnp.concatenate(two, axis=0)
    pick = scalar_onehot(child_s, key_s[0], (rb, owners))
    first = past + steps - past
    for k in range(past):
        conv_ref[k] = pick_rows(pick, [h[first + k : first + k + 1, :] for h in held]).astype(BF16)
    for copy in large:
        copy.wait()


def add_kernel(a_ref, b_ref, sum_ref, short_ref):
    total = a_ref[...] + b_ref[...].astype(F32)
    sum_ref[...] = total
    short_ref[...] = total.astype(BF16)


def start_kernel(n_msgs, n_pairs, text, pick_ref, after_ref, *rest):
    del after_ref
    msgs, rest = rest[:n_msgs], rest[n_msgs:]
    pairs, (own_ref, slot_ref, state_s) = rest[:n_pairs], rest[n_pairs:]
    n_state = own_ref.shape[0]
    held = [ref[i].astype(F32) for ref, i in blocks(msgs)]
    owners = len(held)
    numbers = jnp.concatenate([h[text - 1 : text, :] for h in held], axis=0)
    states = [h[text:, :] for h in held]
    for ref in pairs:
        both = ref[0].astype(F32)
        states[1], states[3] = both[:n_state, :], both[n_state:, :]
    for k, state in enumerate(states):
        state_s[k] = state
    own = pick_ref[...]
    slot = slot_onehot(numbers, owners)

    def two(m, carry):
        picked = []
        for n in (2 * m, 2 * m + 1):
            rows = [state_s[k, pl.ds(n, 1), :] for k in range(owners)]
            own_ref[n] = pick_rows(own, rows)
            picked.append(pick_rows(slot, rows))
        slot_ref[m] = jnp.concatenate(picked, axis=0)
        return carry

    lax.fori_loop(0, n_state // 2, two, 0)


def decode_kernel(
    key_hbm,
    child_hbm,
    act_ref,
    gate_ref,
    own_ref,
    slot_ref,
    rate_ref,
    twin_ref,
    dtw_ref,
    dtb_ref,
    skip_ref,
    part_ref,
    other_ref,
    dec_ref,
    child_ssm,
    key_s,
    child_s,
    delta_s,
    gain_s,
    slot_delta_s,
    slot_gain_s,
    b_s,
    c_s,
    twin_b_s,
    slots_s,
    line_s,
    sems,
):
    scalars = [
        pltpu.make_async_copy(key_hbm, key_s, sems.at[0]),
        pltpu.make_async_copy(child_hbm, child_s, sems.at[1]),
    ]
    for copy in scalars:
        copy.start()
    rb, steps, channels = dec_ref.shape
    rank = dtw_ref.shape[0]
    n_state = rate_ref.shape[0]
    n_slots = slots_s.shape[0]
    own_rows = steps * rb
    chunks = channels // LANES

    proj = part_ref[...] + other_ref[...].astype(F32)
    delta_in = proj[:, :rank].astype(BF16)
    delta = jnp.dot(delta_in, dtw_ref[...], preferred_element_type=F32) + dtb_ref[...]
    delta = jnp.maximum(delta, 0.0) + jnp.log(1.0 + jnp.exp(-jnp.abs(delta)))
    gain = delta * act_ref[...]
    delta_s[...] = delta[:own_rows, :]
    gain_s[...] = gain[:own_rows, :]

    def column(at, n, rows):
        return jnp.broadcast_to(at[:, n : n + 1], (rows, LANES))

    for t in range(steps):
        at = slice(own_rows + t * n_slots, own_rows + (t + 1) * n_slots)
        slot_delta_s[t] = jnp.concatenate([delta[at, :]] * 2, axis=0)
        slot_gain_s[t] = jnp.concatenate([gain[at, :]] * 2, axis=0)
        twice = jnp.concatenate([proj[at, rank:]] * 2, axis=0)
        upper = lax.broadcasted_iota(jnp.int32, (2 * n_slots, LANES), 0) < n_slots
        for m in range(n_state // 2):
            twin_b_s[m, t] = jnp.where(
                upper, column(twice, 2 * m, 2 * n_slots), column(twice, 2 * m + 1, 2 * n_slots)
            )
    for n in range(n_state):
        b_s[n] = column(proj[:own_rows, rank:], n, own_rows)
        c_s[n] = column(proj[:own_rows, rank:], n_state + n, own_rows)

    def slot_chunk(chunk, carry):
        columns = pl.ds(pl.multiple_of(chunk * LANES, LANES), LANES)
        delta = [slot_delta_s[t, :, columns] for t in range(steps)]
        gain = [slot_gain_s[t, :, columns] for t in range(steps)]
        for m in range(n_state // 2):
            rate = twin_ref[m, :, columns]
            state = slot_ref[m, :, columns]
            for t in range(steps):
                state = jnp.exp2(delta[t] * rate) * state + gain[t] * twin_b_s[m, t]
            slots_s[:, 2 * m, columns] = state[:n_slots, :]
            slots_s[:, 2 * m + 1, columns] = state[n_slots:, :]
        return carry

    lax.fori_loop(0, chunks, slot_chunk, 0)
    for copy in scalars:
        copy.wait()
    copies = []
    for j in range(rb):
        at = jnp.bitwise_xor(child_s[j], key_s[0])
        copy = pltpu.make_async_copy(slots_s.at[at], child_ssm.at[j], sems.at[2 + j])
        copy.start()
        copies.append(copy)

    def own_chunk(chunk, carry):
        columns = pl.ds(pl.multiple_of(chunk * LANES, LANES), LANES)
        at = [pl.ds(t * rb, rb) for t in range(steps)]
        delta = [delta_s[a, columns] for a in at]
        gain = [gain_s[a, columns] for a in at]
        sums = [skip_ref[:, columns] * act_ref[a, columns] for a in at]
        for n in range(n_state):
            rate = rate_ref[n : n + 1, columns]
            state = own_ref[n, :, columns]
            for t in range(steps):
                state = jnp.exp2(delta[t] * rate) * state + gain[t] * b_s[n, at[t], :]
                sums[t] = sums[t] + c_s[n, at[t], :] * state
        for t in range(steps):
            line_s[pl.ds(t, rb, stride=steps), :] = sums[t] * gate_ref[t, :, columns]
        dec_ref[:, :, columns] = line_s[...].reshape(rb, steps, LANES).astype(BF16)
        return carry

    lax.fori_loop(0, chunks, own_chunk, 0)
    for copy in copies:
        copy.wait()


def on_device(
    prompt_ssm,
    prompt_conv,
    prompt_of,
    step_in,
    conv_weight,
    conv_bias,
    x_weight,
    dt_weight,
    dt_bias,
    a_log,
    skip,
    send_rows,
    child_slot,
):
    owners = lax.axis_size("branch")
    tensors = lax.axis_size("tensor")
    assert owners & (owners - 1) == 0 and tensors & (tensors - 1) == 0
    assert prompt_ssm.shape[0] == 1 and send_rows.shape[2] == 1
    rb, steps, _, channels = step_in.shape
    taps = conv_weight.shape[0]
    width = x_weight.shape[1]
    n_state = a_log.shape[0]
    rows = steps * (rb + owners)
    short = taps - 1 + steps + 1
    depth = short + n_state
    direct = owners == DIRECT
    me = lax.axis_index("branch").astype(jnp.int32).reshape(1)
    key = pinned(me if direct else jnp.zeros((1,), jnp.int32))

    if direct:
        msg_shapes = [(1, d, channels) for d in (depth, short, depth, short)]
    else:
        msg_shapes = [(owners, depth, channels)]
    msgs = call(
        functools.partial(pack_kernel, direct),
        [shaped(s, BF16) for s in msg_shapes],
        [hbm()] * 6,
        [vmem()] * len(msg_shapes),
        [
            pltpu.SMEM((1,), jnp.int32),
            pltpu.SMEM((owners,), jnp.int32),
            pltpu.SMEM((rb,), jnp.int32),
            pltpu.VMEM(step_in.shape, BF16),
            pltpu.VMEM(prompt_conv.shape, BF16),
            pltpu.VMEM(prompt_ssm.shape, F32),
            pltpu.SemaphoreType.DMA((9,)),
        ],
        nbytes=owners * depth * channels * 2,
    )(
        key,
        pinned(send_rows.reshape(owners)),
        pinned(prompt_of),
        pinned(step_in),
        pinned(prompt_conv),
        pinned(prompt_ssm),
    )
    if direct:
        own = msgs[0]
        came = {k: swap(msgs[k], "branch", k) for k in (2, 3, 1)}
        msgs = [own] + [came[k] for k in range(1, owners)]
        pair = call(
            functools.partial(pair_kernel, short),
            shaped((1, 2 * n_state, channels), BF16),
            [vmem()] * 2,
            vmem(),
            nbytes=8 * n_state * channels,
        )(msgs[0], msgs[2])
        pairs, after = [swap(pair, "branch", 1)], own
    else:
        msgs = [lax.all_to_all(msgs[0], "branch", split_axis=0, concat_axis=0, tiled=True)]
        pairs, after = [], msgs[0]
    n_msgs = len(msgs)
    base, gate, pick, taps_near, bias_near, weight_near = call(
        prepare_kernel,
        [
            shaped((steps, rb, channels), F32),
            shaped((steps, rb, channels), F32),
            shaped((rb, owners), F32),
            shaped((taps, channels), F32),
            shaped((1, channels), F32),
            shaped((width, channels), BF16),
        ],
        [hbm(), hbm(), vmem(), hbm(), hbm(), hbm(), anywhere()],
        [vmem()] * 6,
        [
            pltpu.SMEM((1,), jnp.int32),
            pltpu.SMEM((rb,), jnp.int32),
            pltpu.SemaphoreType.DMA((4 + WEIGHT_PARTS,)),
        ],
        flops=10 * steps * rb * channels,
        nbytes=12 * steps * rb * channels,
        trans=steps * rb * channels,
    )(
        key,
        pinned(prompt_of),
        step_in,
        pinned(conv_weight),
        pinned(conv_bias[None]),
        pinned(x_weight.T),
        after,
    )
    act, part = call(
        functools.partial(project_kernel, n_msgs),
        [
            shaped((rows, channels), F32),
            shaped((rows, width), F32),
        ],
        [vmem()] * (5 + n_msgs),
        [vmem()] * 2,
        flops=2 * rows * channels * width,
        nbytes=channels * width * 2 + rows * (channels + width) * 4,
        trans=rows * channels,
    )(pick, base, taps_near, bias_near, weight_near, *msgs)
    other = swap(part, "tensor", 1)
    distance = 2
    while distance < tensors:
        part, brief = call(
            add_kernel,
            [shaped((rows, width), F32), shaped((rows, width), BF16)],
            [vmem()] * 2,
            [vmem()] * 2,
            flops=rows * width,
            nbytes=rows * width * 14,
        )(part, other)
        other = swap(brief, "tensor", distance)
        distance *= 2

    rate, twin, child_conv, dtw_near, dtb_near, skip_near = call(
        functools.partial(fetch_kernel, n_msgs, steps),
        [
            shaped((n_state, channels), F32),
            shaped((n_state // 2, 2 * owners, channels), F32),
            shaped((taps - 1, rb, channels), BF16),
            shaped(dt_weight.shape, BF16),
            shaped((1, channels), F32),
            shaped((1, channels), F32),
        ],
        [hbm()] * 6 + [anywhere()] + [vmem()] * n_msgs,
        [vmem()] * 6,
        [
            pltpu.SMEM((1,), jnp.int32),
            pltpu.SMEM((rb,), jnp.int32),
            pltpu.VMEM((n_state, channels), F32),
            pltpu.SemaphoreType.DMA((5 + DT_PARTS,)),
        ],
        flops=4 * n_state * channels,
        nbytes=4 * n_state * (rb + owners) * channels,
    )(
        key,
        pinned(child_slot),
        pinned(a_log),
        pinned(dt_weight),
        pinned(dt_bias[None]),
        pinned(skip[None]),
        part,
        *msgs,
    )
    own_start, slot_start = call(
        functools.partial(start_kernel, n_msgs, len(pairs), short),
        [
            shaped((n_state, rb, channels), F32),
            shaped((n_state // 2, 2 * owners, channels), F32),
        ],
        [vmem(), anywhere()] + [vmem()] * (n_msgs + len(pairs)),
        [vmem()] * 2,
        [pltpu.VMEM((owners, n_state, channels), F32)],
        flops=2 * owners * n_state * (rb + owners) * channels,
        nbytes=4 * n_state * (rb + owners) * channels,
    )(pick, part, *msgs, *pairs)

    decoded, child_ssm = call(
        decode_kernel,
        [
            shaped((rb, steps, channels), BF16),
            shaped((rb, n_state, channels), F32),
        ],
        [hbm()] * 2 + [vmem()] * 11,
        [vmem(), anywhere()],
        [
            pltpu.SMEM((1,), jnp.int32),
            pltpu.SMEM((rb,), jnp.int32),
            pltpu.VMEM((steps * rb, channels), F32),
            pltpu.VMEM((steps * rb, channels), F32),
            pltpu.VMEM((steps, 2 * owners, channels), F32),
            pltpu.VMEM((steps, 2 * owners, channels), F32),
            pltpu.VMEM((n_state, steps * rb, LANES), F32),
            pltpu.VMEM((n_state, steps * rb, LANES), F32),
            pltpu.VMEM((n_state // 2, steps, 2 * owners, LANES), F32),
            pltpu.VMEM((owners, n_state, channels), F32),
            pltpu.VMEM((steps * rb, LANES), F32),
            pltpu.SemaphoreType.DMA((2 + rb,)),
        ],
        flops=8 * rows * n_state * channels,
        nbytes=(rb + owners) * n_state * channels * 4,
        trans=rows * n_state * channels,
    )(
        key,
        pinned(child_slot),
        act,
        gate,
        own_start,
        slot_start,
        rate,
        twin,
        dtw_near,
        dtb_near,
        skip_near,
        part,
        other,
    )
    return (decoded, child_ssm, jnp.transpose(child_conv, (1, 0, 2)))


def solution(mesh):
    placed = (
        P(("replica", "branch"), None, "tensor"),
        P(("replica", "branch"), None, "tensor"),
        P(("replica", "branch")),
        P(("replica", "branch"), None, None, "tensor"),
        P(None, "tensor"),
        P("tensor"),
        P("tensor", None),
        P(None, "tensor"),
        P("tensor"),
        P(None, "tensor"),
        P("tensor"),
        P(("replica", "branch"), None, None),
        P(("replica", "branch")),
    )
    return jax.shard_map(
        on_device,
        mesh=mesh,
        in_specs=placed,
        out_specs=(
            P(("replica", "branch"), None, "tensor"),
            P(("replica", "branch"), None, "tensor"),
            P(("replica", "branch"), None, "tensor"),
        ),
        check_vma=False,
    )
```

```python
import functools
import math

import jax
import jax.numpy as jnp
from jax import lax
from jax.experimental import pallas as pl
from jax.experimental.pallas import tpu as pltpu
from jax.sharding import PartitionSpec as P

F32 = jnp.float32
BF16 = jnp.bfloat16
LANES = 128
VMEM_LIMIT = 48 * 2**20
WEIGHT_PARTS = 6
DT_PARTS = 4
DIRECT = 4
ORDER = (0, 2, 3, 1)


def vmem():
    return pl.BlockSpec(memory_space=pltpu.VMEM)


def hbm():
    return pl.BlockSpec(memory_space=pltpu.HBM)


def anywhere():
    return pl.BlockSpec(memory_space=pl.ANY)


def pinned(array):
    return pltpu.with_memory_space_constraint(array, pltpu.HBM)


def shaped(shape, dtype):
    return jax.ShapeDtypeStruct(shape, dtype)


def call(kernel, outs, in_specs, out_specs, scratch=(), flops=0, nbytes=0, trans=0):
    return pl.pallas_call(
        kernel,
        out_shape=outs,
        in_specs=in_specs,
        out_specs=out_specs,
        scratch_shapes=list(scratch),
        compiler_params=pltpu.CompilerParams(vmem_limit_bytes=VMEM_LIMIT),
        cost_estimate=pl.CostEstimate(flops=flops, bytes_accessed=nbytes, transcendentals=trans),
    )


def swap(value, axis, distance):
    size = lax.axis_size(axis)
    return lax.ppermute(value, axis, [(i, i ^ distance) for i in range(size)])


def all_of(copies):
    for copy in copies:
        copy.start()
    for copy in copies:
        copy.wait()


def blocks(refs):
    if len(refs) == DIRECT:
        refs = [refs[ORDER.index(k)] for k in range(DIRECT)]
    return [(ref, i) for ref in refs for i in range(ref.shape[0])]


def in_parts(source, target, sems, first, count):
    rows = source.shape[0] // count
    at = [pl.ds(i * rows, rows) for i in range(count)]
    return [
        pltpu.make_async_copy(source.at[a], target.at[a], sems.at[first + i])
        for i, a in enumerate(at)
    ]


def scalar_onehot(numbers_s, key, shape):
    row_of = lax.broadcasted_iota(jnp.int32, shape, 0)
    wanted = jnp.zeros(shape, jnp.int32)
    for b in range(shape[0]):
        wanted = jnp.where(row_of == b, jnp.bitwise_xor(numbers_s[b], key), wanted)
    return (wanted == lax.broadcasted_iota(jnp.int32, shape, 1)).astype(F32)


def pick_rows(pick, rows):
    total = pick[:, 0:1] * rows[0]
    for k in range(1, len(rows)):
        total = total + pick[:, k : k + 1] * rows[k]
    return total


def pack_kernel(direct, key_hbm, rows_hbm, prompt_hbm, step_hbm, conv_hbm, ssm_hbm, *rest):
    outs, (key_s, rows_s, prompt_s, step, conv, ssm, sems) = rest[:-7], rest[-7:]
    owners = rows_hbm.shape[0]
    channels = step_hbm.shape[3]
    copies = [
        pltpu.make_async_copy(key_hbm, key_s, sems.at[4]),
        pltpu.make_async_copy(rows_hbm, rows_s, sems.at[0]),
        pltpu.make_async_copy(prompt_hbm, prompt_s, sems.at[1]),
        pltpu.make_async_copy(conv_hbm, conv, sems.at[2]),
        pltpu.make_async_copy(ssm_hbm, ssm, sems.at[3]),
    ]
    all_of(copies + in_parts(step_hbm, step, sems, 5, 4))
    key = key_s[0]
    window = conv[0].astype(F32)
    for k, (ref, i) in enumerate(blocks(outs)):
        target = jnp.bitwise_xor(key, k)
        row = jnp.maximum(rows_s[target], 0)
        xs = step[row, :, 0, :].astype(F32)
        told = jnp.bitwise_xor(prompt_s[row], target) if direct else prompt_s[row]
        pieces = [window, xs, jnp.full((1, channels), told.astype(F32), F32)]
        if ref.shape[1] > sum(p.shape[0] for p in pieces):
            pieces.append(ssm[0])
        ref[i] = jnp.concatenate(pieces, axis=0).astype(BF16)


def silu(v):
    return v / (1.0 + jnp.exp(-v))


def pair_kernel(text, own_ref, other_ref, pair_ref):
    states = [ref[0].astype(F32)[text:, :] for ref in (own_ref, other_ref)]
    pair_ref[0] = jnp.concatenate(states, axis=0).astype(BF16)


def prepare_kernel(
    key_hbm, prompt_hbm, step_ref, cw_hbm, cb_hbm, xwt_hbm, after_ref, *rest
):
    del after_ref
    base_ref, gate_ref, pick_ref, cw_ref, cb_ref, xwt_ref, key_s, prompt_s, sems = rest
    small = [
        pltpu.make_async_copy(cw_hbm, cw_ref, sems.at[0]),
        pltpu.make_async_copy(cb_hbm, cb_ref, sems.at[1]),
        pltpu.make_async_copy(key_hbm, key_s, sems.at[2]),
        pltpu.make_async_copy(prompt_hbm, prompt_s, sems.at[3]),
    ]
    large = in_parts(xwt_hbm, xwt_ref, sems, 4, WEIGHT_PARTS)
    for copy in small + large:
        copy.start()
    steps = step_ref.shape[1]
    taps = cw_hbm.shape[0]
    xs = [step_ref[:, t, 0, :].astype(F32) for t in range(steps)]
    for t in range(steps):
        gate_ref[t] = silu(step_ref[:, t, 1, :].astype(F32))
    for copy in small:
        copy.wait()
    for t in range(steps):
        total = cw_ref[taps - 1 : taps, :] * xs[t] + cb_ref[...]
        for k in range(max(0, taps - 1 - t), taps - 1):
            total = total + cw_ref[k : k + 1, :] * xs[t + k - taps + 1]
        base_ref[t] = total
    pick_ref[...] = scalar_onehot(prompt_s, key_s[0], pick_ref.shape)
    for copy in large:
        copy.wait()


def slot_onehot(numbers, owners):
    column = lax.broadcasted_iota(jnp.int32, (numbers.shape[0], owners), 1)
    return (numbers[:, :owners].astype(jnp.int32) == column).astype(F32)


def project_kernel(n_msgs, pick_ref, base_ref, cw_ref, cb_ref, xwt_ref, *rest):
    msgs, (act_ref, part_ref) = rest[:n_msgs], rest[n_msgs:]
    taps = cw_ref.shape[0]
    steps, rb, _ = base_ref.shape
    past = taps - 1
    held = [ref[i].astype(F32) for ref, i in blocks(msgs)]
    owners = len(held)
    windows = [[h[k : k + 1, :] for h in held] for k in range(past)]
    own = pick_ref[...]
    own_windows = [pick_rows(own, w) for w in windows]
    for t in range(steps):
        conv = base_ref[t]
        for k in range(past - t):
            conv = conv + cw_ref[k : k + 1, :] * own_windows[t + k]
        act_ref[t * rb : (t + 1) * rb, :] = silu(conv)

    def line_of(row):
        return jnp.concatenate([h[row : row + 1, :] for h in held], axis=0)

    slot = slot_onehot(line_of(past + steps), owners)
    line = [pick_rows(slot, w) for w in windows]
    line += [line_of(past + t) for t in range(steps)]
    row = steps * rb
    for t in range(steps):
        conv = cw_ref[past:taps, :] * line[t + past] + cb_ref[...]
        for k in range(past):
            conv = conv + cw_ref[k : k + 1, :] * line[t + k]
        act_ref[row : row + owners, :] = silu(conv)
        row += owners
    part_ref[...] = lax.dot_general(
        act_ref[...].astype(BF16),
        xwt_ref[...],
        (((1,), (1,)), ((), ())),
        preferred_element_type=F32,
    )


def fetch_kernel(
    n_msgs, steps, key_hbm, child_hbm, alog_hbm, dtw_hbm, dtb_hbm, skip_hbm, after_ref, *rest
):
    del after_ref
    msgs, rest = rest[:n_msgs], rest[n_msgs:]
    rate_ref, twin_ref, conv_ref, dtw_ref, dtb_ref, skip_ref, key_s, child_s, alog, sems = rest
    small = [
        pltpu.make_async_copy(key_hbm, key_s, sems.at[0]),
        pltpu.make_async_copy(child_hbm, child_s, sems.at[1]),
        pltpu.make_async_copy(alog_hbm, alog, sems.at[2]),
        pltpu.make_async_copy(dtb_hbm, dtb_ref, sems.at[3]),
        pltpu.make_async_copy(skip_hbm, skip_ref, sems.at[4]),
    ]
    large = in_parts(dtw_hbm, dtw_ref, sems, 5, DT_PARTS)
    for copy in small + large:
        copy.start()
    past, rb, channels = conv_ref.shape
    held = [ref[i].astype(F32) for ref, i in blocks(msgs)]
    for copy in small:
        copy.wait()
    owners = len(held)
    rate = jnp.exp(alog[...]) * (-math.log2(math.e))
    rate_ref[...] = rate
    half = (owners, channels)
    for m in range(rate.shape[0] // 2):
        two = [jnp.broadcast_to(rate[n : n + 1, :], half) for n in (2 * m, 2 * m + 1)]
        twin_ref[m] = jnp.concatenate(two, axis=0)
    pick = scalar_onehot(child_s, key_s[0], (rb, owners))
    first = past + steps - past
    for k in range(past):
        conv_ref[k] = pick_rows(pick, [h[first + k : first + k + 1, :] for h in held]).astype(BF16)
    for copy in large:
        copy.wait()


def add_kernel(a_ref, b_ref, sum_ref, short_ref):
    total = a_ref[...] + b_ref[...].astype(F32)
    sum_ref[...] = total
    short_ref[...] = total.astype(BF16)


def start_kernel(n_msgs, n_pairs, text, pick_ref, after_ref, *rest):
    del after_ref
    msgs, rest = rest[:n_msgs], rest[n_msgs:]
    pairs, (own_ref, slot_ref, state_s) = rest[:n_pairs], rest[n_pairs:]
    n_state = own_ref.shape[0]
    held = [ref[i].astype(F32) for ref, i in blocks(msgs)]
    owners = len(held)
    numbers = jnp.concatenate([h[text - 1 : text, :] for h in held], axis=0)
    states = [h[text:, :] for h in held]
    for ref in pairs:
        both = ref[0].astype(F32)
        states[1], states[3] = both[:n_state, :], both[n_state:, :]
    for k, state in enumerate(states):
        state_s[k] = state
    own = pick_ref[...]
    slot = slot_onehot(numbers, owners)

    def two(m, carry):
        picked = []
        for n in (2 * m, 2 * m + 1):
            rows = [state_s[k, pl.ds(n, 1), :] for k in range(owners)]
            own_ref[n] = pick_rows(own, rows)
            picked.append(pick_rows(slot, rows))
        slot_ref[m] = jnp.concatenate(picked, axis=0)
        return carry

    lax.fori_loop(0, n_state // 2, two, 0)


def decode_kernel(
    key_hbm,
    child_hbm,
    act_ref,
    gate_ref,
    own_ref,
    slot_ref,
    rate_ref,
    twin_ref,
    dtw_ref,
    dtb_ref,
    skip_ref,
    part_ref,
    other_ref,
    dec_ref,
    child_ssm,
    key_s,
    child_s,
    delta_s,
    gain_s,
    slot_delta_s,
    slot_gain_s,
    b_s,
    c_s,
    twin_b_s,
    slots_s,
    line_s,
    sems,
):
    scalars = [
        pltpu.make_async_copy(key_hbm, key_s, sems.at[0]),
        pltpu.make_async_copy(child_hbm, child_s, sems.at[1]),
    ]
    for copy in scalars:
        copy.start()
    rb, steps, channels = dec_ref.shape
    rank = dtw_ref.shape[0]
    n_state = rate_ref.shape[0]
    n_slots = slots_s.shape[0]
    own_rows = steps * rb
    chunks = channels // LANES

    proj = part_ref[...] + other_ref[...].astype(F32)
    delta_in = proj[:, :rank].astype(BF16)
    delta = jnp.dot(delta_in, dtw_ref[...], preferred_element_type=F32) + dtb_ref[...]
    delta = jnp.maximum(delta, 0.0) + jnp.log(1.0 + jnp.exp(-jnp.abs(delta)))
    gain = delta * act_ref[...]
    delta_s[...] = delta[:own_rows, :]
    gain_s[...] = gain[:own_rows, :]

    def column(at, n, rows):
        return jnp.broadcast_to(at[:, n : n + 1], (rows, LANES))

    for t in range(steps):
        at = slice(own_rows + t * n_slots, own_rows + (t + 1) * n_slots)
        slot_delta_s[t] = jnp.concatenate([delta[at, :]] * 2, axis=0)
        slot_gain_s[t] = jnp.concatenate([gain[at, :]] * 2, axis=0)
        twice = jnp.concatenate([proj[at, rank:]] * 2, axis=0)
        upper = lax.broadcasted_iota(jnp.int32, (2 * n_slots, LANES), 0) < n_slots
        for m in range(n_state // 2):
            twin_b_s[m, t] = jnp.where(
                upper, column(twice, 2 * m, 2 * n_slots), column(twice, 2 * m + 1, 2 * n_slots)
            )
    for n in range(n_state):
        b_s[n] = column(proj[:own_rows, rank:], n, own_rows)
        c_s[n] = column(proj[:own_rows, rank:], n_state + n, own_rows)

    def slot_chunk(chunk, carry):
        columns = pl.ds(pl.multiple_of(chunk * LANES, LANES), LANES)
        delta = [slot_delta_s[t, :, columns] for t in range(steps)]
        gain = [slot_gain_s[t, :, columns] for t in range(steps)]
        for m in range(n_state // 2):
            rate = twin_ref[m, :, columns]
            state = slot_ref[m, :, columns]
            for t in range(steps):
                state = jnp.exp2(delta[t] * rate) * state + gain[t] * twin_b_s[m, t]
            slots_s[:, 2 * m, columns] = state[:n_slots, :]
            slots_s[:, 2 * m + 1, columns] = state[n_slots:, :]
        return carry

    lax.fori_loop(0, chunks, slot_chunk, 0)
    for copy in scalars:
        copy.wait()
    copies = []
    for j in range(rb):
        at = jnp.bitwise_xor(child_s[j], key_s[0])
        copy = pltpu.make_async_copy(slots_s.at[at], child_ssm.at[j], sems.at[2 + j])
        copy.start()
        copies.append(copy)

    def own_chunk(chunk, carry):
        columns = pl.ds(pl.multiple_of(chunk * LANES, LANES), LANES)
        at = [pl.ds(t * rb, rb) for t in range(steps)]
        delta = [delta_s[a, columns] for a in at]
        gain = [gain_s[a, columns] for a in at]
        sums = [skip_ref[:, columns] * act_ref[a, columns] for a in at]
        for n in range(n_state):
            rate = rate_ref[n : n + 1, columns]
            state = own_ref[n, :, columns]
            for t in range(steps):
                state = jnp.exp2(delta[t] * rate) * state + gain[t] * b_s[n, at[t], :]
                sums[t] = sums[t] + c_s[n, at[t], :] * state
        for t in range(steps):
            line_s[pl.ds(t, rb, stride=steps), :] = sums[t] * gate_ref[t, :, columns]
        dec_ref[:, :, columns] = line_s[...].reshape(rb, steps, LANES).astype(BF16)
        return carry

    lax.fori_loop(0, chunks, own_chunk, 0)
    for copy in copies:
        copy.wait()


def on_device(
    prompt_ssm,
    prompt_conv,
    prompt_of,
    step_in,
    conv_weight,
    conv_bias,
    x_weight,
    dt_weight,
    dt_bias,
    a_log,
    skip,
    send_rows,
    child_slot,
):
    owners = lax.axis_size("branch")
    tensors = lax.axis_size("tensor")
    assert owners & (owners - 1) == 0 and tensors & (tensors - 1) == 0
    assert prompt_ssm.shape[0] == 1 and send_rows.shape[2] == 1
    rb, steps, _, channels = step_in.shape
    taps = conv_weight.shape[0]
    width = x_weight.shape[1]
    n_state = a_log.shape[0]
    rows = steps * (rb + owners)
    short = taps - 1 + steps + 1
    depth = short + n_state
    direct = owners == DIRECT
    me = lax.axis_index("branch").astype(jnp.int32).reshape(1)
    key = pinned(me if direct else jnp.zeros((1,), jnp.int32))

    if direct:
        msg_shapes = [(1, depth if k in (0, 2) else short, channels) for k in ORDER]
    else:
        msg_shapes = [(owners, depth, channels)]
    msgs = call(
        functools.partial(pack_kernel, direct),
        [shaped(s, BF16) for s in msg_shapes],
        [hbm()] * 6,
        [vmem()] * len(msg_shapes),
        [
            pltpu.SMEM((1,), jnp.int32),
            pltpu.SMEM((owners,), jnp.int32),
            pltpu.SMEM((rb,), jnp.int32),
            pltpu.VMEM(step_in.shape, BF16),
            pltpu.VMEM(prompt_conv.shape, BF16),
            pltpu.VMEM(prompt_ssm.shape, F32),
            pltpu.SemaphoreType.DMA((9,)),
        ],
        nbytes=owners * depth * channels * 2,
    )(
        key,
        pinned(send_rows.reshape(owners)),
        pinned(prompt_of),
        pinned(step_in),
        pinned(prompt_conv),
        pinned(prompt_ssm),
    )
    if direct:
        own = msgs[0]
        msgs = [own] + [swap(msgs[i], "branch", ORDER[i]) for i in range(1, owners)]
        pair = call(
            functools.partial(pair_kernel, short),
            shaped((1, 2 * n_state, channels), BF16),
            [vmem()] * 2,
            vmem(),
            nbytes=8 * n_state * channels,
        )(own, msgs[ORDER.index(2)])
        pairs, after = [swap(pair, "branch", 1)], own
    else:
        msgs = [lax.all_to_all(msgs[0], "branch", split_axis=0, concat_axis=0, tiled=True)]
        pairs, after = [], msgs[0]
    n_msgs = len(msgs)
    base, gate, pick, taps_near, bias_near, weight_near = call(
        prepare_kernel,
        [
            shaped((steps, rb, channels), F32),
            shaped((steps, rb, channels), F32),
            shaped((rb, owners), F32),
            shaped((taps, channels), F32),
            shaped((1, channels), F32),
            shaped((width, channels), BF16),
        ],
        [hbm(), hbm(), vmem(), hbm(), hbm(), hbm(), anywhere()],
        [vmem()] * 6,
        [
            pltpu.SMEM((1,), jnp.int32),
            pltpu.SMEM((rb,), jnp.int32),
            pltpu.SemaphoreType.DMA((4 + WEIGHT_PARTS,)),
        ],
        flops=10 * steps * rb * channels,
        nbytes=12 * steps * rb * channels,
        trans=steps * rb * channels,
    )(
        key,
        pinned(prompt_of),
        step_in,
        pinned(conv_weight),
        pinned(conv_bias[None]),
        pinned(x_weight.T),
        after,
    )
    act, part = call(
        functools.partial(project_kernel, n_msgs),
        [
            shaped((rows, channels), F32),
            shaped((rows, width), F32),
        ],
        [vmem()] * (5 + n_msgs),
        [vmem()] * 2,
        flops=2 * rows * channels * width,
        nbytes=channels * width * 2 + rows * (channels + width) * 4,
        trans=rows * channels,
    )(pick, base, taps_near, bias_near, weight_near, *msgs)
    other = swap(part, "tensor", 1)
    distance = 2
    while distance < tensors:
        part, brief = call(
            add_kernel,
            [shaped((rows, width), F32), shaped((rows, width), BF16)],
            [vmem()] * 2,
            [vmem()] * 2,
            flops=rows * width,
            nbytes=rows * width * 14,
        )(part, other)
        other = swap(brief, "tensor", distance)
        distance *= 2

    rate, twin, child_conv, dtw_near, dtb_near, skip_near = call(
        functools.partial(fetch_kernel, n_msgs, steps),
        [
            shaped((n_state, channels), F32),
            shaped((n_state // 2, 2 * owners, channels), F32),
            shaped((taps - 1, rb, channels), BF16),
            shaped(dt_weight.shape, BF16),
            shaped((1, channels), F32),
            shaped((1, channels), F32),
        ],
        [hbm()] * 6 + [anywhere()] + [vmem()] * n_msgs,
        [vmem()] * 6,
        [
            pltpu.SMEM((1,), jnp.int32),
            pltpu.SMEM((rb,), jnp.int32),
            pltpu.VMEM((n_state, channels), F32),
            pltpu.SemaphoreType.DMA((5 + DT_PARTS,)),
        ],
        flops=4 * n_state * channels,
        nbytes=4 * n_state * (rb + owners) * channels,
    )(
        key,
        pinned(child_slot),
        pinned(a_log),
        pinned(dt_weight),
        pinned(dt_bias[None]),
        pinned(skip[None]),
        part,
        *msgs,
    )
    own_start, slot_start = call(
        functools.partial(start_kernel, n_msgs, len(pairs), short),
        [
            shaped((n_state, rb, channels), F32),
            shaped((n_state // 2, 2 * owners, channels), F32),
        ],
        [vmem(), anywhere()] + [vmem()] * (n_msgs + len(pairs)),
        [vmem()] * 2,
        [pltpu.VMEM((owners, n_state, channels), F32)],
        flops=2 * owners * n_state * (rb + owners) * channels,
        nbytes=4 * n_state * (rb + owners) * channels,
    )(pick, part, *msgs, *pairs)

    decoded, child_ssm = call(
        decode_kernel,
        [
            shaped((rb, steps, channels), BF16),
            shaped((rb, n_state, channels), F32),
        ],
        [hbm()] * 2 + [vmem()] * 11,
        [vmem(), anywhere()],
        [
            pltpu.SMEM((1,), jnp.int32),
            pltpu.SMEM((rb,), jnp.int32),
            pltpu.VMEM((steps * rb, channels), F32),
            pltpu.VMEM((steps * rb, channels), F32),
            pltpu.VMEM((steps, 2 * owners, channels), F32),
            pltpu.VMEM((steps, 2 * owners, channels), F32),
            pltpu.VMEM((n_state, steps * rb, LANES), F32),
            pltpu.VMEM((n_state, steps * rb, LANES), F32),
            pltpu.VMEM((n_state // 2, steps, 2 * owners, LANES), F32),
            pltpu.VMEM((owners, n_state, channels), F32),
            pltpu.VMEM((steps * rb, LANES), F32),
            pltpu.SemaphoreType.DMA((2 + rb,)),
        ],
        flops=8 * rows * n_state * channels,
        nbytes=(rb + owners) * n_state * channels * 4,
        trans=rows * n_state * channels,
    )(
        key,
        pinned(child_slot),
        act,
        gate,
        own_start,
        slot_start,
        rate,
        twin,
        dtw_near,
        dtb_near,
        skip_near,
        part,
        other,
    )
    return (decoded, child_ssm, jnp.transpose(child_conv, (1, 0, 2)))


def solution(mesh):
    placed = (
        P(("replica", "branch"), None, "tensor"),
        P(("replica", "branch"), None, "tensor"),
        P(("replica", "branch")),
        P(("replica", "branch"), None, None, "tensor"),
        P(None, "tensor"),
        P("tensor"),
        P("tensor", None),
        P(None, "tensor"),
        P("tensor"),
        P(None, "tensor"),
        P("tensor"),
        P(("replica", "branch"), None, None),
        P(("replica", "branch")),
    )
    return jax.shard_map(
        on_device,
        mesh=mesh,
        in_specs=placed,
        out_specs=(
            P(("replica", "branch"), None, "tensor"),
            P(("replica", "branch"), None, "tensor"),
            P(("replica", "branch"), None, "tensor"),
        ),
        check_vma=False,
    )
```

```python
import functools
import math

import jax
import jax.numpy as jnp
from jax import lax
from jax.experimental import pallas as pl
from jax.experimental.pallas import tpu as pltpu
from jax.sharding import PartitionSpec as P

F32 = jnp.float32
BF16 = jnp.bfloat16
LANES = 128
VMEM_LIMIT = 48 * 2**20
WEIGHT_PARTS = 6
DT_PARTS = 4
DIRECT = 4
ORDER = (0, 2, 3, 1)


def vmem():
    return pl.BlockSpec(memory_space=pltpu.VMEM)


def hbm():
    return pl.BlockSpec(memory_space=pltpu.HBM)


def anywhere():
    return pl.BlockSpec(memory_space=pl.ANY)


def pinned(array):
    return pltpu.with_memory_space_constraint(array, pltpu.HBM)


def shaped(shape, dtype):
    return jax.ShapeDtypeStruct(shape, dtype)


def call(kernel, outs, in_specs, out_specs, scratch=(), flops=0, nbytes=0, trans=0):
    return pl.pallas_call(
        kernel,
        out_shape=outs,
        in_specs=in_specs,
        out_specs=out_specs,
        scratch_shapes=list(scratch),
        compiler_params=pltpu.CompilerParams(vmem_limit_bytes=VMEM_LIMIT),
        cost_estimate=pl.CostEstimate(flops=flops, bytes_accessed=nbytes, transcendentals=trans),
    )


def swap(value, axis, distance):
    size = lax.axis_size(axis)
    return lax.ppermute(value, axis, [(i, i ^ distance) for i in range(size)])


def all_of(copies):
    for copy in copies:
        copy.start()
    for copy in copies:
        copy.wait()


def blocks(refs):
    if len(refs) == DIRECT:
        refs = [refs[ORDER.index(k)] for k in range(DIRECT)]
    return [(ref, i) for ref in refs for i in range(ref.shape[0])]


def in_parts(source, target, sems, first, count):
    rows = source.shape[0] // count
    at = [pl.ds(i * rows, rows) for i in range(count)]
    return [
        pltpu.make_async_copy(source.at[a], target.at[a], sems.at[first + i])
        for i, a in enumerate(at)
    ]


def scalar_onehot(numbers_s, key, shape):
    row_of = lax.broadcasted_iota(jnp.int32, shape, 0)
    wanted = jnp.zeros(shape, jnp.int32)
    for b in range(shape[0]):
        wanted = jnp.where(row_of == b, jnp.bitwise_xor(numbers_s[b], key), wanted)
    return (wanted == lax.broadcasted_iota(jnp.int32, shape, 1)).astype(F32)


def pick_rows(pick, rows):
    total = pick[:, 0:1] * rows[0]
    for k in range(1, len(rows)):
        total = total + pick[:, k : k + 1] * rows[k]
    return total


def pack_kernel(direct, key_hbm, rows_hbm, prompt_hbm, step_hbm, conv_hbm, ssm_hbm, *rest):
    outs, (key_s, rows_s, prompt_s, step, conv, ssm, sems) = rest[:-7], rest[-7:]
    owners = rows_hbm.shape[0]
    channels = step_hbm.shape[3]
    copies = [
        pltpu.make_async_copy(key_hbm, key_s, sems.at[4]),
        pltpu.make_async_copy(rows_hbm, rows_s, sems.at[0]),
        pltpu.make_async_copy(prompt_hbm, prompt_s, sems.at[1]),
        pltpu.make_async_copy(conv_hbm, conv, sems.at[2]),
        pltpu.make_async_copy(ssm_hbm, ssm, sems.at[3]),
    ]
    all_of(copies + in_parts(step_hbm, step, sems, 5, 4))
    key = key_s[0]
    window = conv[0].astype(F32)
    for k, (ref, i) in enumerate(blocks(outs)):
        target = jnp.bitwise_xor(key, k)
        row = jnp.maximum(rows_s[target], 0)
        xs = step[row, :, 0, :].astype(F32)
        told = jnp.bitwise_xor(prompt_s[row], target) if direct else prompt_s[row]
        pieces = [xs, window, jnp.full((1, channels), told.astype(F32), F32)]
        if ref.shape[1] > sum(p.shape[0] for p in pieces):
            pieces.append(ssm[0])
        ref[i] = jnp.concatenate(pieces, axis=0).astype(BF16)


def silu(v):
    return v / (1.0 + jnp.exp(-v))


def pair_kernel(text, own_ref, other_ref, pair_ref):
    states = [ref[0].astype(F32)[text:, :] for ref in (own_ref, other_ref)]
    pair_ref[0] = jnp.concatenate(states, axis=0).astype(BF16)


def prepare_kernel(
    key_hbm,
    prompt_hbm,
    step_ref,
    cw_hbm,
    cb_hbm,
    xwt_hbm,
    alog_hbm,
    dtw_hbm,
    dtb_hbm,
    skip_hbm,
    after_ref,
    base_ref,
    gate_ref,
    pick_ref,
    cw_ref,
    cb_ref,
    xwt_ref,
    rate_ref,
    twin_ref,
    dtw_ref,
    dtb_ref,
    skip_ref,
    key_s,
    prompt_s,
    alog,
    sems,
):
    del after_ref
    small = [
        pltpu.make_async_copy(source, target, sems.at[i])
        for i, (source, target) in enumerate(
            (
                (cw_hbm, cw_ref),
                (cb_hbm, cb_ref),
                (key_hbm, key_s),
                (prompt_hbm, prompt_s),
                (alog_hbm, alog),
                (dtb_hbm, dtb_ref),
                (skip_hbm, skip_ref),
            )
        )
    ]
    large = in_parts(xwt_hbm, xwt_ref, sems, len(small), WEIGHT_PARTS)
    large += in_parts(dtw_hbm, dtw_ref, sems, len(small) + WEIGHT_PARTS, DT_PARTS)
    for copy in small + large:
        copy.start()
    steps = step_ref.shape[1]
    taps = cw_hbm.shape[0]
    xs = [step_ref[:, t, 0, :].astype(F32) for t in range(steps)]
    for t in range(steps):
        gate_ref[t] = silu(step_ref[:, t, 1, :].astype(F32))
    for copy in small:
        copy.wait()
    for t in range(steps):
        total = cw_ref[taps - 1 : taps, :] * xs[t] + cb_ref[...]
        for k in range(max(0, taps - 1 - t), taps - 1):
            total = total + cw_ref[k : k + 1, :] * xs[t + k - taps + 1]
        base_ref[t] = total
    pick_ref[...] = scalar_onehot(prompt_s, key_s[0], pick_ref.shape)
    rate = jnp.exp(alog[...]) * (-math.log2(math.e))
    rate_ref[...] = rate
    half = (twin_ref.shape[1] // 2, rate.shape[1])
    for m in range(rate.shape[0] // 2):
        two = [jnp.broadcast_to(rate[n : n + 1, :], half) for n in (2 * m, 2 * m + 1)]
        twin_ref[m] = jnp.concatenate(two, axis=0)
    for copy in large:
        copy.wait()


def slot_onehot(numbers, owners):
    column = lax.broadcasted_iota(jnp.int32, (numbers.shape[0], owners), 1)
    return (numbers[:, :owners].astype(jnp.int32) == column).astype(F32)


def project_kernel(n_msgs, pick_ref, base_ref, cw_ref, cb_ref, xwt_ref, *rest):
    msgs, (act_ref, part_ref) = rest[:n_msgs], rest[n_msgs:]
    taps = cw_ref.shape[0]
    steps, rb, _ = base_ref.shape
    past = taps - 1
    held = [ref[i].astype(F32) for ref, i in blocks(msgs)]
    owners = len(held)
    windows = [[h[steps + k : steps + k + 1, :] for h in held] for k in range(past)]
    own = pick_ref[...]
    own_windows = [pick_rows(own, w) for w in windows]
    for t in range(steps):
        conv = base_ref[t]
        for k in range(past - t):
            conv = conv + cw_ref[k : k + 1, :] * own_windows[t + k]
        act_ref[t * rb : (t + 1) * rb, :] = silu(conv)

    def line_of(row):
        return jnp.concatenate([h[row : row + 1, :] for h in held], axis=0)

    slot = slot_onehot(line_of(past + steps), owners)
    line = [pick_rows(slot, w) for w in windows]
    line += [line_of(t) for t in range(steps)]
    row = steps * rb
    for t in range(steps):
        conv = cw_ref[past:taps, :] * line[t + past] + cb_ref[...]
        for k in range(past):
            conv = conv + cw_ref[k : k + 1, :] * line[t + k]
        act_ref[row : row + owners, :] = silu(conv)
        row += owners
    part_ref[...] = lax.dot_general(
        act_ref[...].astype(BF16),
        xwt_ref[...],
        (((1,), (1,)), ((), ())),
        preferred_element_type=F32,
    )


def add_kernel(a_ref, b_ref, sum_ref, short_ref):
    total = a_ref[...] + b_ref[...].astype(F32)
    sum_ref[...] = total
    short_ref[...] = total.astype(BF16)


def start_kernel(n_msgs, n_pairs, steps, text, key_hbm, child_hbm, pick_ref, after_ref, *rest):
    del after_ref
    msgs, rest = rest[:n_msgs], rest[n_msgs:]
    pairs, rest = rest[:n_pairs], rest[n_pairs:]
    own_ref, slot_ref, conv_hbm, state_s, conv_s, key_s, child_s, sems = rest
    copies = [
        pltpu.make_async_copy(key_hbm, key_s, sems.at[0]),
        pltpu.make_async_copy(child_hbm, child_s, sems.at[1]),
    ]
    for copy in copies:
        copy.start()
    n_state = own_ref.shape[0]
    past, rb, _ = conv_s.shape
    held = [ref[i].astype(F32) for ref, i in blocks(msgs)]
    owners = len(held)
    numbers = jnp.concatenate([h[text - 1 : text, :] for h in held], axis=0)
    states = [h[text:, :] for h in held]
    for ref in pairs:
        both = ref[0].astype(F32)
        states[1], states[3] = both[:n_state, :], both[n_state:, :]
    for k, state in enumerate(states):
        state_s[k] = state
    own = pick_ref[...]
    slot = slot_onehot(numbers, owners)

    def two(m, carry):
        picked = []
        for n in (2 * m, 2 * m + 1):
            rows = [state_s[k, pl.ds(n, 1), :] for k in range(owners)]
            own_ref[n] = pick_rows(own, rows)
            picked.append(pick_rows(slot, rows))
        slot_ref[m] = jnp.concatenate(picked, axis=0)
        return carry

    for copy in copies:
        copy.wait()
    child = scalar_onehot(child_s, key_s[0], (rb, owners))
    for k in range(past):
        at = steps - past + k
        conv_s[k] = pick_rows(child, [h[at : at + 1, :] for h in held]).astype(BF16)
    out = pltpu.make_async_copy(conv_s, conv_hbm, sems.at[2])
    out.start()
    lax.fori_loop(0, n_state // 2, two, 0)
    out.wait()


def decode_kernel(
    key_hbm,
    child_hbm,
    act_ref,
    gate_ref,
    own_ref,
    slot_ref,
    rate_ref,
    twin_ref,
    dtw_ref,
    dtb_ref,
    skip_ref,
    part_ref,
    other_ref,
    dec_hbm,
    child_ssm,
    key_s,
    child_s,
    delta_s,
    gain_s,
    slot_delta_s,
    slot_gain_s,
    b_s,
    c_s,
    twin_b_s,
    slots_s,
    line_s,
    dec_ref,
    sems,
):
    scalars = [
        pltpu.make_async_copy(key_hbm, key_s, sems.at[0]),
        pltpu.make_async_copy(child_hbm, child_s, sems.at[1]),
    ]
    for copy in scalars:
        copy.start()
    rb, steps, channels = dec_ref.shape
    rank = dtw_ref.shape[0]
    n_state = rate_ref.shape[0]
    n_slots = slots_s.shape[0]
    own_rows = steps * rb
    chunks = channels // LANES

    proj = part_ref[...] + other_ref[...].astype(F32)
    delta_in = proj[:, :rank].astype(BF16)
    delta = jnp.dot(delta_in, dtw_ref[...], preferred_element_type=F32) + dtb_ref[...]
    delta = jnp.maximum(delta, 0.0) + jnp.log(1.0 + jnp.exp(-jnp.abs(delta)))
    gain = delta * act_ref[...]
    delta_s[...] = delta[:own_rows, :]
    gain_s[...] = gain[:own_rows, :]

    def column(at, n, rows):
        return jnp.broadcast_to(at[:, n : n + 1], (rows, LANES))

    for t in range(steps):
        at = slice(own_rows + t * n_slots, own_rows + (t + 1) * n_slots)
        slot_delta_s[t] = jnp.concatenate([delta[at, :]] * 2, axis=0)
        slot_gain_s[t] = jnp.concatenate([gain[at, :]] * 2, axis=0)
        twice = jnp.concatenate([proj[at, rank:]] * 2, axis=0)
        upper = lax.broadcasted_iota(jnp.int32, (2 * n_slots, LANES), 0) < n_slots
        for m in range(n_state // 2):
            twin_b_s[m, t] = jnp.where(
                upper, column(twice, 2 * m, 2 * n_slots), column(twice, 2 * m + 1, 2 * n_slots)
            )
    for n in range(n_state):
        b_s[n] = column(proj[:own_rows, rank:], n, own_rows)
        c_s[n] = column(proj[:own_rows, rank:], n_state + n, own_rows)

    def slot_chunk(chunk, carry):
        columns = pl.ds(pl.multiple_of(chunk * LANES, LANES), LANES)
        delta = [slot_delta_s[t, :, columns] for t in range(steps)]
        gain = [slot_gain_s[t, :, columns] for t in range(steps)]
        for m in range(n_state // 2):
            rate = twin_ref[m, :, columns]
            state = slot_ref[m, :, columns]
            for t in range(steps):
                state = jnp.exp2(delta[t] * rate) * state + gain[t] * twin_b_s[m, t]
            slots_s[:, 2 * m, columns] = state[:n_slots, :]
            slots_s[:, 2 * m + 1, columns] = state[n_slots:, :]
        return carry

    lax.fori_loop(0, chunks, slot_chunk, 0)
    for copy in scalars:
        copy.wait()
    copies = []
    for j in range(rb):
        at = jnp.bitwise_xor(child_s[j], key_s[0])
        copy = pltpu.make_async_copy(slots_s.at[at], child_ssm.at[j], sems.at[2 + j])
        copy.start()
        copies.append(copy)

    def own_chunk(chunk, carry):
        columns = pl.ds(pl.multiple_of(chunk * LANES, LANES), LANES)
        at = [pl.ds(t * rb, rb) for t in range(steps)]
        delta = [delta_s[a, columns] for a in at]
        gain = [gain_s[a, columns] for a in at]
        sums = [skip_ref[:, columns] * act_ref[a, columns] for a in at]
        for n in range(n_state):
            rate = rate_ref[n : n + 1, columns]
            state = own_ref[n, :, columns]
            for t in range(steps):
                state = jnp.exp2(delta[t] * rate) * state + gain[t] * b_s[n, at[t], :]
                sums[t] = sums[t] + c_s[n, at[t], :] * state
        for t in range(steps):
            line_s[pl.ds(t, rb, stride=steps), :] = sums[t] * gate_ref[t, :, columns]
        dec_ref[:, :, columns] = line_s[...].reshape(rb, steps, LANES).astype(BF16)
        leave(chunk).start()
        return carry

    def leave(chunk):
        columns = pl.ds(pl.multiple_of(chunk * LANES, LANES), LANES)
        return pltpu.make_async_copy(
            dec_ref.at[:, :, columns], dec_hbm.at[:, :, columns], sems.at[2 + rb + chunk]
        )

    lax.fori_loop(0, chunks, own_chunk, 0)
    for copy in copies:
        copy.wait()
    for chunk in range(chunks):
        leave(chunk).wait()


def on_device(
    prompt_ssm,
    prompt_conv,
    prompt_of,
    step_in,
    conv_weight,
    conv_bias,
    x_weight,
    dt_weight,
    dt_bias,
    a_log,
    skip,
    send_rows,
    child_slot,
):
    owners = lax.axis_size("branch")
    tensors = lax.axis_size("tensor")
    assert owners & (owners - 1) == 0 and tensors & (tensors - 1) == 0
    assert prompt_ssm.shape[0] == 1 and send_rows.shape[2] == 1
    rb, steps, _, channels = step_in.shape
    taps = conv_weight.shape[0]
    width = x_weight.shape[1]
    n_state = a_log.shape[0]
    rows = steps * (rb + owners)
    short = taps - 1 + steps + 1
    depth = short + n_state
    direct = owners == DIRECT
    me = lax.axis_index("branch").astype(jnp.int32).reshape(1)
    key = pinned(me if direct else jnp.zeros((1,), jnp.int32))

    if direct:
        msg_shapes = [(1, depth if k in (0, 2) else short, channels) for k in ORDER]
    else:
        msg_shapes = [(owners, depth, channels)]
    msgs = call(
        functools.partial(pack_kernel, direct),
        [shaped(s, BF16) for s in msg_shapes],
        [hbm()] * 6,
        [vmem()] * len(msg_shapes),
        [
            pltpu.SMEM((1,), jnp.int32),
            pltpu.SMEM((owners,), jnp.int32),
            pltpu.SMEM((rb,), jnp.int32),
            pltpu.VMEM(step_in.shape, BF16),
            pltpu.VMEM(prompt_conv.shape, BF16),
            pltpu.VMEM(prompt_ssm.shape, F32),
            pltpu.SemaphoreType.DMA((9,)),
        ],
        nbytes=owners * depth * channels * 2,
    )(
        key,
        pinned(send_rows.reshape(owners)),
        pinned(prompt_of),
        pinned(step_in),
        pinned(prompt_conv),
        pinned(prompt_ssm),
    )
    if direct:
        own = msgs[0]
        msgs = [own] + [swap(msgs[i], "branch", ORDER[i]) for i in range(1, owners)]
        pair = call(
            functools.partial(pair_kernel, short),
            shaped((1, 2 * n_state, channels), BF16),
            [vmem()] * 2,
            vmem(),
            nbytes=8 * n_state * channels,
        )(own, msgs[ORDER.index(2)])
        pairs, after = [swap(pair, "branch", 1)], own
    else:
        msgs = [lax.all_to_all(msgs[0], "branch", split_axis=0, concat_axis=0, tiled=True)]
        pairs, after = [], msgs[0]
    n_msgs = len(msgs)
    near = call(
        prepare_kernel,
        [
            shaped((steps, rb, channels), F32),
            shaped((steps, rb, channels), F32),
            shaped((rb, owners), F32),
            shaped((taps, channels), F32),
            shaped((1, channels), F32),
            shaped((width, channels), BF16),
            shaped((n_state, channels), F32),
            shaped((n_state // 2, 2 * owners, channels), F32),
            shaped(dt_weight.shape, BF16),
            shaped((1, channels), F32),
            shaped((1, channels), F32),
        ],
        [hbm(), hbm(), vmem()] + [hbm()] * 7 + [anywhere()],
        [vmem()] * 11,
        [
            pltpu.SMEM((1,), jnp.int32),
            pltpu.SMEM((rb,), jnp.int32),
            pltpu.VMEM((n_state, channels), F32),
            pltpu.SemaphoreType.DMA((7 + WEIGHT_PARTS + DT_PARTS,)),
        ],
        flops=10 * steps * rb * channels,
        nbytes=12 * steps * rb * channels,
        trans=steps * rb * channels,
    )(
        key,
        pinned(prompt_of),
        step_in,
        pinned(conv_weight),
        pinned(conv_bias[None]),
        pinned(x_weight.T),
        pinned(a_log),
        pinned(dt_weight),
        pinned(dt_bias[None]),
        pinned(skip[None]),
        after,
    )
    base, gate, pick, taps_near, bias_near, weight_near = near[:6]
    rate, twin, dtw_near, dtb_near, skip_near = near[6:]
    act, part = call(
        functools.partial(project_kernel, n_msgs),
        [
            shaped((rows, channels), F32),
            shaped((rows, width), F32),
        ],
        [vmem()] * (5 + n_msgs),
        [vmem()] * 2,
        flops=2 * rows * channels * width,
        nbytes=channels * width * 2 + rows * (channels + width) * 4,
        trans=rows * channels,
    )(pick, base, taps_near, bias_near, weight_near, *msgs)
    other = swap(part, "tensor", 1)
    distance = 2
    while distance < tensors:
        part, brief = call(
            add_kernel,
            [shaped((rows, width), F32), shaped((rows, width), BF16)],
            [vmem()] * 2,
            [vmem()] * 2,
            flops=rows * width,
            nbytes=rows * width * 14,
        )(part, other)
        other = swap(brief, "tensor", distance)
        distance *= 2

    own_start, slot_start, child_conv = call(
        functools.partial(start_kernel, n_msgs, len(pairs), steps, short),
        [
            shaped((n_state, rb, channels), F32),
            shaped((n_state // 2, 2 * owners, channels), F32),
            shaped((taps - 1, rb, channels), BF16),
        ],
        [hbm()] * 2 + [vmem(), anywhere()] + [vmem()] * (n_msgs + len(pairs)),
        [vmem()] * 2 + [anywhere()],
        [
            pltpu.VMEM((owners, n_state, channels), F32),
            pltpu.VMEM((taps - 1, rb, channels), BF16),
            pltpu.SMEM((1,), jnp.int32),
            pltpu.SMEM((rb,), jnp.int32),
            pltpu.SemaphoreType.DMA((3,)),
        ],
        flops=2 * owners * n_state * (rb + owners) * channels,
        nbytes=4 * n_state * (rb + owners) * channels,
    )(key, pinned(child_slot), pick, part, *msgs, *pairs)

    decoded, child_ssm = call(
        decode_kernel,
        [
            shaped((rb, steps, channels), BF16),
            shaped((rb, n_state, channels), F32),
        ],
        [hbm()] * 2 + [vmem()] * 11,
        [anywhere()] * 2,
        [
            pltpu.SMEM((1,), jnp.int32),
            pltpu.SMEM((rb,), jnp.int32),
            pltpu.VMEM((steps * rb, channels), F32),
            pltpu.VMEM((steps * rb, channels), F32),
            pltpu.VMEM((steps, 2 * owners, channels), F32),
            pltpu.VMEM((steps, 2 * owners, channels), F32),
            pltpu.VMEM((n_state, steps * rb, LANES), F32),
            pltpu.VMEM((n_state, steps * rb, LANES), F32),
            pltpu.VMEM((n_state // 2, steps, 2 * owners, LANES), F32),
            pltpu.VMEM((owners, n_state, channels), F32),
            pltpu.VMEM((steps * rb, LANES), F32),
            pltpu.VMEM((rb, steps, channels), BF16),
            pltpu.SemaphoreType.DMA((2 + rb + channels // LANES,)),
        ],
        flops=8 * rows * n_state * channels,
        nbytes=(rb + owners) * n_state * channels * 4,
        trans=rows * n_state * channels,
    )(
        key,
        pinned(child_slot),
        act,
        gate,
        own_start,
        slot_start,
        rate,
        twin,
        dtw_near,
        dtb_near,
        skip_near,
        part,
        other,
    )
    return (decoded, child_ssm, jnp.transpose(child_conv, (1, 0, 2)))


def solution(mesh):
    placed = (
        P(("replica", "branch"), None, "tensor"),
        P(("replica", "branch"), None, "tensor"),
        P(("replica", "branch")),
        P(("replica", "branch"), None, None, "tensor"),
        P(None, "tensor"),
        P("tensor"),
        P("tensor", None),
        P(None, "tensor"),
        P("tensor"),
        P(None, "tensor"),
        P("tensor"),
        P(("replica", "branch"), None, None),
        P(("replica", "branch")),
    )
    return jax.shard_map(
        on_device,
        mesh=mesh,
        in_specs=placed,
        out_specs=(
            P(("replica", "branch"), None, "tensor"),
            P(("replica", "branch"), None, "tensor"),
            P(("replica", "branch"), None, "tensor"),
        ),
        check_vma=False,
    )
```

```python
import functools
import math

import jax
import jax.numpy as jnp
from jax import lax
from jax.experimental import pallas as pl
from jax.experimental.pallas import tpu as pltpu
from jax.sharding import PartitionSpec as P

F32 = jnp.float32
BF16 = jnp.bfloat16
LANES = 128
VMEM_LIMIT = 48 * 2**20
WEIGHT_PARTS = 6
DT_PARTS = 4
DIRECT = 4
ROUNDS = ((3, (2, 3)), (2, (2, 3)), (1, (0, 1, 2, 3)), (2, (0, 1)), (3, (0, 1)))


def vmem():
    return pl.BlockSpec(memory_space=pltpu.VMEM)


def hbm():
    return pl.BlockSpec(memory_space=pltpu.HBM)


def anywhere():
    return pl.BlockSpec(memory_space=pl.ANY)


def pinned(array):
    return pltpu.with_memory_space_constraint(array, pltpu.HBM)


def shaped(shape, dtype):
    return jax.ShapeDtypeStruct(shape, dtype)


def call(kernel, outs, in_specs, out_specs, scratch=(), flops=0, nbytes=0, trans=0):
    return pl.pallas_call(
        kernel,
        out_shape=outs,
        in_specs=in_specs,
        out_specs=out_specs,
        scratch_shapes=list(scratch),
        compiler_params=pltpu.CompilerParams(vmem_limit_bytes=VMEM_LIMIT),
        cost_estimate=pl.CostEstimate(flops=flops, bytes_accessed=nbytes, transcendentals=trans),
    )


def swap(value, axis, distance, senders=None):
    senders = range(lax.axis_size(axis)) if senders is None else senders
    return lax.ppermute(value, axis, [(i, i ^ distance) for i in senders])


def all_of(copies):
    for copy in copies:
        copy.start()
    for copy in copies:
        copy.wait()


def read_messages(refs):
    if len(refs) == 1:
        return [refs[0][i].astype(F32) for i in range(refs[0].shape[0])]
    held = [refs[0][0].astype(F32)] + [None] * (DIRECT - 1)
    for ref, (k, _) in zip(refs[1:], ROUNDS):
        came = ref[0].astype(F32)
        held[k] = came if held[k] is None else held[k] + came
    return held


def in_parts(source, target, sems, first, count):
    rows = source.shape[0] // count
    at = [pl.ds(i * rows, rows) for i in range(count)]
    return [
        pltpu.make_async_copy(source.at[a], target.at[a], sems.at[first + i])
        for i, a in enumerate(at)
    ]


def scalar_onehot(numbers_s, key, shape):
    row_of = lax.broadcasted_iota(jnp.int32, shape, 0)
    wanted = jnp.zeros(shape, jnp.int32)
    for b in range(shape[0]):
        wanted = jnp.where(row_of == b, jnp.bitwise_xor(numbers_s[b], key), wanted)
    return (wanted == lax.broadcasted_iota(jnp.int32, shape, 1)).astype(F32)


def pick_rows(pick, rows):
    total = pick[:, 0:1] * rows[0]
    for k in range(1, len(rows)):
        total = total + pick[:, k : k + 1] * rows[k]
    return total


def pack_kernel(direct, key_hbm, rows_hbm, prompt_hbm, step_hbm, conv_hbm, ssm_hbm, *rest):
    outs, (key_s, rows_s, prompt_s, step, conv, ssm, sems) = rest[:-7], rest[-7:]
    owners = rows_hbm.shape[0]
    channels = step_hbm.shape[3]
    copies = [
        pltpu.make_async_copy(key_hbm, key_s, sems.at[4]),
        pltpu.make_async_copy(rows_hbm, rows_s, sems.at[0]),
        pltpu.make_async_copy(prompt_hbm, prompt_s, sems.at[1]),
        pltpu.make_async_copy(conv_hbm, conv, sems.at[2]),
        pltpu.make_async_copy(ssm_hbm, ssm, sems.at[3]),
    ]
    all_of(copies + in_parts(step_hbm, step, sems, 5, 4))
    key = key_s[0]
    window = conv[0].astype(F32)
    for k in range(owners):
        target = jnp.bitwise_xor(key, k)
        row = jnp.maximum(rows_s[target], 0)
        xs = step[row, :, 0, :].astype(F32)
        told = jnp.bitwise_xor(prompt_s[row], target) if direct else prompt_s[row]
        pieces = [xs, window, jnp.full((1, channels), told.astype(F32), F32)]
        message = jnp.concatenate(pieces + [ssm[0]], axis=0).astype(BF16)
        if direct:
            into = [outs[0].at[0]] if k == 0 else []
            into += [ref.at[0] for ref, (d, _) in zip(outs[1:], ROUNDS) if d == k]
        else:
            into = [outs[0].at[k]]
        for ref in into:
            ref[...] = message


def silu(v):
    return v / (1.0 + jnp.exp(-v))


def prepare_kernel(
    key_hbm,
    prompt_hbm,
    step_ref,
    cw_hbm,
    cb_hbm,
    xwt_hbm,
    alog_hbm,
    dtw_hbm,
    dtb_hbm,
    skip_hbm,
    after_ref,
    base_ref,
    gate_ref,
    pick_ref,
    cw_ref,
    cb_ref,
    xwt_ref,
    rate_ref,
    twin_ref,
    dtw_ref,
    dtb_ref,
    skip_ref,
    key_s,
    prompt_s,
    alog,
    sems,
):
    del after_ref
    small = [
        pltpu.make_async_copy(source, target, sems.at[i])
        for i, (source, target) in enumerate(
            (
                (cw_hbm, cw_ref),
                (cb_hbm, cb_ref),
                (key_hbm, key_s),
                (prompt_hbm, prompt_s),
                (alog_hbm, alog),
                (dtb_hbm, dtb_ref),
                (skip_hbm, skip_ref),
            )
        )
    ]
    large = in_parts(xwt_hbm, xwt_ref, sems, len(small), WEIGHT_PARTS)
    large += in_parts(dtw_hbm, dtw_ref, sems, len(small) + WEIGHT_PARTS, DT_PARTS)
    for copy in small + large:
        copy.start()
    steps = step_ref.shape[1]
    taps = cw_hbm.shape[0]
    xs = [step_ref[:, t, 0, :].astype(F32) for t in range(steps)]
    for t in range(steps):
        gate_ref[t] = silu(step_ref[:, t, 1, :].astype(F32))
    for copy in small:
        copy.wait()
    for t in range(steps):
        total = cw_ref[taps - 1 : taps, :] * xs[t] + cb_ref[...]
        for k in range(max(0, taps - 1 - t), taps - 1):
            total = total + cw_ref[k : k + 1, :] * xs[t + k - taps + 1]
        base_ref[t] = total
    pick_ref[...] = scalar_onehot(prompt_s, key_s[0], pick_ref.shape)
    rate = jnp.exp(alog[...]) * (-math.log2(math.e))
    rate_ref[...] = rate
    half = (twin_ref.shape[1] // 2, rate.shape[1])
    for m in range(rate.shape[0] // 2):
        two = [jnp.broadcast_to(rate[n : n + 1, :], half) for n in (2 * m, 2 * m + 1)]
        twin_ref[m] = jnp.concatenate(two, axis=0)
    for copy in large:
        copy.wait()


def slot_onehot(numbers, owners):
    column = lax.broadcasted_iota(jnp.int32, (numbers.shape[0], owners), 1)
    return (numbers[:, :owners].astype(jnp.int32) == column).astype(F32)


def project_kernel(n_msgs, pick_ref, base_ref, cw_ref, cb_ref, xwt_ref, *rest):
    msgs, (act_ref, part_ref) = rest[:n_msgs], rest[n_msgs:]
    taps = cw_ref.shape[0]
    steps, rb, _ = base_ref.shape
    past = taps - 1
    held = read_messages(msgs)
    owners = len(held)
    windows = [[h[steps + k : steps + k + 1, :] for h in held] for k in range(past)]
    own = pick_ref[...]
    own_windows = [pick_rows(own, w) for w in windows]
    for t in range(steps):
        conv = base_ref[t]
        for k in range(past - t):
            conv = conv + cw_ref[k : k + 1, :] * own_windows[t + k]
        act_ref[t * rb : (t + 1) * rb, :] = silu(conv)

    def line_of(row):
        return jnp.concatenate([h[row : row + 1, :] for h in held], axis=0)

    slot = slot_onehot(line_of(past + steps), owners)
    line = [pick_rows(slot, w) for w in windows]
    line += [line_of(t) for t in range(steps)]
    row = steps * rb
    for t in range(steps):
        conv = cw_ref[past:taps, :] * line[t + past] + cb_ref[...]
        for k in range(past):
            conv = conv + cw_ref[k : k + 1, :] * line[t + k]
        act_ref[row : row + owners, :] = silu(conv)
        row += owners
    part_ref[...] = lax.dot_general(
        act_ref[...].astype(BF16),
        xwt_ref[...],
        (((1,), (1,)), ((), ())),
        preferred_element_type=F32,
    )


def add_kernel(a_ref, b_ref, sum_ref, short_ref):
    total = a_ref[...] + b_ref[...].astype(F32)
    sum_ref[...] = total
    short_ref[...] = total.astype(BF16)


def windows_kernel(n_msgs, steps, key_hbm, child_hbm, after_ref, *rest):
    del after_ref
    msgs, (conv_ref, key_s, child_s, sems) = rest[:n_msgs], rest[n_msgs:]
    all_of(
        [
            pltpu.make_async_copy(key_hbm, key_s, sems.at[0]),
            pltpu.make_async_copy(child_hbm, child_s, sems.at[1]),
        ]
    )
    past, rb, _ = conv_ref.shape
    held = read_messages(msgs)
    child = scalar_onehot(child_s, key_s[0], (rb, len(held)))
    for k in range(past):
        at = steps - past + k
        conv_ref[k] = pick_rows(child, [h[at : at + 1, :] for h in held]).astype(BF16)


def start_kernel(n_msgs, text, pick_ref, after_ref, *rest):
    del after_ref
    msgs, (own_ref, slot_ref, state_s) = rest[:n_msgs], rest[n_msgs:]
    n_state = own_ref.shape[0]
    held = read_messages(msgs)
    owners = len(held)
    numbers = jnp.concatenate([h[text - 1 : text, :] for h in held], axis=0)
    for k, h in enumerate(held):
        state_s[k] = h[text:, :]
    own = pick_ref[...]
    slot = slot_onehot(numbers, owners)

    def two(m, carry):
        picked = []
        for n in (2 * m, 2 * m + 1):
            rows = [state_s[k, pl.ds(n, 1), :] for k in range(owners)]
            own_ref[n] = pick_rows(own, rows)
            picked.append(pick_rows(slot, rows))
        slot_ref[m] = jnp.concatenate(picked, axis=0)
        return carry

    lax.fori_loop(0, n_state // 2, two, 0, unroll=owners <= DIRECT)


def decode_kernel(
    key_hbm,
    child_hbm,
    act_ref,
    gate_ref,
    own_ref,
    slot_ref,
    rate_ref,
    twin_ref,
    dtw_ref,
    dtb_ref,
    skip_ref,
    part_ref,
    other_ref,
    dec_ref,
    child_ssm,
    key_s,
    child_s,
    delta_s,
    gain_s,
    slot_delta_s,
    slot_gain_s,
    b_s,
    c_s,
    twin_b_s,
    slots_s,
    line_s,
    sems,
):
    scalars = [
        pltpu.make_async_copy(key_hbm, key_s, sems.at[0]),
        pltpu.make_async_copy(child_hbm, child_s, sems.at[1]),
    ]
    for copy in scalars:
        copy.start()
    rb, steps, channels = dec_ref.shape
    rank = dtw_ref.shape[0]
    n_state = rate_ref.shape[0]
    n_slots = slots_s.shape[0]
    own_rows = steps * rb
    chunks = channels // LANES

    proj = part_ref[...] + other_ref[...].astype(F32)
    delta_in = proj[:, :rank].astype(BF16)
    delta = jnp.dot(delta_in, dtw_ref[...], preferred_element_type=F32) + dtb_ref[...]
    delta = jnp.maximum(delta, 0.0) + jnp.log(1.0 + jnp.exp(-jnp.abs(delta)))
    gain = delta * act_ref[...]
    delta_s[...] = delta[:own_rows, :]
    gain_s[...] = gain[:own_rows, :]

    def column(at, n, rows):
        return jnp.broadcast_to(at[:, n : n + 1], (rows, LANES))

    for t in range(steps):
        at = slice(own_rows + t * n_slots, own_rows + (t + 1) * n_slots)
        slot_delta_s[t] = jnp.concatenate([delta[at, :]] * 2, axis=0)
        slot_gain_s[t] = jnp.concatenate([gain[at, :]] * 2, axis=0)
        twice = jnp.concatenate([proj[at, rank:]] * 2, axis=0)
        upper = lax.broadcasted_iota(jnp.int32, (2 * n_slots, LANES), 0) < n_slots
        for m in range(n_state // 2):
            twin_b_s[m, t] = jnp.where(
                upper, column(twice, 2 * m, 2 * n_slots), column(twice, 2 * m + 1, 2 * n_slots)
            )
    for n in range(n_state):
        b_s[n] = column(proj[:own_rows, rank:], n, own_rows)
        c_s[n] = column(proj[:own_rows, rank:], n_state + n, own_rows)

    def slot_chunk(chunk, carry):
        columns = pl.ds(pl.multiple_of(chunk * LANES, LANES), LANES)
        delta = [slot_delta_s[t, :, columns] for t in range(steps)]
        gain = [slot_gain_s[t, :, columns] for t in range(steps)]
        for m in range(n_state // 2):
            rate = twin_ref[m, :, columns]
            state = slot_ref[m, :, columns]
            for t in range(steps):
                state = jnp.exp2(delta[t] * rate) * state + gain[t] * twin_b_s[m, t]
            slots_s[:, 2 * m, columns] = state[:n_slots, :]
            slots_s[:, 2 * m + 1, columns] = state[n_slots:, :]
        return carry

    lax.fori_loop(0, chunks, slot_chunk, 0)
    for copy in scalars:
        copy.wait()
    copies = []
    for j in range(rb):
        at = jnp.bitwise_xor(child_s[j], key_s[0])
        copy = pltpu.make_async_copy(slots_s.at[at], child_ssm.at[j], sems.at[2 + j])
        copy.start()
        copies.append(copy)

    def own_chunk(chunk, carry):
        columns = pl.ds(pl.multiple_of(chunk * LANES, LANES), LANES)
        at = [pl.ds(t * rb, rb) for t in range(steps)]
        delta = [delta_s[a, columns] for a in at]
        gain = [gain_s[a, columns] for a in at]
        sums = [skip_ref[:, columns] * act_ref[a, columns] for a in at]
        for n in range(n_state):
            rate = rate_ref[n : n + 1, columns]
            state = own_ref[n, :, columns]
            for t in range(steps):
                state = jnp.exp2(delta[t] * rate) * state + gain[t] * b_s[n, at[t], :]
                sums[t] = sums[t] + c_s[n, at[t], :] * state
        for t in range(steps):
            line_s[pl.ds(t, rb, stride=steps), :] = sums[t] * gate_ref[t, :, columns]
        dec_ref[:, :, columns] = line_s[...].reshape(rb, steps, LANES).astype(BF16)
        return carry

    lax.fori_loop(0, chunks, own_chunk, 0)
    for copy in copies:
        copy.wait()


def on_device(
    prompt_ssm,
    prompt_conv,
    prompt_of,
    step_in,
    conv_weight,
    conv_bias,
    x_weight,
    dt_weight,
    dt_bias,
    a_log,
    skip,
    send_rows,
    child_slot,
):
    owners = lax.axis_size("branch")
    tensors = lax.axis_size("tensor")
    assert owners & (owners - 1) == 0 and tensors & (tensors - 1) == 0
    assert prompt_ssm.shape[0] == 1 and send_rows.shape[2] == 1
    rb, steps, _, channels = step_in.shape
    taps = conv_weight.shape[0]
    width = x_weight.shape[1]
    n_state = a_log.shape[0]
    rows = steps * (rb + owners)
    short = taps - 1 + steps + 1
    depth = short + n_state
    direct = owners == DIRECT
    me = lax.axis_index("branch").astype(jnp.int32).reshape(1)
    key = pinned(me if direct else jnp.zeros((1,), jnp.int32))

    if direct:
        msg_shapes = [(1, depth, channels)] * (1 + len(ROUNDS))
    else:
        msg_shapes = [(owners, depth, channels)]
    msgs = call(
        functools.partial(pack_kernel, direct),
        [shaped(s, BF16) for s in msg_shapes],
        [hbm()] * 6,
        [vmem()] * len(msg_shapes),
        [
            pltpu.SMEM((1,), jnp.int32),
            pltpu.SMEM((owners,), jnp.int32),
            pltpu.SMEM((rb,), jnp.int32),
            pltpu.VMEM(step_in.shape, BF16),
            pltpu.VMEM(prompt_conv.shape, BF16),
            pltpu.VMEM(prompt_ssm.shape, F32),
            pltpu.SemaphoreType.DMA((9,)),
        ],
        nbytes=owners * depth * channels * 2,
    )(
        key,
        pinned(send_rows.reshape(owners)),
        pinned(prompt_of),
        pinned(step_in),
        pinned(prompt_conv),
        pinned(prompt_ssm),
    )
    if direct:
        own = msgs[0]
        msgs = [own] + [swap(m, "branch", k, who) for m, (k, who) in zip(msgs[1:], ROUNDS)]
        after = own
    else:
        msgs = [lax.all_to_all(msgs[0], "branch", split_axis=0, concat_axis=0, tiled=True)]
        after = msgs[0]
    n_msgs = len(msgs)
    near = call(
        prepare_kernel,
        [
            shaped((steps, rb, channels), F32),
            shaped((steps, rb, channels), F32),
            shaped((rb, owners), F32),
            shaped((taps, channels), F32),
            shaped((1, channels), F32),
            shaped((width, channels), BF16),
            shaped((n_state, channels), F32),
            shaped((n_state // 2, 2 * owners, channels), F32),
            shaped(dt_weight.shape, BF16),
            shaped((1, channels), F32),
            shaped((1, channels), F32),
        ],
        [hbm(), hbm(), vmem()] + [hbm()] * 7 + [anywhere()],
        [vmem()] * 11,
        [
            pltpu.SMEM((1,), jnp.int32),
            pltpu.SMEM((rb,), jnp.int32),
            pltpu.VMEM((n_state, channels), F32),
            pltpu.SemaphoreType.DMA((7 + WEIGHT_PARTS + DT_PARTS,)),
        ],
        flops=10 * steps * rb * channels,
        nbytes=12 * steps * rb * channels,
        trans=steps * rb * channels,
    )(
        key,
        pinned(prompt_of),
        step_in,
        pinned(conv_weight),
        pinned(conv_bias[None]),
        pinned(x_weight.T),
        pinned(a_log),
        pinned(dt_weight),
        pinned(dt_bias[None]),
        pinned(skip[None]),
        after,
    )
    base, gate, pick, taps_near, bias_near, weight_near = near[:6]
    rate, twin, dtw_near, dtb_near, skip_near = near[6:]
    act, part = call(
        functools.partial(project_kernel, n_msgs),
        [
            shaped((rows, channels), F32),
            shaped((rows, width), F32),
        ],
        [vmem()] * (5 + n_msgs),
        [vmem()] * 2,
        flops=2 * rows * channels * width,
        nbytes=channels * width * 2 + rows * (channels + width) * 4,
        trans=rows * channels,
    )(pick, base, taps_near, bias_near, weight_near, *msgs)
    other = swap(part, "tensor", 1)
    distance = 2
    while distance < tensors:
        part, brief = call(
            add_kernel,
            [shaped((rows, width), F32), shaped((rows, width), BF16)],
            [vmem()] * 2,
            [vmem()] * 2,
            flops=rows * width,
            nbytes=rows * width * 14,
        )(part, other)
        other = swap(brief, "tensor", distance)
        distance *= 2

    child_conv = call(
        functools.partial(windows_kernel, n_msgs, steps),
        shaped((taps - 1, rb, channels), BF16),
        [hbm()] * 2 + [anywhere()] + [vmem()] * n_msgs,
        vmem(),
        [
            pltpu.SMEM((1,), jnp.int32),
            pltpu.SMEM((rb,), jnp.int32),
            pltpu.SemaphoreType.DMA((2,)),
        ],
        flops=2 * owners * taps * rb * channels,
        nbytes=4 * taps * rb * channels,
    )(key, pinned(child_slot), part, *msgs)
    own_start, slot_start = call(
        functools.partial(start_kernel, n_msgs, short),
        [
            shaped((n_state, rb, channels), F32),
            shaped((n_state // 2, 2 * owners, channels), F32),
        ],
        [vmem(), anywhere()] + [vmem()] * n_msgs,
        [vmem()] * 2,
        [pltpu.VMEM((owners, n_state, channels), F32)],
        flops=2 * owners * n_state * (rb + owners) * channels,
        nbytes=4 * n_state * (rb + owners) * channels,
    )(pick, part, *msgs)

    decoded, child_ssm = call(
        decode_kernel,
        [
            shaped((rb, steps, channels), BF16),
            shaped((rb, n_state, channels), F32),
        ],
        [hbm()] * 2 + [vmem()] * 11,
        [vmem(), anywhere()],
        [
            pltpu.SMEM((1,), jnp.int32),
            pltpu.SMEM((rb,), jnp.int32),
            pltpu.VMEM((steps * rb, channels), F32),
            pltpu.VMEM((steps * rb, channels), F32),
            pltpu.VMEM((steps, 2 * owners, channels), F32),
            pltpu.VMEM((steps, 2 * owners, channels), F32),
            pltpu.VMEM((n_state, steps * rb, LANES), F32),
            pltpu.VMEM((n_state, steps * rb, LANES), F32),
            pltpu.VMEM((n_state // 2, steps, 2 * owners, LANES), F32),
            pltpu.VMEM((owners, n_state, channels), F32),
            pltpu.VMEM((steps * rb, LANES), F32),
            pltpu.SemaphoreType.DMA((2 + rb,)),
        ],
        flops=8 * rows * n_state * channels,
        nbytes=(rb + owners) * n_state * channels * 4,
        trans=rows * n_state * channels,
    )(
        key,
        pinned(child_slot),
        act,
        gate,
        own_start,
        slot_start,
        rate,
        twin,
        dtw_near,
        dtb_near,
        skip_near,
        part,
        other,
    )
    return (decoded, child_ssm, jnp.transpose(child_conv, (1, 0, 2)))


def solution(mesh):
    placed = (
        P(("replica", "branch"), None, "tensor"),
        P(("replica", "branch"), None, "tensor"),
        P(("replica", "branch")),
        P(("replica", "branch"), None, None, "tensor"),
        P(None, "tensor"),
        P("tensor"),
        P("tensor", None),
        P(None, "tensor"),
        P("tensor"),
        P(None, "tensor"),
        P("tensor"),
        P(("replica", "branch"), None, None),
        P(("replica", "branch")),
    )
    return jax.shard_map(
        on_device,
        mesh=mesh,
        in_specs=placed,
        out_specs=(
            P(("replica", "branch"), None, "tensor"),
            P(("replica", "branch"), None, "tensor"),
            P(("replica", "branch"), None, "tensor"),
        ),
        check_vma=False,
    )
```

```python
import functools
import math

import jax
import jax.numpy as jnp
from jax import lax
from jax.experimental import pallas as pl
from jax.experimental.pallas import tpu as pltpu
from jax.sharding import PartitionSpec as P

F32 = jnp.float32
BF16 = jnp.bfloat16
LANES = 128
VMEM_LIMIT = 48 * 2**20
WEIGHT_PARTS = 6
DT_PARTS = 4
DIRECT = 4
SENDS = ((2, 3, 1, 0), (3, 2, 0, 1), (1, 0, 3, 2))


def vmem():
    return pl.BlockSpec(memory_space=pltpu.VMEM)


def hbm():
    return pl.BlockSpec(memory_space=pltpu.HBM)


def anywhere():
    return pl.BlockSpec(memory_space=pl.ANY)


def pinned(array):
    return pltpu.with_memory_space_constraint(array, pltpu.HBM)


def shaped(shape, dtype):
    return jax.ShapeDtypeStruct(shape, dtype)


def call(kernel, outs, in_specs, out_specs, scratch=(), flops=0, nbytes=0, trans=0):
    return pl.pallas_call(
        kernel,
        out_shape=outs,
        in_specs=in_specs,
        out_specs=out_specs,
        scratch_shapes=list(scratch),
        compiler_params=pltpu.CompilerParams(vmem_limit_bytes=VMEM_LIMIT),
        cost_estimate=pl.CostEstimate(flops=flops, bytes_accessed=nbytes, transcendentals=trans),
    )


def swap(value, axis, distance):
    size = lax.axis_size(axis)
    return lax.ppermute(value, axis, [(i, i ^ distance) for i in range(size)])


def chosen(number, values):
    total = values[0]
    for i in range(1, len(values)):
        total = jnp.where(number == i, values[i], total)
    return total


def block_of(sender, owner, direct):
    if not direct:
        return sender
    table = [
        [0 if s == r else 1 + [to[s] for to in SENDS].index(r) for s in range(DIRECT)]
        for r in range(DIRECT)
    ]
    places = [chosen(owner, [row[s] for row in table]) for s in range(DIRECT)]
    return chosen(sender, places)


def all_of(copies):
    for copy in copies:
        copy.start()
    for copy in copies:
        copy.wait()


def read_messages(refs):
    return [ref[i].astype(F32) for ref in refs for i in range(ref.shape[0])]


def in_parts(source, target, sems, first, count):
    rows = source.shape[0] // count
    at = [pl.ds(i * rows, rows) for i in range(count)]
    return [
        pltpu.make_async_copy(source.at[a], target.at[a], sems.at[first + i])
        for i, a in enumerate(at)
    ]


def scalar_onehot(senders_s, owner, shape, direct):
    row_of = lax.broadcasted_iota(jnp.int32, shape, 0)
    wanted = jnp.zeros(shape, jnp.int32)
    for b in range(shape[0]):
        wanted = jnp.where(row_of == b, senders_s[b], wanted)
    wanted = block_of(wanted, owner, direct)
    return (wanted == lax.broadcasted_iota(jnp.int32, shape, 1)).astype(F32)


def pick_rows(pick, rows):
    total = pick[:, 0:1] * rows[0]
    for k in range(1, len(rows)):
        total = total + pick[:, k : k + 1] * rows[k]
    return total


def pack_kernel(direct, owner_hbm, rows_hbm, prompt_hbm, step_hbm, conv_hbm, ssm_hbm, *rest):
    outs, (owner_s, rows_s, prompt_s, step, conv, ssm, sems) = rest[:-7], rest[-7:]
    owners = rows_hbm.shape[0]
    channels = step_hbm.shape[3]
    copies = [
        pltpu.make_async_copy(owner_hbm, owner_s, sems.at[4]),
        pltpu.make_async_copy(rows_hbm, rows_s, sems.at[0]),
        pltpu.make_async_copy(prompt_hbm, prompt_s, sems.at[1]),
        pltpu.make_async_copy(conv_hbm, conv, sems.at[2]),
        pltpu.make_async_copy(ssm_hbm, ssm, sems.at[3]),
    ]
    all_of(copies + in_parts(step_hbm, step, sems, 5, 4))
    owner = owner_s[0]
    window = conv[0].astype(F32)

    def write(ref, target):
        row = jnp.maximum(rows_s[target], 0)
        xs = step[row, :, 0, :].astype(F32)
        told = block_of(prompt_s[row], target, direct)
        pieces = [xs, window, jnp.full((1, channels), told.astype(F32), F32)]
        if ref.shape[0] > sum(p.shape[0] for p in pieces):
            pieces.append(ssm[0])
        ref[...] = jnp.concatenate(pieces, axis=0).astype(BF16)

    if direct:
        write(outs[0].at[0], owner)
        for ref, to in zip(outs[1:], SENDS):
            write(ref.at[0], chosen(owner, to))
    else:
        for target in range(owners):
            write(outs[0].at[target], target)


def pair_kernel(text, own_ref, other_ref, pair_ref):
    states = [ref[0].astype(F32)[text:, :] for ref in (own_ref, other_ref)]
    pair_ref[0] = jnp.concatenate(states, axis=0).astype(BF16)


def silu(v):
    return v / (1.0 + jnp.exp(-v))


def prepare_kernel(
    direct,
    owner_hbm,
    prompt_hbm,
    child_hbm,
    step_ref,
    cw_hbm,
    cb_hbm,
    xwt_hbm,
    alog_hbm,
    dtw_hbm,
    dtb_hbm,
    skip_hbm,
    after_ref,
    base_ref,
    gate_ref,
    pick_ref,
    child_ref,
    cw_ref,
    cb_ref,
    xwt_ref,
    rate_ref,
    twin_ref,
    dtw_ref,
    dtb_ref,
    skip_ref,
    owner_s,
    prompt_s,
    child_s,
    alog,
    sems,
):
    del after_ref
    small = [
        pltpu.make_async_copy(source, target, sems.at[i])
        for i, (source, target) in enumerate(
            (
                (cw_hbm, cw_ref),
                (cb_hbm, cb_ref),
                (owner_hbm, owner_s),
                (prompt_hbm, prompt_s),
                (child_hbm, child_s),
                (alog_hbm, alog),
                (dtb_hbm, dtb_ref),
                (skip_hbm, skip_ref),
            )
        )
    ]
    large = in_parts(xwt_hbm, xwt_ref, sems, len(small), WEIGHT_PARTS)
    large += in_parts(dtw_hbm, dtw_ref, sems, len(small) + WEIGHT_PARTS, DT_PARTS)
    for copy in small + large:
        copy.start()
    steps = step_ref.shape[1]
    taps = cw_hbm.shape[0]
    xs = [step_ref[:, t, 0, :].astype(F32) for t in range(steps)]
    for t in range(steps):
        gate_ref[t] = silu(step_ref[:, t, 1, :].astype(F32))
    for copy in small:
        copy.wait()
    for t in range(steps):
        total = cw_ref[taps - 1 : taps, :] * xs[t] + cb_ref[...]
        for k in range(max(0, taps - 1 - t), taps - 1):
            total = total + cw_ref[k : k + 1, :] * xs[t + k - taps + 1]
        base_ref[t] = total
    pick_ref[...] = scalar_onehot(prompt_s, owner_s[0], pick_ref.shape, direct)
    child_ref[...] = scalar_onehot(child_s, owner_s[0], child_ref.shape, direct)
    rate = jnp.exp(alog[...]) * (-math.log2(math.e))
    rate_ref[...] = rate
    half = (twin_ref.shape[1] // 2, rate.shape[1])
    for m in range(rate.shape[0] // 2):
        two = [jnp.broadcast_to(rate[n : n + 1, :], half) for n in (2 * m, 2 * m + 1)]
        twin_ref[m] = jnp.concatenate(two, axis=0)
    for copy in large:
        copy.wait()


def slot_onehot(numbers, owners):
    column = lax.broadcasted_iota(jnp.int32, (numbers.shape[0], owners), 1)
    return (numbers[:, :owners].astype(jnp.int32) == column).astype(F32)


def project_kernel(n_msgs, pick_ref, base_ref, cw_ref, cb_ref, xwt_ref, *rest):
    msgs, (act_ref, part_ref) = rest[:n_msgs], rest[n_msgs:]
    taps = cw_ref.shape[0]
    steps, rb, _ = base_ref.shape
    past = taps - 1
    held = read_messages(msgs)
    owners = len(held)
    windows = [[h[steps + k : steps + k + 1, :] for h in held] for k in range(past)]
    own = pick_ref[...]
    own_windows = [pick_rows(own, w) for w in windows]
    for t in range(steps):
        conv = base_ref[t]
        for k in range(past - t):
            conv = conv + cw_ref[k : k + 1, :] * own_windows[t + k]
        act_ref[t * rb : (t + 1) * rb, :] = silu(conv)

    def line_of(row):
        return jnp.concatenate([h[row : row + 1, :] for h in held], axis=0)

    slot = slot_onehot(line_of(past + steps), owners)
    line = [pick_rows(slot, w) for w in windows]
    line += [line_of(t) for t in range(steps)]
    row = steps * rb
    for t in range(steps):
        conv = cw_ref[past:taps, :] * line[t + past] + cb_ref[...]
        for k in range(past):
            conv = conv + cw_ref[k : k + 1, :] * line[t + k]
        act_ref[row : row + owners, :] = silu(conv)
        row += owners
    part_ref[...] = lax.dot_general(
        act_ref[...].astype(BF16),
        xwt_ref[...],
        (((1,), (1,)), ((), ())),
        preferred_element_type=F32,
    )


def add_kernel(a_ref, b_ref, sum_ref, short_ref):
    total = a_ref[...] + b_ref[...].astype(F32)
    sum_ref[...] = total
    short_ref[...] = total.astype(BF16)


def windows_kernel(n_msgs, steps, child_ref, after_ref, *rest):
    del after_ref
    msgs, (conv_ref,) = rest[:n_msgs], rest[n_msgs:]
    held = read_messages(msgs)
    past = conv_ref.shape[0]
    for k in range(past):
        at = steps - past + k
        rows = [h[at : at + 1, :] for h in held]
        conv_ref[k] = pick_rows(child_ref[...], rows).astype(BF16)


def start_kernel(n_msgs, n_pairs, text, pick_ref, after_ref, *rest):
    del after_ref
    msgs, rest = rest[:n_msgs], rest[n_msgs:]
    pairs, (own_ref, slot_ref, state_s) = rest[:n_pairs], rest[n_pairs:]
    n_state = own_ref.shape[0]
    held = read_messages(msgs)
    owners = len(held)
    numbers = jnp.concatenate([h[text - 1 : text, :] for h in held], axis=0)
    states = [h[text:, :] for h in held]
    for ref in pairs:
        both = ref[0].astype(F32)
        states[3], states[2] = both[:n_state, :], both[n_state:, :]
    for k, state in enumerate(states):
        state_s[k] = state
    own = pick_ref[...]
    slot = slot_onehot(numbers, owners)

    def two(m, carry):
        picked = []
        for n in (2 * m, 2 * m + 1):
            rows = [state_s[k, pl.ds(n, 1), :] for k in range(owners)]
            own_ref[n] = pick_rows(own, rows)
            picked.append(pick_rows(slot, rows))
        slot_ref[m] = jnp.concatenate(picked, axis=0)
        return carry

    lax.fori_loop(0, n_state // 2, two, 0, unroll=owners <= DIRECT)


def decode_kernel(
    direct,
    owner_hbm,
    child_hbm,
    act_ref,
    gate_ref,
    own_ref,
    slot_ref,
    rate_ref,
    twin_ref,
    dtw_ref,
    dtb_ref,
    skip_ref,
    part_ref,
    other_ref,
    dec_ref,
    child_ssm,
    owner_s,
    child_s,
    delta_s,
    gain_s,
    slot_delta_s,
    slot_gain_s,
    b_s,
    c_s,
    twin_b_s,
    slots_s,
    line_s,
    sems,
):
    scalars = [
        pltpu.make_async_copy(owner_hbm, owner_s, sems.at[0]),
        pltpu.make_async_copy(child_hbm, child_s, sems.at[1]),
    ]
    for copy in scalars:
        copy.start()
    rb, steps, channels = dec_ref.shape
    rank = dtw_ref.shape[0]
    n_state = rate_ref.shape[0]
    n_slots = slots_s.shape[0]
    own_rows = steps * rb
    chunks = channels // LANES

    proj = part_ref[...] + other_ref[...].astype(F32)
    delta_in = proj[:, :rank].astype(BF16)
    delta = jnp.dot(delta_in, dtw_ref[...], preferred_element_type=F32) + dtb_ref[...]
    delta = jnp.maximum(delta, 0.0) + jnp.log(1.0 + jnp.exp(-jnp.abs(delta)))
    gain = delta * act_ref[...]
    delta_s[...] = delta[:own_rows, :]
    gain_s[...] = gain[:own_rows, :]

    def column(at, n, rows):
        return jnp.broadcast_to(at[:, n : n + 1], (rows, LANES))

    for t in range(steps):
        at = slice(own_rows + t * n_slots, own_rows + (t + 1) * n_slots)
        slot_delta_s[t] = jnp.concatenate([delta[at, :]] * 2, axis=0)
        slot_gain_s[t] = jnp.concatenate([gain[at, :]] * 2, axis=0)
        twice = jnp.concatenate([proj[at, rank:]] * 2, axis=0)
        upper = lax.broadcasted_iota(jnp.int32, (2 * n_slots, LANES), 0) < n_slots
        for m in range(n_state // 2):
            twin_b_s[m, t] = jnp.where(
                upper, column(twice, 2 * m, 2 * n_slots), column(twice, 2 * m + 1, 2 * n_slots)
            )
    for n in range(n_state):
        b_s[n] = column(proj[:own_rows, rank:], n, own_rows)
        c_s[n] = column(proj[:own_rows, rank:], n_state + n, own_rows)

    def slot_chunk(chunk, carry):
        columns = pl.ds(pl.multiple_of(chunk * LANES, LANES), LANES)
        delta = [slot_delta_s[t, :, columns] for t in range(steps)]
        gain = [slot_gain_s[t, :, columns] for t in range(steps)]
        for m in range(n_state // 2):
            rate = twin_ref[m, :, columns]
            state = slot_ref[m, :, columns]
            for t in range(steps):
                state = jnp.exp2(delta[t] * rate) * state + gain[t] * twin_b_s[m, t]
            slots_s[:, 2 * m, columns] = state[:n_slots, :]
            slots_s[:, 2 * m + 1, columns] = state[n_slots:, :]
        return carry

    lax.fori_loop(0, chunks, slot_chunk, 0)
    for copy in scalars:
        copy.wait()
    copies = []
    for j in range(rb):
        at = block_of(child_s[j], owner_s[0], direct)
        copy = pltpu.make_async_copy(slots_s.at[at], child_ssm.at[j], sems.at[2 + j])
        copy.start()
        copies.append(copy)

    def own_chunk(chunk, carry):
        columns = pl.ds(pl.multiple_of(chunk * LANES, LANES), LANES)
        at = [pl.ds(t * rb, rb) for t in range(steps)]
        delta = [delta_s[a, columns] for a in at]
        gain = [gain_s[a, columns] for a in at]
        sums = [skip_ref[:, columns] * act_ref[a, columns] for a in at]
        for n in range(n_state):
            rate = rate_ref[n : n + 1, columns]
            state = own_ref[n, :, columns]
            for t in range(steps):
                state = jnp.exp2(delta[t] * rate) * state + gain[t] * b_s[n, at[t], :]
                sums[t] = sums[t] + c_s[n, at[t], :] * state
        for t in range(steps):
            line_s[pl.ds(t, rb, stride=steps), :] = sums[t] * gate_ref[t, :, columns]
        dec_ref[:, :, columns] = line_s[...].reshape(rb, steps, LANES).astype(BF16)
        return carry

    lax.fori_loop(0, chunks, own_chunk, 0)
    for copy in copies:
        copy.wait()


def on_device(
    prompt_ssm,
    prompt_conv,
    prompt_of,
    step_in,
    conv_weight,
    conv_bias,
    x_weight,
    dt_weight,
    dt_bias,
    a_log,
    skip,
    send_rows,
    child_slot,
):
    owners = lax.axis_size("branch")
    tensors = lax.axis_size("tensor")
    assert owners & (owners - 1) == 0 and tensors & (tensors - 1) == 0
    assert prompt_ssm.shape[0] == 1 and send_rows.shape[2] == 1
    rb, steps, _, channels = step_in.shape
    taps = conv_weight.shape[0]
    width = x_weight.shape[1]
    n_state = a_log.shape[0]
    rows = steps * (rb + owners)
    short = taps - 1 + steps + 1
    depth = short + n_state
    direct = owners == DIRECT
    owner = pinned(lax.axis_index("branch").astype(jnp.int32).reshape(1))

    if direct:
        msg_shapes = [(1, d, channels) for d in (depth, depth, short, short)]
    else:
        msg_shapes = [(owners, depth, channels)]
    msgs = call(
        functools.partial(pack_kernel, direct),
        [shaped(s, BF16) for s in msg_shapes],
        [hbm()] * 6,
        [vmem()] * len(msg_shapes),
        [
            pltpu.SMEM((1,), jnp.int32),
            pltpu.SMEM((owners,), jnp.int32),
            pltpu.SMEM((rb,), jnp.int32),
            pltpu.VMEM(step_in.shape, BF16),
            pltpu.VMEM(prompt_conv.shape, BF16),
            pltpu.VMEM(prompt_ssm.shape, F32),
            pltpu.SemaphoreType.DMA((9,)),
        ],
        nbytes=owners * depth * channels * 2,
    )(
        owner,
        pinned(send_rows.reshape(owners)),
        pinned(prompt_of),
        pinned(step_in),
        pinned(prompt_conv),
        pinned(prompt_ssm),
    )
    if direct:
        own = msgs[0]
        msgs = [own] + [
            lax.ppermute(m, "branch", list(enumerate(to))) for m, to in zip(msgs[1:], SENDS)
        ]
        pair = call(
            functools.partial(pair_kernel, short),
            shaped((1, 2 * n_state, channels), BF16),
            [vmem()] * 2,
            vmem(),
            nbytes=8 * n_state * channels,
        )(own, msgs[1])
        pairs, after = [swap(pair, "branch", 1)], own
    else:
        msgs = [lax.all_to_all(msgs[0], "branch", split_axis=0, concat_axis=0, tiled=True)]
        pairs, after = [], msgs[0]
    n_msgs = len(msgs)
    near = call(
        functools.partial(prepare_kernel, direct),
        [
            shaped((steps, rb, channels), F32),
            shaped((steps, rb, channels), F32),
            shaped((rb, owners), F32),
            shaped((rb, owners), F32),
            shaped((taps, channels), F32),
            shaped((1, channels), F32),
            shaped((width, channels), BF16),
            shaped((n_state, channels), F32),
            shaped((n_state // 2, 2 * owners, channels), F32),
            shaped(dt_weight.shape, BF16),
            shaped((1, channels), F32),
            shaped((1, channels), F32),
        ],
        [hbm()] * 3 + [vmem()] + [hbm()] * 7 + [anywhere()],
        [vmem()] * 12,
        [
            pltpu.SMEM((1,), jnp.int32),
            pltpu.SMEM((rb,), jnp.int32),
            pltpu.SMEM((rb,), jnp.int32),
            pltpu.VMEM((n_state, channels), F32),
            pltpu.SemaphoreType.DMA((8 + WEIGHT_PARTS + DT_PARTS,)),
        ],
        flops=10 * steps * rb * channels,
        nbytes=12 * steps * rb * channels,
        trans=steps * rb * channels,
    )(
        owner,
        pinned(prompt_of),
        pinned(child_slot),
        step_in,
        pinned(conv_weight),
        pinned(conv_bias[None]),
        pinned(x_weight.T),
        pinned(a_log),
        pinned(dt_weight),
        pinned(dt_bias[None]),
        pinned(skip[None]),
        after,
    )
    base, gate, pick, child_pick, taps_near, bias_near, weight_near = near[:7]
    rate, twin, dtw_near, dtb_near, skip_near = near[7:]
    act, part = call(
        functools.partial(project_kernel, n_msgs),
        [
            shaped((rows, channels), F32),
            shaped((rows, width), F32),
        ],
        [vmem()] * (5 + n_msgs),
        [vmem()] * 2,
        flops=2 * rows * channels * width,
        nbytes=channels * width * 2 + rows * (channels + width) * 4,
        trans=rows * channels,
    )(pick, base, taps_near, bias_near, weight_near, *msgs)
    other = swap(part, "tensor", 1)
    distance = 2
    while distance < tensors:
        part, brief = call(
            add_kernel,
            [shaped((rows, width), F32), shaped((rows, width), BF16)],
            [vmem()] * 2,
            [vmem()] * 2,
            flops=rows * width,
            nbytes=rows * width * 14,
        )(part, other)
        other = swap(brief, "tensor", distance)
        distance *= 2

    child_conv = call(
        functools.partial(windows_kernel, n_msgs, steps),
        shaped((taps - 1, rb, channels), BF16),
        [vmem(), anywhere()] + [vmem()] * n_msgs,
        vmem(),
        flops=2 * owners * taps * rb * channels,
        nbytes=4 * taps * rb * channels,
    )(child_pick, part, *msgs)
    own_start, slot_start = call(
        functools.partial(start_kernel, n_msgs, len(pairs), short),
        [
            shaped((n_state, rb, channels), F32),
            shaped((n_state // 2, 2 * owners, channels), F32),
        ],
        [vmem(), anywhere()] + [vmem()] * (n_msgs + len(pairs)),
        [vmem()] * 2,
        [pltpu.VMEM((owners, n_state, channels), F32)],
        flops=2 * owners * n_state * (rb + owners) * channels,
        nbytes=4 * n_state * (rb + owners) * channels,
    )(pick, part, *msgs, *pairs)

    decoded, child_ssm = call(
        functools.partial(decode_kernel, direct),
        [
            shaped((rb, steps, channels), BF16),
            shaped((rb, n_state, channels), F32),
        ],
        [hbm()] * 2 + [vmem()] * 11,
        [vmem(), anywhere()],
        [
            pltpu.SMEM((1,), jnp.int32),
            pltpu.SMEM((rb,), jnp.int32),
            pltpu.VMEM((steps * rb, channels), F32),
            pltpu.VMEM((steps * rb, channels), F32),
            pltpu.VMEM((steps, 2 * owners, channels), F32),
            pltpu.VMEM((steps, 2 * owners, channels), F32),
            pltpu.VMEM((n_state, steps * rb, LANES), F32),
            pltpu.VMEM((n_state, steps * rb, LANES), F32),
            pltpu.VMEM((n_state // 2, steps, 2 * owners, LANES), F32),
            pltpu.VMEM((owners, n_state, channels), F32),
            pltpu.VMEM((steps * rb, LANES), F32),
            pltpu.SemaphoreType.DMA((2 + rb,)),
        ],
        flops=8 * rows * n_state * channels,
        nbytes=(rb + owners) * n_state * channels * 4,
        trans=rows * n_state * channels,
    )(
        owner,
        pinned(child_slot),
        act,
        gate,
        own_start,
        slot_start,
        rate,
        twin,
        dtw_near,
        dtb_near,
        skip_near,
        part,
        other,
    )
    return (decoded, child_ssm, jnp.transpose(child_conv, (1, 0, 2)))


def solution(mesh):
    placed = (
        P(("replica", "branch"), None, "tensor"),
        P(("replica", "branch"), None, "tensor"),
        P(("replica", "branch")),
        P(("replica", "branch"), None, None, "tensor"),
        P(None, "tensor"),
        P("tensor"),
        P("tensor", None),
        P(None, "tensor"),
        P("tensor"),
        P(None, "tensor"),
        P("tensor"),
        P(("replica", "branch"), None, None),
        P(("replica", "branch")),
    )
    return jax.shard_map(
        on_device,
        mesh=mesh,
        in_specs=placed,
        out_specs=(
            P(("replica", "branch"), None, "tensor"),
            P(("replica", "branch"), None, "tensor"),
            P(("replica", "branch"), None, "tensor"),
        ),
        check_vma=False,
    )
```

```python
import functools
import math

import jax
import jax.numpy as jnp
from jax import lax
from jax.experimental import pallas as pl
from jax.experimental.pallas import tpu as pltpu
from jax.sharding import PartitionSpec as P

F32 = jnp.float32
BF16 = jnp.bfloat16
LANES = 128
VMEM_LIMIT = 48 * 2**20
WEIGHT_PARTS = 6
DT_PARTS = 4
DIRECT = 4
SENDS = ((2, 3, 1, 0), (3, 2, 0, 1), (1, 0, 3, 2))


def vmem():
    return pl.BlockSpec(memory_space=pltpu.VMEM)


def hbm():
    return pl.BlockSpec(memory_space=pltpu.HBM)


def anywhere():
    return pl.BlockSpec(memory_space=pl.ANY)


def pinned(array):
    return pltpu.with_memory_space_constraint(array, pltpu.HBM)


def shaped(shape, dtype):
    return jax.ShapeDtypeStruct(shape, dtype)


def call(kernel, outs, in_specs, out_specs, scratch=(), flops=0, nbytes=0, trans=0):
    return pl.pallas_call(
        kernel,
        out_shape=outs,
        in_specs=in_specs,
        out_specs=out_specs,
        scratch_shapes=list(scratch),
        compiler_params=pltpu.CompilerParams(vmem_limit_bytes=VMEM_LIMIT),
        cost_estimate=pl.CostEstimate(flops=flops, bytes_accessed=nbytes, transcendentals=trans),
    )


def swap(value, axis, distance):
    size = lax.axis_size(axis)
    return lax.ppermute(value, axis, [(i, i ^ distance) for i in range(size)])


def chosen(number, values):
    total = values[0]
    for i in range(1, len(values)):
        total = jnp.where(number == i, values[i], total)
    return total


def block_of(sender, owner, direct):
    if not direct:
        return sender
    table = [
        [0 if s == r else 1 + [to[s] for to in SENDS].index(r) for s in range(DIRECT)]
        for r in range(DIRECT)
    ]
    places = [chosen(owner, [row[s] for row in table]) for s in range(DIRECT)]
    return places[sender] if isinstance(sender, int) else chosen(sender, places)


def all_of(copies):
    for copy in copies:
        copy.start()
    for copy in copies:
        copy.wait()


def read_messages(refs):
    return [ref[i].astype(F32) for ref in refs for i in range(ref.shape[0])]


def in_parts(source, target, sems, first, count):
    rows = source.shape[0] // count
    at = [pl.ds(i * rows, rows) for i in range(count)]
    return [
        pltpu.make_async_copy(source.at[a], target.at[a], sems.at[first + i])
        for i, a in enumerate(at)
    ]


def scalar_onehot(senders_s, owner, shape, direct):
    row_of = lax.broadcasted_iota(jnp.int32, shape, 0)
    wanted = jnp.zeros(shape, jnp.int32)
    for b in range(shape[0]):
        wanted = jnp.where(row_of == b, senders_s[b], wanted)
    wanted = block_of(wanted, owner, direct)
    return (wanted == lax.broadcasted_iota(jnp.int32, shape, 1)).astype(F32)


def pick_rows(pick, rows):
    total = pick[:, 0:1] * rows[0]
    for k in range(1, len(rows)):
        total = total + pick[:, k : k + 1] * rows[k]
    return total


def pack_kernel(direct, owner_hbm, rows_hbm, prompt_hbm, step_hbm, conv_hbm, ssm_hbm, *rest):
    outs, (owner_s, rows_s, prompt_s, step, conv, ssm, sems) = rest[:-7], rest[-7:]
    owners = rows_hbm.shape[0]
    channels = step_hbm.shape[3]
    copies = [
        pltpu.make_async_copy(owner_hbm, owner_s, sems.at[4]),
        pltpu.make_async_copy(rows_hbm, rows_s, sems.at[0]),
        pltpu.make_async_copy(prompt_hbm, prompt_s, sems.at[1]),
        pltpu.make_async_copy(conv_hbm, conv, sems.at[2]),
        pltpu.make_async_copy(ssm_hbm, ssm, sems.at[3]),
    ]
    all_of(copies + in_parts(step_hbm, step, sems, 5, 4))
    owner = owner_s[0]
    window = conv[0].astype(F32)

    def write(ref, target):
        row = jnp.maximum(rows_s[target], 0)
        xs = step[row, :, 0, :].astype(F32)
        number = prompt_s[row].astype(F32)
        pieces = [xs, window, jnp.full((1, channels), number, F32)]
        if ref.shape[0] > sum(p.shape[0] for p in pieces):
            pieces.append(ssm[0])
        ref[...] = jnp.concatenate(pieces, axis=0).astype(BF16)

    if direct:
        write(outs[0].at[0], owner)
        for ref, to in zip(outs[1:], SENDS):
            write(ref.at[0], chosen(owner, to))
    else:
        for target in range(owners):
            write(outs[0].at[target], target)


def pair_kernel(text, own_ref, other_ref, pair_ref):
    states = [ref[0].astype(F32)[text:, :] for ref in (own_ref, other_ref)]
    pair_ref[0] = jnp.concatenate(states, axis=0).astype(BF16)


def silu(v):
    return v / (1.0 + jnp.exp(-v))


def prepare_kernel(
    direct,
    owner_hbm,
    prompt_hbm,
    child_hbm,
    step_ref,
    cw_hbm,
    cb_hbm,
    xwt_hbm,
    alog_hbm,
    dtw_hbm,
    dtb_hbm,
    skip_hbm,
    after_ref,
    base_ref,
    gate_ref,
    pick_ref,
    child_ref,
    sender_ref,
    cw_ref,
    cb_ref,
    xwt_ref,
    rate_ref,
    twin_ref,
    dtw_ref,
    dtb_ref,
    skip_ref,
    owner_s,
    prompt_s,
    child_s,
    alog,
    sems,
):
    del after_ref
    small = [
        pltpu.make_async_copy(source, target, sems.at[i])
        for i, (source, target) in enumerate(
            (
                (cw_hbm, cw_ref),
                (cb_hbm, cb_ref),
                (owner_hbm, owner_s),
                (prompt_hbm, prompt_s),
                (child_hbm, child_s),
                (alog_hbm, alog),
                (dtb_hbm, dtb_ref),
                (skip_hbm, skip_ref),
            )
        )
    ]
    large = in_parts(xwt_hbm, xwt_ref, sems, len(small), WEIGHT_PARTS)
    large += in_parts(dtw_hbm, dtw_ref, sems, len(small) + WEIGHT_PARTS, DT_PARTS)
    for copy in small + large:
        copy.start()
    steps = step_ref.shape[1]
    taps = cw_hbm.shape[0]
    xs = [step_ref[:, t, 0, :].astype(F32) for t in range(steps)]
    for t in range(steps):
        gate_ref[t] = silu(step_ref[:, t, 1, :].astype(F32))
    for copy in small:
        copy.wait()
    for t in range(steps):
        total = cw_ref[taps - 1 : taps, :] * xs[t] + cb_ref[...]
        for k in range(max(0, taps - 1 - t), taps - 1):
            total = total + cw_ref[k : k + 1, :] * xs[t + k - taps + 1]
        base_ref[t] = total
    pick_ref[...] = scalar_onehot(prompt_s, owner_s[0], pick_ref.shape, direct)
    child_ref[...] = scalar_onehot(child_s, owner_s[0], child_ref.shape, direct)
    column = lax.broadcasted_iota(jnp.int32, sender_ref.shape, 1)
    sender = column
    for sent in range(sender_ref.shape[1] if direct else 0):
        sender = jnp.where(column == block_of(sent, owner_s[0], direct), sent, sender)
    sender_ref[...] = sender.astype(F32)
    rate = jnp.exp(alog[...]) * (-math.log2(math.e))
    rate_ref[...] = rate
    half = (twin_ref.shape[1] // 2, rate.shape[1])
    for m in range(rate.shape[0] // 2):
        two = [jnp.broadcast_to(rate[n : n + 1, :], half) for n in (2 * m, 2 * m + 1)]
        twin_ref[m] = jnp.concatenate(two, axis=0)
    for copy in large:
        copy.wait()


def slot_onehot(numbers, sender_ref):
    owners = sender_ref.shape[1]
    return (numbers[:, :owners] == sender_ref[...]).astype(F32)


def project_kernel(n_msgs, pick_ref, sender_ref, base_ref, cw_ref, cb_ref, xwt_ref, *rest):
    msgs, (act_ref, part_ref, short_ref) = rest[:n_msgs], rest[n_msgs:]
    taps = cw_ref.shape[0]
    steps, rb, _ = base_ref.shape
    past = taps - 1
    held = read_messages(msgs)
    owners = len(held)
    windows = [[h[steps + k : steps + k + 1, :] for h in held] for k in range(past)]
    own = pick_ref[...]
    own_windows = [pick_rows(own, w) for w in windows]
    for t in range(steps):
        conv = base_ref[t]
        for k in range(past - t):
            conv = conv + cw_ref[k : k + 1, :] * own_windows[t + k]
        act_ref[t * rb : (t + 1) * rb, :] = silu(conv)

    def line_of(row):
        return jnp.concatenate([h[row : row + 1, :] for h in held], axis=0)

    slot = slot_onehot(line_of(past + steps), sender_ref)
    line = [pick_rows(slot, w) for w in windows]
    line += [line_of(t) for t in range(steps)]
    row = steps * rb
    for t in range(steps):
        conv = cw_ref[past:taps, :] * line[t + past] + cb_ref[...]
        for k in range(past):
            conv = conv + cw_ref[k : k + 1, :] * line[t + k]
        act_ref[row : row + owners, :] = silu(conv)
        row += owners
    part = lax.dot_general(
        act_ref[...].astype(BF16),
        xwt_ref[...],
        (((1,), (1,)), ((), ())),
        preferred_element_type=F32,
    )
    part_ref[...] = part
    short_ref[...] = part.astype(BF16)


def add_kernel(a_ref, b_ref, sum_ref, short_ref):
    total = a_ref[...] + b_ref[...].astype(F32)
    sum_ref[...] = total
    short_ref[...] = total.astype(BF16)


def windows_kernel(n_msgs, steps, child_ref, after_ref, *rest):
    del after_ref
    msgs, (conv_ref,) = rest[:n_msgs], rest[n_msgs:]
    held = read_messages(msgs)
    past = conv_ref.shape[0]
    for k in range(past):
        at = steps - past + k
        rows = [h[at : at + 1, :] for h in held]
        conv_ref[k] = pick_rows(child_ref[...], rows).astype(BF16)


def start_kernel(n_msgs, n_pairs, text, pick_ref, sender_ref, after_ref, *rest):
    del after_ref
    msgs, rest = rest[:n_msgs], rest[n_msgs:]
    pairs, (own_ref, slot_ref, state_s) = rest[:n_pairs], rest[n_pairs:]
    n_state = own_ref.shape[0]
    held = read_messages(msgs)
    owners = len(held)
    numbers = jnp.concatenate([h[text - 1 : text, :] for h in held], axis=0)
    states = [h[text:, :] for h in held]
    for ref in pairs:
        both = ref[0].astype(F32)
        states[3], states[2] = both[:n_state, :], both[n_state:, :]
    for k, state in enumerate(states):
        state_s[k] = state
    own = pick_ref[...]
    slot = slot_onehot(numbers, sender_ref)

    def two(m, carry):
        picked = []
        for n in (2 * m, 2 * m + 1):
            rows = [state_s[k, pl.ds(n, 1), :] for k in range(owners)]
            own_ref[n] = pick_rows(own, rows)
            picked.append(pick_rows(slot, rows))
        slot_ref[m] = jnp.concatenate(picked, axis=0)
        return carry

    lax.fori_loop(0, n_state // 2, two, 0, unroll=owners <= DIRECT)


def decode_kernel(
    direct,
    owner_hbm,
    child_hbm,
    act_ref,
    gate_ref,
    own_ref,
    slot_ref,
    rate_ref,
    twin_ref,
    dtw_ref,
    dtb_ref,
    skip_ref,
    part_ref,
    other_ref,
    dec_ref,
    child_ssm,
    owner_s,
    child_s,
    delta_s,
    gain_s,
    slot_delta_s,
    slot_gain_s,
    b_s,
    c_s,
    twin_b_s,
    slots_s,
    line_s,
    sems,
):
    scalars = [
        pltpu.make_async_copy(owner_hbm, owner_s, sems.at[0]),
        pltpu.make_async_copy(child_hbm, child_s, sems.at[1]),
    ]
    for copy in scalars:
        copy.start()
    rb, steps, channels = dec_ref.shape
    rank = dtw_ref.shape[0]
    n_state = rate_ref.shape[0]
    n_slots = slots_s.shape[0]
    own_rows = steps * rb
    chunks = channels // LANES

    proj = part_ref[...] + other_ref[...].astype(F32)
    delta_in = proj[:, :rank].astype(BF16)
    delta = jnp.dot(delta_in, dtw_ref[...], preferred_element_type=F32) + dtb_ref[...]
    delta = jnp.maximum(delta, 0.0) + jnp.log(1.0 + jnp.exp(-jnp.abs(delta)))
    gain = delta * act_ref[...]
    delta_s[...] = delta[:own_rows, :]
    gain_s[...] = gain[:own_rows, :]

    def column(at, n, rows):
        return jnp.broadcast_to(at[:, n : n + 1], (rows, LANES))

    for t in range(steps):
        at = slice(own_rows + t * n_slots, own_rows + (t + 1) * n_slots)
        slot_delta_s[t] = jnp.concatenate([delta[at, :]] * 2, axis=0)
        slot_gain_s[t] = jnp.concatenate([gain[at, :]] * 2, axis=0)
        twice = jnp.concatenate([proj[at, rank:]] * 2, axis=0)
        upper = lax.broadcasted_iota(jnp.int32, (2 * n_slots, LANES), 0) < n_slots
        for m in range(n_state // 2):
            twin_b_s[m, t] = jnp.where(
                upper, column(twice, 2 * m, 2 * n_slots), column(twice, 2 * m + 1, 2 * n_slots)
            )
    for n in range(n_state):
        b_s[n] = column(proj[:own_rows, rank:], n, own_rows)
        c_s[n] = column(proj[:own_rows, rank:], n_state + n, own_rows)

    def slot_chunk(chunk, carry):
        columns = pl.ds(pl.multiple_of(chunk * LANES, LANES), LANES)
        delta = [slot_delta_s[t, :, columns] for t in range(steps)]
        gain = [slot_gain_s[t, :, columns] for t in range(steps)]
        for m in range(n_state // 2):
            rate = twin_ref[m, :, columns]
            state = slot_ref[m, :, columns]
            for t in range(steps):
                state = jnp.exp2(delta[t] * rate) * state + gain[t] * twin_b_s[m, t]
            slots_s[:, 2 * m, columns] = state[:n_slots, :]
            slots_s[:, 2 * m + 1, columns] = state[n_slots:, :]
        return carry

    lax.fori_loop(0, chunks, slot_chunk, 0)
    for copy in scalars:
        copy.wait()
    copies = []
    for j in range(rb):
        at = block_of(child_s[j], owner_s[0], direct)
        copy = pltpu.make_async_copy(slots_s.at[at], child_ssm.at[j], sems.at[2 + j])
        copy.start()
        copies.append(copy)

    def own_chunk(chunk, carry):
        columns = pl.ds(pl.multiple_of(chunk * LANES, LANES), LANES)
        at = [pl.ds(t * rb, rb) for t in range(steps)]
        delta = [delta_s[a, columns] for a in at]
        gain = [gain_s[a, columns] for a in at]
        sums = [skip_ref[:, columns] * act_ref[a, columns] for a in at]
        for n in range(n_state):
            rate = rate_ref[n : n + 1, columns]
            state = own_ref[n, :, columns]
            for t in range(steps):
                state = jnp.exp2(delta[t] * rate) * state + gain[t] * b_s[n, at[t], :]
                sums[t] = sums[t] + c_s[n, at[t], :] * state
        for t in range(steps):
            line_s[pl.ds(t, rb, stride=steps), :] = sums[t] * gate_ref[t, :, columns]
        dec_ref[:, :, columns] = line_s[...].reshape(rb, steps, LANES).astype(BF16)
        return carry

    lax.fori_loop(0, chunks, own_chunk, 0)
    for copy in copies:
        copy.wait()


def on_device(
    prompt_ssm,
    prompt_conv,
    prompt_of,
    step_in,
    conv_weight,
    conv_bias,
    x_weight,
    dt_weight,
    dt_bias,
    a_log,
    skip,
    send_rows,
    child_slot,
):
    owners = lax.axis_size("branch")
    tensors = lax.axis_size("tensor")
    assert owners & (owners - 1) == 0 and tensors & (tensors - 1) == 0
    assert prompt_ssm.shape[0] == 1 and send_rows.shape[2] == 1
    rb, steps, _, channels = step_in.shape
    taps = conv_weight.shape[0]
    width = x_weight.shape[1]
    n_state = a_log.shape[0]
    rows = steps * (rb + owners)
    short = taps - 1 + steps + 1
    depth = short + n_state
    direct = owners == DIRECT
    owner = pinned(lax.axis_index("branch").astype(jnp.int32).reshape(1))

    if direct:
        msg_shapes = [(1, d, channels) for d in (depth, depth, short, short)]
    else:
        msg_shapes = [(owners, depth, channels)]
    msgs = call(
        functools.partial(pack_kernel, direct),
        [shaped(s, BF16) for s in msg_shapes],
        [hbm()] * 6,
        [vmem()] * len(msg_shapes),
        [
            pltpu.SMEM((1,), jnp.int32),
            pltpu.SMEM((owners,), jnp.int32),
            pltpu.SMEM((rb,), jnp.int32),
            pltpu.VMEM(step_in.shape, BF16),
            pltpu.VMEM(prompt_conv.shape, BF16),
            pltpu.VMEM(prompt_ssm.shape, F32),
            pltpu.SemaphoreType.DMA((9,)),
        ],
        nbytes=owners * depth * channels * 2,
    )(
        owner,
        pinned(send_rows.reshape(owners)),
        pinned(prompt_of),
        pinned(step_in),
        pinned(prompt_conv),
        pinned(prompt_ssm),
    )
    if direct:
        own = msgs[0]
        msgs = [own] + [
            lax.ppermute(m, "branch", list(enumerate(to))) for m, to in zip(msgs[1:], SENDS)
        ]
        pair = call(
            functools.partial(pair_kernel, short),
            shaped((1, 2 * n_state, channels), BF16),
            [vmem()] * 2,
            vmem(),
            nbytes=8 * n_state * channels,
        )(own, msgs[1])
        pairs, after = [swap(pair, "branch", 1)], own
    else:
        msgs = [lax.all_to_all(msgs[0], "branch", split_axis=0, concat_axis=0, tiled=True)]
        pairs, after = [], msgs[0]
    n_msgs = len(msgs)
    near = call(
        functools.partial(prepare_kernel, direct),
        [
            shaped((steps, rb, channels), F32),
            shaped((steps, rb, channels), F32),
            shaped((rb, owners), F32),
            shaped((rb, owners), F32),
            shaped((1, owners), F32),
            shaped((taps, channels), F32),
            shaped((1, channels), F32),
            shaped((width, channels), BF16),
            shaped((n_state, channels), F32),
            shaped((n_state // 2, 2 * owners, channels), F32),
            shaped(dt_weight.shape, BF16),
            shaped((1, channels), F32),
            shaped((1, channels), F32),
        ],
        [hbm()] * 3 + [vmem()] + [hbm()] * 7 + [anywhere()],
        [vmem()] * 13,
        [
            pltpu.SMEM((1,), jnp.int32),
            pltpu.SMEM((rb,), jnp.int32),
            pltpu.SMEM((rb,), jnp.int32),
            pltpu.VMEM((n_state, channels), F32),
            pltpu.SemaphoreType.DMA((8 + WEIGHT_PARTS + DT_PARTS,)),
        ],
        flops=10 * steps * rb * channels,
        nbytes=12 * steps * rb * channels,
        trans=steps * rb * channels,
    )(
        owner,
        pinned(prompt_of),
        pinned(child_slot),
        step_in,
        pinned(conv_weight),
        pinned(conv_bias[None]),
        pinned(x_weight.T),
        pinned(a_log),
        pinned(dt_weight),
        pinned(dt_bias[None]),
        pinned(skip[None]),
        after,
    )
    base, gate, pick, child_pick, sender, taps_near, bias_near, weight_near = near[:8]
    rate, twin, dtw_near, dtb_near, skip_near = near[8:]
    act, part, brief = call(
        functools.partial(project_kernel, n_msgs),
        [
            shaped((rows, channels), F32),
            shaped((rows, width), F32),
            shaped((rows, width), BF16),
        ],
        [vmem()] * (6 + n_msgs),
        [vmem()] * 3,
        flops=2 * rows * channels * width,
        nbytes=channels * width * 2 + rows * (channels + width) * 4,
        trans=rows * channels,
    )(pick, sender, base, taps_near, bias_near, weight_near, *msgs)
    other = swap(brief, "tensor", 1)
    distance = 2
    while distance < tensors:
        part, brief = call(
            add_kernel,
            [shaped((rows, width), F32), shaped((rows, width), BF16)],
            [vmem()] * 2,
            [vmem()] * 2,
            flops=rows * width,
            nbytes=rows * width * 14,
        )(part, other)
        other = swap(brief, "tensor", 2 * distance - 1)
        distance *= 2

    child_conv = call(
        functools.partial(windows_kernel, n_msgs, steps),
        shaped((taps - 1, rb, channels), BF16),
        [vmem(), anywhere()] + [vmem()] * n_msgs,
        vmem(),
        flops=2 * owners * taps * rb * channels,
        nbytes=4 * taps * rb * channels,
    )(child_pick, part, *msgs)
    own_start, slot_start = call(
        functools.partial(start_kernel, n_msgs, len(pairs), short),
        [
            shaped((n_state, rb, channels), F32),
            shaped((n_state // 2, 2 * owners, channels), F32),
        ],
        [vmem()] * 2 + [anywhere()] + [vmem()] * (n_msgs + len(pairs)),
        [vmem()] * 2,
        [pltpu.VMEM((owners, n_state, channels), F32)],
        flops=2 * owners * n_state * (rb + owners) * channels,
        nbytes=4 * n_state * (rb + owners) * channels,
    )(pick, sender, part, *msgs, *pairs)

    decoded, child_ssm = call(
        functools.partial(decode_kernel, direct),
        [
            shaped((rb, steps, channels), BF16),
            shaped((rb, n_state, channels), F32),
        ],
        [hbm()] * 2 + [vmem()] * 11,
        [vmem(), anywhere()],
        [
            pltpu.SMEM((1,), jnp.int32),
            pltpu.SMEM((rb,), jnp.int32),
            pltpu.VMEM((steps * rb, channels), F32),
            pltpu.VMEM((steps * rb, channels), F32),
            pltpu.VMEM((steps, 2 * owners, channels), F32),
            pltpu.VMEM((steps, 2 * owners, channels), F32),
            pltpu.VMEM((n_state, steps * rb, LANES), F32),
            pltpu.VMEM((n_state, steps * rb, LANES), F32),
            pltpu.VMEM((n_state // 2, steps, 2 * owners, LANES), F32),
            pltpu.VMEM((owners, n_state, channels), F32),
            pltpu.VMEM((steps * rb, LANES), F32),
            pltpu.SemaphoreType.DMA((2 + rb,)),
        ],
        flops=8 * rows * n_state * channels,
        nbytes=(rb + owners) * n_state * channels * 4,
        trans=rows * n_state * channels,
    )(
        owner,
        pinned(child_slot),
        act,
        gate,
        own_start,
        slot_start,
        rate,
        twin,
        dtw_near,
        dtb_near,
        skip_near,
        part,
        other,
    )
    return (decoded, child_ssm, jnp.transpose(child_conv, (1, 0, 2)))


def solution(mesh):
    placed = (
        P(("replica", "branch"), None, "tensor"),
        P(("replica", "branch"), None, "tensor"),
        P(("replica", "branch")),
        P(("replica", "branch"), None, None, "tensor"),
        P(None, "tensor"),
        P("tensor"),
        P("tensor", None),
        P(None, "tensor"),
        P("tensor"),
        P(None, "tensor"),
        P("tensor"),
        P(("replica", "branch"), None, None),
        P(("replica", "branch")),
    )
    return jax.shard_map(
        on_device,
        mesh=mesh,
        in_specs=placed,
        out_specs=(
            P(("replica", "branch"), None, "tensor"),
            P(("replica", "branch"), None, "tensor"),
            P(("replica", "branch"), None, "tensor"),
        ),
        check_vma=False,
    )
```

```python
import functools
import math

import jax
import jax.numpy as jnp
from jax import lax
from jax.experimental import pallas as pl
from jax.experimental.pallas import tpu as pltpu
from jax.sharding import PartitionSpec as P

F32 = jnp.float32
BF16 = jnp.bfloat16
LANES = 128
VMEM_LIMIT = 48 * 2**20
WEIGHT_PARTS = 6
DT_PARTS = 4
SLOT_UNROLL = 4
OWN_UNROLL = 2
DIRECT = 4
SENDS = ((2, 3, 1, 0), (3, 2, 0, 1), (1, 0, 3, 2))


def vmem():
    return pl.BlockSpec(memory_space=pltpu.VMEM)


def hbm():
    return pl.BlockSpec(memory_space=pltpu.HBM)


def anywhere():
    return pl.BlockSpec(memory_space=pl.ANY)


def pinned(array):
    return pltpu.with_memory_space_constraint(array, pltpu.HBM)


def shaped(shape, dtype):
    return jax.ShapeDtypeStruct(shape, dtype)


def call(kernel, outs, in_specs, out_specs, scratch=(), flops=0, nbytes=0, trans=0):
    return pl.pallas_call(
        kernel,
        out_shape=outs,
        in_specs=in_specs,
        out_specs=out_specs,
        scratch_shapes=list(scratch),
        compiler_params=pltpu.CompilerParams(vmem_limit_bytes=VMEM_LIMIT),
        cost_estimate=pl.CostEstimate(flops=flops, bytes_accessed=nbytes, transcendentals=trans),
    )


def swap(value, axis, distance):
    size = lax.axis_size(axis)
    return lax.ppermute(value, axis, [(i, i ^ distance) for i in range(size)])


def chosen(number, values):
    total = values[0]
    for i in range(1, len(values)):
        total = jnp.where(number == i, values[i], total)
    return total


def block_of(sender, owner, direct):
    if not direct:
        return sender
    table = [
        [0 if s == r else 1 + [to[s] for to in SENDS].index(r) for s in range(DIRECT)]
        for r in range(DIRECT)
    ]
    places = [chosen(owner, [row[s] for row in table]) for s in range(DIRECT)]
    return places[sender] if isinstance(sender, int) else chosen(sender, places)


def all_of(copies):
    for copy in copies:
        copy.start()
    for copy in copies:
        copy.wait()


def read_messages(refs):
    return [ref[i].astype(F32) for ref in refs for i in range(ref.shape[0])]


def in_parts(source, target, sems, first, count):
    rows = source.shape[0] // count
    at = [pl.ds(i * rows, rows) for i in range(count)]
    return [
        pltpu.make_async_copy(source.at[a], target.at[a], sems.at[first + i])
        for i, a in enumerate(at)
    ]


def scalar_onehot(senders_s, owner, shape, direct):
    row_of = lax.broadcasted_iota(jnp.int32, shape, 0)
    wanted = jnp.zeros(shape, jnp.int32)
    for b in range(shape[0]):
        wanted = jnp.where(row_of == b, senders_s[b], wanted)
    wanted = block_of(wanted, owner, direct)
    return (wanted == lax.broadcasted_iota(jnp.int32, shape, 1)).astype(F32)


def pick_rows(pick, rows):
    total = pick[:, 0:1] * rows[0]
    for k in range(1, len(rows)):
        total = total + pick[:, k : k + 1] * rows[k]
    return total


def pack_kernel(direct, owner_hbm, rows_hbm, prompt_hbm, step_hbm, conv_hbm, ssm_hbm, *rest):
    outs, (owner_s, rows_s, prompt_s, step, conv, ssm, sems) = rest[:-7], rest[-7:]
    owners = rows_hbm.shape[0]
    channels = step_hbm.shape[3]
    copies = [
        pltpu.make_async_copy(owner_hbm, owner_s, sems.at[4]),
        pltpu.make_async_copy(rows_hbm, rows_s, sems.at[0]),
        pltpu.make_async_copy(prompt_hbm, prompt_s, sems.at[1]),
        pltpu.make_async_copy(conv_hbm, conv, sems.at[2]),
        pltpu.make_async_copy(ssm_hbm, ssm, sems.at[3]),
    ]
    all_of(copies + in_parts(step_hbm, step, sems, 5, 4))
    owner = owner_s[0]
    window = conv[0].astype(F32)

    def write(ref, target):
        row = jnp.maximum(rows_s[target], 0)
        xs = step[row, :, 0, :].astype(F32)
        number = prompt_s[row].astype(F32)
        pieces = [xs, window, jnp.full((1, channels), number, F32)]
        if ref.shape[0] > sum(p.shape[0] for p in pieces):
            pieces.append(ssm[0])
        ref[...] = jnp.concatenate(pieces, axis=0).astype(BF16)

    if direct:
        write(outs[0].at[0], owner)
        for ref, to in zip(outs[1:], SENDS):
            write(ref.at[0], chosen(owner, to))
    else:
        for target in range(owners):
            write(outs[0].at[target], target)


def pair_kernel(text, own_ref, other_ref, pair_ref):
    states = [ref[0].astype(F32)[text:, :] for ref in (own_ref, other_ref)]
    pair_ref[0] = jnp.concatenate(states, axis=0).astype(BF16)


def silu(v):
    return v / (1.0 + jnp.exp(-v))


def prepare_kernel(
    direct,
    owner_hbm,
    prompt_hbm,
    child_hbm,
    step_ref,
    cw_hbm,
    cb_hbm,
    xwt_hbm,
    alog_hbm,
    dtw_hbm,
    dtb_hbm,
    skip_hbm,
    after_ref,
    base_ref,
    gate_ref,
    pick_ref,
    child_ref,
    sender_ref,
    cw_ref,
    cb_ref,
    xwt_ref,
    rate_ref,
    twin_ref,
    dtw_ref,
    dtb_ref,
    skip_ref,
    owner_s,
    prompt_s,
    child_s,
    alog,
    sems,
):
    del after_ref
    small = [
        pltpu.make_async_copy(source, target, sems.at[i])
        for i, (source, target) in enumerate(
            (
                (cw_hbm, cw_ref),
                (cb_hbm, cb_ref),
                (owner_hbm, owner_s),
                (prompt_hbm, prompt_s),
                (child_hbm, child_s),
                (alog_hbm, alog),
                (dtb_hbm, dtb_ref),
                (skip_hbm, skip_ref),
            )
        )
    ]
    large = in_parts(xwt_hbm, xwt_ref, sems, len(small), WEIGHT_PARTS)
    large += in_parts(dtw_hbm, dtw_ref, sems, len(small) + WEIGHT_PARTS, DT_PARTS)
    for copy in small + large:
        copy.start()
    steps = step_ref.shape[1]
    taps = cw_hbm.shape[0]
    xs = [step_ref[:, t, 0, :].astype(F32) for t in range(steps)]
    for t in range(steps):
        gate_ref[t] = silu(step_ref[:, t, 1, :].astype(F32))
    for copy in small:
        copy.wait()
    for t in range(steps):
        total = cw_ref[taps - 1 : taps, :] * xs[t] + cb_ref[...]
        for k in range(max(0, taps - 1 - t), taps - 1):
            total = total + cw_ref[k : k + 1, :] * xs[t + k - taps + 1]
        base_ref[t] = total
    pick_ref[...] = scalar_onehot(prompt_s, owner_s[0], pick_ref.shape, direct)
    child_ref[...] = scalar_onehot(child_s, owner_s[0], child_ref.shape, direct)
    column = lax.broadcasted_iota(jnp.int32, sender_ref.shape, 1)
    sender = column
    for sent in range(sender_ref.shape[1] if direct else 0):
        sender = jnp.where(column == block_of(sent, owner_s[0], direct), sent, sender)
    sender_ref[...] = sender.astype(F32)
    rate = jnp.exp(alog[...]) * (-math.log2(math.e))
    rate_ref[...] = rate
    half = (twin_ref.shape[1] // 2, rate.shape[1])
    for m in range(rate.shape[0] // 2):
        two = [jnp.broadcast_to(rate[n : n + 1, :], half) for n in (2 * m, 2 * m + 1)]
        twin_ref[m] = jnp.concatenate(two, axis=0)
    for copy in large:
        copy.wait()


def slot_onehot(numbers, sender_ref):
    owners = sender_ref.shape[1]
    return (numbers[:, :owners] == sender_ref[...]).astype(F32)


def project_kernel(n_msgs, pick_ref, sender_ref, base_ref, cw_ref, cb_ref, xwt_ref, *rest):
    msgs, (act_ref, part_ref, short_ref) = rest[:n_msgs], rest[n_msgs:]
    taps = cw_ref.shape[0]
    steps, rb, _ = base_ref.shape
    past = taps - 1
    held = read_messages(msgs)
    owners = len(held)
    windows = [[h[steps + k : steps + k + 1, :] for h in held] for k in range(past)]
    own = pick_ref[...]
    own_windows = [pick_rows(own, w) for w in windows]
    for t in range(steps):
        conv = base_ref[t]
        for k in range(past - t):
            conv = conv + cw_ref[k : k + 1, :] * own_windows[t + k]
        act_ref[t * rb : (t + 1) * rb, :] = silu(conv)

    def line_of(row):
        return jnp.concatenate([h[row : row + 1, :] for h in held], axis=0)

    slot = slot_onehot(line_of(past + steps), sender_ref)
    line = [pick_rows(slot, w) for w in windows]
    line += [line_of(t) for t in range(steps)]
    row = steps * rb
    for t in range(steps):
        conv = cw_ref[past:taps, :] * line[t + past] + cb_ref[...]
        for k in range(past):
            conv = conv + cw_ref[k : k + 1, :] * line[t + k]
        act_ref[row : row + owners, :] = silu(conv)
        row += owners
    part = lax.dot_general(
        act_ref[...].astype(BF16),
        xwt_ref[...],
        (((1,), (1,)), ((), ())),
        preferred_element_type=F32,
    )
    part_ref[...] = part
    short_ref[...] = part.astype(BF16)


def add_kernel(a_ref, b_ref, sum_ref, short_ref):
    total = a_ref[...] + b_ref[...].astype(F32)
    sum_ref[...] = total
    short_ref[...] = total.astype(BF16)


def windows_kernel(n_msgs, steps, child_ref, after_ref, *rest):
    del after_ref
    msgs, (conv_ref,) = rest[:n_msgs], rest[n_msgs:]
    held = read_messages(msgs)
    past = conv_ref.shape[0]
    for k in range(past):
        at = steps - past + k
        rows = [h[at : at + 1, :] for h in held]
        conv_ref[k] = pick_rows(child_ref[...], rows).astype(BF16)


def start_kernel(n_msgs, n_pairs, text, pick_ref, sender_ref, after_ref, *rest):
    del after_ref
    msgs, rest = rest[:n_msgs], rest[n_msgs:]
    pairs, (own_ref, slot_ref, state_s) = rest[:n_pairs], rest[n_pairs:]
    n_state = own_ref.shape[0]
    held = read_messages(msgs)
    owners = len(held)
    numbers = jnp.concatenate([h[text - 1 : text, :] for h in held], axis=0)
    states = [h[text:, :] for h in held]
    for ref in pairs:
        both = ref[0].astype(F32)
        states[3], states[2] = both[:n_state, :], both[n_state:, :]
    for k, state in enumerate(states):
        state_s[k] = state
    own = pick_ref[...]
    slot = slot_onehot(numbers, sender_ref)

    def two(m, carry):
        picked = []
        for n in (2 * m, 2 * m + 1):
            rows = [state_s[k, pl.ds(n, 1), :] for k in range(owners)]
            own_ref[n] = pick_rows(own, rows)
            picked.append(pick_rows(slot, rows))
        slot_ref[m] = jnp.concatenate(picked, axis=0)
        return carry

    lax.fori_loop(0, n_state // 2, two, 0, unroll=owners <= DIRECT)


def decode_kernel(
    direct,
    owner_hbm,
    child_hbm,
    act_ref,
    gate_ref,
    own_ref,
    slot_ref,
    rate_ref,
    twin_ref,
    dtw_ref,
    dtb_ref,
    skip_ref,
    part_ref,
    other_ref,
    dec_ref,
    child_ssm,
    owner_s,
    child_s,
    delta_s,
    gain_s,
    slot_delta_s,
    slot_gain_s,
    b_s,
    c_s,
    twin_b_s,
    slots_s,
    line_s,
    sems,
):
    scalars = [
        pltpu.make_async_copy(owner_hbm, owner_s, sems.at[0]),
        pltpu.make_async_copy(child_hbm, child_s, sems.at[1]),
    ]
    for copy in scalars:
        copy.start()
    rb, steps, channels = dec_ref.shape
    rank = dtw_ref.shape[0]
    n_state = rate_ref.shape[0]
    n_slots = slots_s.shape[0]
    own_rows = steps * rb
    chunks = channels // LANES

    proj = part_ref[...] + other_ref[...].astype(F32)
    delta_in = proj[:, :rank].astype(BF16)
    delta = jnp.dot(delta_in, dtw_ref[...], preferred_element_type=F32) + dtb_ref[...]
    delta = jnp.maximum(delta, 0.0) + jnp.log(1.0 + jnp.exp(-jnp.abs(delta)))
    gain = delta * act_ref[...]
    delta_s[...] = delta[:own_rows, :]
    gain_s[...] = gain[:own_rows, :]

    def column(at, n, rows):
        return jnp.broadcast_to(at[:, n : n + 1], (rows, LANES))

    for t in range(steps):
        at = slice(own_rows + t * n_slots, own_rows + (t + 1) * n_slots)
        slot_delta_s[t] = jnp.concatenate([delta[at, :]] * 2, axis=0)
        slot_gain_s[t] = jnp.concatenate([gain[at, :]] * 2, axis=0)
        twice = jnp.concatenate([proj[at, rank:]] * 2, axis=0)
        upper = lax.broadcasted_iota(jnp.int32, (2 * n_slots, LANES), 0) < n_slots
        for m in range(n_state // 2):
            twin_b_s[m, t] = jnp.where(
                upper, column(twice, 2 * m, 2 * n_slots), column(twice, 2 * m + 1, 2 * n_slots)
            )
    for n in range(n_state):
        b_s[n] = column(proj[:own_rows, rank:], n, own_rows)
        c_s[n] = column(proj[:own_rows, rank:], n_state + n, own_rows)

    def slot_chunk(chunk, carry):
        columns = pl.ds(pl.multiple_of(chunk * LANES, LANES), LANES)
        delta = [slot_delta_s[t, :, columns] for t in range(steps)]
        gain = [slot_gain_s[t, :, columns] for t in range(steps)]
        for m in range(n_state // 2):
            rate = twin_ref[m, :, columns]
            state = slot_ref[m, :, columns]
            for t in range(steps):
                state = jnp.exp2(delta[t] * rate) * state + gain[t] * twin_b_s[m, t]
            slots_s[:, 2 * m, columns] = state[:n_slots, :]
            slots_s[:, 2 * m + 1, columns] = state[n_slots:, :]
        return carry

    lax.fori_loop(0, chunks, slot_chunk, 0, unroll=SLOT_UNROLL)
    for copy in scalars:
        copy.wait()
    copies = []
    for j in range(rb):
        at = block_of(child_s[j], owner_s[0], direct)
        copy = pltpu.make_async_copy(slots_s.at[at], child_ssm.at[j], sems.at[2 + j])
        copy.start()
        copies.append(copy)

    def own_chunk(chunk, carry):
        columns = pl.ds(pl.multiple_of(chunk * LANES, LANES), LANES)
        at = [pl.ds(t * rb, rb) for t in range(steps)]
        delta = [delta_s[a, columns] for a in at]
        gain = [gain_s[a, columns] for a in at]
        sums = [skip_ref[:, columns] * act_ref[a, columns] for a in at]
        for n in range(n_state):
            rate = rate_ref[n : n + 1, columns]
            state = own_ref[n, :, columns]
            for t in range(steps):
                state = jnp.exp2(delta[t] * rate) * state + gain[t] * b_s[n, at[t], :]
                sums[t] = sums[t] + c_s[n, at[t], :] * state
        for t in range(steps):
            line_s[chunk, pl.ds(t, rb, stride=steps), :] = sums[t] * gate_ref[t, :, columns]
        return carry

    lax.fori_loop(0, chunks, own_chunk, 0, unroll=OWN_UNROLL)
    for chunk in range(chunks):
        columns = slice(chunk * LANES, (chunk + 1) * LANES)
        dec_ref[:, :, columns] = line_s[chunk].reshape(rb, steps, LANES).astype(BF16)
    for copy in copies:
        copy.wait()


def on_device(
    prompt_ssm,
    prompt_conv,
    prompt_of,
    step_in,
    conv_weight,
    conv_bias,
    x_weight,
    dt_weight,
    dt_bias,
    a_log,
    skip,
    send_rows,
    child_slot,
):
    owners = lax.axis_size("branch")
    tensors = lax.axis_size("tensor")
    assert owners & (owners - 1) == 0 and tensors & (tensors - 1) == 0
    assert prompt_ssm.shape[0] == 1 and send_rows.shape[2] == 1
    rb, steps, _, channels = step_in.shape
    taps = conv_weight.shape[0]
    width = x_weight.shape[1]
    n_state = a_log.shape[0]
    rows = steps * (rb + owners)
    short = taps - 1 + steps + 1
    depth = short + n_state
    direct = owners == DIRECT
    owner = pinned(lax.axis_index("branch").astype(jnp.int32).reshape(1))

    if direct:
        msg_shapes = [(1, d, channels) for d in (depth, depth, short, short)]
    else:
        msg_shapes = [(owners, depth, channels)]
    msgs = call(
        functools.partial(pack_kernel, direct),
        [shaped(s, BF16) for s in msg_shapes],
        [hbm()] * 6,
        [vmem()] * len(msg_shapes),
        [
            pltpu.SMEM((1,), jnp.int32),
            pltpu.SMEM((owners,), jnp.int32),
            pltpu.SMEM((rb,), jnp.int32),
            pltpu.VMEM(step_in.shape, BF16),
            pltpu.VMEM(prompt_conv.shape, BF16),
            pltpu.VMEM(prompt_ssm.shape, F32),
            pltpu.SemaphoreType.DMA((9,)),
        ],
        nbytes=owners * depth * channels * 2,
    )(
        owner,
        pinned(send_rows.reshape(owners)),
        pinned(prompt_of),
        pinned(step_in),
        pinned(prompt_conv),
        pinned(prompt_ssm),
    )
    if direct:
        own = msgs[0]
        msgs = [own] + [
            lax.ppermute(m, "branch", list(enumerate(to))) for m, to in zip(msgs[1:], SENDS)
        ]
        pair = call(
            functools.partial(pair_kernel, short),
            shaped((1, 2 * n_state, channels), BF16),
            [vmem()] * 2,
            vmem(),
            nbytes=8 * n_state * channels,
        )(own, msgs[1])
        pairs, after = [swap(pair, "branch", 1)], own
    else:
        msgs = [lax.all_to_all(msgs[0], "branch", split_axis=0, concat_axis=0, tiled=True)]
        pairs, after = [], msgs[0]
    n_msgs = len(msgs)
    near = call(
        functools.partial(prepare_kernel, direct),
        [
            shaped((steps, rb, channels), F32),
            shaped((steps, rb, channels), F32),
            shaped((rb, owners), F32),
            shaped((rb, owners), F32),
            shaped((1, owners), F32),
            shaped((taps, channels), F32),
            shaped((1, channels), F32),
            shaped((width, channels), BF16),
            shaped((n_state, channels), F32),
            shaped((n_state // 2, 2 * owners, channels), F32),
            shaped(dt_weight.shape, BF16),
            shaped((1, channels), F32),
            shaped((1, channels), F32),
        ],
        [hbm()] * 3 + [vmem()] + [hbm()] * 7 + [anywhere()],
        [vmem()] * 13,
        [
            pltpu.SMEM((1,), jnp.int32),
            pltpu.SMEM((rb,), jnp.int32),
            pltpu.SMEM((rb,), jnp.int32),
            pltpu.VMEM((n_state, channels), F32),
            pltpu.SemaphoreType.DMA((8 + WEIGHT_PARTS + DT_PARTS,)),
        ],
        flops=10 * steps * rb * channels,
        nbytes=12 * steps * rb * channels,
        trans=steps * rb * channels,
    )(
        owner,
        pinned(prompt_of),
        pinned(child_slot),
        step_in,
        pinned(conv_weight),
        pinned(conv_bias[None]),
        pinned(x_weight.T),
        pinned(a_log),
        pinned(dt_weight),
        pinned(dt_bias[None]),
        pinned(skip[None]),
        after,
    )
    base, gate, pick, child_pick, sender, taps_near, bias_near, weight_near = near[:8]
    rate, twin, dtw_near, dtb_near, skip_near = near[8:]
    act, part, brief = call(
        functools.partial(project_kernel, n_msgs),
        [
            shaped((rows, channels), F32),
            shaped((rows, width), F32),
            shaped((rows, width), BF16),
        ],
        [vmem()] * (6 + n_msgs),
        [vmem()] * 3,
        flops=2 * rows * channels * width,
        nbytes=channels * width * 2 + rows * (channels + width) * 4,
        trans=rows * channels,
    )(pick, sender, base, taps_near, bias_near, weight_near, *msgs)
    other = swap(brief, "tensor", 1)
    distance = 2
    while distance < tensors:
        part, brief = call(
            add_kernel,
            [shaped((rows, width), F32), shaped((rows, width), BF16)],
            [vmem()] * 2,
            [vmem()] * 2,
            flops=rows * width,
            nbytes=rows * width * 14,
        )(part, other)
        other = swap(brief, "tensor", 2 * distance - 1)
        distance *= 2

    child_conv = call(
        functools.partial(windows_kernel, n_msgs, steps),
        shaped((taps - 1, rb, channels), BF16),
        [vmem(), anywhere()] + [vmem()] * n_msgs,
        vmem(),
        flops=2 * owners * taps * rb * channels,
        nbytes=4 * taps * rb * channels,
    )(child_pick, part, *msgs)
    own_start, slot_start = call(
        functools.partial(start_kernel, n_msgs, len(pairs), short),
        [
            shaped((n_state, rb, channels), F32),
            shaped((n_state // 2, 2 * owners, channels), F32),
        ],
        [vmem()] * 2 + [anywhere()] + [vmem()] * (n_msgs + len(pairs)),
        [vmem()] * 2,
        [pltpu.VMEM((owners, n_state, channels), F32)],
        flops=2 * owners * n_state * (rb + owners) * channels,
        nbytes=4 * n_state * (rb + owners) * channels,
    )(pick, sender, part, *msgs, *pairs)

    decoded, child_ssm = call(
        functools.partial(decode_kernel, direct),
        [
            shaped((rb, steps, channels), BF16),
            shaped((rb, n_state, channels), F32),
        ],
        [hbm()] * 2 + [vmem()] * 11,
        [vmem(), anywhere()],
        [
            pltpu.SMEM((1,), jnp.int32),
            pltpu.SMEM((rb,), jnp.int32),
            pltpu.VMEM((steps * rb, channels), F32),
            pltpu.VMEM((steps * rb, channels), F32),
            pltpu.VMEM((steps, 2 * owners, channels), F32),
            pltpu.VMEM((steps, 2 * owners, channels), F32),
            pltpu.VMEM((n_state, steps * rb, LANES), F32),
            pltpu.VMEM((n_state, steps * rb, LANES), F32),
            pltpu.VMEM((n_state // 2, steps, 2 * owners, LANES), F32),
            pltpu.VMEM((owners, n_state, channels), F32),
            pltpu.VMEM((channels // LANES, steps * rb, LANES), F32),
            pltpu.SemaphoreType.DMA((2 + rb,)),
        ],
        flops=8 * rows * n_state * channels,
        nbytes=(rb + owners) * n_state * channels * 4,
        trans=rows * n_state * channels,
    )(
        owner,
        pinned(child_slot),
        act,
        gate,
        own_start,
        slot_start,
        rate,
        twin,
        dtw_near,
        dtb_near,
        skip_near,
        part,
        other,
    )
    return (decoded, child_ssm, jnp.transpose(child_conv, (1, 0, 2)))


def solution(mesh):
    placed = (
        P(("replica", "branch"), None, "tensor"),
        P(("replica", "branch"), None, "tensor"),
        P(("replica", "branch")),
        P(("replica", "branch"), None, None, "tensor"),
        P(None, "tensor"),
        P("tensor"),
        P("tensor", None),
        P(None, "tensor"),
        P("tensor"),
        P(None, "tensor"),
        P("tensor"),
        P(("replica", "branch"), None, None),
        P(("replica", "branch")),
    )
    return jax.shard_map(
        on_device,
        mesh=mesh,
        in_specs=placed,
        out_specs=(
            P(("replica", "branch"), None, "tensor"),
            P(("replica", "branch"), None, "tensor"),
            P(("replica", "branch"), None, "tensor"),
        ),
        check_vma=False,
    )
```

```python
import functools
import math

import jax
import jax.numpy as jnp
from jax import lax
from jax.experimental import pallas as pl
from jax.experimental.pallas import tpu as pltpu
from jax.sharding import PartitionSpec as P

F32 = jnp.float32
BF16 = jnp.bfloat16
LANES = 128
VMEM_LIMIT = 48 * 2**20
WEIGHT_PARTS = 6
DT_PARTS = 4
DIRECT = 4
SENDS = ((2, 3, 1, 0), (3, 2, 0, 1), (1, 0, 3, 2))


def vmem():
    return pl.BlockSpec(memory_space=pltpu.VMEM)


def hbm():
    return pl.BlockSpec(memory_space=pltpu.HBM)


def anywhere():
    return pl.BlockSpec(memory_space=pl.ANY)


def pinned(array):
    return pltpu.with_memory_space_constraint(array, pltpu.HBM)


def shaped(shape, dtype):
    return jax.ShapeDtypeStruct(shape, dtype)


def call(kernel, outs, in_specs, out_specs, scratch=(), flops=0, nbytes=0, trans=0):
    return pl.pallas_call(
        kernel,
        out_shape=outs,
        in_specs=in_specs,
        out_specs=out_specs,
        scratch_shapes=list(scratch),
        compiler_params=pltpu.CompilerParams(vmem_limit_bytes=VMEM_LIMIT),
        cost_estimate=pl.CostEstimate(flops=flops, bytes_accessed=nbytes, transcendentals=trans),
    )


def swap(value, axis, distance):
    size = lax.axis_size(axis)
    return lax.ppermute(value, axis, [(i, i ^ distance) for i in range(size)])


def chosen(number, values):
    total = values[0]
    for i in range(1, len(values)):
        total = jnp.where(number == i, values[i], total)
    return total


def block_of(sender, owner, direct):
    if not direct:
        return sender
    table = [
        [0 if s == r else 1 + [to[s] for to in SENDS].index(r) for s in range(DIRECT)]
        for r in range(DIRECT)
    ]
    places = [chosen(owner, [row[s] for row in table]) for s in range(DIRECT)]
    return places[sender] if isinstance(sender, int) else chosen(sender, places)


def all_of(copies):
    for copy in copies:
        copy.start()
    for copy in copies:
        copy.wait()


def read_messages(refs):
    return [ref[i].astype(F32) for ref in refs for i in range(ref.shape[0])]


def in_parts(source, target, sems, first, count):
    rows = source.shape[0] // count
    at = [pl.ds(i * rows, rows) for i in range(count)]
    return [
        pltpu.make_async_copy(source.at[a], target.at[a], sems.at[first + i])
        for i, a in enumerate(at)
    ]


def scalar_onehot(senders_s, owner, shape, direct):
    row_of = lax.broadcasted_iota(jnp.int32, shape, 0)
    wanted = jnp.zeros(shape, jnp.int32)
    for b in range(shape[0]):
        wanted = jnp.where(row_of == b, senders_s[b], wanted)
    wanted = block_of(wanted, owner, direct)
    return (wanted == lax.broadcasted_iota(jnp.int32, shape, 1)).astype(F32)


def pick_rows(pick, rows):
    total = pick[:, 0:1] * rows[0]
    for k in range(1, len(rows)):
        total = total + pick[:, k : k + 1] * rows[k]
    return total


def pack_kernel(direct, owner_hbm, rows_hbm, prompt_hbm, step_hbm, conv_hbm, ssm_hbm, *rest):
    outs, (owner_s, rows_s, prompt_s, step, conv, ssm, sems) = rest[:-7], rest[-7:]
    owners = rows_hbm.shape[0]
    channels = step_hbm.shape[3]
    copies = [
        pltpu.make_async_copy(owner_hbm, owner_s, sems.at[4]),
        pltpu.make_async_copy(rows_hbm, rows_s, sems.at[0]),
        pltpu.make_async_copy(prompt_hbm, prompt_s, sems.at[1]),
        pltpu.make_async_copy(conv_hbm, conv, sems.at[2]),
        pltpu.make_async_copy(ssm_hbm, ssm, sems.at[3]),
    ]
    all_of(copies + in_parts(step_hbm, step, sems, 5, 4))
    owner = owner_s[0]
    window = conv[0].astype(F32)

    def write(ref, target):
        row = jnp.maximum(rows_s[target], 0)
        xs = step[row, :, 0, :].astype(F32)
        number = prompt_s[row].astype(F32)
        pieces = [xs, window, jnp.full((1, channels), number, F32)]
        if ref.shape[0] > sum(p.shape[0] for p in pieces):
            pieces.append(ssm[0])
        ref[...] = jnp.concatenate(pieces, axis=0).astype(BF16)

    if direct:
        write(outs[0].at[0], owner)
        for ref, to in zip(outs[1:], SENDS):
            write(ref.at[0], chosen(owner, to))
    else:
        for target in range(owners):
            write(outs[0].at[target], target)


def pair_kernel(text, ssm_ref, came_ref, after_ref, pair_ref):
    del after_ref
    state = ssm_ref[0]
    head = state.astype(BF16).astype(F32)
    came = came_ref[0].astype(F32)[text:, :]
    pair_ref[0] = jnp.concatenate([head, state - head, came], axis=0).astype(BF16)


def silu(v):
    return v / (1.0 + jnp.exp(-v))


def prepare_kernel(
    direct,
    owner_hbm,
    prompt_hbm,
    child_hbm,
    step_ref,
    cw_hbm,
    cb_hbm,
    xwt_hbm,
    alog_hbm,
    dtw_hbm,
    dtb_hbm,
    skip_hbm,
    after_ref,
    base_ref,
    gate_ref,
    pick_ref,
    child_ref,
    sender_ref,
    cw_ref,
    cb_ref,
    xwt_ref,
    rate_ref,
    twin_ref,
    dtw_ref,
    dtb_ref,
    skip_ref,
    owner_s,
    prompt_s,
    child_s,
    alog,
    sems,
):
    del after_ref
    small = [
        pltpu.make_async_copy(source, target, sems.at[i])
        for i, (source, target) in enumerate(
            (
                (cw_hbm, cw_ref),
                (cb_hbm, cb_ref),
                (owner_hbm, owner_s),
                (prompt_hbm, prompt_s),
                (child_hbm, child_s),
                (alog_hbm, alog),
                (dtb_hbm, dtb_ref),
                (skip_hbm, skip_ref),
            )
        )
    ]
    large = in_parts(xwt_hbm, xwt_ref, sems, len(small), WEIGHT_PARTS)
    large += in_parts(dtw_hbm, dtw_ref, sems, len(small) + WEIGHT_PARTS, DT_PARTS)
    for copy in small + large:
        copy.start()
    steps = step_ref.shape[1]
    taps = cw_hbm.shape[0]
    xs = [step_ref[:, t, 0, :].astype(F32) for t in range(steps)]
    for t in range(steps):
        gate_ref[t] = silu(step_ref[:, t, 1, :].astype(F32))
    for copy in small:
        copy.wait()
    for t in range(steps):
        total = cw_ref[taps - 1 : taps, :] * xs[t] + cb_ref[...]
        for k in range(max(0, taps - 1 - t), taps - 1):
            total = total + cw_ref[k : k + 1, :] * xs[t + k - taps + 1]
        base_ref[t] = total
    pick_ref[...] = scalar_onehot(prompt_s, owner_s[0], pick_ref.shape, direct)
    child_ref[...] = scalar_onehot(child_s, owner_s[0], child_ref.shape, direct)
    column = lax.broadcasted_iota(jnp.int32, sender_ref.shape, 1)
    sender = column
    for sent in range(sender_ref.shape[1] if direct else 0):
        sender = jnp.where(column == block_of(sent, owner_s[0], direct), sent, sender)
    sender_ref[...] = sender.astype(F32)
    rate = jnp.exp(alog[...]) * (-math.log2(math.e))
    rate_ref[...] = rate
    half = (twin_ref.shape[1] // 2, rate.shape[1])
    for m in range(rate.shape[0] // 2):
        two = [jnp.broadcast_to(rate[n : n + 1, :], half) for n in (2 * m, 2 * m + 1)]
        twin_ref[m] = jnp.concatenate(two, axis=0)
    for copy in large:
        copy.wait()


def slot_onehot(numbers, sender_ref):
    owners = sender_ref.shape[1]
    return (numbers[:, :owners] == sender_ref[...]).astype(F32)


def project_kernel(n_msgs, pick_ref, sender_ref, base_ref, cw_ref, cb_ref, xwt_ref, *rest):
    msgs, (act_ref, part_ref, short_ref) = rest[:n_msgs], rest[n_msgs:]
    taps = cw_ref.shape[0]
    steps, rb, _ = base_ref.shape
    past = taps - 1
    held = read_messages(msgs)
    owners = len(held)
    windows = [[h[steps + k : steps + k + 1, :] for h in held] for k in range(past)]
    own = pick_ref[...]
    own_windows = [pick_rows(own, w) for w in windows]
    for t in range(steps):
        conv = base_ref[t]
        for k in range(past - t):
            conv = conv + cw_ref[k : k + 1, :] * own_windows[t + k]
        act_ref[t * rb : (t + 1) * rb, :] = silu(conv)

    def line_of(row):
        return jnp.concatenate([h[row : row + 1, :] for h in held], axis=0)

    slot = slot_onehot(line_of(past + steps), sender_ref)
    line = [pick_rows(slot, w) for w in windows]
    line += [line_of(t) for t in range(steps)]
    row = steps * rb
    for t in range(steps):
        conv = cw_ref[past:taps, :] * line[t + past] + cb_ref[...]
        for k in range(past):
            conv = conv + cw_ref[k : k + 1, :] * line[t + k]
        act_ref[row : row + owners, :] = silu(conv)
        row += owners
    part = lax.dot_general(
        act_ref[...].astype(BF16),
        xwt_ref[...],
        (((1,), (1,)), ((), ())),
        preferred_element_type=F32,
    )
    part_ref[...] = part
    short_ref[...] = part.astype(BF16)


def add_kernel(a_ref, b_ref, sum_ref, short_ref):
    total = a_ref[...] + b_ref[...].astype(F32)
    sum_ref[...] = total
    short_ref[...] = total.astype(BF16)


def windows_kernel(n_msgs, steps, child_ref, after_ref, *rest):
    del after_ref
    msgs, (conv_ref,) = rest[:n_msgs], rest[n_msgs:]
    held = read_messages(msgs)
    past = conv_ref.shape[0]
    for k in range(past):
        at = steps - past + k
        rows = [h[at : at + 1, :] for h in held]
        conv_ref[k] = pick_rows(child_ref[...], rows).astype(BF16)


def start_kernel(n_msgs, direct, text, pick_ref, sender_ref, after_ref, *rest):
    del after_ref
    msgs, rest = rest[:n_msgs], rest[n_msgs:]
    apart, (own_ref, slot_ref, state_s) = rest[:-3], rest[-3:]
    n_state = own_ref.shape[0]
    held = read_messages(msgs)
    owners = len(held)
    numbers = jnp.concatenate([h[text - 1 : text, :] for h in held], axis=0)
    states = [h[text:, :] for h in held]
    if direct:
        ssm_ref, pair_ref = apart
        head, low, came = [
            pair_ref[0].astype(F32)[i * n_state : (i + 1) * n_state, :] for i in range(3)
        ]
        states[0], states[2], states[3] = ssm_ref[0], came, head + low
    for k, state in enumerate(states):
        state_s[k] = state
    own = pick_ref[...]
    slot = slot_onehot(numbers, sender_ref)

    def two(m, carry):
        picked = []
        for n in (2 * m, 2 * m + 1):
            rows = [state_s[k, pl.ds(n, 1), :] for k in range(owners)]
            own_ref[n] = pick_rows(own, rows)
            picked.append(pick_rows(slot, rows))
        slot_ref[m] = jnp.concatenate(picked, axis=0)
        return carry

    lax.fori_loop(0, n_state // 2, two, 0, unroll=owners <= DIRECT)


def decode_kernel(
    direct,
    owner_hbm,
    child_hbm,
    act_ref,
    gate_ref,
    own_ref,
    slot_ref,
    rate_ref,
    twin_ref,
    dtw_ref,
    dtb_ref,
    skip_ref,
    part_ref,
    other_ref,
    dec_ref,
    child_ssm,
    owner_s,
    child_s,
    delta_s,
    gain_s,
    slot_delta_s,
    slot_gain_s,
    b_s,
    c_s,
    twin_b_s,
    slots_s,
    line_s,
    sems,
):
    scalars = [
        pltpu.make_async_copy(owner_hbm, owner_s, sems.at[0]),
        pltpu.make_async_copy(child_hbm, child_s, sems.at[1]),
    ]
    for copy in scalars:
        copy.start()
    rb, steps, channels = dec_ref.shape
    rank = dtw_ref.shape[0]
    n_state = rate_ref.shape[0]
    n_slots = slots_s.shape[0]
    own_rows = steps * rb
    chunks = channels // LANES

    proj = part_ref[...] + other_ref[...].astype(F32)
    delta_in = proj[:, :rank].astype(BF16)
    delta = jnp.dot(delta_in, dtw_ref[...], preferred_element_type=F32) + dtb_ref[...]
    delta = jnp.maximum(delta, 0.0) + jnp.log(1.0 + jnp.exp(-jnp.abs(delta)))
    gain = delta * act_ref[...]
    delta_s[...] = delta[:own_rows, :]
    gain_s[...] = gain[:own_rows, :]

    def column(at, n, rows):
        return jnp.broadcast_to(at[:, n : n + 1], (rows, LANES))

    for t in range(steps):
        at = slice(own_rows + t * n_slots, own_rows + (t + 1) * n_slots)
        slot_delta_s[t] = jnp.concatenate([delta[at, :]] * 2, axis=0)
        slot_gain_s[t] = jnp.concatenate([gain[at, :]] * 2, axis=0)
        twice = jnp.concatenate([proj[at, rank:]] * 2, axis=0)
        upper = lax.broadcasted_iota(jnp.int32, (2 * n_slots, LANES), 0) < n_slots
        for m in range(n_state // 2):
            twin_b_s[m, t] = jnp.where(
                upper, column(twice, 2 * m, 2 * n_slots), column(twice, 2 * m + 1, 2 * n_slots)
            )
    for n in range(n_state):
        b_s[n] = column(proj[:own_rows, rank:], n, own_rows)
        c_s[n] = column(proj[:own_rows, rank:], n_state + n, own_rows)

    def slot_chunk(chunk, carry):
        columns = pl.ds(pl.multiple_of(chunk * LANES, LANES), LANES)
        delta = [slot_delta_s[t, :, columns] for t in range(steps)]
        gain = [slot_gain_s[t, :, columns] for t in range(steps)]
        for m in range(n_state // 2):
            rate = twin_ref[m, :, columns]
            state = slot_ref[m, :, columns]
            for t in range(steps):
                state = jnp.exp2(delta[t] * rate) * state + gain[t] * twin_b_s[m, t]
            slots_s[:, 2 * m, columns] = state[:n_slots, :]
            slots_s[:, 2 * m + 1, columns] = state[n_slots:, :]
        return carry

    lax.fori_loop(0, chunks, slot_chunk, 0)
    for copy in scalars:
        copy.wait()
    copies = []
    for j in range(rb):
        at = block_of(child_s[j], owner_s[0], direct)
        copy = pltpu.make_async_copy(slots_s.at[at], child_ssm.at[j], sems.at[2 + j])
        copy.start()
        copies.append(copy)

    def own_chunk(chunk, carry):
        columns = pl.ds(pl.multiple_of(chunk * LANES, LANES), LANES)
        at = [pl.ds(t * rb, rb) for t in range(steps)]
        delta = [delta_s[a, columns] for a in at]
        gain = [gain_s[a, columns] for a in at]
        sums = [skip_ref[:, columns] * act_ref[a, columns] for a in at]
        for n in range(n_state):
            rate = rate_ref[n : n + 1, columns]
            state = own_ref[n, :, columns]
            for t in range(steps):
                state = jnp.exp2(delta[t] * rate) * state + gain[t] * b_s[n, at[t], :]
                sums[t] = sums[t] + c_s[n, at[t], :] * state
        for t in range(steps):
            line_s[pl.ds(t, rb, stride=steps), :] = sums[t] * gate_ref[t, :, columns]
        dec_ref[:, :, columns] = line_s[...].reshape(rb, steps, LANES).astype(BF16)
        return carry

    lax.fori_loop(0, chunks, own_chunk, 0)
    for copy in copies:
        copy.wait()


def on_device(
    prompt_ssm,
    prompt_conv,
    prompt_of,
    step_in,
    conv_weight,
    conv_bias,
    x_weight,
    dt_weight,
    dt_bias,
    a_log,
    skip,
    send_rows,
    child_slot,
):
    owners = lax.axis_size("branch")
    tensors = lax.axis_size("tensor")
    assert owners & (owners - 1) == 0 and tensors & (tensors - 1) == 0
    assert prompt_ssm.shape[0] == 1 and send_rows.shape[2] == 1
    rb, steps, _, channels = step_in.shape
    taps = conv_weight.shape[0]
    width = x_weight.shape[1]
    n_state = a_log.shape[0]
    rows = steps * (rb + owners)
    short = taps - 1 + steps + 1
    depth = short + n_state
    direct = owners == DIRECT
    owner = pinned(lax.axis_index("branch").astype(jnp.int32).reshape(1))

    if direct:
        msg_shapes = [(1, d, channels) for d in (short, depth, short, short)]
    else:
        msg_shapes = [(owners, depth, channels)]
    msgs = call(
        functools.partial(pack_kernel, direct),
        [shaped(s, BF16) for s in msg_shapes],
        [hbm()] * 6,
        [vmem()] * len(msg_shapes),
        [
            pltpu.SMEM((1,), jnp.int32),
            pltpu.SMEM((owners,), jnp.int32),
            pltpu.SMEM((rb,), jnp.int32),
            pltpu.VMEM(step_in.shape, BF16),
            pltpu.VMEM(prompt_conv.shape, BF16),
            pltpu.VMEM(prompt_ssm.shape, F32),
            pltpu.SemaphoreType.DMA((9,)),
        ],
        nbytes=owners * depth * channels * 2,
    )(
        owner,
        pinned(send_rows.reshape(owners)),
        pinned(prompt_of),
        pinned(step_in),
        pinned(prompt_conv),
        pinned(prompt_ssm),
    )
    if direct:
        own = msgs[0]
        msgs = [own] + [
            lax.ppermute(m, "branch", list(enumerate(to))) for m, to in zip(msgs[1:], SENDS)
        ]
        after = own
    else:
        msgs = [lax.all_to_all(msgs[0], "branch", split_axis=0, concat_axis=0, tiled=True)]
        after = msgs[0]
    n_msgs = len(msgs)
    near = call(
        functools.partial(prepare_kernel, direct),
        [
            shaped((steps, rb, channels), F32),
            shaped((steps, rb, channels), F32),
            shaped((rb, owners), F32),
            shaped((rb, owners), F32),
            shaped((1, owners), F32),
            shaped((taps, channels), F32),
            shaped((1, channels), F32),
            shaped((width, channels), BF16),
            shaped((n_state, channels), F32),
            shaped((n_state // 2, 2 * owners, channels), F32),
            shaped(dt_weight.shape, BF16),
            shaped((1, channels), F32),
            shaped((1, channels), F32),
        ],
        [hbm()] * 3 + [vmem()] + [hbm()] * 7 + [anywhere()],
        [vmem()] * 13,
        [
            pltpu.SMEM((1,), jnp.int32),
            pltpu.SMEM((rb,), jnp.int32),
            pltpu.SMEM((rb,), jnp.int32),
            pltpu.VMEM((n_state, channels), F32),
            pltpu.SemaphoreType.DMA((8 + WEIGHT_PARTS + DT_PARTS,)),
        ],
        flops=10 * steps * rb * channels,
        nbytes=12 * steps * rb * channels,
        trans=steps * rb * channels,
    )(
        owner,
        pinned(prompt_of),
        pinned(child_slot),
        step_in,
        pinned(conv_weight),
        pinned(conv_bias[None]),
        pinned(x_weight.T),
        pinned(a_log),
        pinned(dt_weight),
        pinned(dt_bias[None]),
        pinned(skip[None]),
        after,
    )
    base, gate, pick, child_pick, sender, taps_near, bias_near, weight_near = near[:8]
    rate, twin, dtw_near, dtb_near, skip_near = near[8:]
    states = []
    if direct:
        pair = call(
            functools.partial(pair_kernel, short),
            shaped((1, 3 * n_state, channels), BF16),
            [vmem()] * 2 + [anywhere()],
            vmem(),
            nbytes=12 * n_state * channels,
        )(prompt_ssm, msgs[1], pick)
        states = [prompt_ssm, swap(pair, "branch", 1)]
    act, part, brief = call(
        functools.partial(project_kernel, n_msgs),
        [
            shaped((rows, channels), F32),
            shaped((rows, width), F32),
            shaped((rows, width), BF16),
        ],
        [vmem()] * (6 + n_msgs),
        [vmem()] * 3,
        flops=2 * rows * channels * width,
        nbytes=channels * width * 2 + rows * (channels + width) * 4,
        trans=rows * channels,
    )(pick, sender, base, taps_near, bias_near, weight_near, *msgs)
    other = swap(brief, "tensor", 1)
    distance = 2
    while distance < tensors:
        part, brief = call(
            add_kernel,
            [shaped((rows, width), F32), shaped((rows, width), BF16)],
            [vmem()] * 2,
            [vmem()] * 2,
            flops=rows * width,
            nbytes=rows * width * 14,
        )(part, other)
        other = swap(brief, "tensor", 2 * distance - 1)
        distance *= 2

    child_conv = call(
        functools.partial(windows_kernel, n_msgs, steps),
        shaped((taps - 1, rb, channels), BF16),
        [vmem(), anywhere()] + [vmem()] * n_msgs,
        vmem(),
        flops=2 * owners * taps * rb * channels,
        nbytes=4 * taps * rb * channels,
    )(child_pick, part, *msgs)
    own_start, slot_start = call(
        functools.partial(start_kernel, n_msgs, direct, short),
        [
            shaped((n_state, rb, channels), F32),
            shaped((n_state // 2, 2 * owners, channels), F32),
        ],
        [vmem()] * 2 + [anywhere()] + [vmem()] * (n_msgs + len(states)),
        [vmem()] * 2,
        [pltpu.VMEM((owners, n_state, channels), F32)],
        flops=2 * owners * n_state * (rb + owners) * channels,
        nbytes=4 * n_state * (rb + owners) * channels,
    )(pick, sender, part, *msgs, *states)

    decoded, child_ssm = call(
        functools.partial(decode_kernel, direct),
        [
            shaped((rb, steps, channels), BF16),
            shaped((rb, n_state, channels), F32),
        ],
        [hbm()] * 2 + [vmem()] * 11,
        [vmem(), anywhere()],
        [
            pltpu.SMEM((1,), jnp.int32),
            pltpu.SMEM((rb,), jnp.int32),
            pltpu.VMEM((steps * rb, channels), F32),
            pltpu.VMEM((steps * rb, channels), F32),
            pltpu.VMEM((steps, 2 * owners, channels), F32),
            pltpu.VMEM((steps, 2 * owners, channels), F32),
            pltpu.VMEM((n_state, steps * rb, LANES), F32),
            pltpu.VMEM((n_state, steps * rb, LANES), F32),
            pltpu.VMEM((n_state // 2, steps, 2 * owners, LANES), F32),
            pltpu.VMEM((owners, n_state, channels), F32),
            pltpu.VMEM((steps * rb, LANES), F32),
            pltpu.SemaphoreType.DMA((2 + rb,)),
        ],
        flops=8 * rows * n_state * channels,
        nbytes=(rb + owners) * n_state * channels * 4,
        trans=rows * n_state * channels,
    )(
        owner,
        pinned(child_slot),
        act,
        gate,
        own_start,
        slot_start,
        rate,
        twin,
        dtw_near,
        dtb_near,
        skip_near,
        part,
        other,
    )
    return (decoded, child_ssm, jnp.transpose(child_conv, (1, 0, 2)))


def solution(mesh):
    placed = (
        P(("replica", "branch"), None, "tensor"),
        P(("replica", "branch"), None, "tensor"),
        P(("replica", "branch")),
        P(("replica", "branch"), None, None, "tensor"),
        P(None, "tensor"),
        P("tensor"),
        P("tensor", None),
        P(None, "tensor"),
        P("tensor"),
        P(None, "tensor"),
        P("tensor"),
        P(("replica", "branch"), None, None),
        P(("replica", "branch")),
    )
    return jax.shard_map(
        on_device,
        mesh=mesh,
        in_specs=placed,
        out_specs=(
            P(("replica", "branch"), None, "tensor"),
            P(("replica", "branch"), None, "tensor"),
            P(("replica", "branch"), None, "tensor"),
        ),
        check_vma=False,
    )
```

```python
import functools
import math

import jax
import jax.numpy as jnp
from jax import lax
from jax.experimental import pallas as pl
from jax.experimental.pallas import tpu as pltpu
from jax.sharding import PartitionSpec as P

F32 = jnp.float32
BF16 = jnp.bfloat16
LANES = 128
VMEM_LIMIT = 48 * 2**20
WEIGHT_PARTS = 6
STEP_PARTS = 4
DIRECT = 4
SENDS = ((2, 3, 1, 0), (3, 2, 0, 1), (1, 0, 3, 2))


def vmem():
    return pl.BlockSpec(memory_space=pltpu.VMEM)


def hbm():
    return pl.BlockSpec(memory_space=pltpu.HBM)


def anywhere():
    return pl.BlockSpec(memory_space=pl.ANY)


def pinned(array):
    return pltpu.with_memory_space_constraint(array, pltpu.HBM)


def shaped(shape, dtype):
    return jax.ShapeDtypeStruct(shape, dtype)


def call(kernel, outs, in_specs, out_specs, scratch=(), flops=0, nbytes=0, trans=0):
    return pl.pallas_call(
        kernel,
        out_shape=outs,
        in_specs=in_specs,
        out_specs=out_specs,
        scratch_shapes=list(scratch),
        compiler_params=pltpu.CompilerParams(vmem_limit_bytes=VMEM_LIMIT),
        cost_estimate=pl.CostEstimate(flops=flops, bytes_accessed=nbytes, transcendentals=trans),
    )


def swap(value, axis, distance):
    size = lax.axis_size(axis)
    return lax.ppermute(value, axis, [(i, i ^ distance) for i in range(size)])


def chosen(number, values):
    total = values[0]
    for i in range(1, len(values)):
        total = jnp.where(number == i, values[i], total)
    return total


def block_of(sender, owner, direct):
    if not direct:
        return sender
    table = [
        [0 if s == r else 1 + [to[s] for to in SENDS].index(r) for s in range(DIRECT)]
        for r in range(DIRECT)
    ]
    places = [chosen(owner, [row[s] for row in table]) for s in range(DIRECT)]
    return places[sender] if isinstance(sender, int) else chosen(sender, places)


def all_of(copies):
    for copy in copies:
        copy.start()
    for copy in copies:
        copy.wait()


def read_messages(refs):
    return [ref[i].astype(F32) for ref in refs for i in range(ref.shape[0])]


def in_parts(source, target, sems, first, count):
    rows = source.shape[0] // count
    at = [pl.ds(i * rows, rows) for i in range(count)]
    return [
        pltpu.make_async_copy(source.at[a], target.at[a], sems.at[first + i])
        for i, a in enumerate(at)
    ]


def scalar_onehot(senders_s, owner, shape, direct):
    row_of = lax.broadcasted_iota(jnp.int32, shape, 0)
    wanted = jnp.zeros(shape, jnp.int32)
    for b in range(shape[0]):
        wanted = jnp.where(row_of == b, senders_s[b], wanted)
    wanted = block_of(wanted, owner, direct)
    return (wanted == lax.broadcasted_iota(jnp.int32, shape, 1)).astype(F32)


def pick_rows(pick, rows):
    total = pick[:, 0:1] * rows[0]
    for k in range(1, len(rows)):
        total = total + pick[:, k : k + 1] * rows[k]
    return total


def pack_kernel(direct, owner_hbm, rows_hbm, prompt_hbm, step_hbm, conv_hbm, ssm_hbm, *rest):
    outs, (owner_s, rows_s, prompt_s, step, conv, ssm, sems) = rest[:-7], rest[-7:]
    owners = rows_hbm.shape[0]
    channels = step_hbm.shape[3]
    copies = [
        pltpu.make_async_copy(owner_hbm, owner_s, sems.at[4]),
        pltpu.make_async_copy(rows_hbm, rows_s, sems.at[0]),
        pltpu.make_async_copy(prompt_hbm, prompt_s, sems.at[1]),
        pltpu.make_async_copy(conv_hbm, conv, sems.at[2]),
        pltpu.make_async_copy(ssm_hbm, ssm, sems.at[3]),
    ]
    all_of(copies + in_parts(step_hbm, step, sems, 5, STEP_PARTS))
    owner = owner_s[0]
    window = conv[0].astype(F32)

    def write(ref, target):
        row = jnp.maximum(rows_s[target], 0)
        xs = step[row, :, 0, :].astype(F32)
        number = prompt_s[row].astype(F32)
        pieces = [xs, window, jnp.full((1, channels), number, F32)]
        if ref.shape[0] > sum(p.shape[0] for p in pieces):
            pieces.append(ssm[0])
        ref[...] = jnp.concatenate(pieces, axis=0).astype(BF16)

    if direct:
        write(outs[0].at[0], owner)
        for ref, to in zip(outs[1:], SENDS):
            write(ref.at[0], chosen(owner, to))
    else:
        for target in range(owners):
            write(outs[0].at[target], target)


def pair_kernel(text, ssm_ref, came_ref, after_ref, pair_ref):
    del after_ref
    state = ssm_ref[0]
    head = state.astype(BF16).astype(F32)
    came = came_ref[0].astype(F32)[text:, :]
    pair_ref[0] = jnp.concatenate([head, state - head, came], axis=0).astype(BF16)


def silu(v):
    return v / (1.0 + jnp.exp(-v))


def prepare_kernel(
    direct,
    owner_hbm,
    prompt_hbm,
    child_hbm,
    step_hbm,
    cw_hbm,
    cb_hbm,
    xwt_hbm,
    alog_hbm,
    dtb_hbm,
    skip_hbm,
    after_ref,
    base_ref,
    gate_ref,
    pick_ref,
    child_ref,
    sender_ref,
    cw_ref,
    cb_ref,
    xwt_ref,
    rate_ref,
    twin_ref,
    dtb_ref,
    skip_ref,
    step_ref,
    owner_s,
    prompt_s,
    child_s,
    alog,
    sems,
):
    del after_ref
    small = [
        pltpu.make_async_copy(source, target, sems.at[i])
        for i, (source, target) in enumerate(
            (
                (cw_hbm, cw_ref),
                (cb_hbm, cb_ref),
                (owner_hbm, owner_s),
                (prompt_hbm, prompt_s),
                (child_hbm, child_s),
                (alog_hbm, alog),
                (dtb_hbm, dtb_ref),
                (skip_hbm, skip_ref),
            )
        )
    ]
    inputs = in_parts(step_hbm, step_ref, sems, len(small), STEP_PARTS)
    large = in_parts(xwt_hbm, xwt_ref, sems, len(small) + STEP_PARTS, WEIGHT_PARTS)
    for copy in inputs + small + large:
        copy.start()
    for copy in inputs:
        copy.wait()
    steps = step_ref.shape[1]
    taps = cw_hbm.shape[0]
    xs = [step_ref[:, t, 0, :].astype(F32) for t in range(steps)]
    for t in range(steps):
        gate_ref[t] = silu(step_ref[:, t, 1, :].astype(F32))
    for copy in small:
        copy.wait()
    for t in range(steps):
        total = cw_ref[taps - 1 : taps, :] * xs[t] + cb_ref[...]
        for k in range(max(0, taps - 1 - t), taps - 1):
            total = total + cw_ref[k : k + 1, :] * xs[t + k - taps + 1]
        base_ref[t] = total
    pick_ref[...] = scalar_onehot(prompt_s, owner_s[0], pick_ref.shape, direct)
    child_ref[...] = scalar_onehot(child_s, owner_s[0], child_ref.shape, direct)
    column = lax.broadcasted_iota(jnp.int32, sender_ref.shape, 1)
    sender = column
    for sent in range(sender_ref.shape[1] if direct else 0):
        sender = jnp.where(column == block_of(sent, owner_s[0], direct), sent, sender)
    sender_ref[...] = sender.astype(F32)
    rate = jnp.exp(alog[...]) * (-math.log2(math.e))
    rate_ref[...] = rate
    half = (twin_ref.shape[1] // 2, rate.shape[1])
    for m in range(rate.shape[0] // 2):
        two = [jnp.broadcast_to(rate[n : n + 1, :], half) for n in (2 * m, 2 * m + 1)]
        twin_ref[m] = jnp.concatenate(two, axis=0)
    for copy in large:
        copy.wait()


def slot_onehot(numbers, sender_ref):
    owners = sender_ref.shape[1]
    return (numbers[:, :owners] == sender_ref[...]).astype(F32)


def project_kernel(n_msgs, pick_ref, sender_ref, base_ref, cw_ref, cb_ref, xwt_ref, *rest):
    msgs, (act_ref, part_ref, short_ref) = rest[:n_msgs], rest[n_msgs:]
    taps = cw_ref.shape[0]
    steps, rb, _ = base_ref.shape
    past = taps - 1
    held = read_messages(msgs)
    owners = len(held)
    windows = [[h[steps + k : steps + k + 1, :] for h in held] for k in range(past)]
    own = pick_ref[...]
    own_windows = [pick_rows(own, w) for w in windows]
    for t in range(steps):
        conv = base_ref[t]
        for k in range(past - t):
            conv = conv + cw_ref[k : k + 1, :] * own_windows[t + k]
        act_ref[t * rb : (t + 1) * rb, :] = silu(conv)

    def line_of(row):
        return jnp.concatenate([h[row : row + 1, :] for h in held], axis=0)

    slot = slot_onehot(line_of(past + steps), sender_ref)
    line = [pick_rows(slot, w) for w in windows]
    line += [line_of(t) for t in range(steps)]
    row = steps * rb
    for t in range(steps):
        conv = cw_ref[past:taps, :] * line[t + past] + cb_ref[...]
        for k in range(past):
            conv = conv + cw_ref[k : k + 1, :] * line[t + k]
        act_ref[row : row + owners, :] = silu(conv)
        row += owners
    part = lax.dot_general(
        act_ref[...].astype(BF16),
        xwt_ref[...],
        (((1,), (1,)), ((), ())),
        preferred_element_type=F32,
    )
    part_ref[...] = part
    short_ref[...] = part.astype(BF16)


def add_kernel(a_ref, b_ref, sum_ref, short_ref):
    total = a_ref[...] + b_ref[...].astype(F32)
    sum_ref[...] = total
    short_ref[...] = total.astype(BF16)


def windows_kernel(n_msgs, steps, child_ref, after_ref, *rest):
    del after_ref
    msgs, (conv_ref,) = rest[:n_msgs], rest[n_msgs:]
    held = read_messages(msgs)
    past = conv_ref.shape[0]
    for k in range(past):
        at = steps - past + k
        rows = [h[at : at + 1, :] for h in held]
        conv_ref[k] = pick_rows(child_ref[...], rows).astype(BF16)


def start_kernel(n_msgs, direct, text, pick_ref, sender_ref, after_ref, *rest):
    del after_ref
    msgs, rest = rest[:n_msgs], rest[n_msgs:]
    apart, (own_ref, slot_ref, state_s) = rest[:-3], rest[-3:]
    n_state = own_ref.shape[0]
    held = read_messages(msgs)
    owners = len(held)
    numbers = jnp.concatenate([h[text - 1 : text, :] for h in held], axis=0)
    states = [h[text:, :] for h in held]
    if direct:
        ssm_ref, pair_ref = apart
        head, low, came = [
            pair_ref[0].astype(F32)[i * n_state : (i + 1) * n_state, :] for i in range(3)
        ]
        states[0], states[2], states[3] = ssm_ref[0], came, head + low
    for k, state in enumerate(states):
        state_s[k] = state
    own = pick_ref[...]
    slot = slot_onehot(numbers, sender_ref)

    def two(m, carry):
        picked = []
        for n in (2 * m, 2 * m + 1):
            rows = [state_s[k, pl.ds(n, 1), :] for k in range(owners)]
            own_ref[n] = pick_rows(own, rows)
            picked.append(pick_rows(slot, rows))
        slot_ref[m] = jnp.concatenate(picked, axis=0)
        return carry

    lax.fori_loop(0, n_state // 2, two, 0, unroll=owners <= DIRECT)


def decode_kernel(
    direct,
    owner_hbm,
    child_hbm,
    act_ref,
    gate_ref,
    own_ref,
    slot_ref,
    rate_ref,
    twin_ref,
    dtw_ref,
    dtb_ref,
    skip_ref,
    part_ref,
    other_ref,
    dec_ref,
    child_ssm,
    owner_s,
    child_s,
    delta_s,
    gain_s,
    slot_delta_s,
    slot_gain_s,
    b_s,
    c_s,
    twin_b_s,
    slots_s,
    line_s,
    sems,
):
    scalars = [
        pltpu.make_async_copy(owner_hbm, owner_s, sems.at[0]),
        pltpu.make_async_copy(child_hbm, child_s, sems.at[1]),
    ]
    for copy in scalars:
        copy.start()
    rb, steps, channels = dec_ref.shape
    rank = dtw_ref.shape[0]
    n_state = rate_ref.shape[0]
    n_slots = slots_s.shape[0]
    own_rows = steps * rb
    chunks = channels // LANES

    proj = part_ref[...] + other_ref[...].astype(F32)
    delta_in = proj[:, :rank].astype(BF16)
    delta = jnp.dot(delta_in, dtw_ref[...], preferred_element_type=F32) + dtb_ref[...]
    delta = jnp.maximum(delta, 0.0) + jnp.log(1.0 + jnp.exp(-jnp.abs(delta)))
    gain = delta * act_ref[...]
    delta_s[...] = delta[:own_rows, :]
    gain_s[...] = gain[:own_rows, :]

    def column(at, n, rows):
        return jnp.broadcast_to(at[:, n : n + 1], (rows, LANES))

    for t in range(steps):
        at = slice(own_rows + t * n_slots, own_rows + (t + 1) * n_slots)
        slot_delta_s[t] = jnp.concatenate([delta[at, :]] * 2, axis=0)
        slot_gain_s[t] = jnp.concatenate([gain[at, :]] * 2, axis=0)
        twice = jnp.concatenate([proj[at, rank:]] * 2, axis=0)
        upper = lax.broadcasted_iota(jnp.int32, (2 * n_slots, LANES), 0) < n_slots
        for m in range(n_state // 2):
            twin_b_s[m, t] = jnp.where(
                upper, column(twice, 2 * m, 2 * n_slots), column(twice, 2 * m + 1, 2 * n_slots)
            )
    for n in range(n_state):
        b_s[n] = column(proj[:own_rows, rank:], n, own_rows)
        c_s[n] = column(proj[:own_rows, rank:], n_state + n, own_rows)

    def slot_chunk(chunk, carry):
        columns = pl.ds(pl.multiple_of(chunk * LANES, LANES), LANES)
        delta = [slot_delta_s[t, :, columns] for t in range(steps)]
        gain = [slot_gain_s[t, :, columns] for t in range(steps)]
        for m in range(n_state // 2):
            rate = twin_ref[m, :, columns]
            state = slot_ref[m, :, columns]
            for t in range(steps):
                state = jnp.exp2(delta[t] * rate) * state + gain[t] * twin_b_s[m, t]
            slots_s[:, 2 * m, columns] = state[:n_slots, :]
            slots_s[:, 2 * m + 1, columns] = state[n_slots:, :]
        return carry

    lax.fori_loop(0, chunks, slot_chunk, 0)
    for copy in scalars:
        copy.wait()
    copies = []
    for j in range(rb):
        at = block_of(child_s[j], owner_s[0], direct)
        copy = pltpu.make_async_copy(slots_s.at[at], child_ssm.at[j], sems.at[2 + j])
        copy.start()
        copies.append(copy)

    def own_chunk(chunk, carry):
        columns = pl.ds(pl.multiple_of(chunk * LANES, LANES), LANES)
        at = [pl.ds(t * rb, rb) for t in range(steps)]
        delta = [delta_s[a, columns] for a in at]
        gain = [gain_s[a, columns] for a in at]
        sums = [skip_ref[:, columns] * act_ref[a, columns] for a in at]
        for n in range(n_state):
            rate = rate_ref[n : n + 1, columns]
            state = own_ref[n, :, columns]
            for t in range(steps):
                state = jnp.exp2(delta[t] * rate) * state + gain[t] * b_s[n, at[t], :]
                sums[t] = sums[t] + c_s[n, at[t], :] * state
        for t in range(steps):
            line_s[pl.ds(t, rb, stride=steps), :] = sums[t] * gate_ref[t, :, columns]
        dec_ref[:, :, columns] = line_s[...].reshape(rb, steps, LANES).astype(BF16)
        return carry

    lax.fori_loop(0, chunks, own_chunk, 0)
    for copy in copies:
        copy.wait()


def on_device(
    prompt_ssm,
    prompt_conv,
    prompt_of,
    step_in,
    conv_weight,
    conv_bias,
    x_weight,
    dt_weight,
    dt_bias,
    a_log,
    skip,
    send_rows,
    child_slot,
):
    owners = lax.axis_size("branch")
    tensors = lax.axis_size("tensor")
    assert owners & (owners - 1) == 0 and tensors & (tensors - 1) == 0
    assert prompt_ssm.shape[0] == 1 and send_rows.shape[2] == 1
    rb, steps, _, channels = step_in.shape
    taps = conv_weight.shape[0]
    width = x_weight.shape[1]
    n_state = a_log.shape[0]
    rows = steps * (rb + owners)
    short = taps - 1 + steps + 1
    depth = short + n_state
    direct = owners == DIRECT
    owner = pinned(lax.axis_index("branch").astype(jnp.int32).reshape(1))

    if direct:
        msg_shapes = [(1, d, channels) for d in (short, depth, short, short)]
    else:
        msg_shapes = [(owners, depth, channels)]
    msgs = call(
        functools.partial(pack_kernel, direct),
        [shaped(s, BF16) for s in msg_shapes],
        [hbm()] * 6,
        [vmem()] * len(msg_shapes),
        [
            pltpu.SMEM((1,), jnp.int32),
            pltpu.SMEM((owners,), jnp.int32),
            pltpu.SMEM((rb,), jnp.int32),
            pltpu.VMEM(step_in.shape, BF16),
            pltpu.VMEM(prompt_conv.shape, BF16),
            pltpu.VMEM(prompt_ssm.shape, F32),
            pltpu.SemaphoreType.DMA((5 + STEP_PARTS,)),
        ],
        nbytes=owners * depth * channels * 2,
    )(
        owner,
        pinned(send_rows.reshape(owners)),
        pinned(prompt_of),
        pinned(step_in),
        pinned(prompt_conv),
        pinned(prompt_ssm),
    )
    if direct:
        own = msgs[0]
        msgs = [own] + [
            lax.ppermute(m, "branch", list(enumerate(to))) for m, to in zip(msgs[1:], SENDS)
        ]
        after = own
    else:
        msgs = [lax.all_to_all(msgs[0], "branch", split_axis=0, concat_axis=0, tiled=True)]
        after = msgs[0]
    n_msgs = len(msgs)
    near = call(
        functools.partial(prepare_kernel, direct),
        [
            shaped((steps, rb, channels), F32),
            shaped((steps, rb, channels), F32),
            shaped((rb, owners), F32),
            shaped((rb, owners), F32),
            shaped((1, owners), F32),
            shaped((taps, channels), F32),
            shaped((1, channels), F32),
            shaped((width, channels), BF16),
            shaped((n_state, channels), F32),
            shaped((n_state // 2, 2 * owners, channels), F32),
            shaped((1, channels), F32),
            shaped((1, channels), F32),
        ],
        [hbm()] * 10 + [anywhere()],
        [vmem()] * 12,
        [
            pltpu.VMEM(step_in.shape, BF16),
            pltpu.SMEM((1,), jnp.int32),
            pltpu.SMEM((rb,), jnp.int32),
            pltpu.SMEM((rb,), jnp.int32),
            pltpu.VMEM((n_state, channels), F32),
            pltpu.SemaphoreType.DMA((8 + WEIGHT_PARTS + STEP_PARTS,)),
        ],
        flops=10 * steps * rb * channels,
        nbytes=12 * steps * rb * channels,
        trans=steps * rb * channels,
    )(
        owner,
        pinned(prompt_of),
        pinned(child_slot),
        pinned(step_in),
        pinned(conv_weight),
        pinned(conv_bias[None]),
        pinned(x_weight.T),
        pinned(a_log),
        pinned(dt_bias[None]),
        pinned(skip[None]),
        after,
    )
    base, gate, pick, child_pick, sender, taps_near, bias_near, weight_near = near[:8]
    rate, twin, dtb_near, skip_near = near[8:]
    states = []
    if direct:
        pair = call(
            functools.partial(pair_kernel, short),
            shaped((1, 3 * n_state, channels), BF16),
            [vmem()] * 2 + [anywhere()],
            vmem(),
            nbytes=12 * n_state * channels,
        )(prompt_ssm, msgs[1], pick)
        states = [prompt_ssm, swap(pair, "branch", 1)]
    act, part, brief = call(
        functools.partial(project_kernel, n_msgs),
        [
            shaped((rows, channels), F32),
            shaped((rows, width), F32),
            shaped((rows, width), BF16),
        ],
        [vmem()] * (6 + n_msgs),
        [vmem()] * 3,
        flops=2 * rows * channels * width,
        nbytes=channels * width * 2 + rows * (channels + width) * 4,
        trans=rows * channels,
    )(pick, sender, base, taps_near, bias_near, weight_near, *msgs)
    other = swap(brief, "tensor", 1)
    distance = 2
    while distance < tensors:
        part, brief = call(
            add_kernel,
            [shaped((rows, width), F32), shaped((rows, width), BF16)],
            [vmem()] * 2,
            [vmem()] * 2,
            flops=rows * width,
            nbytes=rows * width * 14,
        )(part, other)
        other = swap(brief, "tensor", 2 * distance - 1)
        distance *= 2

    child_conv = call(
        functools.partial(windows_kernel, n_msgs, steps),
        shaped((taps - 1, rb, channels), BF16),
        [vmem(), anywhere()] + [vmem()] * n_msgs,
        vmem(),
        flops=2 * owners * taps * rb * channels,
        nbytes=4 * taps * rb * channels,
    )(child_pick, part, *msgs)
    own_start, slot_start = call(
        functools.partial(start_kernel, n_msgs, direct, short),
        [
            shaped((n_state, rb, channels), F32),
            shaped((n_state // 2, 2 * owners, channels), F32),
        ],
        [vmem()] * 2 + [anywhere()] + [vmem()] * (n_msgs + len(states)),
        [vmem()] * 2,
        [pltpu.VMEM((owners, n_state, channels), F32)],
        flops=2 * owners * n_state * (rb + owners) * channels,
        nbytes=4 * n_state * (rb + owners) * channels,
    )(pick, sender, part, *msgs, *states)

    decoded, child_ssm = call(
        functools.partial(decode_kernel, direct),
        [
            shaped((rb, steps, channels), BF16),
            shaped((rb, n_state, channels), F32),
        ],
        [hbm()] * 2 + [vmem()] * 11,
        [vmem(), anywhere()],
        [
            pltpu.SMEM((1,), jnp.int32),
            pltpu.SMEM((rb,), jnp.int32),
            pltpu.VMEM((steps * rb, channels), F32),
            pltpu.VMEM((steps * rb, channels), F32),
            pltpu.VMEM((steps, 2 * owners, channels), F32),
            pltpu.VMEM((steps, 2 * owners, channels), F32),
            pltpu.VMEM((n_state, steps * rb, LANES), F32),
            pltpu.VMEM((n_state, steps * rb, LANES), F32),
            pltpu.VMEM((n_state // 2, steps, 2 * owners, LANES), F32),
            pltpu.VMEM((owners, n_state, channels), F32),
            pltpu.VMEM((steps * rb, LANES), F32),
            pltpu.SemaphoreType.DMA((2 + rb,)),
        ],
        flops=8 * rows * n_state * channels,
        nbytes=(rb + owners) * n_state * channels * 4,
        trans=rows * n_state * channels,
    )(
        owner,
        pinned(child_slot),
        act,
        gate,
        own_start,
        slot_start,
        rate,
        twin,
        dt_weight,
        dtb_near,
        skip_near,
        part,
        other,
    )
    return (decoded, child_ssm, jnp.transpose(child_conv, (1, 0, 2)))


def solution(mesh):
    placed = (
        P(("replica", "branch"), None, "tensor"),
        P(("replica", "branch"), None, "tensor"),
        P(("replica", "branch")),
        P(("replica", "branch"), None, None, "tensor"),
        P(None, "tensor"),
        P("tensor"),
        P("tensor", None),
        P(None, "tensor"),
        P("tensor"),
        P(None, "tensor"),
        P("tensor"),
        P(("replica", "branch"), None, None),
        P(("replica", "branch")),
    )
    return jax.shard_map(
        on_device,
        mesh=mesh,
        in_specs=placed,
        out_specs=(
            P(("replica", "branch"), None, "tensor"),
            P(("replica", "branch"), None, "tensor"),
            P(("replica", "branch"), None, "tensor"),
        ),
        check_vma=False,
    )
```

```python
import functools
import math

import jax
import jax.numpy as jnp
from jax import lax
from jax.experimental import pallas as pl
from jax.experimental.pallas import tpu as pltpu
from jax.sharding import PartitionSpec as P

F32 = jnp.float32
BF16 = jnp.bfloat16
LANES = 128
VMEM_LIMIT = 48 * 2**20
WEIGHT_PARTS = 6
STEP_PARTS = 4
DIRECT = 4
SENDS = ((2, 3, 1, 0), (3, 2, 0, 1), (1, 0, 3, 2))


def vmem():
    return pl.BlockSpec(memory_space=pltpu.VMEM)


def hbm():
    return pl.BlockSpec(memory_space=pltpu.HBM)


def anywhere():
    return pl.BlockSpec(memory_space=pl.ANY)


def pinned(array):
    return pltpu.with_memory_space_constraint(array, pltpu.HBM)


def shaped(shape, dtype):
    return jax.ShapeDtypeStruct(shape, dtype)


def call(kernel, outs, in_specs, out_specs, scratch=(), flops=0, nbytes=0, trans=0):
    return pl.pallas_call(
        kernel,
        out_shape=outs,
        in_specs=in_specs,
        out_specs=out_specs,
        scratch_shapes=list(scratch),
        compiler_params=pltpu.CompilerParams(vmem_limit_bytes=VMEM_LIMIT),
        cost_estimate=pl.CostEstimate(flops=flops, bytes_accessed=nbytes, transcendentals=trans),
    )


def swap(value, axis, distance):
    size = lax.axis_size(axis)
    return lax.ppermute(value, axis, [(i, i ^ distance) for i in range(size)])


def chosen(number, values):
    total = values[0]
    for i in range(1, len(values)):
        total = jnp.where(number == i, values[i], total)
    return total


def block_of(sender, owner, direct):
    if not direct:
        return sender
    table = [
        [0 if s == r else 1 + [to[s] for to in SENDS].index(r) for s in range(DIRECT)]
        for r in range(DIRECT)
    ]
    places = [chosen(owner, [row[s] for row in table]) for s in range(DIRECT)]
    return places[sender] if isinstance(sender, int) else chosen(sender, places)


def all_of(copies):
    for copy in copies:
        copy.start()
    for copy in copies:
        copy.wait()


def read_messages(refs):
    return [ref[i].astype(F32) for ref in refs for i in range(ref.shape[0])]


def in_parts(source, target, sems, first, count):
    rows = source.shape[0] // count
    at = [pl.ds(i * rows, rows) for i in range(count)]
    return [
        pltpu.make_async_copy(source.at[a], target.at[a], sems.at[first + i])
        for i, a in enumerate(at)
    ]


def scalar_onehot(senders_s, owner, shape, direct):
    row_of = lax.broadcasted_iota(jnp.int32, shape, 0)
    wanted = jnp.zeros(shape, jnp.int32)
    for b in range(shape[0]):
        wanted = jnp.where(row_of == b, senders_s[b], wanted)
    wanted = block_of(wanted, owner, direct)
    return (wanted == lax.broadcasted_iota(jnp.int32, shape, 1)).astype(F32)


def each_chunk(body, chunks, straight):
    if straight:
        for chunk in range(chunks):
            body(slice(chunk * LANES, (chunk + 1) * LANES))
        return

    def step(chunk, carry):
        body(pl.ds(pl.multiple_of(chunk * LANES, LANES), LANES))
        return carry

    lax.fori_loop(0, chunks, step, 0)


def pick_rows(pick, rows):
    total = pick[:, 0:1] * rows[0]
    for k in range(1, len(rows)):
        total = total + pick[:, k : k + 1] * rows[k]
    return total


def pack_kernel(direct, owner_hbm, rows_hbm, prompt_hbm, step_hbm, conv_hbm, ssm_hbm, *rest):
    outs, (owner_s, rows_s, prompt_s, step, conv, ssm, sems) = rest[:-7], rest[-7:]
    owners = rows_hbm.shape[0]
    channels = step_hbm.shape[3]
    copies = [
        pltpu.make_async_copy(owner_hbm, owner_s, sems.at[4]),
        pltpu.make_async_copy(rows_hbm, rows_s, sems.at[0]),
        pltpu.make_async_copy(prompt_hbm, prompt_s, sems.at[1]),
        pltpu.make_async_copy(conv_hbm, conv, sems.at[2]),
        pltpu.make_async_copy(ssm_hbm, ssm, sems.at[3]),
    ]
    all_of(copies + in_parts(step_hbm, step, sems, 5, STEP_PARTS))
    owner = owner_s[0]
    window = conv[0].astype(F32)

    def write(ref, target):
        row = jnp.maximum(rows_s[target], 0)
        xs = step[row, :, 0, :].astype(F32)
        number = prompt_s[row].astype(F32)
        pieces = [xs, window, jnp.full((1, channels), number, F32)]
        if ref.shape[0] > sum(p.shape[0] for p in pieces):
            pieces.append(ssm[0])
        ref[...] = jnp.concatenate(pieces, axis=0).astype(BF16)

    if direct:
        write(outs[0].at[0], owner)
        for ref, to in zip(outs[1:], SENDS):
            write(ref.at[0], chosen(owner, to))
    else:
        for target in range(owners):
            write(outs[0].at[target], target)


def pair_kernel(text, ssm_ref, came_ref, after_ref, pair_ref):
    del after_ref
    state = ssm_ref[0]
    head = state.astype(BF16).astype(F32)
    came = came_ref[0].astype(F32)[text:, :]
    pair_ref[0] = jnp.concatenate([head, state - head, came], axis=0).astype(BF16)


def silu(v):
    return v / (1.0 + jnp.exp(-v))


def prepare_kernel(
    direct,
    owner_hbm,
    prompt_hbm,
    child_hbm,
    step_hbm,
    cw_hbm,
    cb_hbm,
    xwt_hbm,
    alog_hbm,
    dtb_hbm,
    skip_hbm,
    after_ref,
    base_ref,
    gate_ref,
    pick_ref,
    child_ref,
    sender_ref,
    cw_ref,
    cb_ref,
    xwt_ref,
    rate_ref,
    twin_ref,
    dtb_ref,
    skip_ref,
    step_ref,
    owner_s,
    prompt_s,
    child_s,
    alog,
    sems,
):
    del after_ref
    small = [
        pltpu.make_async_copy(source, target, sems.at[i])
        for i, (source, target) in enumerate(
            (
                (cw_hbm, cw_ref),
                (cb_hbm, cb_ref),
                (owner_hbm, owner_s),
                (prompt_hbm, prompt_s),
                (child_hbm, child_s),
                (alog_hbm, alog),
                (dtb_hbm, dtb_ref),
                (skip_hbm, skip_ref),
            )
        )
    ]
    inputs = in_parts(step_hbm, step_ref, sems, len(small), STEP_PARTS)
    large = in_parts(xwt_hbm, xwt_ref, sems, len(small) + STEP_PARTS, WEIGHT_PARTS)
    for copy in inputs + small + large:
        copy.start()
    for copy in inputs:
        copy.wait()
    steps = step_ref.shape[1]
    taps = cw_hbm.shape[0]
    xs = [step_ref[:, t, 0, :].astype(F32) for t in range(steps)]
    for t in range(steps):
        gate_ref[t] = silu(step_ref[:, t, 1, :].astype(F32))
    for copy in small:
        copy.wait()
    for t in range(steps):
        total = cw_ref[taps - 1 : taps, :] * xs[t] + cb_ref[...]
        for k in range(max(0, taps - 1 - t), taps - 1):
            total = total + cw_ref[k : k + 1, :] * xs[t + k - taps + 1]
        base_ref[t] = total
    pick_ref[...] = scalar_onehot(prompt_s, owner_s[0], pick_ref.shape, direct)
    child_ref[...] = scalar_onehot(child_s, owner_s[0], child_ref.shape, direct)
    column = lax.broadcasted_iota(jnp.int32, sender_ref.shape, 1)
    sender = column
    for sent in range(sender_ref.shape[1] if direct else 0):
        sender = jnp.where(column == block_of(sent, owner_s[0], direct), sent, sender)
    sender_ref[...] = sender.astype(F32)
    rate = jnp.exp(alog[...]) * (-math.log2(math.e))
    rate_ref[...] = rate
    half = (twin_ref.shape[1] // 2, rate.shape[1])
    for m in range(rate.shape[0] // 2):
        two = [jnp.broadcast_to(rate[n : n + 1, :], half) for n in (2 * m, 2 * m + 1)]
        twin_ref[m] = jnp.concatenate(two, axis=0)
    for copy in large:
        copy.wait()


def slot_onehot(numbers, sender_ref):
    owners = sender_ref.shape[1]
    return (numbers[:, :owners] == sender_ref[...]).astype(F32)


def project_kernel(n_msgs, pick_ref, sender_ref, base_ref, cw_ref, cb_ref, xwt_ref, *rest):
    msgs, (act_ref, part_ref, short_ref) = rest[:n_msgs], rest[n_msgs:]
    taps = cw_ref.shape[0]
    steps, rb, _ = base_ref.shape
    past = taps - 1
    held = read_messages(msgs)
    owners = len(held)
    windows = [[h[steps + k : steps + k + 1, :] for h in held] for k in range(past)]
    own = pick_ref[...]
    own_windows = [pick_rows(own, w) for w in windows]
    for t in range(steps):
        conv = base_ref[t]
        for k in range(past - t):
            conv = conv + cw_ref[k : k + 1, :] * own_windows[t + k]
        act_ref[t * rb : (t + 1) * rb, :] = silu(conv)

    def line_of(row):
        return jnp.concatenate([h[row : row + 1, :] for h in held], axis=0)

    slot = slot_onehot(line_of(past + steps), sender_ref)
    line = [pick_rows(slot, w) for w in windows]
    line += [line_of(t) for t in range(steps)]
    row = steps * rb
    for t in range(steps):
        conv = cw_ref[past:taps, :] * line[t + past] + cb_ref[...]
        for k in range(past):
            conv = conv + cw_ref[k : k + 1, :] * line[t + k]
        act_ref[row : row + owners, :] = silu(conv)
        row += owners
    part = lax.dot_general(
        act_ref[...].astype(BF16),
        xwt_ref[...],
        (((1,), (1,)), ((), ())),
        preferred_element_type=F32,
    )
    part_ref[...] = part
    short_ref[...] = part.astype(BF16)


def add_kernel(a_ref, b_ref, sum_ref, short_ref):
    total = a_ref[...] + b_ref[...].astype(F32)
    sum_ref[...] = total
    short_ref[...] = total.astype(BF16)


def windows_kernel(n_msgs, steps, child_ref, after_ref, *rest):
    del after_ref
    msgs, (conv_ref,) = rest[:n_msgs], rest[n_msgs:]
    held = read_messages(msgs)
    past = conv_ref.shape[0]
    for k in range(past):
        at = steps - past + k
        rows = [h[at : at + 1, :] for h in held]
        conv_ref[k] = pick_rows(child_ref[...], rows).astype(BF16)


def start_kernel(n_msgs, direct, text, pick_ref, sender_ref, after_ref, *rest):
    del after_ref
    msgs, rest = rest[:n_msgs], rest[n_msgs:]
    apart, (own_ref, slot_ref, state_s) = rest[:-3], rest[-3:]
    n_state = own_ref.shape[0]
    held = read_messages(msgs)
    owners = len(held)
    numbers = jnp.concatenate([h[text - 1 : text, :] for h in held], axis=0)
    states = [h[text:, :] for h in held]
    if direct:
        ssm_ref, pair_ref = apart
        head, low, came = [
            pair_ref[0].astype(F32)[i * n_state : (i + 1) * n_state, :] for i in range(3)
        ]
        states[0], states[2], states[3] = ssm_ref[0], came, head + low
    for k, state in enumerate(states):
        state_s[k] = state
    own = pick_ref[...]
    slot = slot_onehot(numbers, sender_ref)

    def two(m, carry):
        picked = []
        for n in (2 * m, 2 * m + 1):
            rows = [state_s[k, pl.ds(n, 1), :] for k in range(owners)]
            own_ref[n] = pick_rows(own, rows)
            picked.append(pick_rows(slot, rows))
        slot_ref[m] = jnp.concatenate(picked, axis=0)
        return carry

    lax.fori_loop(0, n_state // 2, two, 0, unroll=owners <= DIRECT)


def decode_kernel(
    direct,
    owner_hbm,
    child_hbm,
    act_ref,
    gate_ref,
    own_ref,
    slot_ref,
    rate_ref,
    twin_ref,
    dtw_ref,
    dtb_ref,
    skip_ref,
    part_ref,
    other_ref,
    dec_ref,
    child_ssm,
    owner_s,
    child_s,
    delta_s,
    gain_s,
    slot_delta_s,
    slot_gain_s,
    b_s,
    c_s,
    twin_b_s,
    slots_s,
    line_s,
    sems,
):
    scalars = [
        pltpu.make_async_copy(owner_hbm, owner_s, sems.at[0]),
        pltpu.make_async_copy(child_hbm, child_s, sems.at[1]),
    ]
    for copy in scalars:
        copy.start()
    rb, steps, channels = dec_ref.shape
    rank = dtw_ref.shape[0]
    n_state = rate_ref.shape[0]
    n_slots = slots_s.shape[0]
    own_rows = steps * rb
    chunks = channels // LANES

    proj = part_ref[...] + other_ref[...].astype(F32)
    delta_in = proj[:, :rank].astype(BF16)
    delta = jnp.dot(delta_in, dtw_ref[...], preferred_element_type=F32) + dtb_ref[...]
    delta = jnp.maximum(delta, 0.0) + jnp.log(1.0 + jnp.exp(-jnp.abs(delta)))
    gain = delta * act_ref[...]
    delta_s[...] = delta[:own_rows, :]
    gain_s[...] = gain[:own_rows, :]

    def column(at, n, rows):
        return jnp.broadcast_to(at[:, n : n + 1], (rows, LANES))

    for t in range(steps):
        at = slice(own_rows + t * n_slots, own_rows + (t + 1) * n_slots)
        slot_delta_s[t] = jnp.concatenate([delta[at, :]] * 2, axis=0)
        slot_gain_s[t] = jnp.concatenate([gain[at, :]] * 2, axis=0)
        twice = jnp.concatenate([proj[at, rank:]] * 2, axis=0)
        upper = lax.broadcasted_iota(jnp.int32, (2 * n_slots, LANES), 0) < n_slots
        for m in range(n_state // 2):
            twin_b_s[m, t] = jnp.where(
                upper, column(twice, 2 * m, 2 * n_slots), column(twice, 2 * m + 1, 2 * n_slots)
            )
    for n in range(n_state):
        b_s[n] = column(proj[:own_rows, rank:], n, own_rows)
        c_s[n] = column(proj[:own_rows, rank:], n_state + n, own_rows)

    def slot_chunk(columns):
        delta = [slot_delta_s[t, :, columns] for t in range(steps)]
        gain = [slot_gain_s[t, :, columns] for t in range(steps)]
        for m in range(n_state // 2):
            rate = twin_ref[m, :, columns]
            state = slot_ref[m, :, columns]
            for t in range(steps):
                state = jnp.exp2(delta[t] * rate) * state + gain[t] * twin_b_s[m, t]
            slots_s[:, 2 * m, columns] = state[:n_slots, :]
            slots_s[:, 2 * m + 1, columns] = state[n_slots:, :]

    each_chunk(slot_chunk, chunks, direct)
    for copy in scalars:
        copy.wait()
    copies = []
    for j in range(rb):
        at = block_of(child_s[j], owner_s[0], direct)
        copy = pltpu.make_async_copy(slots_s.at[at], child_ssm.at[j], sems.at[2 + j])
        copy.start()
        copies.append(copy)

    def own_chunk(columns):
        at = [pl.ds(t * rb, rb) for t in range(steps)]
        delta = [delta_s[a, columns] for a in at]
        gain = [gain_s[a, columns] for a in at]
        sums = [skip_ref[:, columns] * act_ref[a, columns] for a in at]
        for n in range(n_state):
            rate = rate_ref[n : n + 1, columns]
            state = own_ref[n, :, columns]
            for t in range(steps):
                state = jnp.exp2(delta[t] * rate) * state + gain[t] * b_s[n, at[t], :]
                sums[t] = sums[t] + c_s[n, at[t], :] * state
        for t in range(steps):
            line_s[pl.ds(t, rb, stride=steps), :] = sums[t] * gate_ref[t, :, columns]
        dec_ref[:, :, columns] = line_s[...].reshape(rb, steps, LANES).astype(BF16)

    each_chunk(own_chunk, chunks, direct)
    for copy in copies:
        copy.wait()


def on_device(
    prompt_ssm,
    prompt_conv,
    prompt_of,
    step_in,
    conv_weight,
    conv_bias,
    x_weight,
    dt_weight,
    dt_bias,
    a_log,
    skip,
    send_rows,
    child_slot,
):
    owners = lax.axis_size("branch")
    tensors = lax.axis_size("tensor")
    assert owners & (owners - 1) == 0 and tensors & (tensors - 1) == 0
    assert prompt_ssm.shape[0] == 1 and send_rows.shape[2] == 1
    rb, steps, _, channels = step_in.shape
    taps = conv_weight.shape[0]
    width = x_weight.shape[1]
    n_state = a_log.shape[0]
    rows = steps * (rb + owners)
    short = taps - 1 + steps + 1
    depth = short + n_state
    direct = owners == DIRECT
    owner = pinned(lax.axis_index("branch").astype(jnp.int32).reshape(1))

    if direct:
        msg_shapes = [(1, d, channels) for d in (short, depth, short, short)]
    else:
        msg_shapes = [(owners, depth, channels)]
    msgs = call(
        functools.partial(pack_kernel, direct),
        [shaped(s, BF16) for s in msg_shapes],
        [hbm()] * 6,
        [vmem()] * len(msg_shapes),
        [
            pltpu.SMEM((1,), jnp.int32),
            pltpu.SMEM((owners,), jnp.int32),
            pltpu.SMEM((rb,), jnp.int32),
            pltpu.VMEM(step_in.shape, BF16),
            pltpu.VMEM(prompt_conv.shape, BF16),
            pltpu.VMEM(prompt_ssm.shape, F32),
            pltpu.SemaphoreType.DMA((5 + STEP_PARTS,)),
        ],
        nbytes=owners * depth * channels * 2,
    )(
        owner,
        pinned(send_rows.reshape(owners)),
        pinned(prompt_of),
        pinned(step_in),
        pinned(prompt_conv),
        pinned(prompt_ssm),
    )
    if direct:
        own = msgs[0]
        msgs = [own] + [
            lax.ppermute(m, "branch", list(enumerate(to))) for m, to in zip(msgs[1:], SENDS)
        ]
        after = own
    else:
        msgs = [lax.all_to_all(msgs[0], "branch", split_axis=0, concat_axis=0, tiled=True)]
        after = msgs[0]
    n_msgs = len(msgs)
    near = call(
        functools.partial(prepare_kernel, direct),
        [
            shaped((steps, rb, channels), F32),
            shaped((steps, rb, channels), F32),
            shaped((rb, owners), F32),
            shaped((rb, owners), F32),
            shaped((1, owners), F32),
            shaped((taps, channels), F32),
            shaped((1, channels), F32),
            shaped((width, channels), BF16),
            shaped((n_state, channels), F32),
            shaped((n_state // 2, 2 * owners, channels), F32),
            shaped((1, channels), F32),
            shaped((1, channels), F32),
        ],
        [hbm()] * 10 + [anywhere()],
        [vmem()] * 12,
        [
            pltpu.VMEM(step_in.shape, BF16),
            pltpu.SMEM((1,), jnp.int32),
            pltpu.SMEM((rb,), jnp.int32),
            pltpu.SMEM((rb,), jnp.int32),
            pltpu.VMEM((n_state, channels), F32),
            pltpu.SemaphoreType.DMA((8 + WEIGHT_PARTS + STEP_PARTS,)),
        ],
        flops=10 * steps * rb * channels,
        nbytes=12 * steps * rb * channels,
        trans=steps * rb * channels,
    )(
        owner,
        pinned(prompt_of),
        pinned(child_slot),
        pinned(step_in),
        pinned(conv_weight),
        pinned(conv_bias[None]),
        pinned(x_weight.T),
        pinned(a_log),
        pinned(dt_bias[None]),
        pinned(skip[None]),
        after,
    )
    base, gate, pick, child_pick, sender, taps_near, bias_near, weight_near = near[:8]
    rate, twin, dtb_near, skip_near = near[8:]
    states = []
    if direct:
        pair = call(
            functools.partial(pair_kernel, short),
            shaped((1, 3 * n_state, channels), BF16),
            [vmem()] * 2 + [anywhere()],
            vmem(),
            nbytes=12 * n_state * channels,
        )(prompt_ssm, msgs[1], pick)
        states = [prompt_ssm, swap(pair, "branch", 1)]
    act, part, brief = call(
        functools.partial(project_kernel, n_msgs),
        [
            shaped((rows, channels), F32),
            shaped((rows, width), F32),
            shaped((rows, width), BF16),
        ],
        [vmem()] * (6 + n_msgs),
        [vmem()] * 3,
        flops=2 * rows * channels * width,
        nbytes=channels * width * 2 + rows * (channels + width) * 4,
        trans=rows * channels,
    )(pick, sender, base, taps_near, bias_near, weight_near, *msgs)
    other = swap(brief, "tensor", 1)
    distance = 2
    while distance < tensors:
        part, brief = call(
            add_kernel,
            [shaped((rows, width), F32), shaped((rows, width), BF16)],
            [vmem()] * 2,
            [vmem()] * 2,
            flops=rows * width,
            nbytes=rows * width * 14,
        )(part, other)
        other = swap(brief, "tensor", 2 * distance - 1)
        distance *= 2

    child_conv = call(
        functools.partial(windows_kernel, n_msgs, steps),
        shaped((taps - 1, rb, channels), BF16),
        [vmem(), anywhere()] + [vmem()] * n_msgs,
        vmem(),
        flops=2 * owners * taps * rb * channels,
        nbytes=4 * taps * rb * channels,
    )(child_pick, part, *msgs)
    own_start, slot_start = call(
        functools.partial(start_kernel, n_msgs, direct, short),
        [
            shaped((n_state, rb, channels), F32),
            shaped((n_state // 2, 2 * owners, channels), F32),
        ],
        [vmem()] * 2 + [anywhere()] + [vmem()] * (n_msgs + len(states)),
        [vmem()] * 2,
        [pltpu.VMEM((owners, n_state, channels), F32)],
        flops=2 * owners * n_state * (rb + owners) * channels,
        nbytes=4 * n_state * (rb + owners) * channels,
    )(pick, sender, part, *msgs, *states)

    decoded, child_ssm = call(
        functools.partial(decode_kernel, direct),
        [
            shaped((rb, steps, channels), BF16),
            shaped((rb, n_state, channels), F32),
        ],
        [hbm()] * 2 + [vmem()] * 11,
        [vmem(), anywhere()],
        [
            pltpu.SMEM((1,), jnp.int32),
            pltpu.SMEM((rb,), jnp.int32),
            pltpu.VMEM((steps * rb, channels), F32),
            pltpu.VMEM((steps * rb, channels), F32),
            pltpu.VMEM((steps, 2 * owners, channels), F32),
            pltpu.VMEM((steps, 2 * owners, channels), F32),
            pltpu.VMEM((n_state, steps * rb, LANES), F32),
            pltpu.VMEM((n_state, steps * rb, LANES), F32),
            pltpu.VMEM((n_state // 2, steps, 2 * owners, LANES), F32),
            pltpu.VMEM((owners, n_state, channels), F32),
            pltpu.VMEM((steps * rb, LANES), F32),
            pltpu.SemaphoreType.DMA((2 + rb,)),
        ],
        flops=8 * rows * n_state * channels,
        nbytes=(rb + owners) * n_state * channels * 4,
        trans=rows * n_state * channels,
    )(
        owner,
        pinned(child_slot),
        act,
        gate,
        own_start,
        slot_start,
        rate,
        twin,
        dt_weight,
        dtb_near,
        skip_near,
        part,
        other,
    )
    return (decoded, child_ssm, jnp.transpose(child_conv, (1, 0, 2)))


def solution(mesh):
    placed = (
        P(("replica", "branch"), None, "tensor"),
        P(("replica", "branch"), None, "tensor"),
        P(("replica", "branch")),
        P(("replica", "branch"), None, None, "tensor"),
        P(None, "tensor"),
        P("tensor"),
        P("tensor", None),
        P(None, "tensor"),
        P("tensor"),
        P(None, "tensor"),
        P("tensor"),
        P(("replica", "branch"), None, None),
        P(("replica", "branch")),
    )
    return jax.shard_map(
        on_device,
        mesh=mesh,
        in_specs=placed,
        out_specs=(
            P(("replica", "branch"), None, "tensor"),
            P(("replica", "branch"), None, "tensor"),
            P(("replica", "branch"), None, "tensor"),
        ),
        check_vma=False,
    )
```

```python
import functools
import math

import jax
import jax.numpy as jnp
from jax import lax
from jax.experimental import pallas as pl
from jax.experimental.pallas import tpu as pltpu
from jax.sharding import PartitionSpec as P

F32 = jnp.float32
BF16 = jnp.bfloat16
LANES = 128
VMEM_LIMIT = 48 * 2**20
WEIGHT_PARTS = 6
STEP_PARTS = 4
DIRECT = 4
SENDS = ((2, 3, 1, 0), (3, 2, 0, 1), (1, 0, 3, 2))


def vmem():
    return pl.BlockSpec(memory_space=pltpu.VMEM)


def hbm():
    return pl.BlockSpec(memory_space=pltpu.HBM)


def anywhere():
    return pl.BlockSpec(memory_space=pl.ANY)


def pinned(array):
    return pltpu.with_memory_space_constraint(array, pltpu.HBM)


def shaped(shape, dtype):
    return jax.ShapeDtypeStruct(shape, dtype)


def call(kernel, outs, in_specs, out_specs, scratch=(), flops=0, nbytes=0, trans=0):
    return pl.pallas_call(
        kernel,
        out_shape=outs,
        in_specs=in_specs,
        out_specs=out_specs,
        scratch_shapes=list(scratch),
        compiler_params=pltpu.CompilerParams(vmem_limit_bytes=VMEM_LIMIT),
        cost_estimate=pl.CostEstimate(flops=flops, bytes_accessed=nbytes, transcendentals=trans),
    )


def swap(value, axis, distance):
    size = lax.axis_size(axis)
    return lax.ppermute(value, axis, [(i, i ^ distance) for i in range(size)])


def chosen(number, values):
    total = values[0]
    for i in range(1, len(values)):
        total = jnp.where(number == i, values[i], total)
    return total


def block_of(sender, owner, direct):
    if not direct:
        return sender
    table = [
        [0 if s == r else 1 + [to[s] for to in SENDS].index(r) for s in range(DIRECT)]
        for r in range(DIRECT)
    ]
    places = [chosen(owner, [row[s] for row in table]) for s in range(DIRECT)]
    return places[sender] if isinstance(sender, int) else chosen(sender, places)


def all_of(copies):
    for copy in copies:
        copy.start()
    for copy in copies:
        copy.wait()


def read_messages(refs):
    return [ref[i].astype(F32) for ref in refs for i in range(ref.shape[0])]


def in_parts(source, target, sems, first, count):
    rows = source.shape[0] // count
    at = [pl.ds(i * rows, rows) for i in range(count)]
    return [
        pltpu.make_async_copy(source.at[a], target.at[a], sems.at[first + i])
        for i, a in enumerate(at)
    ]


def scalar_onehot(senders_s, owner, shape, direct):
    row_of = lax.broadcasted_iota(jnp.int32, shape, 0)
    wanted = jnp.zeros(shape, jnp.int32)
    for b in range(shape[0]):
        wanted = jnp.where(row_of == b, senders_s[b], wanted)
    wanted = block_of(wanted, owner, direct)
    return (wanted == lax.broadcasted_iota(jnp.int32, shape, 1)).astype(F32)


def each_chunk(body, chunks, straight):
    if straight:
        for chunk in range(chunks):
            body(slice(chunk * LANES, (chunk + 1) * LANES))
        return

    def step(chunk, carry):
        body(pl.ds(pl.multiple_of(chunk * LANES, LANES), LANES))
        return carry

    lax.fori_loop(0, chunks, step, 0)


def pick_rows(pick, rows):
    total = pick[:, 0:1] * rows[0]
    for k in range(1, len(rows)):
        total = total + pick[:, k : k + 1] * rows[k]
    return total


def pack_kernel(direct, owner_hbm, rows_hbm, prompt_hbm, step_hbm, conv_hbm, ssm_hbm, *rest):
    outs, (owner_s, rows_s, prompt_s, step, conv, ssm, sems) = rest[:-7], rest[-7:]
    owners = rows_hbm.shape[0]
    channels = step_hbm.shape[3]
    copies = [
        pltpu.make_async_copy(owner_hbm, owner_s, sems.at[4]),
        pltpu.make_async_copy(rows_hbm, rows_s, sems.at[0]),
        pltpu.make_async_copy(prompt_hbm, prompt_s, sems.at[1]),
        pltpu.make_async_copy(conv_hbm, conv, sems.at[2]),
        pltpu.make_async_copy(ssm_hbm, ssm, sems.at[3]),
    ]
    all_of(copies + in_parts(step_hbm, step, sems, 5, STEP_PARTS))
    owner = owner_s[0]
    window = conv[0].astype(F32)

    def write(ref, target):
        row = jnp.maximum(rows_s[target], 0)
        xs = step[row, :, 0, :].astype(F32)
        number = prompt_s[row].astype(F32)
        pieces = [xs, window, jnp.full((1, channels), number, F32)]
        if ref.shape[0] > sum(p.shape[0] for p in pieces):
            pieces.append(ssm[0])
        ref[...] = jnp.concatenate(pieces, axis=0).astype(BF16)

    if direct:
        write(outs[0].at[0], owner)
        for ref, to in zip(outs[1:], SENDS):
            write(ref.at[0], chosen(owner, to))
    else:
        for target in range(owners):
            write(outs[0].at[target], target)


def pair_kernel(text, ssm_ref, came_ref, after_ref, pair_ref):
    del after_ref
    state = ssm_ref[0]
    head = state.astype(BF16).astype(F32)
    came = came_ref[0].astype(F32)[text:, :]
    pair_ref[0] = jnp.concatenate([head, state - head, came], axis=0).astype(BF16)


def silu(v):
    return v / (1.0 + jnp.exp(-v))


def prepare_kernel(
    direct,
    owner_hbm,
    prompt_hbm,
    child_hbm,
    step_hbm,
    cw_hbm,
    cb_hbm,
    xwt_hbm,
    alog_hbm,
    dtb_hbm,
    skip_hbm,
    after_ref,
    base_ref,
    gate_ref,
    pick_ref,
    child_ref,
    sender_ref,
    cw_ref,
    cb_ref,
    xwt_ref,
    rate_ref,
    twin_ref,
    dtb_ref,
    skip_ref,
    step_ref,
    owner_s,
    prompt_s,
    child_s,
    alog,
    sems,
):
    del after_ref
    small = [
        pltpu.make_async_copy(source, target, sems.at[i])
        for i, (source, target) in enumerate(
            (
                (cw_hbm, cw_ref),
                (cb_hbm, cb_ref),
                (owner_hbm, owner_s),
                (prompt_hbm, prompt_s),
                (child_hbm, child_s),
                (alog_hbm, alog),
                (dtb_hbm, dtb_ref),
                (skip_hbm, skip_ref),
            )
        )
    ]
    inputs = in_parts(step_hbm, step_ref, sems, len(small), STEP_PARTS)
    large = in_parts(xwt_hbm, xwt_ref, sems, len(small) + STEP_PARTS, WEIGHT_PARTS)
    for copy in inputs + small + large:
        copy.start()
    for copy in inputs:
        copy.wait()
    steps = step_ref.shape[1]
    taps = cw_hbm.shape[0]
    xs = [step_ref[:, t, 0, :].astype(F32) for t in range(steps)]
    for t in range(steps):
        gate_ref[t] = silu(step_ref[:, t, 1, :].astype(F32))
    for copy in small:
        copy.wait()
    for t in range(steps):
        total = cw_ref[taps - 1 : taps, :] * xs[t] + cb_ref[...]
        for k in range(max(0, taps - 1 - t), taps - 1):
            total = total + cw_ref[k : k + 1, :] * xs[t + k - taps + 1]
        base_ref[t] = total
    pick_ref[...] = scalar_onehot(prompt_s, owner_s[0], pick_ref.shape, direct)
    child_ref[...] = scalar_onehot(child_s, owner_s[0], child_ref.shape, direct)
    column = lax.broadcasted_iota(jnp.int32, sender_ref.shape, 1)
    sender = column
    for sent in range(sender_ref.shape[1] if direct else 0):
        sender = jnp.where(column == block_of(sent, owner_s[0], direct), sent, sender)
    sender_ref[...] = sender.astype(F32)
    rate = jnp.exp(alog[...]) * (-math.log2(math.e))
    rate_ref[...] = rate
    half = (twin_ref.shape[1] // 2, rate.shape[1])
    for m in range(rate.shape[0] // 2):
        two = [jnp.broadcast_to(rate[n : n + 1, :], half) for n in (2 * m, 2 * m + 1)]
        twin_ref[m] = jnp.concatenate(two, axis=0)
    for copy in large:
        copy.wait()


def slot_onehot(numbers, sender_ref):
    owners = sender_ref.shape[1]
    return (numbers[:, :owners] == sender_ref[...]).astype(F32)


def project_kernel(n_msgs, pick_ref, sender_ref, base_ref, cw_ref, cb_ref, xwt_ref, *rest):
    msgs, (act_ref, part_ref, short_ref) = rest[:n_msgs], rest[n_msgs:]
    taps = cw_ref.shape[0]
    steps, rb, _ = base_ref.shape
    past = taps - 1
    held = read_messages(msgs)
    owners = len(held)
    windows = [[h[steps + k : steps + k + 1, :] for h in held] for k in range(past)]
    own = pick_ref[...]
    own_windows = [pick_rows(own, w) for w in windows]
    for t in range(steps):
        conv = base_ref[t]
        for k in range(past - t):
            conv = conv + cw_ref[k : k + 1, :] * own_windows[t + k]
        act_ref[t * rb : (t + 1) * rb, :] = silu(conv)

    def line_of(row):
        return jnp.concatenate([h[row : row + 1, :] for h in held], axis=0)

    slot = slot_onehot(line_of(past + steps), sender_ref)
    line = [pick_rows(slot, w) for w in windows]
    line += [line_of(t) for t in range(steps)]
    row = steps * rb
    for t in range(steps):
        conv = cw_ref[past:taps, :] * line[t + past] + cb_ref[...]
        for k in range(past):
            conv = conv + cw_ref[k : k + 1, :] * line[t + k]
        act_ref[row : row + owners, :] = silu(conv)
        row += owners
    part = lax.dot_general(
        act_ref[...].astype(BF16),
        xwt_ref[...],
        (((1,), (1,)), ((), ())),
        preferred_element_type=F32,
    )
    part_ref[...] = part
    short_ref[...] = part.astype(BF16)


def add_kernel(a_ref, b_ref, sum_ref, short_ref):
    total = a_ref[...] + b_ref[...].astype(F32)
    sum_ref[...] = total
    short_ref[...] = total.astype(BF16)


def windows_kernel(n_msgs, steps, child_ref, after_ref, *rest):
    del after_ref
    msgs, (conv_ref,) = rest[:n_msgs], rest[n_msgs:]
    held = read_messages(msgs)
    past = conv_ref.shape[0]
    for k in range(past):
        at = steps - past + k
        rows = [h[at : at + 1, :] for h in held]
        conv_ref[k] = pick_rows(child_ref[...], rows).astype(BF16)


def start_kernel(n_msgs, direct, text, pick_ref, sender_ref, after_ref, *rest):
    del after_ref
    msgs, rest = rest[:n_msgs], rest[n_msgs:]
    apart, (own_ref, slot_ref, state_s) = rest[:-3], rest[-3:]
    n_state = own_ref.shape[0]
    held = read_messages(msgs)
    owners = len(held)
    numbers = jnp.concatenate([h[text - 1 : text, :] for h in held], axis=0)
    states = [h[text:, :] for h in held]
    if direct:
        ssm_ref, pair_ref = apart
        head, low, came = [
            pair_ref[0].astype(F32)[i * n_state : (i + 1) * n_state, :] for i in range(3)
        ]
        states[0], states[2], states[3] = ssm_ref[0], came, head + low
    for k, state in enumerate(states):
        state_s[k] = state
    own = pick_ref[...]
    slot = slot_onehot(numbers, sender_ref)

    def two(m, carry):
        picked = []
        for n in (2 * m, 2 * m + 1):
            rows = [state_s[k, pl.ds(n, 1), :] for k in range(owners)]
            own_ref[n] = pick_rows(own, rows)
            picked.append(pick_rows(slot, rows))
        slot_ref[m] = jnp.concatenate(picked, axis=0)
        return carry

    lax.fori_loop(0, n_state // 2, two, 0, unroll=owners <= DIRECT)


def decode_kernel(
    direct,
    owner_hbm,
    child_hbm,
    act_ref,
    gate_ref,
    own_ref,
    slot_ref,
    rate_ref,
    twin_ref,
    dtw_ref,
    dtb_ref,
    skip_ref,
    part_ref,
    other_ref,
    dec_ref,
    child_ssm,
    owner_s,
    child_s,
    delta_s,
    gain_s,
    slot_delta_s,
    slot_gain_s,
    b_s,
    c_s,
    twin_b_s,
    slots_s,
    line_s,
    sems,
):
    scalars = [
        pltpu.make_async_copy(owner_hbm, owner_s, sems.at[0]),
        pltpu.make_async_copy(child_hbm, child_s, sems.at[1]),
    ]
    for copy in scalars:
        copy.start()
    rb, steps, channels = dec_ref.shape
    rank = dtw_ref.shape[0]
    n_state = rate_ref.shape[0]
    n_slots = slots_s.shape[0]
    own_rows = steps * rb
    chunks = channels // LANES

    def sums_of(rows):
        proj = part_ref[rows, :] + other_ref[rows, :].astype(F32)
        delta_in = proj[:, :rank].astype(BF16)
        delta = jnp.dot(delta_in, dtw_ref[...], preferred_element_type=F32) + dtb_ref[...]
        delta = jnp.maximum(delta, 0.0) + jnp.log(1.0 + jnp.exp(-jnp.abs(delta)))
        return proj, delta, delta * act_ref[rows, :]

    def column(at, n, rows):
        return jnp.broadcast_to(at[:, n : n + 1], (rows, LANES))

    proj, delta, gain = sums_of(slice(own_rows, own_rows + steps * n_slots))
    for t in range(steps):
        at = slice(t * n_slots, (t + 1) * n_slots)
        slot_delta_s[t] = jnp.concatenate([delta[at, :]] * 2, axis=0)
        slot_gain_s[t] = jnp.concatenate([gain[at, :]] * 2, axis=0)
        twice = jnp.concatenate([proj[at, rank:]] * 2, axis=0)
        upper = lax.broadcasted_iota(jnp.int32, (2 * n_slots, LANES), 0) < n_slots
        for m in range(n_state // 2):
            twin_b_s[m, t] = jnp.where(
                upper, column(twice, 2 * m, 2 * n_slots), column(twice, 2 * m + 1, 2 * n_slots)
            )

    def slot_chunk(columns):
        delta = [slot_delta_s[t, :, columns] for t in range(steps)]
        gain = [slot_gain_s[t, :, columns] for t in range(steps)]
        for m in range(n_state // 2):
            rate = twin_ref[m, :, columns]
            state = slot_ref[m, :, columns]
            for t in range(steps):
                state = jnp.exp2(delta[t] * rate) * state + gain[t] * twin_b_s[m, t]
            slots_s[:, 2 * m, columns] = state[:n_slots, :]
            slots_s[:, 2 * m + 1, columns] = state[n_slots:, :]

    each_chunk(slot_chunk, chunks, direct)
    for copy in scalars:
        copy.wait()
    copies = []
    for j in range(rb):
        at = block_of(child_s[j], owner_s[0], direct)
        copy = pltpu.make_async_copy(slots_s.at[at], child_ssm.at[j], sems.at[2 + j])
        copy.start()
        copies.append(copy)

    proj, delta, gain = sums_of(slice(0, own_rows))
    delta_s[...] = delta
    gain_s[...] = gain
    for n in range(n_state):
        b_s[n] = column(proj[:, rank:], n, own_rows)
        c_s[n] = column(proj[:, rank:], n_state + n, own_rows)

    def own_chunk(columns):
        at = [pl.ds(t * rb, rb) for t in range(steps)]
        delta = [delta_s[a, columns] for a in at]
        gain = [gain_s[a, columns] for a in at]
        sums = [skip_ref[:, columns] * act_ref[a, columns] for a in at]
        for n in range(n_state):
            rate = rate_ref[n : n + 1, columns]
            state = own_ref[n, :, columns]
            for t in range(steps):
                state = jnp.exp2(delta[t] * rate) * state + gain[t] * b_s[n, at[t], :]
                sums[t] = sums[t] + c_s[n, at[t], :] * state
        for t in range(steps):
            line_s[pl.ds(t, rb, stride=steps), :] = sums[t] * gate_ref[t, :, columns]
        dec_ref[:, :, columns] = line_s[...].reshape(rb, steps, LANES).astype(BF16)

    each_chunk(own_chunk, chunks, False)
    for copy in copies:
        copy.wait()


def on_device(
    prompt_ssm,
    prompt_conv,
    prompt_of,
    step_in,
    conv_weight,
    conv_bias,
    x_weight,
    dt_weight,
    dt_bias,
    a_log,
    skip,
    send_rows,
    child_slot,
):
    owners = lax.axis_size("branch")
    tensors = lax.axis_size("tensor")
    assert owners & (owners - 1) == 0 and tensors & (tensors - 1) == 0
    assert prompt_ssm.shape[0] == 1 and send_rows.shape[2] == 1
    rb, steps, _, channels = step_in.shape
    taps = conv_weight.shape[0]
    width = x_weight.shape[1]
    n_state = a_log.shape[0]
    rows = steps * (rb + owners)
    short = taps - 1 + steps + 1
    depth = short + n_state
    direct = owners == DIRECT
    owner = pinned(lax.axis_index("branch").astype(jnp.int32).reshape(1))

    if direct:
        msg_shapes = [(1, d, channels) for d in (short, depth, short, short)]
    else:
        msg_shapes = [(owners, depth, channels)]
    msgs = call(
        functools.partial(pack_kernel, direct),
        [shaped(s, BF16) for s in msg_shapes],
        [hbm()] * 6,
        [vmem()] * len(msg_shapes),
        [
            pltpu.SMEM((1,), jnp.int32),
            pltpu.SMEM((owners,), jnp.int32),
            pltpu.SMEM((rb,), jnp.int32),
            pltpu.VMEM(step_in.shape, BF16),
            pltpu.VMEM(prompt_conv.shape, BF16),
            pltpu.VMEM(prompt_ssm.shape, F32),
            pltpu.SemaphoreType.DMA((5 + STEP_PARTS,)),
        ],
        nbytes=owners * depth * channels * 2,
    )(
        owner,
        pinned(send_rows.reshape(owners)),
        pinned(prompt_of),
        pinned(step_in),
        pinned(prompt_conv),
        pinned(prompt_ssm),
    )
    if direct:
        own = msgs[0]
        msgs = [own] + [
            lax.ppermute(m, "branch", list(enumerate(to))) for m, to in zip(msgs[1:], SENDS)
        ]
        after = own
    else:
        msgs = [lax.all_to_all(msgs[0], "branch", split_axis=0, concat_axis=0, tiled=True)]
        after = msgs[0]
    n_msgs = len(msgs)
    near = call(
        functools.partial(prepare_kernel, direct),
        [
            shaped((steps, rb, channels), F32),
            shaped((steps, rb, channels), F32),
            shaped((rb, owners), F32),
            shaped((rb, owners), F32),
            shaped((1, owners), F32),
            shaped((taps, channels), F32),
            shaped((1, channels), F32),
            shaped((width, channels), BF16),
            shaped((n_state, channels), F32),
            shaped((n_state // 2, 2 * owners, channels), F32),
            shaped((1, channels), F32),
            shaped((1, channels), F32),
        ],
        [hbm()] * 10 + [anywhere()],
        [vmem()] * 12,
        [
            pltpu.VMEM(step_in.shape, BF16),
            pltpu.SMEM((1,), jnp.int32),
            pltpu.SMEM((rb,), jnp.int32),
            pltpu.SMEM((rb,), jnp.int32),
            pltpu.VMEM((n_state, channels), F32),
            pltpu.SemaphoreType.DMA((8 + WEIGHT_PARTS + STEP_PARTS,)),
        ],
        flops=10 * steps * rb * channels,
        nbytes=12 * steps * rb * channels,
        trans=steps * rb * channels,
    )(
        owner,
        pinned(prompt_of),
        pinned(child_slot),
        pinned(step_in),
        pinned(conv_weight),
        pinned(conv_bias[None]),
        pinned(x_weight.T),
        pinned(a_log),
        pinned(dt_bias[None]),
        pinned(skip[None]),
        after,
    )
    base, gate, pick, child_pick, sender, taps_near, bias_near, weight_near = near[:8]
    rate, twin, dtb_near, skip_near = near[8:]
    states = []
    if direct:
        pair = call(
            functools.partial(pair_kernel, short),
            shaped((1, 3 * n_state, channels), BF16),
            [vmem()] * 2 + [anywhere()],
            vmem(),
            nbytes=12 * n_state * channels,
        )(prompt_ssm, msgs[1], pick)
        states = [prompt_ssm, swap(pair, "branch", 1)]
    act, part, brief = call(
        functools.partial(project_kernel, n_msgs),
        [
            shaped((rows, channels), F32),
            shaped((rows, width), F32),
            shaped((rows, width), BF16),
        ],
        [vmem()] * (6 + n_msgs),
        [vmem()] * 3,
        flops=2 * rows * channels * width,
        nbytes=channels * width * 2 + rows * (channels + width) * 4,
        trans=rows * channels,
    )(pick, sender, base, taps_near, bias_near, weight_near, *msgs)
    other = swap(brief, "tensor", 1)
    distance = 2
    while distance < tensors:
        part, brief = call(
            add_kernel,
            [shaped((rows, width), F32), shaped((rows, width), BF16)],
            [vmem()] * 2,
            [vmem()] * 2,
            flops=rows * width,
            nbytes=rows * width * 14,
        )(part, other)
        other = swap(brief, "tensor", 2 * distance - 1)
        distance *= 2

    child_conv = call(
        functools.partial(windows_kernel, n_msgs, steps),
        shaped((taps - 1, rb, channels), BF16),
        [vmem(), anywhere()] + [vmem()] * n_msgs,
        vmem(),
        flops=2 * owners * taps * rb * channels,
        nbytes=4 * taps * rb * channels,
    )(child_pick, part, *msgs)
    own_start, slot_start = call(
        functools.partial(start_kernel, n_msgs, direct, short),
        [
            shaped((n_state, rb, channels), F32),
            shaped((n_state // 2, 2 * owners, channels), F32),
        ],
        [vmem()] * 2 + [anywhere()] + [vmem()] * (n_msgs + len(states)),
        [vmem()] * 2,
        [pltpu.VMEM((owners, n_state, channels), F32)],
        flops=2 * owners * n_state * (rb + owners) * channels,
        nbytes=4 * n_state * (rb + owners) * channels,
    )(pick, sender, part, *msgs, *states)

    decoded, child_ssm = call(
        functools.partial(decode_kernel, direct),
        [
            shaped((rb, steps, channels), BF16),
            shaped((rb, n_state, channels), F32),
        ],
        [hbm()] * 2 + [vmem()] * 11,
        [vmem(), anywhere()],
        [
            pltpu.SMEM((1,), jnp.int32),
            pltpu.SMEM((rb,), jnp.int32),
            pltpu.VMEM((steps * rb, channels), F32),
            pltpu.VMEM((steps * rb, channels), F32),
            pltpu.VMEM((steps, 2 * owners, channels), F32),
            pltpu.VMEM((steps, 2 * owners, channels), F32),
            pltpu.VMEM((n_state, steps * rb, LANES), F32),
            pltpu.VMEM((n_state, steps * rb, LANES), F32),
            pltpu.VMEM((n_state // 2, steps, 2 * owners, LANES), F32),
            pltpu.VMEM((owners, n_state, channels), F32),
            pltpu.VMEM((steps * rb, LANES), F32),
            pltpu.SemaphoreType.DMA((2 + rb,)),
        ],
        flops=8 * rows * n_state * channels,
        nbytes=(rb + owners) * n_state * channels * 4,
        trans=rows * n_state * channels,
    )(
        owner,
        pinned(child_slot),
        act,
        gate,
        own_start,
        slot_start,
        rate,
        twin,
        dt_weight,
        dtb_near,
        skip_near,
        part,
        other,
    )
    return (decoded, child_ssm, jnp.transpose(child_conv, (1, 0, 2)))


def solution(mesh):
    placed = (
        P(("replica", "branch"), None, "tensor"),
        P(("replica", "branch"), None, "tensor"),
        P(("replica", "branch")),
        P(("replica", "branch"), None, None, "tensor"),
        P(None, "tensor"),
        P("tensor"),
        P("tensor", None),
        P(None, "tensor"),
        P("tensor"),
        P(None, "tensor"),
        P("tensor"),
        P(("replica", "branch"), None, None),
        P(("replica", "branch")),
    )
    return jax.shard_map(
        on_device,
        mesh=mesh,
        in_specs=placed,
        out_specs=(
            P(("replica", "branch"), None, "tensor"),
            P(("replica", "branch"), None, "tensor"),
            P(("replica", "branch"), None, "tensor"),
        ),
        check_vma=False,
    )
```

```python
import functools
import math

import jax
import jax.numpy as jnp
from jax import lax
from jax.experimental import pallas as pl
from jax.experimental.pallas import tpu as pltpu
from jax.sharding import PartitionSpec as P

F32 = jnp.float32
BF16 = jnp.bfloat16
LANES = 128
ROWS = 8
WIDE = 2
VMEM_LIMIT = 48 * 2**20
WEIGHT_PARTS = 6
STEP_PARTS = 4
DIRECT = 4
SENDS = ((2, 3, 1, 0), (3, 2, 0, 1), (1, 0, 3, 2))


def vmem():
    return pl.BlockSpec(memory_space=pltpu.VMEM)


def hbm():
    return pl.BlockSpec(memory_space=pltpu.HBM)


def anywhere():
    return pl.BlockSpec(memory_space=pl.ANY)


def pinned(array):
    return pltpu.with_memory_space_constraint(array, pltpu.HBM)


def shaped(shape, dtype):
    return jax.ShapeDtypeStruct(shape, dtype)


def call(kernel, outs, in_specs, out_specs, scratch=(), flops=0, nbytes=0, trans=0):
    return pl.pallas_call(
        kernel,
        out_shape=outs,
        in_specs=in_specs,
        out_specs=out_specs,
        scratch_shapes=list(scratch),
        compiler_params=pltpu.CompilerParams(vmem_limit_bytes=VMEM_LIMIT),
        cost_estimate=pl.CostEstimate(flops=flops, bytes_accessed=nbytes, transcendentals=trans),
    )


def swap(value, axis, distance):
    size = lax.axis_size(axis)
    return lax.ppermute(value, axis, [(i, i ^ distance) for i in range(size)])


def chosen(number, values):
    total = values[0]
    for i in range(1, len(values)):
        total = jnp.where(number == i, values[i], total)
    return total


def block_of(sender, owner, direct):
    if not direct:
        return sender
    table = [
        [0 if s == r else 1 + [to[s] for to in SENDS].index(r) for s in range(DIRECT)]
        for r in range(DIRECT)
    ]
    places = [chosen(owner, [row[s] for row in table]) for s in range(DIRECT)]
    return places[sender] if isinstance(sender, int) else chosen(sender, places)


def all_of(copies):
    for copy in copies:
        copy.start()
    for copy in copies:
        copy.wait()


def read_messages(refs):
    return [ref[i].astype(F32) for ref in refs for i in range(ref.shape[0])]


def in_parts(source, target, sems, first, count):
    rows = source.shape[0] // count
    at = [pl.ds(i * rows, rows) for i in range(count)]
    return [
        pltpu.make_async_copy(source.at[a], target.at[a], sems.at[first + i])
        for i, a in enumerate(at)
    ]


def scalar_onehot(senders_s, owner, shape, direct):
    row_of = lax.broadcasted_iota(jnp.int32, shape, 0)
    wanted = jnp.zeros(shape, jnp.int32)
    for b in range(shape[0]):
        wanted = jnp.where(row_of == b, senders_s[b], wanted)
    wanted = block_of(wanted, owner, direct)
    return (wanted == lax.broadcasted_iota(jnp.int32, shape, 1)).astype(F32)


def pick_rows(pick, rows):
    total = pick[:, 0:1] * rows[0]
    for k in range(1, len(rows)):
        total = total + pick[:, k : k + 1] * rows[k]
    return total


def pack_kernel(direct, owner_hbm, rows_hbm, prompt_hbm, step_hbm, conv_hbm, ssm_hbm, *rest):
    outs, (owner_s, rows_s, prompt_s, step, conv, ssm, sems) = rest[:-7], rest[-7:]
    owners = rows_hbm.shape[0]
    channels = step_hbm.shape[3]
    copies = [
        pltpu.make_async_copy(owner_hbm, owner_s, sems.at[4]),
        pltpu.make_async_copy(rows_hbm, rows_s, sems.at[0]),
        pltpu.make_async_copy(prompt_hbm, prompt_s, sems.at[1]),
        pltpu.make_async_copy(conv_hbm, conv, sems.at[2]),
        pltpu.make_async_copy(ssm_hbm, ssm, sems.at[3]),
    ]
    all_of(copies + in_parts(step_hbm, step, sems, 5, STEP_PARTS))
    owner = owner_s[0]
    window = conv[0].astype(F32)

    def write(ref, target):
        row = jnp.maximum(rows_s[target], 0)
        xs = step[row, :, 0, :].astype(F32)
        number = prompt_s[row].astype(F32)
        pieces = [xs, window, jnp.full((1, channels), number, F32)]
        if ref.shape[0] > sum(p.shape[0] for p in pieces):
            pieces.append(ssm[0])
        ref[...] = jnp.concatenate(pieces, axis=0).astype(BF16)

    if direct:
        write(outs[0].at[0], owner)
        for ref, to in zip(outs[1:], SENDS):
            write(ref.at[0], chosen(owner, to))
    else:
        for target in range(owners):
            write(outs[0].at[target], target)


def pair_kernel(text, ssm_ref, came_ref, after_ref, pair_ref):
    del after_ref
    state = ssm_ref[0]
    head = state.astype(BF16).astype(F32)
    came = came_ref[0].astype(F32)[text:, :]
    pair_ref[0] = jnp.concatenate([head, state - head, came], axis=0).astype(BF16)


def silu(v):
    return v / (1.0 + jnp.exp(-v))


def prepare_kernel(
    direct,
    owner_hbm,
    prompt_hbm,
    child_hbm,
    step_hbm,
    cw_hbm,
    cb_hbm,
    xwt_hbm,
    alog_hbm,
    dtb_hbm,
    skip_hbm,
    after_ref,
    base_ref,
    gate_ref,
    pick_ref,
    child_ref,
    sender_ref,
    cw_ref,
    cb_ref,
    xwt_ref,
    rate_ref,
    twin_ref,
    dtb_ref,
    skip_ref,
    step_ref,
    owner_s,
    prompt_s,
    child_s,
    alog,
    sems,
):
    del after_ref
    small = [
        pltpu.make_async_copy(source, target, sems.at[i])
        for i, (source, target) in enumerate(
            (
                (cw_hbm, cw_ref),
                (cb_hbm, cb_ref),
                (owner_hbm, owner_s),
                (prompt_hbm, prompt_s),
                (child_hbm, child_s),
                (alog_hbm, alog),
                (dtb_hbm, dtb_ref),
                (skip_hbm, skip_ref),
            )
        )
    ]
    inputs = in_parts(step_hbm, step_ref, sems, len(small), STEP_PARTS)
    large = in_parts(xwt_hbm, xwt_ref, sems, len(small) + STEP_PARTS, WEIGHT_PARTS)
    for copy in inputs + small + large:
        copy.start()
    for copy in inputs:
        copy.wait()
    steps = step_ref.shape[1]
    taps = cw_hbm.shape[0]
    xs = [step_ref[:, t, 0, :].astype(F32) for t in range(steps)]
    for t in range(steps):
        gate_ref[t] = silu(step_ref[:, t, 1, :].astype(F32))
    for copy in small:
        copy.wait()
    for t in range(steps):
        total = cw_ref[taps - 1 : taps, :] * xs[t] + cb_ref[...]
        for k in range(max(0, taps - 1 - t), taps - 1):
            total = total + cw_ref[k : k + 1, :] * xs[t + k - taps + 1]
        base_ref[t] = total
    pick_ref[...] = scalar_onehot(prompt_s, owner_s[0], pick_ref.shape, direct)
    child_ref[...] = scalar_onehot(child_s, owner_s[0], child_ref.shape, direct)
    column = lax.broadcasted_iota(jnp.int32, sender_ref.shape, 1)
    sender = column
    for sent in range(sender_ref.shape[1] if direct else 0):
        sender = jnp.where(column == block_of(sent, owner_s[0], direct), sent, sender)
    sender_ref[...] = sender.astype(F32)
    rate = jnp.exp(alog[...]) * (-math.log2(math.e))
    rate_ref[...] = rate
    half = (twin_ref.shape[1] // 2, rate.shape[1])
    for m in range(rate.shape[0] // 2):
        two = [jnp.broadcast_to(rate[n : n + 1, :], half) for n in (2 * m, 2 * m + 1)]
        twin_ref[m] = jnp.concatenate(two, axis=0)
    for copy in large:
        copy.wait()


def slot_onehot(numbers, sender_ref):
    owners = sender_ref.shape[1]
    return (numbers[:, :owners] == sender_ref[...]).astype(F32)


def project_kernel(n_msgs, pick_ref, sender_ref, base_ref, cw_ref, cb_ref, xwt_ref, *rest):
    msgs, (act_ref, part_ref, short_ref) = rest[:n_msgs], rest[n_msgs:]
    taps = cw_ref.shape[0]
    steps, rb, _ = base_ref.shape
    past = taps - 1
    held = read_messages(msgs)
    owners = len(held)
    windows = [[h[steps + k : steps + k + 1, :] for h in held] for k in range(past)]
    own = pick_ref[...]
    own_windows = [pick_rows(own, w) for w in windows]
    for t in range(steps):
        conv = base_ref[t]
        for k in range(past - t):
            conv = conv + cw_ref[k : k + 1, :] * own_windows[t + k]
        act_ref[t * rb : (t + 1) * rb, :] = silu(conv)

    def line_of(row):
        return jnp.concatenate([h[row : row + 1, :] for h in held], axis=0)

    slot = slot_onehot(line_of(past + steps), sender_ref)
    line = [pick_rows(slot, w) for w in windows]
    line += [line_of(t) for t in range(steps)]
    row = steps * rb
    for t in range(steps):
        conv = cw_ref[past:taps, :] * line[t + past] + cb_ref[...]
        for k in range(past):
            conv = conv + cw_ref[k : k + 1, :] * line[t + k]
        act_ref[row : row + owners, :] = silu(conv)
        row += owners
    part = lax.dot_general(
        act_ref[...].astype(BF16),
        xwt_ref[...],
        (((1,), (1,)), ((), ())),
        preferred_element_type=F32,
    )
    part_ref[...] = part
    short_ref[...] = part.astype(BF16)


def add_kernel(a_ref, b_ref, sum_ref, short_ref):
    total = a_ref[...] + b_ref[...].astype(F32)
    sum_ref[...] = total
    short_ref[...] = total.astype(BF16)


def windows_kernel(n_msgs, steps, child_ref, after_ref, *rest):
    del after_ref
    msgs, (conv_ref,) = rest[:n_msgs], rest[n_msgs:]
    held = read_messages(msgs)
    past = conv_ref.shape[0]
    for k in range(past):
        at = steps - past + k
        rows = [h[at : at + 1, :] for h in held]
        conv_ref[k] = pick_rows(child_ref[...], rows).astype(BF16)


def start_kernel(n_msgs, direct, text, pick_ref, sender_ref, after_ref, *rest):
    del after_ref
    msgs, rest = rest[:n_msgs], rest[n_msgs:]
    apart, (own_ref, slot_ref, state_s) = rest[:-3], rest[-3:]
    n_state = own_ref.shape[0]
    held = read_messages(msgs)
    owners = len(held)
    numbers = jnp.concatenate([h[text - 1 : text, :] for h in held], axis=0)
    states = [h[text:, :] for h in held]
    if direct:
        ssm_ref, pair_ref = apart
        head, low, came = [
            pair_ref[0].astype(F32)[i * n_state : (i + 1) * n_state, :] for i in range(3)
        ]
        states[0], states[2], states[3] = ssm_ref[0], came, head + low
    for k, state in enumerate(states):
        state_s[k] = state
    own = pick_ref[...]
    slot = slot_onehot(numbers, sender_ref)

    def two(m, carry):
        picked = []
        for n in (2 * m, 2 * m + 1):
            rows = [state_s[k, pl.ds(n, 1), :] for k in range(owners)]
            own_ref[n] = pick_rows(own, rows)
            picked.append(pick_rows(slot, rows))
        slot_ref[m] = jnp.concatenate(picked, axis=0)
        return carry

    lax.fori_loop(0, n_state // 2, two, 0, unroll=owners <= DIRECT)


def decode_kernel(
    direct,
    owner_hbm,
    child_hbm,
    act_ref,
    gate_ref,
    own_ref,
    slot_ref,
    rate_ref,
    twin_ref,
    dtw_ref,
    dtb_ref,
    skip_ref,
    part_ref,
    other_ref,
    dec_ref,
    child_ssm,
    owner_s,
    child_s,
    delta_s,
    gain_s,
    slot_delta_s,
    slot_gain_s,
    b_s,
    c_s,
    twin_b_s,
    slots_s,
    line_s,
    sems,
):
    scalars = [
        pltpu.make_async_copy(owner_hbm, owner_s, sems.at[0]),
        pltpu.make_async_copy(child_hbm, child_s, sems.at[1]),
    ]
    for copy in scalars:
        copy.start()
    rb, steps, channels = dec_ref.shape
    rank = dtw_ref.shape[0]
    n_state = rate_ref.shape[0]
    n_slots = slots_s.shape[0]
    own_rows = steps * rb
    chunks = channels // (WIDE * LANES)

    proj = part_ref[...] + other_ref[...].astype(F32)
    delta_in = proj[:, :rank].astype(BF16)
    delta = jnp.dot(delta_in, dtw_ref[...], preferred_element_type=F32) + dtb_ref[...]
    delta = jnp.maximum(delta, 0.0) + jnp.log(1.0 + jnp.exp(-jnp.abs(delta)))
    gain = delta * act_ref[...]
    delta_s[...] = delta[:own_rows, :]
    gain_s[...] = gain[:own_rows, :]

    def column(at, n, rows):
        return jnp.broadcast_to(at[:, n : n + 1], (rows, LANES))

    for t in range(steps):
        at = slice(own_rows + t * n_slots, own_rows + (t + 1) * n_slots)
        slot_delta_s[t] = jnp.concatenate([delta[at, :]] * 2, axis=0)
        slot_gain_s[t] = jnp.concatenate([gain[at, :]] * 2, axis=0)
        twice = jnp.concatenate([proj[at, rank:]] * 2, axis=0)
        upper = lax.broadcasted_iota(jnp.int32, (2 * n_slots, LANES), 0) < n_slots
        for m in range(n_state // 2):
            twin_b_s[m, t] = jnp.where(
                upper, column(twice, 2 * m, 2 * n_slots), column(twice, 2 * m + 1, 2 * n_slots)
            )
    for n in range(n_state):
        b_s[n] = column(proj[:own_rows, rank:], n, own_rows)
        c_s[n] = column(proj[:own_rows, rank:], n_state + n, own_rows)

    def wide(part):
        return jnp.concatenate([part] * WIDE, axis=1)

    def slot_chunk(chunk, carry):
        columns = pl.ds(pl.multiple_of(chunk * WIDE * LANES, WIDE * LANES), WIDE * LANES)
        delta = [slot_delta_s[t, :, columns] for t in range(steps)]
        gain = [slot_gain_s[t, :, columns] for t in range(steps)]
        for m in range(n_state // 2):
            rate = twin_ref[m, :, columns]
            state = slot_ref[m, :, columns]
            for t in range(steps):
                state = jnp.exp2(delta[t] * rate) * state + gain[t] * wide(twin_b_s[m, t])
            slots_s[:, 2 * m, columns] = state[:n_slots, :]
            slots_s[:, 2 * m + 1, columns] = state[n_slots:, :]
        return carry

    lax.fori_loop(0, chunks, slot_chunk, 0)
    for copy in scalars:
        copy.wait()
    copies = []
    for j in range(rb):
        at = block_of(child_s[j], owner_s[0], direct)
        copy = pltpu.make_async_copy(slots_s.at[at], child_ssm.at[j], sems.at[2 + j])
        copy.start()
        copies.append(copy)

    def own_chunk(chunk, carry):
        columns = pl.ds(pl.multiple_of(chunk * WIDE * LANES, WIDE * LANES), WIDE * LANES)
        for first in range(0, rb, ROWS):
            at = [pl.ds(t * rb + first, ROWS) for t in range(steps)]
            delta = [delta_s[a, columns] for a in at]
            gain = [gain_s[a, columns] for a in at]
            sums = [skip_ref[:, columns] * act_ref[a, columns] for a in at]
            for n in range(n_state):
                rate = rate_ref[n : n + 1, columns]
                state = own_ref[n, pl.ds(first, ROWS), columns]
                for t in range(steps):
                    state = jnp.exp2(delta[t] * rate) * state + gain[t] * wide(b_s[n, at[t], :])
                    sums[t] = sums[t] + wide(c_s[n, at[t], :]) * state
            for t in range(steps):
                out = sums[t] * gate_ref[t, pl.ds(first, ROWS), columns]
                for w in range(WIDE):
                    line_s[w, pl.ds(first * steps + t, ROWS, stride=steps), :] = out[
                        :, w * LANES : (w + 1) * LANES
                    ]
        for w in range(WIDE):
            some = pl.ds(pl.multiple_of((chunk * WIDE + w) * LANES, LANES), LANES)
            dec_ref[:, :, some] = line_s[w].reshape(rb, steps, LANES).astype(BF16)
        return carry

    lax.fori_loop(0, chunks, own_chunk, 0)
    for copy in copies:
        copy.wait()


def on_device(
    prompt_ssm,
    prompt_conv,
    prompt_of,
    step_in,
    conv_weight,
    conv_bias,
    x_weight,
    dt_weight,
    dt_bias,
    a_log,
    skip,
    send_rows,
    child_slot,
):
    owners = lax.axis_size("branch")
    tensors = lax.axis_size("tensor")
    assert owners & (owners - 1) == 0 and tensors & (tensors - 1) == 0
    assert prompt_ssm.shape[0] == 1 and send_rows.shape[2] == 1
    rb, steps, _, channels = step_in.shape
    taps = conv_weight.shape[0]
    width = x_weight.shape[1]
    n_state = a_log.shape[0]
    rows = steps * (rb + owners)
    short = taps - 1 + steps + 1
    depth = short + n_state
    direct = owners == DIRECT
    owner = pinned(lax.axis_index("branch").astype(jnp.int32).reshape(1))

    if direct:
        msg_shapes = [(1, d, channels) for d in (short, depth, short, short)]
    else:
        msg_shapes = [(owners, depth, channels)]
    msgs = call(
        functools.partial(pack_kernel, direct),
        [shaped(s, BF16) for s in msg_shapes],
        [hbm()] * 6,
        [vmem()] * len(msg_shapes),
        [
            pltpu.SMEM((1,), jnp.int32),
            pltpu.SMEM((owners,), jnp.int32),
            pltpu.SMEM((rb,), jnp.int32),
            pltpu.VMEM(step_in.shape, BF16),
            pltpu.VMEM(prompt_conv.shape, BF16),
            pltpu.VMEM(prompt_ssm.shape, F32),
            pltpu.SemaphoreType.DMA((5 + STEP_PARTS,)),
        ],
        nbytes=owners * depth * channels * 2,
    )(
        owner,
        pinned(send_rows.reshape(owners)),
        pinned(prompt_of),
        pinned(step_in),
        pinned(prompt_conv),
        pinned(prompt_ssm),
    )
    if direct:
        own = msgs[0]
        msgs = [own] + [
            lax.ppermute(m, "branch", list(enumerate(to))) for m, to in zip(msgs[1:], SENDS)
        ]
        after = own
    else:
        msgs = [lax.all_to_all(msgs[0], "branch", split_axis=0, concat_axis=0, tiled=True)]
        after = msgs[0]
    n_msgs = len(msgs)
    near = call(
        functools.partial(prepare_kernel, direct),
        [
            shaped((steps, rb, channels), F32),
            shaped((steps, rb, channels), F32),
            shaped((rb, owners), F32),
            shaped((rb, owners), F32),
            shaped((1, owners), F32),
            shaped((taps, channels), F32),
            shaped((1, channels), F32),
            shaped((width, channels), BF16),
            shaped((n_state, channels), F32),
            shaped((n_state // 2, 2 * owners, channels), F32),
            shaped((1, channels), F32),
            shaped((1, channels), F32),
        ],
        [hbm()] * 10 + [anywhere()],
        [vmem()] * 12,
        [
            pltpu.VMEM(step_in.shape, BF16),
            pltpu.SMEM((1,), jnp.int32),
            pltpu.SMEM((rb,), jnp.int32),
            pltpu.SMEM((rb,), jnp.int32),
            pltpu.VMEM((n_state, channels), F32),
            pltpu.SemaphoreType.DMA((8 + WEIGHT_PARTS + STEP_PARTS,)),
        ],
        flops=10 * steps * rb * channels,
        nbytes=12 * steps * rb * channels,
        trans=steps * rb * channels,
    )(
        owner,
        pinned(prompt_of),
        pinned(child_slot),
        pinned(step_in),
        pinned(conv_weight),
        pinned(conv_bias[None]),
        pinned(x_weight.T),
        pinned(a_log),
        pinned(dt_bias[None]),
        pinned(skip[None]),
        after,
    )
    base, gate, pick, child_pick, sender, taps_near, bias_near, weight_near = near[:8]
    rate, twin, dtb_near, skip_near = near[8:]
    states = []
    if direct:
        pair = call(
            functools.partial(pair_kernel, short),
            shaped((1, 3 * n_state, channels), BF16),
            [vmem()] * 2 + [anywhere()],
            vmem(),
            nbytes=12 * n_state * channels,
        )(prompt_ssm, msgs[1], pick)
        states = [prompt_ssm, swap(pair, "branch", 1)]
    act, part, brief = call(
        functools.partial(project_kernel, n_msgs),
        [
            shaped((rows, channels), F32),
            shaped((rows, width), F32),
            shaped((rows, width), BF16),
        ],
        [vmem()] * (6 + n_msgs),
        [vmem()] * 3,
        flops=2 * rows * channels * width,
        nbytes=channels * width * 2 + rows * (channels + width) * 4,
        trans=rows * channels,
    )(pick, sender, base, taps_near, bias_near, weight_near, *msgs)
    other = swap(brief, "tensor", 1)
    distance = 2
    while distance < tensors:
        part, brief = call(
            add_kernel,
            [shaped((rows, width), F32), shaped((rows, width), BF16)],
            [vmem()] * 2,
            [vmem()] * 2,
            flops=rows * width,
            nbytes=rows * width * 14,
        )(part, other)
        other = swap(brief, "tensor", 2 * distance - 1)
        distance *= 2

    child_conv = call(
        functools.partial(windows_kernel, n_msgs, steps),
        shaped((taps - 1, rb, channels), BF16),
        [vmem(), anywhere()] + [vmem()] * n_msgs,
        vmem(),
        flops=2 * owners * taps * rb * channels,
        nbytes=4 * taps * rb * channels,
    )(child_pick, part, *msgs)
    own_start, slot_start = call(
        functools.partial(start_kernel, n_msgs, direct, short),
        [
            shaped((n_state, rb, channels), F32),
            shaped((n_state // 2, 2 * owners, channels), F32),
        ],
        [vmem()] * 2 + [anywhere()] + [vmem()] * (n_msgs + len(states)),
        [vmem()] * 2,
        [pltpu.VMEM((owners, n_state, channels), F32)],
        flops=2 * owners * n_state * (rb + owners) * channels,
        nbytes=4 * n_state * (rb + owners) * channels,
    )(pick, sender, part, *msgs, *states)

    decoded, child_ssm = call(
        functools.partial(decode_kernel, direct),
        [
            shaped((rb, steps, channels), BF16),
            shaped((rb, n_state, channels), F32),
        ],
        [hbm()] * 2 + [vmem()] * 11,
        [vmem(), anywhere()],
        [
            pltpu.SMEM((1,), jnp.int32),
            pltpu.SMEM((rb,), jnp.int32),
            pltpu.VMEM((steps * rb, channels), F32),
            pltpu.VMEM((steps * rb, channels), F32),
            pltpu.VMEM((steps, 2 * owners, channels), F32),
            pltpu.VMEM((steps, 2 * owners, channels), F32),
            pltpu.VMEM((n_state, steps * rb, LANES), F32),
            pltpu.VMEM((n_state, steps * rb, LANES), F32),
            pltpu.VMEM((n_state // 2, steps, 2 * owners, LANES), F32),
            pltpu.VMEM((owners, n_state, channels), F32),
            pltpu.VMEM((WIDE, steps * rb, LANES), F32),
            pltpu.SemaphoreType.DMA((2 + rb,)),
        ],
        flops=8 * rows * n_state * channels,
        nbytes=(rb + owners) * n_state * channels * 4,
        trans=rows * n_state * channels,
    )(
        owner,
        pinned(child_slot),
        act,
        gate,
        own_start,
        slot_start,
        rate,
        twin,
        dt_weight,
        dtb_near,
        skip_near,
        part,
        other,
    )
    return (decoded, child_ssm, jnp.transpose(child_conv, (1, 0, 2)))


def solution(mesh):
    placed = (
        P(("replica", "branch"), None, "tensor"),
        P(("replica", "branch"), None, "tensor"),
        P(("replica", "branch")),
        P(("replica", "branch"), None, None, "tensor"),
        P(None, "tensor"),
        P("tensor"),
        P("tensor", None),
        P(None, "tensor"),
        P("tensor"),
        P(None, "tensor"),
        P("tensor"),
        P(("replica", "branch"), None, None),
        P(("replica", "branch")),
    )
    return jax.shard_map(
        on_device,
        mesh=mesh,
        in_specs=placed,
        out_specs=(
            P(("replica", "branch"), None, "tensor"),
            P(("replica", "branch"), None, "tensor"),
            P(("replica", "branch"), None, "tensor"),
        ),
        check_vma=False,
    )
```

```python
import functools
import math

import jax
import jax.numpy as jnp
from jax import lax
from jax.experimental import pallas as pl
from jax.experimental.pallas import tpu as pltpu
from jax.sharding import PartitionSpec as P

F32 = jnp.float32
BF16 = jnp.bfloat16
LANES = 128
ROWS = 8
WIDE = 2
VMEM_LIMIT = 48 * 2**20
WEIGHT_PARTS = 6
STEP_PARTS = 4
DIRECT = 4
SENDS = ((2, 3, 1, 0), (3, 2, 0, 1), (1, 0, 3, 2))


def vmem():
    return pl.BlockSpec(memory_space=pltpu.VMEM)


def hbm():
    return pl.BlockSpec(memory_space=pltpu.HBM)


def anywhere():
    return pl.BlockSpec(memory_space=pl.ANY)


def pinned(array):
    return pltpu.with_memory_space_constraint(array, pltpu.HBM)


def shaped(shape, dtype):
    return jax.ShapeDtypeStruct(shape, dtype)


def call(kernel, outs, in_specs, out_specs, scratch=(), flops=0, nbytes=0, trans=0):
    return pl.pallas_call(
        kernel,
        out_shape=outs,
        in_specs=in_specs,
        out_specs=out_specs,
        scratch_shapes=list(scratch),
        compiler_params=pltpu.CompilerParams(vmem_limit_bytes=VMEM_LIMIT),
        cost_estimate=pl.CostEstimate(flops=flops, bytes_accessed=nbytes, transcendentals=trans),
    )


def swap(value, axis, distance):
    size = lax.axis_size(axis)
    return lax.ppermute(value, axis, [(i, i ^ distance) for i in range(size)])


def chosen(number, values):
    total = values[0]
    for i in range(1, len(values)):
        total = jnp.where(number == i, values[i], total)
    return total


def block_of(sender, owner, direct):
    if not direct:
        return sender
    table = [
        [0 if s == r else 1 + [to[s] for to in SENDS].index(r) for s in range(DIRECT)]
        for r in range(DIRECT)
    ]
    places = [chosen(owner, [row[s] for row in table]) for s in range(DIRECT)]
    return places[sender] if isinstance(sender, int) else chosen(sender, places)


def all_of(copies):
    for copy in copies:
        copy.start()
    for copy in copies:
        copy.wait()


def read_messages(refs):
    return [ref[i].astype(F32) for ref in refs for i in range(ref.shape[0])]


def in_parts(source, target, sems, first, count):
    rows = source.shape[0] // count
    at = [pl.ds(i * rows, rows) for i in range(count)]
    return [
        pltpu.make_async_copy(source.at[a], target.at[a], sems.at[first + i])
        for i, a in enumerate(at)
    ]


def scalar_onehot(senders_s, owner, shape, direct):
    row_of = lax.broadcasted_iota(jnp.int32, shape, 0)
    wanted = jnp.zeros(shape, jnp.int32)
    for b in range(shape[0]):
        wanted = jnp.where(row_of == b, senders_s[b], wanted)
    wanted = block_of(wanted, owner, direct)
    return (wanted == lax.broadcasted_iota(jnp.int32, shape, 1)).astype(F32)


def pick_rows(pick, rows):
    total = pick[:, 0:1] * rows[0]
    for k in range(1, len(rows)):
        total = total + pick[:, k : k + 1] * rows[k]
    return total


def pack_kernel(direct, owner_hbm, rows_hbm, prompt_hbm, step_hbm, conv_hbm, ssm_hbm, *rest):
    outs, (owner_s, rows_s, prompt_s, step, conv, ssm, sems) = rest[:-7], rest[-7:]
    owners = rows_hbm.shape[0]
    channels = step_hbm.shape[3]
    copies = [
        pltpu.make_async_copy(owner_hbm, owner_s, sems.at[4]),
        pltpu.make_async_copy(rows_hbm, rows_s, sems.at[0]),
        pltpu.make_async_copy(prompt_hbm, prompt_s, sems.at[1]),
        pltpu.make_async_copy(conv_hbm, conv, sems.at[2]),
        pltpu.make_async_copy(ssm_hbm, ssm, sems.at[3]),
    ]
    all_of(copies + in_parts(step_hbm, step, sems, 5, STEP_PARTS))
    owner = owner_s[0]
    window = conv[0].astype(F32)

    def write(ref, target):
        row = jnp.maximum(rows_s[target], 0)
        xs = step[row, :, 0, :].astype(F32)
        number = prompt_s[row].astype(F32)
        pieces = [xs, window, jnp.full((1, channels), number, F32)]
        if ref.shape[0] > sum(p.shape[0] for p in pieces):
            pieces.append(ssm[0])
        ref[...] = jnp.concatenate(pieces, axis=0).astype(BF16)

    if direct:
        write(outs[0].at[0], owner)
        for ref, to in zip(outs[1:], SENDS):
            write(ref.at[0], chosen(owner, to))
    else:
        for target in range(owners):
            write(outs[0].at[target], target)


def pair_kernel(text, ssm_ref, came_ref, after_ref, pair_ref):
    del after_ref
    state = ssm_ref[0]
    head = state.astype(BF16).astype(F32)
    came = came_ref[0].astype(F32)[text:, :]
    pair_ref[0] = jnp.concatenate([head, state - head, came], axis=0).astype(BF16)


def silu(v):
    return v / (1.0 + jnp.exp(-v))


def prepare_kernel(
    direct,
    owner_hbm,
    prompt_hbm,
    child_hbm,
    step_hbm,
    cw_hbm,
    cb_hbm,
    xwt_hbm,
    alog_hbm,
    dtb_hbm,
    skip_hbm,
    after_ref,
    base_ref,
    gate_ref,
    pick_ref,
    child_ref,
    sender_ref,
    cw_ref,
    cb_ref,
    xwt_ref,
    rate_ref,
    twin_ref,
    dtb_ref,
    skip_ref,
    step_ref,
    owner_s,
    prompt_s,
    child_s,
    alog,
    sems,
):
    del after_ref
    small = [
        pltpu.make_async_copy(source, target, sems.at[i])
        for i, (source, target) in enumerate(
            (
                (cw_hbm, cw_ref),
                (cb_hbm, cb_ref),
                (owner_hbm, owner_s),
                (prompt_hbm, prompt_s),
                (child_hbm, child_s),
                (alog_hbm, alog),
                (dtb_hbm, dtb_ref),
                (skip_hbm, skip_ref),
            )
        )
    ]
    inputs = in_parts(step_hbm, step_ref, sems, len(small), STEP_PARTS)
    large = in_parts(xwt_hbm, xwt_ref, sems, len(small) + STEP_PARTS, WEIGHT_PARTS)
    for copy in inputs + small + large:
        copy.start()
    for copy in inputs:
        copy.wait()
    steps = step_ref.shape[1]
    taps = cw_hbm.shape[0]
    xs = [step_ref[:, t, 0, :].astype(F32) for t in range(steps)]
    for t in range(steps):
        gate_ref[t] = silu(step_ref[:, t, 1, :].astype(F32))
    for copy in small:
        copy.wait()
    for t in range(steps):
        total = cw_ref[taps - 1 : taps, :] * xs[t] + cb_ref[...]
        for k in range(max(0, taps - 1 - t), taps - 1):
            total = total + cw_ref[k : k + 1, :] * xs[t + k - taps + 1]
        base_ref[t] = total
    pick_ref[...] = scalar_onehot(prompt_s, owner_s[0], pick_ref.shape, direct)
    child_ref[...] = scalar_onehot(child_s, owner_s[0], child_ref.shape, direct)
    column = lax.broadcasted_iota(jnp.int32, sender_ref.shape, 1)
    sender = column
    for sent in range(sender_ref.shape[1] if direct else 0):
        sender = jnp.where(column == block_of(sent, owner_s[0], direct), sent, sender)
    sender_ref[...] = sender.astype(F32)
    rate = jnp.exp(alog[...]) * (-math.log2(math.e))
    rate_ref[...] = rate
    half = (twin_ref.shape[1] // 2, rate.shape[1])
    for m in range(rate.shape[0] // 2):
        two = [jnp.broadcast_to(rate[n : n + 1, :], half) for n in (2 * m, 2 * m + 1)]
        twin_ref[m] = jnp.concatenate(two, axis=0)
    for copy in large:
        copy.wait()


def softplus(v):
    return jnp.maximum(v, 0.0) + jnp.log(1.0 + jnp.exp(-jnp.abs(v)))


def slot_onehot(numbers, sender_ref):
    owners = sender_ref.shape[1]
    return (numbers[:, :owners] == sender_ref[...]).astype(F32)


def project_kernel(n_msgs, pick_ref, sender_ref, base_ref, cw_ref, cb_ref, xwt_ref, *rest):
    msgs, (act_ref, part_ref, short_ref) = rest[:n_msgs], rest[n_msgs:]
    taps = cw_ref.shape[0]
    steps, rb, _ = base_ref.shape
    past = taps - 1
    held = read_messages(msgs)
    owners = len(held)
    windows = [[h[steps + k : steps + k + 1, :] for h in held] for k in range(past)]
    own = pick_ref[...]
    own_windows = [pick_rows(own, w) for w in windows]
    for t in range(steps):
        conv = base_ref[t]
        for k in range(past - t):
            conv = conv + cw_ref[k : k + 1, :] * own_windows[t + k]
        act_ref[t * rb : (t + 1) * rb, :] = silu(conv)

    def line_of(row):
        return jnp.concatenate([h[row : row + 1, :] for h in held], axis=0)

    slot = slot_onehot(line_of(past + steps), sender_ref)
    line = [pick_rows(slot, w) for w in windows]
    line += [line_of(t) for t in range(steps)]
    row = steps * rb
    for t in range(steps):
        conv = cw_ref[past:taps, :] * line[t + past] + cb_ref[...]
        for k in range(past):
            conv = conv + cw_ref[k : k + 1, :] * line[t + k]
        act_ref[row : row + owners, :] = silu(conv)
        row += owners
    part = lax.dot_general(
        act_ref[...].astype(BF16),
        xwt_ref[...],
        (((1,), (1,)), ((), ())),
        preferred_element_type=F32,
    )
    part_ref[...] = part
    short_ref[...] = part.astype(BF16)


def add_kernel(a_ref, b_ref, sum_ref, short_ref):
    total = a_ref[...] + b_ref[...].astype(F32)
    sum_ref[...] = total
    short_ref[...] = total.astype(BF16)


def windows_kernel(n_msgs, steps, child_ref, after_ref, *rest):
    del after_ref
    msgs, (conv_ref,) = rest[:n_msgs], rest[n_msgs:]
    held = read_messages(msgs)
    past = conv_ref.shape[0]
    for k in range(past):
        at = steps - past + k
        rows = [h[at : at + 1, :] for h in held]
        conv_ref[k] = pick_rows(child_ref[...], rows).astype(BF16)


def start_kernel(n_msgs, direct, text, pick_ref, sender_ref, after_ref, *rest):
    del after_ref
    msgs, rest = rest[:n_msgs], rest[n_msgs:]
    apart, (own_ref, slot_ref, state_s) = rest[:-3], rest[-3:]
    n_state = own_ref.shape[0]
    held = read_messages(msgs)
    owners = len(held)
    numbers = jnp.concatenate([h[text - 1 : text, :] for h in held], axis=0)
    states = [h[text:, :] for h in held]
    if direct:
        ssm_ref, pair_ref = apart
        head, low, came = [
            pair_ref[0].astype(F32)[i * n_state : (i + 1) * n_state, :] for i in range(3)
        ]
        states[0], states[2], states[3] = ssm_ref[0], came, head + low
    for k, state in enumerate(states):
        state_s[k] = state
    own = pick_ref[...]
    slot = slot_onehot(numbers, sender_ref)

    def two(m, carry):
        picked = []
        for n in (2 * m, 2 * m + 1):
            rows = [state_s[k, pl.ds(n, 1), :] for k in range(owners)]
            own_ref[n] = pick_rows(own, rows)
            picked.append(pick_rows(slot, rows))
        slot_ref[m] = jnp.concatenate(picked, axis=0)
        return carry

    lax.fori_loop(0, n_state // 2, two, 0, unroll=owners <= DIRECT)


def decode_kernel(
    direct,
    owner_hbm,
    child_hbm,
    act_ref,
    gate_ref,
    own_ref,
    slot_ref,
    rate_ref,
    twin_ref,
    dtw_ref,
    dtb_ref,
    skip_ref,
    part_ref,
    other_ref,
    dec_ref,
    child_ssm,
    owner_s,
    child_s,
    delta_s,
    gain_s,
    slot_delta_s,
    slot_gain_s,
    b_s,
    c_s,
    twin_b_s,
    slots_s,
    line_s,
    sems,
):
    scalars = [
        pltpu.make_async_copy(owner_hbm, owner_s, sems.at[0]),
        pltpu.make_async_copy(child_hbm, child_s, sems.at[1]),
    ]
    for copy in scalars:
        copy.start()
    rb, steps, channels = dec_ref.shape
    rank = dtw_ref.shape[0]
    n_state = rate_ref.shape[0]
    n_slots = slots_s.shape[0]
    own_rows = steps * rb
    chunks = channels // (WIDE * LANES)

    proj = part_ref[...] + other_ref[...].astype(F32)
    delta_in = proj[:, :rank].astype(BF16)
    raw = jnp.dot(delta_in, dtw_ref[...], preferred_element_type=F32) + dtb_ref[...]
    delta_s[...] = raw[:own_rows, :]
    delta = softplus(raw[own_rows:, :])
    gain = delta * act_ref[own_rows:, :]

    def column(at, n, rows):
        return jnp.broadcast_to(at[:, n : n + 1], (rows, LANES))

    for t in range(steps):
        at = slice(t * n_slots, (t + 1) * n_slots)
        slot_delta_s[t] = jnp.concatenate([delta[at, :]] * 2, axis=0)
        slot_gain_s[t] = jnp.concatenate([gain[at, :]] * 2, axis=0)
        twice = jnp.concatenate([proj[own_rows:, rank:][at, :]] * 2, axis=0)
        upper = lax.broadcasted_iota(jnp.int32, (2 * n_slots, LANES), 0) < n_slots
        for m in range(n_state // 2):
            twin_b_s[m, t] = jnp.where(
                upper, column(twice, 2 * m, 2 * n_slots), column(twice, 2 * m + 1, 2 * n_slots)
            )
    for n in range(n_state):
        b_s[n] = column(proj[:own_rows, rank:], n, own_rows)
        c_s[n] = column(proj[:own_rows, rank:], n_state + n, own_rows)

    def wide(part):
        return jnp.concatenate([part] * WIDE, axis=1)

    def slot_chunk(chunk, carry):
        columns = pl.ds(pl.multiple_of(chunk * WIDE * LANES, WIDE * LANES), WIDE * LANES)
        delta = [slot_delta_s[t, :, columns] for t in range(steps)]
        gain = [slot_gain_s[t, :, columns] for t in range(steps)]
        for m in range(n_state // 2):
            rate = twin_ref[m, :, columns]
            state = slot_ref[m, :, columns]
            for t in range(steps):
                state = jnp.exp2(delta[t] * rate) * state + gain[t] * wide(twin_b_s[m, t])
            slots_s[:, 2 * m, columns] = state[:n_slots, :]
            slots_s[:, 2 * m + 1, columns] = state[n_slots:, :]
        own = softplus(delta_s[:, columns])
        delta_s[:, columns] = own
        gain_s[:, columns] = own * act_ref[:own_rows, columns]
        return carry

    lax.fori_loop(0, chunks, slot_chunk, 0)
    for copy in scalars:
        copy.wait()
    copies = []
    for j in range(rb):
        at = block_of(child_s[j], owner_s[0], direct)
        copy = pltpu.make_async_copy(slots_s.at[at], child_ssm.at[j], sems.at[2 + j])
        copy.start()
        copies.append(copy)

    def own_chunk(chunk, carry):
        columns = pl.ds(pl.multiple_of(chunk * WIDE * LANES, WIDE * LANES), WIDE * LANES)
        for first in range(0, rb, ROWS):
            at = [pl.ds(t * rb + first, ROWS) for t in range(steps)]
            delta = [delta_s[a, columns] for a in at]
            gain = [gain_s[a, columns] for a in at]
            sums = [skip_ref[:, columns] * act_ref[a, columns] for a in at]
            for n in range(n_state):
                rate = rate_ref[n : n + 1, columns]
                state = own_ref[n, pl.ds(first, ROWS), columns]
                for t in range(steps):
                    state = jnp.exp2(delta[t] * rate) * state + gain[t] * wide(b_s[n, at[t], :])
                    sums[t] = sums[t] + wide(c_s[n, at[t], :]) * state
            for t in range(steps):
                out = sums[t] * gate_ref[t, pl.ds(first, ROWS), columns]
                for w in range(WIDE):
                    line_s[w, pl.ds(first * steps + t, ROWS, stride=steps), :] = out[
                        :, w * LANES : (w + 1) * LANES
                    ]
        for w in range(WIDE):
            some = pl.ds(pl.multiple_of((chunk * WIDE + w) * LANES, LANES), LANES)
            dec_ref[:, :, some] = line_s[w].reshape(rb, steps, LANES).astype(BF16)
        return carry

    lax.fori_loop(0, chunks, own_chunk, 0)
    for copy in copies:
        copy.wait()


def on_device(
    prompt_ssm,
    prompt_conv,
    prompt_of,
    step_in,
    conv_weight,
    conv_bias,
    x_weight,
    dt_weight,
    dt_bias,
    a_log,
    skip,
    send_rows,
    child_slot,
):
    owners = lax.axis_size("branch")
    tensors = lax.axis_size("tensor")
    assert owners & (owners - 1) == 0 and tensors & (tensors - 1) == 0
    assert prompt_ssm.shape[0] == 1 and send_rows.shape[2] == 1
    rb, steps, _, channels = step_in.shape
    taps = conv_weight.shape[0]
    width = x_weight.shape[1]
    n_state = a_log.shape[0]
    rows = steps * (rb + owners)
    short = taps - 1 + steps + 1
    depth = short + n_state
    direct = owners == DIRECT
    owner = pinned(lax.axis_index("branch").astype(jnp.int32).reshape(1))

    if direct:
        msg_shapes = [(1, d, channels) for d in (short, depth, short, short)]
    else:
        msg_shapes = [(owners, depth, channels)]
    msgs = call(
        functools.partial(pack_kernel, direct),
        [shaped(s, BF16) for s in msg_shapes],
        [hbm()] * 6,
        [vmem()] * len(msg_shapes),
        [
            pltpu.SMEM((1,), jnp.int32),
            pltpu.SMEM((owners,), jnp.int32),
            pltpu.SMEM((rb,), jnp.int32),
            pltpu.VMEM(step_in.shape, BF16),
            pltpu.VMEM(prompt_conv.shape, BF16),
            pltpu.VMEM(prompt_ssm.shape, F32),
            pltpu.SemaphoreType.DMA((5 + STEP_PARTS,)),
        ],
        nbytes=owners * depth * channels * 2,
    )(
        owner,
        pinned(send_rows.reshape(owners)),
        pinned(prompt_of),
        pinned(step_in),
        pinned(prompt_conv),
        pinned(prompt_ssm),
    )
    if direct:
        own = msgs[0]
        msgs = [own] + [
            lax.ppermute(m, "branch", list(enumerate(to))) for m, to in zip(msgs[1:], SENDS)
        ]
        after = own
    else:
        msgs = [lax.all_to_all(msgs[0], "branch", split_axis=0, concat_axis=0, tiled=True)]
        after = msgs[0]
    n_msgs = len(msgs)
    near = call(
        functools.partial(prepare_kernel, direct),
        [
            shaped((steps, rb, channels), F32),
            shaped((steps, rb, channels), F32),
            shaped((rb, owners), F32),
            shaped((rb, owners), F32),
            shaped((1, owners), F32),
            shaped((taps, channels), F32),
            shaped((1, channels), F32),
            shaped((width, channels), BF16),
            shaped((n_state, channels), F32),
            shaped((n_state // 2, 2 * owners, channels), F32),
            shaped((1, channels), F32),
            shaped((1, channels), F32),
        ],
        [hbm()] * 10 + [anywhere()],
        [vmem()] * 12,
        [
            pltpu.VMEM(step_in.shape, BF16),
            pltpu.SMEM((1,), jnp.int32),
            pltpu.SMEM((rb,), jnp.int32),
            pltpu.SMEM((rb,), jnp.int32),
            pltpu.VMEM((n_state, channels), F32),
            pltpu.SemaphoreType.DMA((8 + WEIGHT_PARTS + STEP_PARTS,)),
        ],
        flops=10 * steps * rb * channels,
        nbytes=12 * steps * rb * channels,
        trans=steps * rb * channels,
    )(
        owner,
        pinned(prompt_of),
        pinned(child_slot),
        pinned(step_in),
        pinned(conv_weight),
        pinned(conv_bias[None]),
        pinned(x_weight.T),
        pinned(a_log),
        pinned(dt_bias[None]),
        pinned(skip[None]),
        after,
    )
    base, gate, pick, child_pick, sender, taps_near, bias_near, weight_near = near[:8]
    rate, twin, dtb_near, skip_near = near[8:]
    states = []
    if direct:
        pair = call(
            functools.partial(pair_kernel, short),
            shaped((1, 3 * n_state, channels), BF16),
            [vmem()] * 2 + [anywhere()],
            vmem(),
            nbytes=12 * n_state * channels,
        )(prompt_ssm, msgs[1], pick)
        states = [prompt_ssm, swap(pair, "branch", 1)]
    act, part, brief = call(
        functools.partial(project_kernel, n_msgs),
        [
            shaped((rows, channels), F32),
            shaped((rows, width), F32),
            shaped((rows, width), BF16),
        ],
        [vmem()] * (6 + n_msgs),
        [vmem()] * 3,
        flops=2 * rows * channels * width,
        nbytes=channels * width * 2 + rows * (channels + width) * 4,
        trans=rows * channels,
    )(pick, sender, base, taps_near, bias_near, weight_near, *msgs)
    other = swap(brief, "tensor", 1)
    distance = 2
    while distance < tensors:
        part, brief = call(
            add_kernel,
            [shaped((rows, width), F32), shaped((rows, width), BF16)],
            [vmem()] * 2,
            [vmem()] * 2,
            flops=rows * width,
            nbytes=rows * width * 14,
        )(part, other)
        other = swap(brief, "tensor", 2 * distance - 1)
        distance *= 2

    child_conv = call(
        functools.partial(windows_kernel, n_msgs, steps),
        shaped((taps - 1, rb, channels), BF16),
        [vmem(), anywhere()] + [vmem()] * n_msgs,
        vmem(),
        flops=2 * owners * taps * rb * channels,
        nbytes=4 * taps * rb * channels,
    )(child_pick, part, *msgs)
    own_start, slot_start = call(
        functools.partial(start_kernel, n_msgs, direct, short),
        [
            shaped((n_state, rb, channels), F32),
            shaped((n_state // 2, 2 * owners, channels), F32),
        ],
        [vmem()] * 2 + [anywhere()] + [vmem()] * (n_msgs + len(states)),
        [vmem()] * 2,
        [pltpu.VMEM((owners, n_state, channels), F32)],
        flops=2 * owners * n_state * (rb + owners) * channels,
        nbytes=4 * n_state * (rb + owners) * channels,
    )(pick, sender, part, *msgs, *states)

    decoded, child_ssm = call(
        functools.partial(decode_kernel, direct),
        [
            shaped((rb, steps, channels), BF16),
            shaped((rb, n_state, channels), F32),
        ],
        [hbm()] * 2 + [vmem()] * 11,
        [vmem(), anywhere()],
        [
            pltpu.SMEM((1,), jnp.int32),
            pltpu.SMEM((rb,), jnp.int32),
            pltpu.VMEM((steps * rb, channels), F32),
            pltpu.VMEM((steps * rb, channels), F32),
            pltpu.VMEM((steps, 2 * owners, channels), F32),
            pltpu.VMEM((steps, 2 * owners, channels), F32),
            pltpu.VMEM((n_state, steps * rb, LANES), F32),
            pltpu.VMEM((n_state, steps * rb, LANES), F32),
            pltpu.VMEM((n_state // 2, steps, 2 * owners, LANES), F32),
            pltpu.VMEM((owners, n_state, channels), F32),
            pltpu.VMEM((WIDE, steps * rb, LANES), F32),
            pltpu.SemaphoreType.DMA((2 + rb,)),
        ],
        flops=8 * rows * n_state * channels,
        nbytes=(rb + owners) * n_state * channels * 4,
        trans=rows * n_state * channels,
    )(
        owner,
        pinned(child_slot),
        act,
        gate,
        own_start,
        slot_start,
        rate,
        twin,
        dt_weight,
        dtb_near,
        skip_near,
        part,
        other,
    )
    return (decoded, child_ssm, jnp.transpose(child_conv, (1, 0, 2)))


def solution(mesh):
    placed = (
        P(("replica", "branch"), None, "tensor"),
        P(("replica", "branch"), None, "tensor"),
        P(("replica", "branch")),
        P(("replica", "branch"), None, None, "tensor"),
        P(None, "tensor"),
        P("tensor"),
        P("tensor", None),
        P(None, "tensor"),
        P("tensor"),
        P(None, "tensor"),
        P("tensor"),
        P(("replica", "branch"), None, None),
        P(("replica", "branch")),
    )
    return jax.shard_map(
        on_device,
        mesh=mesh,
        in_specs=placed,
        out_specs=(
            P(("replica", "branch"), None, "tensor"),
            P(("replica", "branch"), None, "tensor"),
            P(("replica", "branch"), None, "tensor"),
        ),
        check_vma=False,
    )
```

```python
import functools
import math

import jax
import jax.numpy as jnp
from jax import lax
from jax.experimental import pallas as pl
from jax.experimental.pallas import tpu as pltpu
from jax.sharding import PartitionSpec as P

F32 = jnp.float32
BF16 = jnp.bfloat16
LANES = 128
ROWS = 8
WIDE = 2
VMEM_LIMIT = 48 * 2**20
WEIGHT_PARTS = 6
STEP_PARTS = 4
DIRECT = 4
SENDS = ((2, 3, 1, 0), (3, 2, 0, 1), (1, 0, 3, 2))


def vmem():
    return pl.BlockSpec(memory_space=pltpu.VMEM)


def hbm():
    return pl.BlockSpec(memory_space=pltpu.HBM)


def anywhere():
    return pl.BlockSpec(memory_space=pl.ANY)


def pinned(array):
    return pltpu.with_memory_space_constraint(array, pltpu.HBM)


def shaped(shape, dtype):
    return jax.ShapeDtypeStruct(shape, dtype)


def call(kernel, outs, in_specs, out_specs, scratch=(), flops=0, nbytes=0, trans=0):
    return pl.pallas_call(
        kernel,
        out_shape=outs,
        in_specs=in_specs,
        out_specs=out_specs,
        scratch_shapes=list(scratch),
        compiler_params=pltpu.CompilerParams(vmem_limit_bytes=VMEM_LIMIT),
        cost_estimate=pl.CostEstimate(flops=flops, bytes_accessed=nbytes, transcendentals=trans),
    )


def swap(value, axis, distance):
    size = lax.axis_size(axis)
    return lax.ppermute(value, axis, [(i, i ^ distance) for i in range(size)])


def chosen(number, values):
    total = values[0]
    for i in range(1, len(values)):
        total = jnp.where(number == i, values[i], total)
    return total


def blocks_of(owner):
    table = [
        [0 if s == r else 1 + [to[s] for to in SENDS].index(r) for s in range(DIRECT)]
        for r in range(DIRECT)
    ]
    return [chosen(owner, [row[s] for row in table]) for s in range(DIRECT)]


def block_of(sender, owner, direct):
    if not direct:
        return sender
    places = blocks_of(owner)
    return places[sender] if isinstance(sender, int) else chosen(sender, places)


def all_of(copies):
    for copy in copies:
        copy.start()
    for copy in copies:
        copy.wait()


def read_messages(refs):
    return [ref[i].astype(F32) for ref in refs for i in range(ref.shape[0])]


def in_parts(source, target, sems, first, count):
    rows = source.shape[0] // count
    at = [pl.ds(i * rows, rows) for i in range(count)]
    return [
        pltpu.make_async_copy(source.at[a], target.at[a], sems.at[first + i])
        for i, a in enumerate(at)
    ]


def scalar_onehot(senders_s, owner, shape, direct):
    row_of = lax.broadcasted_iota(jnp.int32, shape, 0)
    wanted = jnp.zeros(shape, jnp.int32)
    for b in range(shape[0]):
        wanted = jnp.where(row_of == b, senders_s[b], wanted)
    wanted = block_of(wanted, owner, direct)
    return (wanted == lax.broadcasted_iota(jnp.int32, shape, 1)).astype(F32)


def pick_rows(pick, rows):
    total = pick[:, 0:1] * rows[0]
    for k in range(1, len(rows)):
        total = total + pick[:, k : k + 1] * rows[k]
    return total


def pack_kernel(direct, owner_hbm, rows_hbm, prompt_hbm, step_hbm, conv_hbm, ssm_hbm, *rest):
    outs, (owner_s, rows_s, prompt_s, step, conv, ssm, sems) = rest[:-7], rest[-7:]
    owners = rows_hbm.shape[0]
    channels = step_hbm.shape[3]
    copies = in_parts(step_hbm, step, sems, 5, STEP_PARTS) + [
        pltpu.make_async_copy(owner_hbm, owner_s, sems.at[4]),
        pltpu.make_async_copy(rows_hbm, rows_s, sems.at[0]),
        pltpu.make_async_copy(prompt_hbm, prompt_s, sems.at[1]),
        pltpu.make_async_copy(conv_hbm, conv, sems.at[2]),
        pltpu.make_async_copy(ssm_hbm, ssm, sems.at[3]),
    ]
    all_of(copies)
    owner = owner_s[0]
    window = conv[0].astype(F32)

    def write(ref, target):
        row = jnp.maximum(rows_s[target], 0)
        xs = step[row, :, 0, :].astype(F32)
        number = prompt_s[row].astype(F32)
        pieces = [xs, window, jnp.full((1, channels), number, F32)]
        if ref.shape[0] > sum(p.shape[0] for p in pieces):
            pieces.append(ssm[0])
        ref[...] = jnp.concatenate(pieces, axis=0).astype(BF16)

    if direct:
        write(outs[0].at[0], owner)
        for ref, to in zip(outs[1:], SENDS):
            write(ref.at[0], chosen(owner, to))
    else:
        for target in range(owners):
            write(outs[0].at[target], target)


def pair_kernel(text, ssm_ref, came_ref, after_ref, pair_ref):
    del after_ref
    state = ssm_ref[0]
    head = state.astype(BF16).astype(F32)
    came = came_ref[0].astype(F32)[text:, :]
    pair_ref[0] = jnp.concatenate([head, state - head, came], axis=0).astype(BF16)


def silu(v):
    return v / (1.0 + jnp.exp(-v))


def prepare_kernel(
    direct,
    owner_hbm,
    prompt_hbm,
    child_hbm,
    step_hbm,
    cw_hbm,
    cb_hbm,
    xwt_hbm,
    alog_hbm,
    dtb_hbm,
    skip_hbm,
    after_ref,
    base_ref,
    gate_ref,
    pick_ref,
    child_ref,
    sender_ref,
    cw_ref,
    cb_ref,
    xwt_ref,
    rate_ref,
    twin_ref,
    dtb_ref,
    skip_ref,
    step_ref,
    owner_s,
    prompt_s,
    child_s,
    alog,
    sems,
):
    del after_ref
    small = [
        pltpu.make_async_copy(source, target, sems.at[i])
        for i, (source, target) in enumerate(
            (
                (cw_hbm, cw_ref),
                (cb_hbm, cb_ref),
                (owner_hbm, owner_s),
                (prompt_hbm, prompt_s),
                (child_hbm, child_s),
                (alog_hbm, alog),
                (dtb_hbm, dtb_ref),
                (skip_hbm, skip_ref),
            )
        )
    ]
    inputs = in_parts(step_hbm, step_ref, sems, len(small), STEP_PARTS)
    large = in_parts(xwt_hbm, xwt_ref, sems, len(small) + STEP_PARTS, WEIGHT_PARTS)
    for copy in inputs + small + large:
        copy.start()
    for copy in inputs:
        copy.wait()
    steps = step_ref.shape[1]
    taps = cw_hbm.shape[0]
    xs = [step_ref[:, t, 0, :].astype(F32) for t in range(steps)]
    for t in range(steps):
        gate_ref[t] = silu(step_ref[:, t, 1, :].astype(F32))
    for copy in small:
        copy.wait()
    for t in range(steps):
        total = cw_ref[taps - 1 : taps, :] * xs[t] + cb_ref[...]
        for k in range(max(0, taps - 1 - t), taps - 1):
            total = total + cw_ref[k : k + 1, :] * xs[t + k - taps + 1]
        base_ref[t] = total
    pick_ref[...] = scalar_onehot(prompt_s, owner_s[0], pick_ref.shape, direct)
    child_ref[...] = scalar_onehot(child_s, owner_s[0], child_ref.shape, direct)
    column = lax.broadcasted_iota(jnp.int32, sender_ref.shape, 1)
    sender = column
    for sent in range(sender_ref.shape[1] if direct else 0):
        sender = jnp.where(column == block_of(sent, owner_s[0], direct), sent, sender)
    sender_ref[...] = sender.astype(F32)
    rate = jnp.exp(alog[...]) * (-math.log2(math.e))
    rate_ref[...] = rate
    half = (twin_ref.shape[1] // 2, rate.shape[1])
    for m in range(rate.shape[0] // 2):
        two = [jnp.broadcast_to(rate[n : n + 1, :], half) for n in (2 * m, 2 * m + 1)]
        twin_ref[m] = jnp.concatenate(two, axis=0)
    for copy in large:
        copy.wait()


def slot_onehot(numbers, sender_ref):
    owners = sender_ref.shape[1]
    return (numbers[:, :owners] == sender_ref[...]).astype(F32)


def project_kernel(n_msgs, pick_ref, sender_ref, base_ref, cw_ref, cb_ref, xwt_ref, *rest):
    msgs, (act_ref, part_ref, short_ref) = rest[:n_msgs], rest[n_msgs:]
    taps = cw_ref.shape[0]
    steps, rb, _ = base_ref.shape
    past = taps - 1
    held = read_messages(msgs)
    owners = len(held)
    windows = [[h[steps + k : steps + k + 1, :] for h in held] for k in range(past)]
    own = pick_ref[...]
    own_windows = [pick_rows(own, w) for w in windows]
    for t in range(steps):
        conv = base_ref[t]
        for k in range(past - t):
            conv = conv + cw_ref[k : k + 1, :] * own_windows[t + k]
        act_ref[t * rb : (t + 1) * rb, :] = silu(conv)

    def line_of(row):
        return jnp.concatenate([h[row : row + 1, :] for h in held], axis=0)

    slot = slot_onehot(line_of(past + steps), sender_ref)
    line = [pick_rows(slot, w) for w in windows]
    line += [line_of(t) for t in range(steps)]
    row = steps * rb
    for t in range(steps):
        conv = cw_ref[past:taps, :] * line[t + past] + cb_ref[...]
        for k in range(past):
            conv = conv + cw_ref[k : k + 1, :] * line[t + k]
        act_ref[row : row + owners, :] = silu(conv)
        row += owners
    part = lax.dot_general(
        act_ref[...].astype(BF16),
        xwt_ref[...],
        (((1,), (1,)), ((), ())),
        preferred_element_type=F32,
    )
    part_ref[...] = part
    short_ref[...] = part.astype(BF16)


def add_kernel(a_ref, b_ref, sum_ref, short_ref):
    total = a_ref[...] + b_ref[...].astype(F32)
    sum_ref[...] = total
    short_ref[...] = total.astype(BF16)


def windows_kernel(n_msgs, steps, child_ref, after_ref, *rest):
    del after_ref
    msgs, (conv_ref,) = rest[:n_msgs], rest[n_msgs:]
    held = read_messages(msgs)
    past = conv_ref.shape[0]
    for k in range(past):
        at = steps - past + k
        rows = [h[at : at + 1, :] for h in held]
        conv_ref[k] = pick_rows(child_ref[...], rows).astype(BF16)


def start_kernel(n_msgs, direct, text, pick_ref, sender_ref, after_ref, *rest):
    del after_ref
    msgs, rest = rest[:n_msgs], rest[n_msgs:]
    apart, (own_ref, slot_ref, state_s) = rest[:-3], rest[-3:]
    n_state = own_ref.shape[0]
    held = read_messages(msgs)
    owners = len(held)
    numbers = jnp.concatenate([h[text - 1 : text, :] for h in held], axis=0)
    states = [h[text:, :] for h in held]
    if direct:
        ssm_ref, pair_ref = apart
        head, low, came = [
            pair_ref[0].astype(F32)[i * n_state : (i + 1) * n_state, :] for i in range(3)
        ]
        states[0], states[2], states[3] = ssm_ref[0], came, head + low
    for k, state in enumerate(states):
        state_s[k] = state
    own = pick_ref[...]
    slot = slot_onehot(numbers, sender_ref)

    def two(m, carry):
        picked = []
        for n in (2 * m, 2 * m + 1):
            rows = [state_s[k, pl.ds(n, 1), :] for k in range(owners)]
            own_ref[n] = pick_rows(own, rows)
            picked.append(pick_rows(slot, rows))
        slot_ref[m] = jnp.concatenate(picked, axis=0)
        return carry

    lax.fori_loop(0, n_state // 2, two, 0, unroll=owners <= DIRECT)


def decode_kernel(
    direct,
    owner_hbm,
    child_hbm,
    act_ref,
    gate_ref,
    own_ref,
    slot_ref,
    rate_ref,
    twin_ref,
    dtw_ref,
    dtb_ref,
    skip_ref,
    part_ref,
    other_ref,
    dec_ref,
    child_ssm,
    owner_s,
    child_s,
    delta_s,
    gain_s,
    slot_delta_s,
    slot_gain_s,
    b_s,
    c_s,
    twin_b_s,
    slots_s,
    line_s,
    sems,
):
    scalars = [
        pltpu.make_async_copy(owner_hbm, owner_s, sems.at[0]),
        pltpu.make_async_copy(child_hbm, child_s, sems.at[1]),
    ]
    for copy in scalars:
        copy.start()
    rb, steps, channels = dec_ref.shape
    rank = dtw_ref.shape[0]
    n_state = rate_ref.shape[0]
    n_slots = slots_s.shape[0]
    own_rows = steps * rb
    chunks = channels // (WIDE * LANES)

    proj = part_ref[...] + other_ref[...].astype(F32)
    delta_in = proj[:, :rank].astype(BF16)
    delta = jnp.dot(delta_in, dtw_ref[...], preferred_element_type=F32) + dtb_ref[...]
    delta = jnp.maximum(delta, 0.0) + jnp.log(1.0 + jnp.exp(-jnp.abs(delta)))
    gain = delta * act_ref[...]
    delta_s[...] = delta[:own_rows, :]
    gain_s[...] = gain[:own_rows, :]

    def column(at, n, rows):
        return jnp.broadcast_to(at[:, n : n + 1], (rows, LANES))

    for t in range(steps):
        at = slice(own_rows + t * n_slots, own_rows + (t + 1) * n_slots)
        slot_delta_s[t] = jnp.concatenate([delta[at, :]] * 2, axis=0)
        slot_gain_s[t] = jnp.concatenate([gain[at, :]] * 2, axis=0)
        twice = jnp.concatenate([proj[at, rank:]] * 2, axis=0)
        upper = lax.broadcasted_iota(jnp.int32, (2 * n_slots, LANES), 0) < n_slots
        for m in range(n_state // 2):
            twin_b_s[m, t] = jnp.where(
                upper, column(twice, 2 * m, 2 * n_slots), column(twice, 2 * m + 1, 2 * n_slots)
            )
    for n in range(n_state):
        b_s[n] = column(proj[:own_rows, rank:], n, own_rows)
        c_s[n] = column(proj[:own_rows, rank:], n_state + n, own_rows)

    def wide(part):
        return jnp.concatenate([part] * WIDE, axis=1)

    def slot_chunk(chunk, carry):
        columns = pl.ds(pl.multiple_of(chunk * WIDE * LANES, WIDE * LANES), WIDE * LANES)
        delta = [slot_delta_s[t, :, columns] for t in range(steps)]
        gain = [slot_gain_s[t, :, columns] for t in range(steps)]
        for m in range(n_state // 2):
            rate = twin_ref[m, :, columns]
            state = slot_ref[m, :, columns]
            for t in range(steps):
                state = jnp.exp2(delta[t] * rate) * state + gain[t] * wide(twin_b_s[m, t])
            slots_s[:, 2 * m, columns] = state[:n_slots, :]
            slots_s[:, 2 * m + 1, columns] = state[n_slots:, :]
        return carry

    lax.fori_loop(0, chunks, slot_chunk, 0)
    for copy in scalars:
        copy.wait()
    places = blocks_of(owner_s[0]) if direct else None
    batch = rb // chunks

    def child_copy(j):
        at = chosen(child_s[j], places) if direct else child_s[j]
        return pltpu.make_async_copy(slots_s.at[at], child_ssm.at[j], sems.at[2 + j])

    def own_chunk(chunk, carry):
        columns = pl.ds(pl.multiple_of(chunk * WIDE * LANES, WIDE * LANES), WIDE * LANES)
        for i in range(batch):
            child_copy(chunk * batch + i).start()
        for first in range(0, rb, ROWS):
            at = [pl.ds(t * rb + first, ROWS) for t in range(steps)]
            delta = [delta_s[a, columns] for a in at]
            gain = [gain_s[a, columns] for a in at]
            sums = [skip_ref[:, columns] * act_ref[a, columns] for a in at]
            for n in range(n_state):
                rate = rate_ref[n : n + 1, columns]
                state = own_ref[n, pl.ds(first, ROWS), columns]
                for t in range(steps):
                    state = jnp.exp2(delta[t] * rate) * state + gain[t] * wide(b_s[n, at[t], :])
                    sums[t] = sums[t] + wide(c_s[n, at[t], :]) * state
            for t in range(steps):
                out = sums[t] * gate_ref[t, pl.ds(first, ROWS), columns]
                for w in range(WIDE):
                    line_s[w, pl.ds(first * steps + t, ROWS, stride=steps), :] = out[
                        :, w * LANES : (w + 1) * LANES
                    ]
        for w in range(WIDE):
            some = pl.ds(pl.multiple_of((chunk * WIDE + w) * LANES, LANES), LANES)
            dec_ref[:, :, some] = line_s[w].reshape(rb, steps, LANES).astype(BF16)
        return carry

    lax.fori_loop(0, chunks, own_chunk, 0)
    for j in range(rb):
        child_copy(j).wait()


def on_device(
    prompt_ssm,
    prompt_conv,
    prompt_of,
    step_in,
    conv_weight,
    conv_bias,
    x_weight,
    dt_weight,
    dt_bias,
    a_log,
    skip,
    send_rows,
    child_slot,
):
    owners = lax.axis_size("branch")
    tensors = lax.axis_size("tensor")
    assert owners & (owners - 1) == 0 and tensors & (tensors - 1) == 0
    assert prompt_ssm.shape[0] == 1 and send_rows.shape[2] == 1
    rb, steps, _, channels = step_in.shape
    taps = conv_weight.shape[0]
    width = x_weight.shape[1]
    n_state = a_log.shape[0]
    rows = steps * (rb + owners)
    short = taps - 1 + steps + 1
    depth = short + n_state
    direct = owners == DIRECT
    owner = pinned(lax.axis_index("branch").astype(jnp.int32).reshape(1))

    if direct:
        msg_shapes = [(1, d, channels) for d in (short, depth, short, short)]
    else:
        msg_shapes = [(owners, depth, channels)]
    msgs = call(
        functools.partial(pack_kernel, direct),
        [shaped(s, BF16) for s in msg_shapes],
        [hbm()] * 6,
        [vmem()] * len(msg_shapes),
        [
            pltpu.SMEM((1,), jnp.int32),
            pltpu.SMEM((owners,), jnp.int32),
            pltpu.SMEM((rb,), jnp.int32),
            pltpu.VMEM(step_in.shape, BF16),
            pltpu.VMEM(prompt_conv.shape, BF16),
            pltpu.VMEM(prompt_ssm.shape, F32),
            pltpu.SemaphoreType.DMA((5 + STEP_PARTS,)),
        ],
        nbytes=owners * depth * channels * 2,
    )(
        owner,
        pinned(send_rows.reshape(owners)),
        pinned(prompt_of),
        pinned(step_in),
        pinned(prompt_conv),
        pinned(prompt_ssm),
    )
    if direct:
        own = msgs[0]
        msgs = [own] + [
            lax.ppermute(m, "branch", list(enumerate(to))) for m, to in zip(msgs[1:], SENDS)
        ]
        after = own
    else:
        msgs = [lax.all_to_all(msgs[0], "branch", split_axis=0, concat_axis=0, tiled=True)]
        after = msgs[0]
    n_msgs = len(msgs)
    near = call(
        functools.partial(prepare_kernel, direct),
        [
            shaped((steps, rb, channels), F32),
            shaped((steps, rb, channels), F32),
            shaped((rb, owners), F32),
            shaped((rb, owners), F32),
            shaped((1, owners), F32),
            shaped((taps, channels), F32),
            shaped((1, channels), F32),
            shaped((width, channels), BF16),
            shaped((n_state, channels), F32),
            shaped((n_state // 2, 2 * owners, channels), F32),
            shaped((1, channels), F32),
            shaped((1, channels), F32),
        ],
        [hbm()] * 10 + [anywhere()],
        [vmem()] * 12,
        [
            pltpu.VMEM(step_in.shape, BF16),
            pltpu.SMEM((1,), jnp.int32),
            pltpu.SMEM((rb,), jnp.int32),
            pltpu.SMEM((rb,), jnp.int32),
            pltpu.VMEM((n_state, channels), F32),
            pltpu.SemaphoreType.DMA((8 + WEIGHT_PARTS + STEP_PARTS,)),
        ],
        flops=10 * steps * rb * channels,
        nbytes=12 * steps * rb * channels,
        trans=steps * rb * channels,
    )(
        owner,
        pinned(prompt_of),
        pinned(child_slot),
        pinned(step_in),
        pinned(conv_weight),
        pinned(conv_bias[None]),
        pinned(x_weight.T),
        pinned(a_log),
        pinned(dt_bias[None]),
        pinned(skip[None]),
        after,
    )
    base, gate, pick, child_pick, sender, taps_near, bias_near, weight_near = near[:8]
    rate, twin, dtb_near, skip_near = near[8:]
    states = []
    if direct:
        pair = call(
            functools.partial(pair_kernel, short),
            shaped((1, 3 * n_state, channels), BF16),
            [vmem()] * 2 + [anywhere()],
            vmem(),
            nbytes=12 * n_state * channels,
        )(prompt_ssm, msgs[1], pick)
        states = [prompt_ssm, swap(pair, "branch", 1)]
    act, part, brief = call(
        functools.partial(project_kernel, n_msgs),
        [
            shaped((rows, channels), F32),
            shaped((rows, width), F32),
            shaped((rows, width), BF16),
        ],
        [vmem()] * (6 + n_msgs),
        [vmem()] * 3,
        flops=2 * rows * channels * width,
        nbytes=channels * width * 2 + rows * (channels + width) * 4,
        trans=rows * channels,
    )(pick, sender, base, taps_near, bias_near, weight_near, *msgs)
    other = swap(brief, "tensor", 1)
    distance = 2
    while distance < tensors:
        part, brief = call(
            add_kernel,
            [shaped((rows, width), F32), shaped((rows, width), BF16)],
            [vmem()] * 2,
            [vmem()] * 2,
            flops=rows * width,
            nbytes=rows * width * 14,
        )(part, other)
        other = swap(brief, "tensor", 2 * distance - 1)
        distance *= 2

    child_conv = call(
        functools.partial(windows_kernel, n_msgs, steps),
        shaped((taps - 1, rb, channels), BF16),
        [vmem(), anywhere()] + [vmem()] * n_msgs,
        vmem(),
        flops=2 * owners * taps * rb * channels,
        nbytes=4 * taps * rb * channels,
    )(child_pick, part, *msgs)
    own_start, slot_start = call(
        functools.partial(start_kernel, n_msgs, direct, short),
        [
            shaped((n_state, rb, channels), F32),
            shaped((n_state // 2, 2 * owners, channels), F32),
        ],
        [vmem()] * 2 + [anywhere()] + [vmem()] * (n_msgs + len(states)),
        [vmem()] * 2,
        [pltpu.VMEM((owners, n_state, channels), F32)],
        flops=2 * owners * n_state * (rb + owners) * channels,
        nbytes=4 * n_state * (rb + owners) * channels,
    )(pick, sender, part, *msgs, *states)

    decoded, child_ssm = call(
        functools.partial(decode_kernel, direct),
        [
            shaped((rb, steps, channels), BF16),
            shaped((rb, n_state, channels), F32),
        ],
        [hbm()] * 2 + [vmem()] * 11,
        [vmem(), anywhere()],
        [
            pltpu.SMEM((1,), jnp.int32),
            pltpu.SMEM((rb,), jnp.int32),
            pltpu.VMEM((steps * rb, channels), F32),
            pltpu.VMEM((steps * rb, channels), F32),
            pltpu.VMEM((steps, 2 * owners, channels), F32),
            pltpu.VMEM((steps, 2 * owners, channels), F32),
            pltpu.VMEM((n_state, steps * rb, LANES), F32),
            pltpu.VMEM((n_state, steps * rb, LANES), F32),
            pltpu.VMEM((n_state // 2, steps, 2 * owners, LANES), F32),
            pltpu.VMEM((owners, n_state, channels), F32),
            pltpu.VMEM((WIDE, steps * rb, LANES), F32),
            pltpu.SemaphoreType.DMA((2 + rb,)),
        ],
        flops=8 * rows * n_state * channels,
        nbytes=(rb + owners) * n_state * channels * 4,
        trans=rows * n_state * channels,
    )(
        owner,
        pinned(child_slot),
        act,
        gate,
        own_start,
        slot_start,
        rate,
        twin,
        dt_weight,
        dtb_near,
        skip_near,
        part,
        other,
    )
    return (decoded, child_ssm, jnp.transpose(child_conv, (1, 0, 2)))


def solution(mesh):
    placed = (
        P(("replica", "branch"), None, "tensor"),
        P(("replica", "branch"), None, "tensor"),
        P(("replica", "branch")),
        P(("replica", "branch"), None, None, "tensor"),
        P(None, "tensor"),
        P("tensor"),
        P("tensor", None),
        P(None, "tensor"),
        P("tensor"),
        P(None, "tensor"),
        P("tensor"),
        P(("replica", "branch"), None, None),
        P(("replica", "branch")),
    )
    return jax.shard_map(
        on_device,
        mesh=mesh,
        in_specs=placed,
        out_specs=(
            P(("replica", "branch"), None, "tensor"),
            P(("replica", "branch"), None, "tensor"),
            P(("replica", "branch"), None, "tensor"),
        ),
        check_vma=False,
    )
```

```python
import functools
import math

import jax
import jax.numpy as jnp
from jax import lax
from jax.experimental import pallas as pl
from jax.experimental.pallas import tpu as pltpu
from jax.sharding import PartitionSpec as P

F32 = jnp.float32
BF16 = jnp.bfloat16
LANES = 128
ROWS = 8
WIDE = 2
VMEM_LIMIT = 48 * 2**20
WEIGHT_PARTS = 6
STEP_PARTS = 4
DIRECT = 4
SENDS = ((2, 3, 1, 0), (3, 2, 0, 1), (1, 0, 3, 2))


def vmem():
    return pl.BlockSpec(memory_space=pltpu.VMEM)


def hbm():
    return pl.BlockSpec(memory_space=pltpu.HBM)


def anywhere():
    return pl.BlockSpec(memory_space=pl.ANY)


def pinned(array):
    return pltpu.with_memory_space_constraint(array, pltpu.HBM)


def shaped(shape, dtype):
    return jax.ShapeDtypeStruct(shape, dtype)


def call(kernel, outs, in_specs, out_specs, scratch=(), flops=0, nbytes=0, trans=0):
    return pl.pallas_call(
        kernel,
        out_shape=outs,
        in_specs=in_specs,
        out_specs=out_specs,
        scratch_shapes=list(scratch),
        compiler_params=pltpu.CompilerParams(vmem_limit_bytes=VMEM_LIMIT),
        cost_estimate=pl.CostEstimate(flops=flops, bytes_accessed=nbytes, transcendentals=trans),
    )


def swap(value, axis, distance):
    size = lax.axis_size(axis)
    return lax.ppermute(value, axis, [(i, i ^ distance) for i in range(size)])


def chosen(number, values):
    total = values[0]
    for i in range(1, len(values)):
        total = jnp.where(number == i, values[i], total)
    return total


def blocks_of(owner):
    table = [
        [0 if s == r else 1 + [to[s] for to in SENDS].index(r) for s in range(DIRECT)]
        for r in range(DIRECT)
    ]
    return [chosen(owner, [row[s] for row in table]) for s in range(DIRECT)]


def block_of(sender, owner, direct):
    if not direct:
        return sender
    places = blocks_of(owner)
    return places[sender] if isinstance(sender, int) else chosen(sender, places)


def all_of(copies):
    for copy in copies:
        copy.start()
    for copy in copies:
        copy.wait()


def read_messages(refs):
    return [ref[i].astype(F32) for ref in refs for i in range(ref.shape[0])]


def in_parts(source, target, sems, first, count):
    rows = source.shape[0] // count
    at = [pl.ds(i * rows, rows) for i in range(count)]
    return [
        pltpu.make_async_copy(source.at[a], target.at[a], sems.at[first + i])
        for i, a in enumerate(at)
    ]


def scalar_onehot(senders_s, owner, shape, direct):
    row_of = lax.broadcasted_iota(jnp.int32, shape, 0)
    wanted = jnp.zeros(shape, jnp.int32)
    for b in range(shape[0]):
        wanted = jnp.where(row_of == b, senders_s[b], wanted)
    wanted = block_of(wanted, owner, direct)
    return (wanted == lax.broadcasted_iota(jnp.int32, shape, 1)).astype(F32)


def pick_rows(pick, rows):
    total = pick[:, 0:1] * rows[0]
    for k in range(1, len(rows)):
        total = total + pick[:, k : k + 1] * rows[k]
    return total


def pack_kernel(direct, owner_hbm, rows_hbm, prompt_hbm, step_hbm, conv_hbm, ssm_hbm, *rest):
    outs, (owner_s, rows_s, prompt_s, step, conv, ssm, sems) = rest[:-7], rest[-7:]
    owners = rows_hbm.shape[0]
    channels = step_hbm.shape[3]
    copies = [
        pltpu.make_async_copy(owner_hbm, owner_s, sems.at[4]),
        pltpu.make_async_copy(rows_hbm, rows_s, sems.at[0]),
        pltpu.make_async_copy(prompt_hbm, prompt_s, sems.at[1]),
        pltpu.make_async_copy(conv_hbm, conv, sems.at[2]),
        pltpu.make_async_copy(ssm_hbm, ssm, sems.at[3]),
    ]
    all_of(copies + in_parts(step_hbm, step, sems, 5, STEP_PARTS))
    owner = owner_s[0]
    window = conv[0].astype(F32)

    def write(ref, target):
        row = jnp.maximum(rows_s[target], 0)
        xs = step[row, :, 0, :].astype(F32)
        number = prompt_s[row].astype(F32)
        pieces = [xs, window, jnp.full((1, channels), number, F32)]
        if ref.shape[0] > sum(p.shape[0] for p in pieces):
            pieces.append(ssm[0])
        ref[...] = jnp.concatenate(pieces, axis=0).astype(BF16)

    if direct:
        write(outs[0].at[0], owner)
        for ref, to in zip(outs[1:], SENDS):
            write(ref.at[0], chosen(owner, to))
    else:
        for target in range(owners):
            write(outs[0].at[target], target)


def pair_kernel(text, ssm_ref, came_ref, after_ref, pair_ref):
    del after_ref
    state = ssm_ref[0]
    head = state.astype(BF16).astype(F32)
    came = came_ref[0].astype(F32)[text:, :]
    pair_ref[0] = jnp.concatenate([head, state - head, came], axis=0).astype(BF16)


def silu(v):
    return v / (1.0 + jnp.exp(-v))


def prepare_kernel(
    direct,
    owner_hbm,
    prompt_hbm,
    child_hbm,
    step_hbm,
    cw_hbm,
    cb_hbm,
    xwt_hbm,
    alog_hbm,
    dtb_hbm,
    skip_hbm,
    after_ref,
    base_ref,
    gate_ref,
    pick_ref,
    child_ref,
    sender_ref,
    cw_ref,
    cb_ref,
    xwt_ref,
    rate_ref,
    twin_ref,
    dtb_ref,
    skip_ref,
    step_ref,
    owner_s,
    prompt_s,
    child_s,
    alog,
    sems,
):
    del after_ref
    small = [
        pltpu.make_async_copy(source, target, sems.at[i])
        for i, (source, target) in enumerate(
            (
                (cw_hbm, cw_ref),
                (cb_hbm, cb_ref),
                (owner_hbm, owner_s),
                (prompt_hbm, prompt_s),
                (child_hbm, child_s),
                (alog_hbm, alog),
                (dtb_hbm, dtb_ref),
                (skip_hbm, skip_ref),
            )
        )
    ]
    inputs = in_parts(step_hbm, step_ref, sems, len(small), STEP_PARTS)
    large = in_parts(xwt_hbm, xwt_ref, sems, len(small) + STEP_PARTS, WEIGHT_PARTS)
    for copy in inputs + small + large:
        copy.start()
    for copy in inputs:
        copy.wait()
    steps = step_ref.shape[1]
    taps = cw_hbm.shape[0]
    xs = [step_ref[:, t, 0, :].astype(F32) for t in range(steps)]
    for t in range(steps):
        gate_ref[t] = silu(step_ref[:, t, 1, :].astype(F32))
    for copy in small:
        copy.wait()
    for t in range(steps):
        total = cw_ref[taps - 1 : taps, :] * xs[t] + cb_ref[...]
        for k in range(max(0, taps - 1 - t), taps - 1):
            total = total + cw_ref[k : k + 1, :] * xs[t + k - taps + 1]
        base_ref[t] = total
    pick_ref[...] = scalar_onehot(prompt_s, owner_s[0], pick_ref.shape, direct)
    child_ref[...] = scalar_onehot(child_s, owner_s[0], child_ref.shape, direct)
    column = lax.broadcasted_iota(jnp.int32, sender_ref.shape, 1)
    sender = column
    for sent in range(sender_ref.shape[1] if direct else 0):
        sender = jnp.where(column == block_of(sent, owner_s[0], direct), sent, sender)
    sender_ref[...] = sender.astype(F32)
    rate = jnp.exp(alog[...]) * (-math.log2(math.e))
    rate_ref[...] = rate
    half = (twin_ref.shape[1] // 2, rate.shape[1])
    for m in range(rate.shape[0] // 2):
        two = [jnp.broadcast_to(rate[n : n + 1, :], half) for n in (2 * m, 2 * m + 1)]
        twin_ref[m] = jnp.concatenate(two, axis=0)
    for copy in large:
        copy.wait()


def slot_onehot(numbers, sender_ref):
    owners = sender_ref.shape[1]
    return (numbers[:, :owners] == sender_ref[...]).astype(F32)


def project_kernel(n_msgs, pick_ref, sender_ref, base_ref, cw_ref, cb_ref, xwt_ref, *rest):
    msgs, (act_ref, part_ref, short_ref) = rest[:n_msgs], rest[n_msgs:]
    taps = cw_ref.shape[0]
    steps, rb, _ = base_ref.shape
    past = taps - 1
    held = read_messages(msgs)
    owners = len(held)
    windows = [[h[steps + k : steps + k + 1, :] for h in held] for k in range(past)]
    own = pick_ref[...]
    own_windows = [pick_rows(own, w) for w in windows]
    for t in range(steps):
        conv = base_ref[t]
        for k in range(past - t):
            conv = conv + cw_ref[k : k + 1, :] * own_windows[t + k]
        act_ref[t * rb : (t + 1) * rb, :] = silu(conv)

    def line_of(row):
        return jnp.concatenate([h[row : row + 1, :] for h in held], axis=0)

    slot = slot_onehot(line_of(past + steps), sender_ref)
    line = [pick_rows(slot, w) for w in windows]
    line += [line_of(t) for t in range(steps)]
    row = steps * rb
    for t in range(steps):
        conv = cw_ref[past:taps, :] * line[t + past] + cb_ref[...]
        for k in range(past):
            conv = conv + cw_ref[k : k + 1, :] * line[t + k]
        act_ref[row : row + owners, :] = silu(conv)
        row += owners
    part = lax.dot_general(
        act_ref[...].astype(BF16),
        xwt_ref[...],
        (((1,), (1,)), ((), ())),
        preferred_element_type=F32,
    )
    part_ref[...] = part
    short_ref[...] = part.astype(BF16)


def add_kernel(a_ref, b_ref, sum_ref, short_ref):
    total = a_ref[...] + b_ref[...].astype(F32)
    sum_ref[...] = total
    short_ref[...] = total.astype(BF16)


def windows_kernel(n_msgs, steps, child_ref, after_ref, *rest):
    del after_ref
    msgs, (conv_ref,) = rest[:n_msgs], rest[n_msgs:]
    held = read_messages(msgs)
    past = conv_ref.shape[0]
    for k in range(past):
        at = steps - past + k
        rows = [h[at : at + 1, :] for h in held]
        conv_ref[k] = pick_rows(child_ref[...], rows).astype(BF16)


def start_kernel(n_msgs, direct, text, pick_ref, sender_ref, after_ref, *rest):
    del after_ref
    msgs, rest = rest[:n_msgs], rest[n_msgs:]
    apart, (own_ref, slot_ref, state_s) = rest[:-3], rest[-3:]
    n_state = own_ref.shape[0]
    held = read_messages(msgs)
    owners = len(held)
    numbers = jnp.concatenate([h[text - 1 : text, :] for h in held], axis=0)
    states = [h[text:, :] for h in held]
    if direct:
        ssm_ref, pair_ref = apart
        head, low, came = [
            pair_ref[0].astype(F32)[i * n_state : (i + 1) * n_state, :] for i in range(3)
        ]
        states[0], states[2], states[3] = ssm_ref[0], came, head + low
    for k, state in enumerate(states):
        state_s[k] = state
    own = pick_ref[...]
    slot = slot_onehot(numbers, sender_ref)

    def two(m, carry):
        picked = []
        for n in (2 * m, 2 * m + 1):
            rows = [state_s[k, pl.ds(n, 1), :] for k in range(owners)]
            own_ref[n] = pick_rows(own, rows)
            picked.append(pick_rows(slot, rows))
        slot_ref[m] = jnp.concatenate(picked, axis=0)
        return carry

    lax.fori_loop(0, n_state // 2, two, 0, unroll=owners <= DIRECT)


def decode_kernel(
    direct,
    owner_hbm,
    child_hbm,
    act_ref,
    gate_ref,
    own_ref,
    slot_ref,
    rate_ref,
    twin_ref,
    dtw_ref,
    dtb_ref,
    skip_ref,
    part_ref,
    other_ref,
    dec_ref,
    child_ssm,
    owner_s,
    child_s,
    delta_s,
    gain_s,
    slot_delta_s,
    slot_gain_s,
    b_s,
    c_s,
    twin_b_s,
    slots_s,
    line_s,
    sems,
):
    scalars = [
        pltpu.make_async_copy(owner_hbm, owner_s, sems.at[0]),
        pltpu.make_async_copy(child_hbm, child_s, sems.at[1]),
    ]
    for copy in scalars:
        copy.start()
    rb, steps, channels = dec_ref.shape
    rank = dtw_ref.shape[0]
    n_state = rate_ref.shape[0]
    n_slots = slots_s.shape[0]
    own_rows = steps * rb
    chunks = channels // (WIDE * LANES)

    def sums_of(rows):
        proj = part_ref[rows, :] + other_ref[rows, :].astype(F32)
        delta_in = proj[:, :rank].astype(BF16)
        delta = jnp.dot(delta_in, dtw_ref[...], preferred_element_type=F32) + dtb_ref[...]
        delta = jnp.maximum(delta, 0.0) + jnp.log(1.0 + jnp.exp(-jnp.abs(delta)))
        return proj, delta, delta * act_ref[rows, :]

    def column(at, n, rows):
        return jnp.broadcast_to(at[:, n : n + 1], (rows, LANES))

    proj, delta, gain = sums_of(slice(own_rows, own_rows + steps * n_slots))
    for t in range(steps):
        at = slice(t * n_slots, (t + 1) * n_slots)
        slot_delta_s[t] = jnp.concatenate([delta[at, :]] * 2, axis=0)
        slot_gain_s[t] = jnp.concatenate([gain[at, :]] * 2, axis=0)
        twice = jnp.concatenate([proj[at, rank:]] * 2, axis=0)
        upper = lax.broadcasted_iota(jnp.int32, (2 * n_slots, LANES), 0) < n_slots
        for m in range(n_state // 2):
            twin_b_s[m, t] = jnp.where(
                upper, column(twice, 2 * m, 2 * n_slots), column(twice, 2 * m + 1, 2 * n_slots)
            )

    def wide(part):
        return jnp.concatenate([part] * WIDE, axis=1)

    def slot_chunk(chunk, carry):
        columns = pl.ds(pl.multiple_of(chunk * WIDE * LANES, WIDE * LANES), WIDE * LANES)
        delta = [slot_delta_s[t, :, columns] for t in range(steps)]
        gain = [slot_gain_s[t, :, columns] for t in range(steps)]
        for m in range(n_state // 2):
            rate = twin_ref[m, :, columns]
            state = slot_ref[m, :, columns]
            for t in range(steps):
                state = jnp.exp2(delta[t] * rate) * state + gain[t] * wide(twin_b_s[m, t])
            slots_s[:, 2 * m, columns] = state[:n_slots, :]
            slots_s[:, 2 * m + 1, columns] = state[n_slots:, :]
        return carry

    lax.fori_loop(0, chunks, slot_chunk, 0)
    for copy in scalars:
        copy.wait()
    places = blocks_of(owner_s[0]) if direct else None
    copies = []
    for j in range(rb):
        at = chosen(child_s[j], places) if direct else child_s[j]
        copy = pltpu.make_async_copy(slots_s.at[at], child_ssm.at[j], sems.at[2 + j])
        copy.start()
        copies.append(copy)

    proj, delta, gain = sums_of(slice(0, own_rows))
    delta_s[...] = delta
    gain_s[...] = gain
    for n in range(n_state):
        b_s[n] = column(proj[:, rank:], n, own_rows)
        c_s[n] = column(proj[:, rank:], n_state + n, own_rows)

    def own_chunk(chunk, carry):
        columns = pl.ds(pl.multiple_of(chunk * WIDE * LANES, WIDE * LANES), WIDE * LANES)
        for first in range(0, rb, ROWS):
            at = [pl.ds(t * rb + first, ROWS) for t in range(steps)]
            delta = [delta_s[a, columns] for a in at]
            gain = [gain_s[a, columns] for a in at]
            sums = [skip_ref[:, columns] * act_ref[a, columns] for a in at]
            for n in range(n_state):
                rate = rate_ref[n : n + 1, columns]
                state = own_ref[n, pl.ds(first, ROWS), columns]
                for t in range(steps):
                    state = jnp.exp2(delta[t] * rate) * state + gain[t] * wide(b_s[n, at[t], :])
                    sums[t] = sums[t] + wide(c_s[n, at[t], :]) * state
            for t in range(steps):
                out = sums[t] * gate_ref[t, pl.ds(first, ROWS), columns]
                for w in range(WIDE):
                    line_s[w, pl.ds(first * steps + t, ROWS, stride=steps), :] = out[
                        :, w * LANES : (w + 1) * LANES
                    ]
        for w in range(WIDE):
            some = pl.ds(pl.multiple_of((chunk * WIDE + w) * LANES, LANES), LANES)
            dec_ref[:, :, some] = line_s[w].reshape(rb, steps, LANES).astype(BF16)
        return carry

    lax.fori_loop(0, chunks, own_chunk, 0)
    for copy in copies:
        copy.wait()


def on_device(
    prompt_ssm,
    prompt_conv,
    prompt_of,
    step_in,
    conv_weight,
    conv_bias,
    x_weight,
    dt_weight,
    dt_bias,
    a_log,
    skip,
    send_rows,
    child_slot,
):
    owners = lax.axis_size("branch")
    tensors = lax.axis_size("tensor")
    assert owners & (owners - 1) == 0 and tensors & (tensors - 1) == 0
    assert prompt_ssm.shape[0] == 1 and send_rows.shape[2] == 1
    rb, steps, _, channels = step_in.shape
    taps = conv_weight.shape[0]
    width = x_weight.shape[1]
    n_state = a_log.shape[0]
    rows = steps * (rb + owners)
    short = taps - 1 + steps + 1
    depth = short + n_state
    direct = owners == DIRECT
    owner = pinned(lax.axis_index("branch").astype(jnp.int32).reshape(1))

    if direct:
        msg_shapes = [(1, d, channels) for d in (short, depth, short, short)]
    else:
        msg_shapes = [(owners, depth, channels)]
    msgs = call(
        functools.partial(pack_kernel, direct),
        [shaped(s, BF16) for s in msg_shapes],
        [hbm()] * 6,
        [vmem()] * len(msg_shapes),
        [
            pltpu.SMEM((1,), jnp.int32),
            pltpu.SMEM((owners,), jnp.int32),
            pltpu.SMEM((rb,), jnp.int32),
            pltpu.VMEM(step_in.shape, BF16),
            pltpu.VMEM(prompt_conv.shape, BF16),
            pltpu.VMEM(prompt_ssm.shape, F32),
            pltpu.SemaphoreType.DMA((5 + STEP_PARTS,)),
        ],
        nbytes=owners * depth * channels * 2,
    )(
        owner,
        pinned(send_rows.reshape(owners)),
        pinned(prompt_of),
        pinned(step_in),
        pinned(prompt_conv),
        pinned(prompt_ssm),
    )
    if direct:
        own = msgs[0]
        msgs = [own] + [
            lax.ppermute(m, "branch", list(enumerate(to))) for m, to in zip(msgs[1:], SENDS)
        ]
        after = own
    else:
        msgs = [lax.all_to_all(msgs[0], "branch", split_axis=0, concat_axis=0, tiled=True)]
        after = msgs[0]
    n_msgs = len(msgs)
    near = call(
        functools.partial(prepare_kernel, direct),
        [
            shaped((steps, rb, channels), F32),
            shaped((steps, rb, channels), F32),
            shaped((rb, owners), F32),
            shaped((rb, owners), F32),
            shaped((1, owners), F32),
            shaped((taps, channels), F32),
            shaped((1, channels), F32),
            shaped((width, channels), BF16),
            shaped((n_state, channels), F32),
            shaped((n_state // 2, 2 * owners, channels), F32),
            shaped((1, channels), F32),
            shaped((1, channels), F32),
        ],
        [hbm()] * 10 + [anywhere()],
        [vmem()] * 12,
        [
            pltpu.VMEM(step_in.shape, BF16),
            pltpu.SMEM((1,), jnp.int32),
            pltpu.SMEM((rb,), jnp.int32),
            pltpu.SMEM((rb,), jnp.int32),
            pltpu.VMEM((n_state, channels), F32),
            pltpu.SemaphoreType.DMA((8 + WEIGHT_PARTS + STEP_PARTS,)),
        ],
        flops=10 * steps * rb * channels,
        nbytes=12 * steps * rb * channels,
        trans=steps * rb * channels,
    )(
        owner,
        pinned(prompt_of),
        pinned(child_slot),
        pinned(step_in),
        pinned(conv_weight),
        pinned(conv_bias[None]),
        pinned(x_weight.T),
        pinned(a_log),
        pinned(dt_bias[None]),
        pinned(skip[None]),
        after,
    )
    base, gate, pick, child_pick, sender, taps_near, bias_near, weight_near = near[:8]
    rate, twin, dtb_near, skip_near = near[8:]
    states = []
    if direct:
        pair = call(
            functools.partial(pair_kernel, short),
            shaped((1, 3 * n_state, channels), BF16),
            [vmem()] * 2 + [anywhere()],
            vmem(),
            nbytes=12 * n_state * channels,
        )(prompt_ssm, msgs[1], pick)
        states = [prompt_ssm, swap(pair, "branch", 1)]
    act, part, brief = call(
        functools.partial(project_kernel, n_msgs),
        [
            shaped((rows, channels), F32),
            shaped((rows, width), F32),
            shaped((rows, width), BF16),
        ],
        [vmem()] * (6 + n_msgs),
        [vmem()] * 3,
        flops=2 * rows * channels * width,
        nbytes=channels * width * 2 + rows * (channels + width) * 4,
        trans=rows * channels,
    )(pick, sender, base, taps_near, bias_near, weight_near, *msgs)
    other = swap(brief, "tensor", 1)
    distance = 2
    while distance < tensors:
        part, brief = call(
            add_kernel,
            [shaped((rows, width), F32), shaped((rows, width), BF16)],
            [vmem()] * 2,
            [vmem()] * 2,
            flops=rows * width,
            nbytes=rows * width * 14,
        )(part, other)
        other = swap(brief, "tensor", 2 * distance - 1)
        distance *= 2

    child_conv = call(
        functools.partial(windows_kernel, n_msgs, steps),
        shaped((taps - 1, rb, channels), BF16),
        [vmem(), anywhere()] + [vmem()] * n_msgs,
        vmem(),
        flops=2 * owners * taps * rb * channels,
        nbytes=4 * taps * rb * channels,
    )(child_pick, part, *msgs)
    own_start, slot_start = call(
        functools.partial(start_kernel, n_msgs, direct, short),
        [
            shaped((n_state, rb, channels), F32),
            shaped((n_state // 2, 2 * owners, channels), F32),
        ],
        [vmem()] * 2 + [anywhere()] + [vmem()] * (n_msgs + len(states)),
        [vmem()] * 2,
        [pltpu.VMEM((owners, n_state, channels), F32)],
        flops=2 * owners * n_state * (rb + owners) * channels,
        nbytes=4 * n_state * (rb + owners) * channels,
    )(pick, sender, part, *msgs, *states)

    decoded, child_ssm = call(
        functools.partial(decode_kernel, direct),
        [
            shaped((rb, steps, channels), BF16),
            shaped((rb, n_state, channels), F32),
        ],
        [hbm()] * 2 + [vmem()] * 11,
        [vmem(), anywhere()],
        [
            pltpu.SMEM((1,), jnp.int32),
            pltpu.SMEM((rb,), jnp.int32),
            pltpu.VMEM((steps * rb, channels), F32),
            pltpu.VMEM((steps * rb, channels), F32),
            pltpu.VMEM((steps, 2 * owners, channels), F32),
            pltpu.VMEM((steps, 2 * owners, channels), F32),
            pltpu.VMEM((n_state, steps * rb, LANES), F32),
            pltpu.VMEM((n_state, steps * rb, LANES), F32),
            pltpu.VMEM((n_state // 2, steps, 2 * owners, LANES), F32),
            pltpu.VMEM((owners, n_state, channels), F32),
            pltpu.VMEM((WIDE, steps * rb, LANES), F32),
            pltpu.SemaphoreType.DMA((2 + rb,)),
        ],
        flops=8 * rows * n_state * channels,
        nbytes=(rb + owners) * n_state * channels * 4,
        trans=rows * n_state * channels,
    )(
        owner,
        pinned(child_slot),
        act,
        gate,
        own_start,
        slot_start,
        rate,
        twin,
        dt_weight,
        dtb_near,
        skip_near,
        part,
        other,
    )
    return (decoded, child_ssm, jnp.transpose(child_conv, (1, 0, 2)))


def solution(mesh):
    placed = (
        P(("replica", "branch"), None, "tensor"),
        P(("replica", "branch"), None, "tensor"),
        P(("replica", "branch")),
        P(("replica", "branch"), None, None, "tensor"),
        P(None, "tensor"),
        P("tensor"),
        P("tensor", None),
        P(None, "tensor"),
        P("tensor"),
        P(None, "tensor"),
        P("tensor"),
        P(("replica", "branch"), None, None),
        P(("replica", "branch")),
    )
    return jax.shard_map(
        on_device,
        mesh=mesh,
        in_specs=placed,
        out_specs=(
            P(("replica", "branch"), None, "tensor"),
            P(("replica", "branch"), None, "tensor"),
            P(("replica", "branch"), None, "tensor"),
        ),
        check_vma=False,
    )
```

```python
import functools
import math

import jax
import jax.numpy as jnp
from jax import lax
from jax.experimental import pallas as pl
from jax.experimental.pallas import tpu as pltpu
from jax.sharding import PartitionSpec as P

F32 = jnp.float32
BF16 = jnp.bfloat16
LANES = 128
ROWS = 8
WIDE = 2
VMEM_LIMIT = 48 * 2**20
WEIGHT_PARTS = 6
STEP_PARTS = 4
DIRECT = 4
SENDS = ((2, 3, 1, 0), (3, 2, 0, 1), (1, 0, 3, 2))


def vmem():
    return pl.BlockSpec(memory_space=pltpu.VMEM)


def hbm():
    return pl.BlockSpec(memory_space=pltpu.HBM)


def anywhere():
    return pl.BlockSpec(memory_space=pl.ANY)


def pinned(array):
    return pltpu.with_memory_space_constraint(array, pltpu.HBM)


def shaped(shape, dtype):
    return jax.ShapeDtypeStruct(shape, dtype)


def call(kernel, outs, in_specs, out_specs, scratch=(), flops=0, nbytes=0, trans=0):
    return pl.pallas_call(
        kernel,
        out_shape=outs,
        in_specs=in_specs,
        out_specs=out_specs,
        scratch_shapes=list(scratch),
        compiler_params=pltpu.CompilerParams(vmem_limit_bytes=VMEM_LIMIT),
        cost_estimate=pl.CostEstimate(flops=flops, bytes_accessed=nbytes, transcendentals=trans),
    )


def swap(value, axis, distance):
    size = lax.axis_size(axis)
    return lax.ppermute(value, axis, [(i, i ^ distance) for i in range(size)])


def chosen(number, values):
    total = values[0]
    for i in range(1, len(values)):
        total = jnp.where(number == i, values[i], total)
    return total


def blocks_of(owner):
    table = [
        [0 if s == r else 1 + [to[s] for to in SENDS].index(r) for s in range(DIRECT)]
        for r in range(DIRECT)
    ]
    return [chosen(owner, [row[s] for row in table]) for s in range(DIRECT)]


def block_of(sender, owner, direct):
    if not direct:
        return sender
    places = blocks_of(owner)
    return places[sender] if isinstance(sender, int) else chosen(sender, places)


def all_of(copies):
    for copy in copies:
        copy.start()
    for copy in copies:
        copy.wait()


def read_messages(refs):
    return [ref[i].astype(F32) for ref in refs for i in range(ref.shape[0])]


def in_parts(source, target, sems, first, count):
    rows = source.shape[0] // count
    at = [pl.ds(i * rows, rows) for i in range(count)]
    return [
        pltpu.make_async_copy(source.at[a], target.at[a], sems.at[first + i])
        for i, a in enumerate(at)
    ]


def scalar_onehot(senders_s, owner, shape, direct):
    row_of = lax.broadcasted_iota(jnp.int32, shape, 0)
    wanted = jnp.zeros(shape, jnp.int32)
    for b in range(shape[0]):
        wanted = jnp.where(row_of == b, senders_s[b], wanted)
    wanted = block_of(wanted, owner, direct)
    return (wanted == lax.broadcasted_iota(jnp.int32, shape, 1)).astype(F32)


def pick_rows(pick, rows):
    total = pick[:, 0:1] * rows[0]
    for k in range(1, len(rows)):
        total = total + pick[:, k : k + 1] * rows[k]
    return total


def pack_kernel(direct, owner_hbm, rows_hbm, prompt_hbm, step_hbm, conv_hbm, ssm_hbm, *rest):
    outs, (owner_s, rows_s, prompt_s, step, conv, ssm, sems) = rest[:-7], rest[-7:]
    owners = rows_hbm.shape[0]
    channels = step_hbm.shape[3]
    copies = [
        pltpu.make_async_copy(owner_hbm, owner_s, sems.at[4]),
        pltpu.make_async_copy(rows_hbm, rows_s, sems.at[0]),
        pltpu.make_async_copy(prompt_hbm, prompt_s, sems.at[1]),
        pltpu.make_async_copy(conv_hbm, conv, sems.at[2]),
        pltpu.make_async_copy(ssm_hbm, ssm, sems.at[3]),
    ]
    all_of(copies + in_parts(step_hbm, step, sems, 5, STEP_PARTS))
    owner = owner_s[0]
    window = conv[0].astype(F32)

    def write(ref, target):
        row = jnp.maximum(rows_s[target], 0)
        xs = step[row, :, 0, :].astype(F32)
        number = prompt_s[row].astype(F32)
        pieces = [xs, window, jnp.full((1, channels), number, F32)]
        if ref.shape[0] > sum(p.shape[0] for p in pieces):
            pieces.append(ssm[0])
        ref[...] = jnp.concatenate(pieces, axis=0).astype(BF16)

    if direct:
        write(outs[0].at[0], owner)
        for ref, to in zip(outs[1:], SENDS):
            write(ref.at[0], chosen(owner, to))
    else:
        for target in range(owners):
            write(outs[0].at[target], target)


def pair_kernel(text, ssm_ref, came_ref, after_ref, pair_ref):
    del after_ref
    state = ssm_ref[0]
    head = state.astype(BF16).astype(F32)
    came = came_ref[0].astype(F32)[text:, :]
    pair_ref[0] = jnp.concatenate([head, state - head, came], axis=0).astype(BF16)


def silu(v):
    return v / (1.0 + jnp.exp(-v))


def prepare_kernel(
    direct,
    owner_hbm,
    prompt_hbm,
    child_hbm,
    step_hbm,
    cw_hbm,
    cb_hbm,
    xwt_hbm,
    alog_hbm,
    dtb_hbm,
    skip_hbm,
    after_ref,
    base_ref,
    gate_ref,
    pick_ref,
    child_ref,
    sender_ref,
    cw_ref,
    cb_ref,
    xwt_ref,
    rate_ref,
    twin_ref,
    dtb_ref,
    skip_ref,
    step_ref,
    owner_s,
    prompt_s,
    child_s,
    alog,
    sems,
):
    del after_ref
    small = [
        pltpu.make_async_copy(source, target, sems.at[i])
        for i, (source, target) in enumerate(
            (
                (cw_hbm, cw_ref),
                (cb_hbm, cb_ref),
                (owner_hbm, owner_s),
                (prompt_hbm, prompt_s),
                (child_hbm, child_s),
                (alog_hbm, alog),
                (dtb_hbm, dtb_ref),
                (skip_hbm, skip_ref),
            )
        )
    ]
    inputs = in_parts(step_hbm, step_ref, sems, len(small), STEP_PARTS)
    large = in_parts(xwt_hbm, xwt_ref, sems, len(small) + STEP_PARTS, WEIGHT_PARTS)
    for copy in inputs + small + large:
        copy.start()
    for copy in inputs:
        copy.wait()
    steps = step_ref.shape[1]
    taps = cw_hbm.shape[0]
    xs = [step_ref[:, t, 0, :].astype(F32) for t in range(steps)]
    for t in range(steps):
        gate_ref[t] = silu(step_ref[:, t, 1, :].astype(F32))
    for copy in small:
        copy.wait()
    for t in range(steps):
        total = cw_ref[taps - 1 : taps, :] * xs[t] + cb_ref[...]
        for k in range(max(0, taps - 1 - t), taps - 1):
            total = total + cw_ref[k : k + 1, :] * xs[t + k - taps + 1]
        base_ref[t] = total
    pick_ref[...] = scalar_onehot(prompt_s, owner_s[0], pick_ref.shape, direct)
    child_ref[...] = scalar_onehot(child_s, owner_s[0], child_ref.shape, direct)
    column = lax.broadcasted_iota(jnp.int32, sender_ref.shape, 1)
    sender = column
    for sent in range(sender_ref.shape[1] if direct else 0):
        sender = jnp.where(column == block_of(sent, owner_s[0], direct), sent, sender)
    sender_ref[...] = sender.astype(F32)
    rate = jnp.exp(alog[...]) * (-math.log2(math.e))
    rate_ref[...] = rate
    half = (twin_ref.shape[1] // 2, rate.shape[1])
    for m in range(rate.shape[0] // 2):
        two = [jnp.broadcast_to(rate[n : n + 1, :], half) for n in (2 * m, 2 * m + 1)]
        twin_ref[m] = jnp.concatenate(two, axis=0)
    for copy in large:
        copy.wait()


def slot_onehot(numbers, sender_ref):
    owners = sender_ref.shape[1]
    return (numbers[:, :owners] == sender_ref[...]).astype(F32)


def project_kernel(n_msgs, pick_ref, sender_ref, base_ref, cw_ref, cb_ref, xwt_ref, *rest):
    msgs, (act_ref, part_ref, short_ref) = rest[:n_msgs], rest[n_msgs:]
    taps = cw_ref.shape[0]
    steps, rb, _ = base_ref.shape
    past = taps - 1
    held = read_messages(msgs)
    owners = len(held)
    windows = [[h[steps + k : steps + k + 1, :] for h in held] for k in range(past)]
    own = pick_ref[...]
    own_windows = [pick_rows(own, w) for w in windows]
    for t in range(steps):
        conv = base_ref[t]
        for k in range(past - t):
            conv = conv + cw_ref[k : k + 1, :] * own_windows[t + k]
        act_ref[t * rb : (t + 1) * rb, :] = silu(conv)

    def line_of(row):
        return jnp.concatenate([h[row : row + 1, :] for h in held], axis=0)

    slot = slot_onehot(line_of(past + steps), sender_ref)
    line = [pick_rows(slot, w) for w in windows]
    line += [line_of(t) for t in range(steps)]
    row = steps * rb
    for t in range(steps):
        conv = cw_ref[past:taps, :] * line[t + past] + cb_ref[...]
        for k in range(past):
            conv = conv + cw_ref[k : k + 1, :] * line[t + k]
        act_ref[row : row + owners, :] = silu(conv)
        row += owners
    part = lax.dot_general(
        act_ref[...].astype(BF16),
        xwt_ref[...],
        (((1,), (1,)), ((), ())),
        preferred_element_type=F32,
    )
    part_ref[...] = part
    short_ref[...] = part.astype(BF16)


def add_kernel(a_ref, b_ref, after_ref, sum_ref, short_ref):
    del after_ref
    total = a_ref[...] + b_ref[...].astype(F32)
    sum_ref[...] = total
    short_ref[...] = total.astype(BF16)


def windows_kernel(n_msgs, steps, child_ref, after_ref, *rest):
    del after_ref
    msgs, (conv_ref,) = rest[:n_msgs], rest[n_msgs:]
    held = read_messages(msgs)
    past = conv_ref.shape[0]
    for k in range(past):
        at = steps - past + k
        rows = [h[at : at + 1, :] for h in held]
        conv_ref[k] = pick_rows(child_ref[...], rows).astype(BF16)


def start_kernel(n_msgs, direct, text, pick_ref, sender_ref, after_ref, *rest):
    del after_ref
    msgs, rest = rest[:n_msgs], rest[n_msgs:]
    apart, (own_ref, slot_ref, state_s) = rest[:-3], rest[-3:]
    n_state = own_ref.shape[0]
    held = read_messages(msgs)
    owners = len(held)
    numbers = jnp.concatenate([h[text - 1 : text, :] for h in held], axis=0)
    states = [h[text:, :] for h in held]
    if direct:
        ssm_ref, pair_ref = apart
        head, low, came = [
            pair_ref[0].astype(F32)[i * n_state : (i + 1) * n_state, :] for i in range(3)
        ]
        states[0], states[2], states[3] = ssm_ref[0], came, head + low
    for k, state in enumerate(states):
        state_s[k] = state
    own = pick_ref[...]
    slot = slot_onehot(numbers, sender_ref)

    def two(m, carry):
        picked = []
        for n in (2 * m, 2 * m + 1):
            rows = [state_s[k, pl.ds(n, 1), :] for k in range(owners)]
            own_ref[n] = pick_rows(own, rows)
            picked.append(pick_rows(slot, rows))
        slot_ref[m] = jnp.concatenate(picked, axis=0)
        return carry

    lax.fori_loop(0, n_state // 2, two, 0, unroll=owners <= DIRECT)


def decode_kernel(
    direct,
    owner_hbm,
    child_hbm,
    act_ref,
    gate_ref,
    own_ref,
    slot_ref,
    rate_ref,
    twin_ref,
    dtw_ref,
    dtb_ref,
    skip_ref,
    part_ref,
    other_ref,
    dec_ref,
    child_ssm,
    owner_s,
    child_s,
    delta_s,
    gain_s,
    slot_delta_s,
    slot_gain_s,
    b_s,
    c_s,
    twin_b_s,
    slots_s,
    line_s,
    sems,
):
    scalars = [
        pltpu.make_async_copy(owner_hbm, owner_s, sems.at[0]),
        pltpu.make_async_copy(child_hbm, child_s, sems.at[1]),
    ]
    for copy in scalars:
        copy.start()
    rb, steps, channels = dec_ref.shape
    rank = dtw_ref.shape[0]
    n_state = rate_ref.shape[0]
    n_slots = slots_s.shape[0]
    own_rows = steps * rb
    chunks = channels // (WIDE * LANES)

    proj = part_ref[...] + other_ref[...].astype(F32)
    delta_in = proj[:, :rank].astype(BF16)
    delta = jnp.dot(delta_in, dtw_ref[...], preferred_element_type=F32) + dtb_ref[...]
    delta = jnp.maximum(delta, 0.0) + jnp.log(1.0 + jnp.exp(-jnp.abs(delta)))
    gain = delta * act_ref[...]
    delta_s[...] = delta[:own_rows, :]
    gain_s[...] = gain[:own_rows, :]

    def column(at, n, rows):
        return jnp.broadcast_to(at[:, n : n + 1], (rows, LANES))

    for t in range(steps):
        at = slice(own_rows + t * n_slots, own_rows + (t + 1) * n_slots)
        slot_delta_s[t] = jnp.concatenate([delta[at, :]] * 2, axis=0)
        slot_gain_s[t] = jnp.concatenate([gain[at, :]] * 2, axis=0)
        twice = jnp.concatenate([proj[at, rank:]] * 2, axis=0)
        upper = lax.broadcasted_iota(jnp.int32, (2 * n_slots, LANES), 0) < n_slots
        for m in range(n_state // 2):
            twin_b_s[m, t] = jnp.where(
                upper, column(twice, 2 * m, 2 * n_slots), column(twice, 2 * m + 1, 2 * n_slots)
            )
    for n in range(n_state):
        b_s[n] = column(proj[:own_rows, rank:], n, own_rows)
        c_s[n] = column(proj[:own_rows, rank:], n_state + n, own_rows)

    def wide(part):
        return jnp.concatenate([part] * WIDE, axis=1)

    def slot_chunk(chunk, carry):
        columns = pl.ds(pl.multiple_of(chunk * WIDE * LANES, WIDE * LANES), WIDE * LANES)
        delta = [slot_delta_s[t, :, columns] for t in range(steps)]
        gain = [slot_gain_s[t, :, columns] for t in range(steps)]
        for m in range(n_state // 2):
            rate = twin_ref[m, :, columns]
            state = slot_ref[m, :, columns]
            for t in range(steps):
                state = jnp.exp2(delta[t] * rate) * state + gain[t] * wide(twin_b_s[m, t])
            slots_s[:, 2 * m, columns] = state[:n_slots, :]
            slots_s[:, 2 * m + 1, columns] = state[n_slots:, :]
        return carry

    lax.fori_loop(0, chunks, slot_chunk, 0)
    for copy in scalars:
        copy.wait()
    places = blocks_of(owner_s[0]) if direct else None
    copies = []
    for j in range(rb):
        at = chosen(child_s[j], places) if direct else child_s[j]
        copy = pltpu.make_async_copy(slots_s.at[at], child_ssm.at[j], sems.at[2 + j])
        copy.start()
        copies.append(copy)

    def own_chunk(chunk, carry):
        columns = pl.ds(pl.multiple_of(chunk * WIDE * LANES, WIDE * LANES), WIDE * LANES)
        for first in range(0, rb, ROWS):
            at = [pl.ds(t * rb + first, ROWS) for t in range(steps)]
            delta = [delta_s[a, columns] for a in at]
            gain = [gain_s[a, columns] for a in at]
            sums = [skip_ref[:, columns] * act_ref[a, columns] for a in at]
            for n in range(n_state):
                rate = rate_ref[n : n + 1, columns]
                state = own_ref[n, pl.ds(first, ROWS), columns]
                for t in range(steps):
                    state = jnp.exp2(delta[t] * rate) * state + gain[t] * wide(b_s[n, at[t], :])
                    sums[t] = sums[t] + wide(c_s[n, at[t], :]) * state
            for t in range(steps):
                out = sums[t] * gate_ref[t, pl.ds(first, ROWS), columns]
                for w in range(WIDE):
                    line_s[w, pl.ds(first * steps + t, ROWS, stride=steps), :] = out[
                        :, w * LANES : (w + 1) * LANES
                    ]
        for w in range(WIDE):
            some = pl.ds(pl.multiple_of((chunk * WIDE + w) * LANES, LANES), LANES)
            dec_ref[:, :, some] = line_s[w].reshape(rb, steps, LANES).astype(BF16)
        return carry

    lax.fori_loop(0, chunks, own_chunk, 0)
    for copy in copies:
        copy.wait()


def on_device(
    prompt_ssm,
    prompt_conv,
    prompt_of,
    step_in,
    conv_weight,
    conv_bias,
    x_weight,
    dt_weight,
    dt_bias,
    a_log,
    skip,
    send_rows,
    child_slot,
):
    owners = lax.axis_size("branch")
    tensors = lax.axis_size("tensor")
    assert owners & (owners - 1) == 0 and tensors & (tensors - 1) == 0
    assert prompt_ssm.shape[0] == 1 and send_rows.shape[2] == 1
    rb, steps, _, channels = step_in.shape
    taps = conv_weight.shape[0]
    width = x_weight.shape[1]
    n_state = a_log.shape[0]
    rows = steps * (rb + owners)
    short = taps - 1 + steps + 1
    depth = short + n_state
    direct = owners == DIRECT
    owner = pinned(lax.axis_index("branch").astype(jnp.int32).reshape(1))

    if direct:
        msg_shapes = [(1, d, channels) for d in (short, depth, short, short)]
    else:
        msg_shapes = [(owners, depth, channels)]
    msgs = call(
        functools.partial(pack_kernel, direct),
        [shaped(s, BF16) for s in msg_shapes],
        [hbm()] * 6,
        [vmem()] * len(msg_shapes),
        [
            pltpu.SMEM((1,), jnp.int32),
            pltpu.SMEM((owners,), jnp.int32),
            pltpu.SMEM((rb,), jnp.int32),
            pltpu.VMEM(step_in.shape, BF16),
            pltpu.VMEM(prompt_conv.shape, BF16),
            pltpu.VMEM(prompt_ssm.shape, F32),
            pltpu.SemaphoreType.DMA((5 + STEP_PARTS,)),
        ],
        nbytes=owners * depth * channels * 2,
    )(
        owner,
        pinned(send_rows.reshape(owners)),
        pinned(prompt_of),
        pinned(step_in),
        pinned(prompt_conv),
        pinned(prompt_ssm),
    )
    if direct:
        own = msgs[0]
        msgs = [own] + [
            lax.ppermute(m, "branch", list(enumerate(to))) for m, to in zip(msgs[1:], SENDS)
        ]
        after = own
    else:
        msgs = [lax.all_to_all(msgs[0], "branch", split_axis=0, concat_axis=0, tiled=True)]
        after = msgs[0]
    n_msgs = len(msgs)
    near = call(
        functools.partial(prepare_kernel, direct),
        [
            shaped((steps, rb, channels), F32),
            shaped((steps, rb, channels), F32),
            shaped((rb, owners), F32),
            shaped((rb, owners), F32),
            shaped((1, owners), F32),
            shaped((taps, channels), F32),
            shaped((1, channels), F32),
            shaped((width, channels), BF16),
            shaped((n_state, channels), F32),
            shaped((n_state // 2, 2 * owners, channels), F32),
            shaped((1, channels), F32),
            shaped((1, channels), F32),
        ],
        [hbm()] * 10 + [anywhere()],
        [vmem()] * 12,
        [
            pltpu.VMEM(step_in.shape, BF16),
            pltpu.SMEM((1,), jnp.int32),
            pltpu.SMEM((rb,), jnp.int32),
            pltpu.SMEM((rb,), jnp.int32),
            pltpu.VMEM((n_state, channels), F32),
            pltpu.SemaphoreType.DMA((8 + WEIGHT_PARTS + STEP_PARTS,)),
        ],
        flops=10 * steps * rb * channels,
        nbytes=12 * steps * rb * channels,
        trans=steps * rb * channels,
    )(
        owner,
        pinned(prompt_of),
        pinned(child_slot),
        pinned(step_in),
        pinned(conv_weight),
        pinned(conv_bias[None]),
        pinned(x_weight.T),
        pinned(a_log),
        pinned(dt_bias[None]),
        pinned(skip[None]),
        after,
    )
    base, gate, pick, child_pick, sender, taps_near, bias_near, weight_near = near[:8]
    rate, twin, dtb_near, skip_near = near[8:]
    states = []
    if direct:
        pair = call(
            functools.partial(pair_kernel, short),
            shaped((1, 3 * n_state, channels), BF16),
            [vmem()] * 2 + [anywhere()],
            vmem(),
            nbytes=12 * n_state * channels,
        )(prompt_ssm, msgs[1], pick)
        states = [prompt_ssm, swap(pair, "branch", 1)]
    act, part, brief = call(
        functools.partial(project_kernel, n_msgs),
        [
            shaped((rows, channels), F32),
            shaped((rows, width), F32),
            shaped((rows, width), BF16),
        ],
        [vmem()] * (6 + n_msgs),
        [vmem()] * 3,
        flops=2 * rows * channels * width,
        nbytes=channels * width * 2 + rows * (channels + width) * 4,
        trans=rows * channels,
    )(pick, sender, base, taps_near, bias_near, weight_near, *msgs)
    other = swap(brief, "tensor", tensors - 1)
    child_conv = call(
        functools.partial(windows_kernel, n_msgs, steps),
        shaped((taps - 1, rb, channels), BF16),
        [vmem(), anywhere()] + [vmem()] * n_msgs,
        vmem(),
        flops=2 * owners * taps * rb * channels,
        nbytes=4 * taps * rb * channels,
    )(child_pick, part, *msgs)
    total, distance = part, 1
    while 2 * distance < tensors:
        total, brief = call(
            add_kernel,
            [shaped((rows, width), F32), shaped((rows, width), BF16)],
            [vmem()] * 2 + [anywhere()],
            [vmem()] * 2,
            flops=rows * width,
            nbytes=rows * width * 14,
        )(total, other, child_conv)
        other = swap(brief, "tensor", distance)
        distance *= 2

    own_start, slot_start = call(
        functools.partial(start_kernel, n_msgs, direct, short),
        [
            shaped((n_state, rb, channels), F32),
            shaped((n_state // 2, 2 * owners, channels), F32),
        ],
        [vmem()] * 2 + [anywhere()] + [vmem()] * (n_msgs + len(states)),
        [vmem()] * 2,
        [pltpu.VMEM((owners, n_state, channels), F32)],
        flops=2 * owners * n_state * (rb + owners) * channels,
        nbytes=4 * n_state * (rb + owners) * channels,
    )(pick, sender, total, *msgs, *states)

    decoded, child_ssm = call(
        functools.partial(decode_kernel, direct),
        [
            shaped((rb, steps, channels), BF16),
            shaped((rb, n_state, channels), F32),
        ],
        [hbm()] * 2 + [vmem()] * 11,
        [vmem(), anywhere()],
        [
            pltpu.SMEM((1,), jnp.int32),
            pltpu.SMEM((rb,), jnp.int32),
            pltpu.VMEM((steps * rb, channels), F32),
            pltpu.VMEM((steps * rb, channels), F32),
            pltpu.VMEM((steps, 2 * owners, channels), F32),
            pltpu.VMEM((steps, 2 * owners, channels), F32),
            pltpu.VMEM((n_state, steps * rb, LANES), F32),
            pltpu.VMEM((n_state, steps * rb, LANES), F32),
            pltpu.VMEM((n_state // 2, steps, 2 * owners, LANES), F32),
            pltpu.VMEM((owners, n_state, channels), F32),
            pltpu.VMEM((WIDE, steps * rb, LANES), F32),
            pltpu.SemaphoreType.DMA((2 + rb,)),
        ],
        flops=8 * rows * n_state * channels,
        nbytes=(rb + owners) * n_state * channels * 4,
        trans=rows * n_state * channels,
    )(
        owner,
        pinned(child_slot),
        act,
        gate,
        own_start,
        slot_start,
        rate,
        twin,
        dt_weight,
        dtb_near,
        skip_near,
        total,
        other,
    )
    return (decoded, child_ssm, jnp.transpose(child_conv, (1, 0, 2)))


def solution(mesh):
    placed = (
        P(("replica", "branch"), None, "tensor"),
        P(("replica", "branch"), None, "tensor"),
        P(("replica", "branch")),
        P(("replica", "branch"), None, None, "tensor"),
        P(None, "tensor"),
        P("tensor"),
        P("tensor", None),
        P(None, "tensor"),
        P("tensor"),
        P(None, "tensor"),
        P("tensor"),
        P(("replica", "branch"), None, None),
        P(("replica", "branch")),
    )
    return jax.shard_map(
        on_device,
        mesh=mesh,
        in_specs=placed,
        out_specs=(
            P(("replica", "branch"), None, "tensor"),
            P(("replica", "branch"), None, "tensor"),
            P(("replica", "branch"), None, "tensor"),
        ),
        check_vma=False,
    )
```

```python
import functools
import math

import jax
import jax.numpy as jnp
from jax import lax
from jax.experimental import pallas as pl
from jax.experimental.pallas import tpu as pltpu
from jax.sharding import PartitionSpec as P

F32 = jnp.float32
BF16 = jnp.bfloat16
LANES = 128
ROWS = 8
WIDE = 2
VMEM_LIMIT = 48 * 2**20
WEIGHT_PARTS = 6
STEP_PARTS = 4
DIRECT = 4
SENDS = ((2, 3, 1, 0), (3, 2, 0, 1), (1, 0, 3, 2))


def vmem():
    return pl.BlockSpec(memory_space=pltpu.VMEM)


def hbm():
    return pl.BlockSpec(memory_space=pltpu.HBM)


def anywhere():
    return pl.BlockSpec(memory_space=pl.ANY)


def pinned(array):
    return pltpu.with_memory_space_constraint(array, pltpu.HBM)


def shaped(shape, dtype):
    return jax.ShapeDtypeStruct(shape, dtype)


def call(kernel, outs, in_specs, out_specs, scratch=(), flops=0, nbytes=0, trans=0):
    return pl.pallas_call(
        kernel,
        out_shape=outs,
        in_specs=in_specs,
        out_specs=out_specs,
        scratch_shapes=list(scratch),
        compiler_params=pltpu.CompilerParams(vmem_limit_bytes=VMEM_LIMIT),
        cost_estimate=pl.CostEstimate(flops=flops, bytes_accessed=nbytes, transcendentals=trans),
    )


def swap(value, axis, distance):
    size = lax.axis_size(axis)
    return lax.ppermute(value, axis, [(i, i ^ distance) for i in range(size)])


def chosen(number, values):
    total = values[0]
    for i in range(1, len(values)):
        total = jnp.where(number == i, values[i], total)
    return total


def blocks_of(owner):
    table = [
        [0 if s == r else 1 + [to[s] for to in SENDS].index(r) for s in range(DIRECT)]
        for r in range(DIRECT)
    ]
    return [chosen(owner, [row[s] for row in table]) for s in range(DIRECT)]


def all_of(copies):
    for copy in copies:
        copy.start()
    for copy in copies:
        copy.wait()


def read_messages(refs):
    return [ref[i].astype(F32) for ref in refs for i in range(ref.shape[0])]


def in_parts(source, target, sems, first, count):
    rows = source.shape[0] // count
    at = [pl.ds(i * rows, rows) for i in range(count)]
    return [
        pltpu.make_async_copy(source.at[a], target.at[a], sems.at[first + i])
        for i, a in enumerate(at)
    ]


def scalar_onehot(senders_s, places, shape):
    row_of = lax.broadcasted_iota(jnp.int32, shape, 0)
    wanted = jnp.zeros(shape, jnp.int32)
    for b in range(shape[0]):
        wanted = jnp.where(row_of == b, senders_s[b], wanted)
    wanted = wanted if places is None else chosen(wanted, places)
    return (wanted == lax.broadcasted_iota(jnp.int32, shape, 1)).astype(F32)


def pick_rows(pick, rows):
    total = pick[:, 0:1] * rows[0]
    for k in range(1, len(rows)):
        total = total + pick[:, k : k + 1] * rows[k]
    return total


def pack_kernel(direct, owner_hbm, rows_hbm, prompt_hbm, step_hbm, conv_hbm, ssm_hbm, *rest):
    outs, (owner_s, rows_s, prompt_s, step, conv, ssm, sems) = rest[:-7], rest[-7:]
    owners = rows_hbm.shape[0]
    channels = step_hbm.shape[3]
    copies = [
        pltpu.make_async_copy(owner_hbm, owner_s, sems.at[4]),
        pltpu.make_async_copy(rows_hbm, rows_s, sems.at[0]),
        pltpu.make_async_copy(prompt_hbm, prompt_s, sems.at[1]),
        pltpu.make_async_copy(conv_hbm, conv, sems.at[2]),
        pltpu.make_async_copy(ssm_hbm, ssm, sems.at[3]),
    ]
    all_of(copies + in_parts(step_hbm, step, sems, 5, STEP_PARTS))
    owner = owner_s[0]
    window = conv[0].astype(F32)

    def write(ref, target):
        row = jnp.maximum(rows_s[target], 0)
        xs = step[row, :, 0, :].astype(F32)
        number = prompt_s[row].astype(F32)
        pieces = [xs, window, jnp.full((1, channels), number, F32)]
        if ref.shape[0] > sum(p.shape[0] for p in pieces):
            pieces.append(ssm[0])
        ref[...] = jnp.concatenate(pieces, axis=0).astype(BF16)

    if direct:
        write(outs[0].at[0], owner)
        for ref, to in zip(outs[1:], SENDS):
            write(ref.at[0], chosen(owner, to))
    else:
        for target in range(owners):
            write(outs[0].at[target], target)


def pair_kernel(text, ssm_ref, came_ref, after_ref, pair_ref):
    del after_ref
    state = ssm_ref[0]
    head = state.astype(BF16).astype(F32)
    came = came_ref[0].astype(F32)[text:, :]
    pair_ref[0] = jnp.concatenate([head, state - head, came], axis=0).astype(BF16)


def silu(v):
    return v / (1.0 + jnp.exp(-v))


def prepare_kernel(
    direct,
    owner_hbm,
    prompt_hbm,
    child_hbm,
    step_hbm,
    cw_hbm,
    cb_hbm,
    xwt_hbm,
    alog_hbm,
    dtb_hbm,
    skip_hbm,
    after_ref,
    base_ref,
    gate_ref,
    pick_ref,
    child_ref,
    sender_ref,
    cw_ref,
    cb_ref,
    xwt_ref,
    rate_ref,
    twin_ref,
    dtb_ref,
    skip_ref,
    step_ref,
    owner_s,
    prompt_s,
    child_s,
    alog,
    sems,
):
    del after_ref
    small = [
        pltpu.make_async_copy(source, target, sems.at[i])
        for i, (source, target) in enumerate(
            (
                (cw_hbm, cw_ref),
                (cb_hbm, cb_ref),
                (owner_hbm, owner_s),
                (prompt_hbm, prompt_s),
                (child_hbm, child_s),
                (alog_hbm, alog),
                (dtb_hbm, dtb_ref),
                (skip_hbm, skip_ref),
            )
        )
    ]
    inputs = in_parts(step_hbm, step_ref, sems, len(small), STEP_PARTS)
    large = in_parts(xwt_hbm, xwt_ref, sems, len(small) + STEP_PARTS, WEIGHT_PARTS)
    for copy in inputs + small + large:
        copy.start()
    for copy in inputs:
        copy.wait()
    steps = step_ref.shape[1]
    taps = cw_hbm.shape[0]
    xs = [step_ref[:, t, 0, :].astype(F32) for t in range(steps)]
    for t in range(steps):
        gate_ref[t] = silu(step_ref[:, t, 1, :].astype(F32))
    for copy in small:
        copy.wait()
    for t in range(steps):
        total = cw_ref[taps - 1 : taps, :] * xs[t] + cb_ref[...]
        for k in range(max(0, taps - 1 - t), taps - 1):
            total = total + cw_ref[k : k + 1, :] * xs[t + k - taps + 1]
        base_ref[t] = total
    places = blocks_of(owner_s[0]) if direct else None
    pick_ref[...] = scalar_onehot(prompt_s, places, pick_ref.shape)
    child_ref[...] = scalar_onehot(child_s, places, child_ref.shape)
    column = lax.broadcasted_iota(jnp.int32, sender_ref.shape, 1)
    sender = column
    for sent, place in enumerate(places or []):
        sender = jnp.where(column == place, sent, sender)
    sender_ref[...] = sender.astype(F32)
    rate = jnp.exp(alog[...]) * (-math.log2(math.e))
    rate_ref[...] = rate
    half = (twin_ref.shape[1] // 2, rate.shape[1])
    for m in range(rate.shape[0] // 2):
        two = [jnp.broadcast_to(rate[n : n + 1, :], half) for n in (2 * m, 2 * m + 1)]
        twin_ref[m] = jnp.concatenate(two, axis=0)
    for copy in large:
        copy.wait()


def slot_onehot(numbers, sender_ref):
    owners = sender_ref.shape[1]
    return (numbers[:, :owners] == sender_ref[...]).astype(F32)


def project_kernel(n_msgs, pick_ref, sender_ref, base_ref, cw_ref, cb_ref, xwt_ref, *rest):
    msgs, (act_ref, part_ref, short_ref) = rest[:n_msgs], rest[n_msgs:]
    taps = cw_ref.shape[0]
    steps, rb, _ = base_ref.shape
    past = taps - 1
    held = read_messages(msgs)
    owners = len(held)
    windows = [[h[steps + k : steps + k + 1, :] for h in held] for k in range(past)]
    own = pick_ref[...]
    own_windows = [pick_rows(own, w) for w in windows]
    for t in range(steps):
        conv = base_ref[t]
        for k in range(past - t):
            conv = conv + cw_ref[k : k + 1, :] * own_windows[t + k]
        act_ref[t * rb : (t + 1) * rb, :] = silu(conv)

    def line_of(row):
        return jnp.concatenate([h[row : row + 1, :] for h in held], axis=0)

    slot = slot_onehot(line_of(past + steps), sender_ref)
    line = [pick_rows(slot, w) for w in windows]
    line += [line_of(t) for t in range(steps)]
    row = steps * rb
    for t in range(steps):
        conv = cw_ref[past:taps, :] * line[t + past] + cb_ref[...]
        for k in range(past):
            conv = conv + cw_ref[k : k + 1, :] * line[t + k]
        act_ref[row : row + owners, :] = silu(conv)
        row += owners
    part = lax.dot_general(
        act_ref[...].astype(BF16),
        xwt_ref[...],
        (((1,), (1,)), ((), ())),
        preferred_element_type=F32,
    )
    part_ref[...] = part
    short_ref[...] = part.astype(BF16)


def add_kernel(a_ref, b_ref, sum_ref, short_ref):
    total = a_ref[...] + b_ref[...].astype(F32)
    sum_ref[...] = total
    short_ref[...] = total.astype(BF16)


def windows_kernel(n_msgs, steps, child_ref, after_ref, *rest):
    del after_ref
    msgs, (conv_ref,) = rest[:n_msgs], rest[n_msgs:]
    held = read_messages(msgs)
    past = conv_ref.shape[0]
    for k in range(past):
        at = steps - past + k
        rows = [h[at : at + 1, :] for h in held]
        conv_ref[k] = pick_rows(child_ref[...], rows).astype(BF16)


def start_kernel(n_msgs, direct, text, pick_ref, sender_ref, after_ref, *rest):
    del after_ref
    msgs, rest = rest[:n_msgs], rest[n_msgs:]
    apart, (own_ref, slot_ref, state_s) = rest[:-3], rest[-3:]
    n_state = own_ref.shape[0]
    held = read_messages(msgs)
    owners = len(held)
    numbers = jnp.concatenate([h[text - 1 : text, :] for h in held], axis=0)
    states = [h[text:, :] for h in held]
    if direct:
        ssm_ref, pair_ref = apart
        head, low, came = [
            pair_ref[0].astype(F32)[i * n_state : (i + 1) * n_state, :] for i in range(3)
        ]
        states[0], states[2], states[3] = ssm_ref[0], came, head + low
    for k, state in enumerate(states):
        state_s[k] = state
    own = pick_ref[...]
    slot = slot_onehot(numbers, sender_ref)

    def two(m, carry):
        picked = []
        for n in (2 * m, 2 * m + 1):
            rows = [state_s[k, pl.ds(n, 1), :] for k in range(owners)]
            own_ref[n] = pick_rows(own, rows)
            picked.append(pick_rows(slot, rows))
        slot_ref[m] = jnp.concatenate(picked, axis=0)
        return carry

    lax.fori_loop(0, n_state // 2, two, 0, unroll=owners <= DIRECT)


def decode_kernel(
    direct,
    owner_hbm,
    child_hbm,
    act_ref,
    gate_ref,
    own_ref,
    slot_ref,
    rate_ref,
    twin_ref,
    dtw_ref,
    dtb_ref,
    skip_ref,
    part_ref,
    other_ref,
    dec_ref,
    child_ssm,
    owner_s,
    child_s,
    delta_s,
    gain_s,
    slot_delta_s,
    slot_gain_s,
    b_s,
    c_s,
    twin_b_s,
    slots_s,
    line_s,
    sems,
):
    scalars = [
        pltpu.make_async_copy(owner_hbm, owner_s, sems.at[0]),
        pltpu.make_async_copy(child_hbm, child_s, sems.at[1]),
    ]
    for copy in scalars:
        copy.start()
    rb, steps, channels = dec_ref.shape
    rank = dtw_ref.shape[0]
    n_state = rate_ref.shape[0]
    n_slots = slots_s.shape[0]
    own_rows = steps * rb
    chunks = channels // (WIDE * LANES)

    proj = part_ref[...] + other_ref[...].astype(F32)
    delta_in = proj[:, :rank].astype(BF16)
    delta = jnp.dot(delta_in, dtw_ref[...], preferred_element_type=F32) + dtb_ref[...]
    delta = jnp.maximum(delta, 0.0) + jnp.log(1.0 + jnp.exp(-jnp.abs(delta)))
    gain = delta * act_ref[...]
    delta_s[...] = delta[:own_rows, :]
    gain_s[...] = gain[:own_rows, :]

    def column(at, n, rows):
        return jnp.broadcast_to(at[:, n : n + 1], (rows, LANES))

    for t in range(steps):
        at = slice(own_rows + t * n_slots, own_rows + (t + 1) * n_slots)
        slot_delta_s[t] = jnp.concatenate([delta[at, :]] * 2, axis=0)
        slot_gain_s[t] = jnp.concatenate([gain[at, :]] * 2, axis=0)
        twice = jnp.concatenate([proj[at, rank:]] * 2, axis=0)
        upper = lax.broadcasted_iota(jnp.int32, (2 * n_slots, LANES), 0) < n_slots
        for m in range(n_state // 2):
            twin_b_s[m, t] = jnp.where(
                upper, column(twice, 2 * m, 2 * n_slots), column(twice, 2 * m + 1, 2 * n_slots)
            )
    for n in range(n_state):
        b_s[n] = column(proj[:own_rows, rank:], n, own_rows)
        c_s[n] = column(proj[:own_rows, rank:], n_state + n, own_rows)

    def wide(part):
        return jnp.concatenate([part] * WIDE, axis=1)

    def slot_chunk(chunk, carry):
        columns = pl.ds(pl.multiple_of(chunk * WIDE * LANES, WIDE * LANES), WIDE * LANES)
        delta = [slot_delta_s[t, :, columns] for t in range(steps)]
        gain = [slot_gain_s[t, :, columns] for t in range(steps)]
        for m in range(n_state // 2):
            rate = twin_ref[m, :, columns]
            state = slot_ref[m, :, columns]
            for t in range(steps):
                state = jnp.exp2(delta[t] * rate) * state + gain[t] * wide(twin_b_s[m, t])
            slots_s[:, 2 * m, columns] = state[:n_slots, :]
            slots_s[:, 2 * m + 1, columns] = state[n_slots:, :]
        return carry

    lax.fori_loop(0, chunks, slot_chunk, 0)
    for copy in scalars:
        copy.wait()
    places = blocks_of(owner_s[0]) if direct else None
    copies = []
    for j in range(rb):
        at = chosen(child_s[j], places) if direct else child_s[j]
        copy = pltpu.make_async_copy(slots_s.at[at], child_ssm.at[j], sems.at[2 + j])
        copy.start()
        copies.append(copy)

    def own_chunk(chunk, carry):
        columns = pl.ds(pl.multiple_of(chunk * WIDE * LANES, WIDE * LANES), WIDE * LANES)
        for first in range(0, rb, ROWS):
            at = [pl.ds(t * rb + first, ROWS) for t in range(steps)]
            delta = [delta_s[a, columns] for a in at]
            gain = [gain_s[a, columns] for a in at]
            sums = [skip_ref[:, columns] * act_ref[a, columns] for a in at]
            for n in range(n_state):
                rate = rate_ref[n : n + 1, columns]
                state = own_ref[n, pl.ds(first, ROWS), columns]
                for t in range(steps):
                    state = jnp.exp2(delta[t] * rate) * state + gain[t] * wide(b_s[n, at[t], :])
                    sums[t] = sums[t] + wide(c_s[n, at[t], :]) * state
            for t in range(steps):
                out = sums[t] * gate_ref[t, pl.ds(first, ROWS), columns]
                for w in range(WIDE):
                    line_s[w, pl.ds(first * steps + t, ROWS, stride=steps), :] = out[
                        :, w * LANES : (w + 1) * LANES
                    ]
        for w in range(WIDE):
            some = pl.ds(pl.multiple_of((chunk * WIDE + w) * LANES, LANES), LANES)
            dec_ref[:, :, some] = line_s[w].reshape(rb, steps, LANES).astype(BF16)
        return carry

    lax.fori_loop(0, chunks, own_chunk, 0)
    for copy in copies:
        copy.wait()


def on_device(
    prompt_ssm,
    prompt_conv,
    prompt_of,
    step_in,
    conv_weight,
    conv_bias,
    x_weight,
    dt_weight,
    dt_bias,
    a_log,
    skip,
    send_rows,
    child_slot,
):
    owners = lax.axis_size("branch")
    tensors = lax.axis_size("tensor")
    assert owners & (owners - 1) == 0 and tensors & (tensors - 1) == 0
    assert prompt_ssm.shape[0] == 1 and send_rows.shape[2] == 1
    rb, steps, _, channels = step_in.shape
    taps = conv_weight.shape[0]
    width = x_weight.shape[1]
    n_state = a_log.shape[0]
    rows = steps * (rb + owners)
    short = taps - 1 + steps + 1
    depth = short + n_state
    direct = owners == DIRECT
    owner = pinned(lax.axis_index("branch").astype(jnp.int32).reshape(1))

    if direct:
        msg_shapes = [(1, d, channels) for d in (short, depth, short, short)]
    else:
        msg_shapes = [(owners, depth, channels)]
    msgs = call(
        functools.partial(pack_kernel, direct),
        [shaped(s, BF16) for s in msg_shapes],
        [hbm()] * 6,
        [vmem()] * len(msg_shapes),
        [
            pltpu.SMEM((1,), jnp.int32),
            pltpu.SMEM((owners,), jnp.int32),
            pltpu.SMEM((rb,), jnp.int32),
            pltpu.VMEM(step_in.shape, BF16),
            pltpu.VMEM(prompt_conv.shape, BF16),
            pltpu.VMEM(prompt_ssm.shape, F32),
            pltpu.SemaphoreType.DMA((5 + STEP_PARTS,)),
        ],
        nbytes=owners * depth * channels * 2,
    )(
        owner,
        pinned(send_rows.reshape(owners)),
        pinned(prompt_of),
        pinned(step_in),
        pinned(prompt_conv),
        pinned(prompt_ssm),
    )
    if direct:
        own = msgs[0]
        msgs = [own] + [
            lax.ppermute(m, "branch", list(enumerate(to))) for m, to in zip(msgs[1:], SENDS)
        ]
        after = own
    else:
        msgs = [lax.all_to_all(msgs[0], "branch", split_axis=0, concat_axis=0, tiled=True)]
        after = msgs[0]
    n_msgs = len(msgs)
    near = call(
        functools.partial(prepare_kernel, direct),
        [
            shaped((steps, rb, channels), F32),
            shaped((steps, rb, channels), F32),
            shaped((rb, owners), F32),
            shaped((rb, owners), F32),
            shaped((1, owners), F32),
            shaped((taps, channels), F32),
            shaped((1, channels), F32),
            shaped((width, channels), BF16),
            shaped((n_state, channels), F32),
            shaped((n_state // 2, 2 * owners, channels), F32),
            shaped((1, channels), F32),
            shaped((1, channels), F32),
        ],
        [hbm()] * 10 + [anywhere()],
        [vmem()] * 12,
        [
            pltpu.VMEM(step_in.shape, BF16),
            pltpu.SMEM((1,), jnp.int32),
            pltpu.SMEM((rb,), jnp.int32),
            pltpu.SMEM((rb,), jnp.int32),
            pltpu.VMEM((n_state, channels), F32),
            pltpu.SemaphoreType.DMA((8 + WEIGHT_PARTS + STEP_PARTS,)),
        ],
        flops=10 * steps * rb * channels,
        nbytes=12 * steps * rb * channels,
        trans=steps * rb * channels,
    )(
        owner,
        pinned(prompt_of),
        pinned(child_slot),
        pinned(step_in),
        pinned(conv_weight),
        pinned(conv_bias[None]),
        pinned(x_weight.T),
        pinned(a_log),
        pinned(dt_bias[None]),
        pinned(skip[None]),
        after,
    )
    base, gate, pick, child_pick, sender, taps_near, bias_near, weight_near = near[:8]
    rate, twin, dtb_near, skip_near = near[8:]
    states = []
    if direct:
        pair = call(
            functools.partial(pair_kernel, short),
            shaped((1, 3 * n_state, channels), BF16),
            [vmem()] * 2 + [anywhere()],
            vmem(),
            nbytes=12 * n_state * channels,
        )(prompt_ssm, msgs[1], pick)
        states = [prompt_ssm, swap(pair, "branch", 1)]
    act, part, brief = call(
        functools.partial(project_kernel, n_msgs),
        [
            shaped((rows, channels), F32),
            shaped((rows, width), F32),
            shaped((rows, width), BF16),
        ],
        [vmem()] * (6 + n_msgs),
        [vmem()] * 3,
        flops=2 * rows * channels * width,
        nbytes=channels * width * 2 + rows * (channels + width) * 4,
        trans=rows * channels,
    )(pick, sender, base, taps_near, bias_near, weight_near, *msgs)
    other = swap(brief, "tensor", 1)
    distance = 2
    while distance < tensors:
        part, brief = call(
            add_kernel,
            [shaped((rows, width), F32), shaped((rows, width), BF16)],
            [vmem()] * 2,
            [vmem()] * 2,
            flops=rows * width,
            nbytes=rows * width * 14,
        )(part, other)
        other = swap(brief, "tensor", 2 * distance - 1)
        distance *= 2

    child_conv = call(
        functools.partial(windows_kernel, n_msgs, steps),
        shaped((taps - 1, rb, channels), BF16),
        [vmem(), anywhere()] + [vmem()] * n_msgs,
        vmem(),
        flops=2 * owners * taps * rb * channels,
        nbytes=4 * taps * rb * channels,
    )(child_pick, part, *msgs)
    own_start, slot_start = call(
        functools.partial(start_kernel, n_msgs, direct, short),
        [
            shaped((n_state, rb, channels), F32),
            shaped((n_state // 2, 2 * owners, channels), F32),
        ],
        [vmem()] * 2 + [anywhere()] + [vmem()] * (n_msgs + len(states)),
        [vmem()] * 2,
        [pltpu.VMEM((owners, n_state, channels), F32)],
        flops=2 * owners * n_state * (rb + owners) * channels,
        nbytes=4 * n_state * (rb + owners) * channels,
    )(pick, sender, part, *msgs, *states)

    decoded, child_ssm = call(
        functools.partial(decode_kernel, direct),
        [
            shaped((rb, steps, channels), BF16),
            shaped((rb, n_state, channels), F32),
        ],
        [hbm()] * 2 + [vmem()] * 11,
        [vmem(), anywhere()],
        [
            pltpu.SMEM((1,), jnp.int32),
            pltpu.SMEM((rb,), jnp.int32),
            pltpu.VMEM((steps * rb, channels), F32),
            pltpu.VMEM((steps * rb, channels), F32),
            pltpu.VMEM((steps, 2 * owners, channels), F32),
            pltpu.VMEM((steps, 2 * owners, channels), F32),
            pltpu.VMEM((n_state, steps * rb, LANES), F32),
            pltpu.VMEM((n_state, steps * rb, LANES), F32),
            pltpu.VMEM((n_state // 2, steps, 2 * owners, LANES), F32),
            pltpu.VMEM((owners, n_state, channels), F32),
            pltpu.VMEM((WIDE, steps * rb, LANES), F32),
            pltpu.SemaphoreType.DMA((2 + rb,)),
        ],
        flops=8 * rows * n_state * channels,
        nbytes=(rb + owners) * n_state * channels * 4,
        trans=rows * n_state * channels,
    )(
        owner,
        pinned(child_slot),
        act,
        gate,
        own_start,
        slot_start,
        rate,
        twin,
        dt_weight,
        dtb_near,
        skip_near,
        part,
        other,
    )
    return (decoded, child_ssm, jnp.transpose(child_conv, (1, 0, 2)))


def solution(mesh):
    placed = (
        P(("replica", "branch"), None, "tensor"),
        P(("replica", "branch"), None, "tensor"),
        P(("replica", "branch")),
        P(("replica", "branch"), None, None, "tensor"),
        P(None, "tensor"),
        P("tensor"),
        P("tensor", None),
        P(None, "tensor"),
        P("tensor"),
        P(None, "tensor"),
        P("tensor"),
        P(("replica", "branch"), None, None),
        P(("replica", "branch")),
    )
    return jax.shard_map(
        on_device,
        mesh=mesh,
        in_specs=placed,
        out_specs=(
            P(("replica", "branch"), None, "tensor"),
            P(("replica", "branch"), None, "tensor"),
            P(("replica", "branch"), None, "tensor"),
        ),
        check_vma=False,
    )
```

```python
import functools
import math

import jax
import jax.numpy as jnp
from jax import lax
from jax.experimental import pallas as pl
from jax.experimental.pallas import tpu as pltpu
from jax.sharding import PartitionSpec as P

F32 = jnp.float32
BF16 = jnp.bfloat16
LANES = 128
ROWS = 8
WIDE = 2
VMEM_LIMIT = 48 * 2**20
WEIGHT_PARTS = 6
STEP_PARTS = 4
DIRECT = 4
SENDS = ((2, 3, 1, 0), (3, 2, 0, 1), (1, 0, 3, 2))


def vmem():
    return pl.BlockSpec(memory_space=pltpu.VMEM)


def hbm():
    return pl.BlockSpec(memory_space=pltpu.HBM)


def anywhere():
    return pl.BlockSpec(memory_space=pl.ANY)


def pinned(array):
    return pltpu.with_memory_space_constraint(array, pltpu.HBM)


def shaped(shape, dtype):
    return jax.ShapeDtypeStruct(shape, dtype)


def call(kernel, outs, in_specs, out_specs, scratch=(), flops=0, nbytes=0, trans=0):
    return pl.pallas_call(
        kernel,
        out_shape=outs,
        in_specs=in_specs,
        out_specs=out_specs,
        scratch_shapes=list(scratch),
        compiler_params=pltpu.CompilerParams(vmem_limit_bytes=VMEM_LIMIT),
        cost_estimate=pl.CostEstimate(flops=flops, bytes_accessed=nbytes, transcendentals=trans),
    )


def swap(value, axis, distance):
    size = lax.axis_size(axis)
    return lax.ppermute(value, axis, [(i, i ^ distance) for i in range(size)])


def chosen(number, values):
    total = values[0]
    for i in range(1, len(values)):
        total = jnp.where(number == i, values[i], total)
    return total


def blocks_of(owner):
    table = [
        [0 if s == r else 1 + [to[s] for to in SENDS].index(r) for s in range(DIRECT)]
        for r in range(DIRECT)
    ]
    return [chosen(owner, [row[s] for row in table]) for s in range(DIRECT)]


def all_of(copies):
    for copy in copies:
        copy.start()
    for copy in copies:
        copy.wait()


def read_messages(refs):
    return [ref[i].astype(F32) for ref in refs for i in range(ref.shape[0])]


def in_parts(source, target, sems, first, count):
    rows = source.shape[0] // count
    at = [pl.ds(i * rows, rows) for i in range(count)]
    return [
        pltpu.make_async_copy(source.at[a], target.at[a], sems.at[first + i])
        for i, a in enumerate(at)
    ]


def scalar_onehot(senders_s, places, shape):
    row_of = lax.broadcasted_iota(jnp.int32, shape, 0)
    wanted = jnp.zeros(shape, jnp.int32)
    for b in range(shape[0]):
        wanted = jnp.where(row_of == b, senders_s[b], wanted)
    wanted = wanted if places is None else chosen(wanted, places)
    return (wanted == lax.broadcasted_iota(jnp.int32, shape, 1)).astype(F32)


def pick_rows(pick, rows):
    total = pick[:, 0:1] * rows[0]
    for k in range(1, len(rows)):
        total = total + pick[:, k : k + 1] * rows[k]
    return total


def pack_kernel(direct, owner_hbm, rows_hbm, prompt_hbm, step_hbm, conv_hbm, ssm_hbm, *rest):
    outs, (owner_s, rows_s, prompt_s, step, conv, ssm, sems) = rest[:-7], rest[-7:]
    owners = rows_hbm.shape[0]
    channels = step_hbm.shape[3]
    copies = [
        pltpu.make_async_copy(owner_hbm, owner_s, sems.at[4]),
        pltpu.make_async_copy(rows_hbm, rows_s, sems.at[0]),
        pltpu.make_async_copy(prompt_hbm, prompt_s, sems.at[1]),
        pltpu.make_async_copy(conv_hbm, conv, sems.at[2]),
        pltpu.make_async_copy(ssm_hbm, ssm, sems.at[3]),
    ]
    all_of(copies + in_parts(step_hbm, step, sems, 5, STEP_PARTS))
    owner = owner_s[0]
    window = conv[0].astype(F32)

    def write(ref, target):
        row = jnp.maximum(rows_s[target], 0)
        xs = step[row, :, 0, :].astype(F32)
        number = prompt_s[row].astype(F32)
        pieces = [xs, window, jnp.full((1, channels), number, F32)]
        if ref.shape[0] > sum(p.shape[0] for p in pieces):
            pieces.append(ssm[0])
        ref[...] = jnp.concatenate(pieces, axis=0).astype(BF16)

    if direct:
        write(outs[0].at[0], owner)
        for ref, to in zip(outs[1:], SENDS):
            write(ref.at[0], chosen(owner, to))
    else:
        for target in range(owners):
            write(outs[0].at[target], target)


def pair_kernel(text, ssm_ref, came_ref, after_ref, pair_ref):
    del after_ref
    state = ssm_ref[0]
    head = state.astype(BF16).astype(F32)
    came = came_ref[0].astype(F32)[text:, :]
    pair_ref[0] = jnp.concatenate([head, state - head, came], axis=0).astype(BF16)


def silu(v):
    return v / (1.0 + jnp.exp(-v))


def prepare_kernel(
    direct,
    owner_hbm,
    prompt_hbm,
    child_hbm,
    step_ref,
    cw_hbm,
    cb_hbm,
    xwt_hbm,
    alog_hbm,
    dtb_hbm,
    skip_hbm,
    after_ref,
    base_ref,
    gate_ref,
    pick_ref,
    child_ref,
    sender_ref,
    cw_ref,
    cb_ref,
    xwt_ref,
    rate_ref,
    twin_ref,
    dtb_ref,
    skip_ref,
    owner_s,
    prompt_s,
    child_s,
    alog,
    sems,
):
    del after_ref
    small = [
        pltpu.make_async_copy(source, target, sems.at[i])
        for i, (source, target) in enumerate(
            (
                (cw_hbm, cw_ref),
                (cb_hbm, cb_ref),
                (owner_hbm, owner_s),
                (prompt_hbm, prompt_s),
                (child_hbm, child_s),
                (alog_hbm, alog),
                (dtb_hbm, dtb_ref),
                (skip_hbm, skip_ref),
            )
        )
    ]
    large = in_parts(xwt_hbm, xwt_ref, sems, len(small), WEIGHT_PARTS)
    for copy in small + large:
        copy.start()
    steps = step_ref.shape[1]
    taps = cw_hbm.shape[0]
    xs = [step_ref[:, t, 0, :].astype(F32) for t in range(steps)]
    for t in range(steps):
        gate_ref[t] = silu(step_ref[:, t, 1, :].astype(F32))
    for copy in small:
        copy.wait()
    for t in range(steps):
        total = cw_ref[taps - 1 : taps, :] * xs[t] + cb_ref[...]
        for k in range(max(0, taps - 1 - t), taps - 1):
            total = total + cw_ref[k : k + 1, :] * xs[t + k - taps + 1]
        base_ref[t] = total
    places = blocks_of(owner_s[0]) if direct else None
    pick_ref[...] = scalar_onehot(prompt_s, places, pick_ref.shape)
    child_ref[...] = scalar_onehot(child_s, places, child_ref.shape)
    column = lax.broadcasted_iota(jnp.int32, sender_ref.shape, 1)
    sender = column
    for sent, place in enumerate(places or []):
        sender = jnp.where(column == place, sent, sender)
    sender_ref[...] = sender.astype(F32)
    rate = jnp.exp(alog[...]) * (-math.log2(math.e))
    rate_ref[...] = rate
    half = (twin_ref.shape[1] // 2, rate.shape[1])
    for m in range(rate.shape[0] // 2):
        two = [jnp.broadcast_to(rate[n : n + 1, :], half) for n in (2 * m, 2 * m + 1)]
        twin_ref[m] = jnp.concatenate(two, axis=0)
    for copy in large:
        copy.wait()


def slot_onehot(numbers, sender_ref):
    owners = sender_ref.shape[1]
    return (numbers[:, :owners] == sender_ref[...]).astype(F32)


def project_kernel(n_msgs, pick_ref, sender_ref, base_ref, cw_ref, cb_ref, xwt_ref, *rest):
    msgs, (act_ref, part_ref, short_ref) = rest[:n_msgs], rest[n_msgs:]
    taps = cw_ref.shape[0]
    steps, rb, _ = base_ref.shape
    past = taps - 1
    held = read_messages(msgs)
    owners = len(held)
    windows = [[h[steps + k : steps + k + 1, :] for h in held] for k in range(past)]
    own = pick_ref[...]
    own_windows = [pick_rows(own, w) for w in windows]
    for t in range(steps):
        conv = base_ref[t]
        for k in range(past - t):
            conv = conv + cw_ref[k : k + 1, :] * own_windows[t + k]
        act_ref[t * rb : (t + 1) * rb, :] = silu(conv)

    def line_of(row):
        return jnp.concatenate([h[row : row + 1, :] for h in held], axis=0)

    slot = slot_onehot(line_of(past + steps), sender_ref)
    line = [pick_rows(slot, w) for w in windows]
    line += [line_of(t) for t in range(steps)]
    row = steps * rb
    for t in range(steps):
        conv = cw_ref[past:taps, :] * line[t + past] + cb_ref[...]
        for k in range(past):
            conv = conv + cw_ref[k : k + 1, :] * line[t + k]
        act_ref[row : row + owners, :] = silu(conv)
        row += owners
    part = lax.dot_general(
        act_ref[...].astype(BF16),
        xwt_ref[...],
        (((1,), (1,)), ((), ())),
        preferred_element_type=F32,
    )
    part_ref[...] = part
    short_ref[...] = part.astype(BF16)


def add_kernel(a_ref, b_ref, sum_ref, short_ref):
    total = a_ref[...] + b_ref[...].astype(F32)
    sum_ref[...] = total
    short_ref[...] = total.astype(BF16)


def windows_kernel(n_msgs, steps, child_ref, after_ref, *rest):
    del after_ref
    msgs, (conv_ref,) = rest[:n_msgs], rest[n_msgs:]
    held = read_messages(msgs)
    past = conv_ref.shape[0]
    for k in range(past):
        at = steps - past + k
        rows = [h[at : at + 1, :] for h in held]
        conv_ref[k] = pick_rows(child_ref[...], rows).astype(BF16)


def start_kernel(n_msgs, direct, text, pick_ref, sender_ref, after_ref, *rest):
    del after_ref
    msgs, rest = rest[:n_msgs], rest[n_msgs:]
    apart, (own_ref, slot_ref, state_s) = rest[:-3], rest[-3:]
    n_state = own_ref.shape[0]
    held = read_messages(msgs)
    owners = len(held)
    numbers = jnp.concatenate([h[text - 1 : text, :] for h in held], axis=0)
    states = [h[text:, :] for h in held]
    if direct:
        ssm_ref, pair_ref = apart
        head, low, came = [
            pair_ref[0].astype(F32)[i * n_state : (i + 1) * n_state, :] for i in range(3)
        ]
        states[0], states[2], states[3] = ssm_ref[0], came, head + low
    for k, state in enumerate(states):
        state_s[k] = state
    own = pick_ref[...]
    slot = slot_onehot(numbers, sender_ref)

    def two(m, carry):
        picked = []
        for n in (2 * m, 2 * m + 1):
            rows = [state_s[k, pl.ds(n, 1), :] for k in range(owners)]
            own_ref[n] = pick_rows(own, rows)
            picked.append(pick_rows(slot, rows))
        slot_ref[m] = jnp.concatenate(picked, axis=0)
        return carry

    lax.fori_loop(0, n_state // 2, two, 0, unroll=owners <= DIRECT)


def decode_kernel(
    direct,
    owner_hbm,
    child_hbm,
    act_ref,
    gate_ref,
    own_ref,
    slot_ref,
    rate_ref,
    twin_ref,
    dtw_ref,
    dtb_ref,
    skip_ref,
    part_ref,
    other_ref,
    dec_ref,
    child_ssm,
    owner_s,
    child_s,
    delta_s,
    gain_s,
    slot_delta_s,
    slot_gain_s,
    b_s,
    c_s,
    twin_b_s,
    slots_s,
    line_s,
    sems,
):
    scalars = [
        pltpu.make_async_copy(owner_hbm, owner_s, sems.at[0]),
        pltpu.make_async_copy(child_hbm, child_s, sems.at[1]),
    ]
    for copy in scalars:
        copy.start()
    rb, steps, channels = dec_ref.shape
    rank = dtw_ref.shape[0]
    n_state = rate_ref.shape[0]
    n_slots = slots_s.shape[0]
    own_rows = steps * rb
    chunks = channels // (WIDE * LANES)

    proj = part_ref[...] + other_ref[...].astype(F32)
    delta_in = proj[:, :rank].astype(BF16)
    delta = jnp.dot(delta_in, dtw_ref[...], preferred_element_type=F32) + dtb_ref[...]
    delta = jnp.maximum(delta, 0.0) + jnp.log(1.0 + jnp.exp(-jnp.abs(delta)))
    gain = delta * act_ref[...]
    delta_s[...] = delta[:own_rows, :]
    gain_s[...] = gain[:own_rows, :]

    def column(at, n, rows):
        return jnp.broadcast_to(at[:, n : n + 1], (rows, LANES))

    for t in range(steps):
        at = slice(own_rows + t * n_slots, own_rows + (t + 1) * n_slots)
        slot_delta_s[t] = jnp.concatenate([delta[at, :]] * 2, axis=0)
        slot_gain_s[t] = jnp.concatenate([gain[at, :]] * 2, axis=0)
        twice = jnp.concatenate([proj[at, rank:]] * 2, axis=0)
        upper = lax.broadcasted_iota(jnp.int32, (2 * n_slots, LANES), 0) < n_slots
        for m in range(n_state // 2):
            twin_b_s[m, t] = jnp.where(
                upper, column(twice, 2 * m, 2 * n_slots), column(twice, 2 * m + 1, 2 * n_slots)
            )
    for n in range(n_state):
        b_s[n] = column(proj[:own_rows, rank:], n, own_rows)
        c_s[n] = column(proj[:own_rows, rank:], n_state + n, own_rows)

    def wide(part):
        return jnp.concatenate([part] * WIDE, axis=1)

    def slot_chunk(chunk, carry):
        columns = pl.ds(pl.multiple_of(chunk * WIDE * LANES, WIDE * LANES), WIDE * LANES)
        delta = [slot_delta_s[t, :, columns] for t in range(steps)]
        gain = [slot_gain_s[t, :, columns] for t in range(steps)]
        for m in range(n_state // 2):
            rate = twin_ref[m, :, columns]
            state = slot_ref[m, :, columns]
            for t in range(steps):
                state = jnp.exp2(delta[t] * rate) * state + gain[t] * wide(twin_b_s[m, t])
            slots_s[:, 2 * m, columns] = state[:n_slots, :]
            slots_s[:, 2 * m + 1, columns] = state[n_slots:, :]
        return carry

    lax.fori_loop(0, chunks, slot_chunk, 0)
    for copy in scalars:
        copy.wait()
    places = blocks_of(owner_s[0]) if direct else None
    copies = []
    for j in range(rb):
        at = chosen(child_s[j], places) if direct else child_s[j]
        copy = pltpu.make_async_copy(slots_s.at[at], child_ssm.at[j], sems.at[2 + j])
        copy.start()
        copies.append(copy)

    def own_chunk(chunk, carry):
        columns = pl.ds(pl.multiple_of(chunk * WIDE * LANES, WIDE * LANES), WIDE * LANES)
        for first in range(0, rb, ROWS):
            at = [pl.ds(t * rb + first, ROWS) for t in range(steps)]
            delta = [delta_s[a, columns] for a in at]
            gain = [gain_s[a, columns] for a in at]
            sums = [skip_ref[:, columns] * act_ref[a, columns] for a in at]
            for n in range(n_state):
                rate = rate_ref[n : n + 1, columns]
                state = own_ref[n, pl.ds(first, ROWS), columns]
                for t in range(steps):
                    state = jnp.exp2(delta[t] * rate) * state + gain[t] * wide(b_s[n, at[t], :])
                    sums[t] = sums[t] + wide(c_s[n, at[t], :]) * state
            for t in range(steps):
                out = sums[t] * gate_ref[t, pl.ds(first, ROWS), columns]
                for w in range(WIDE):
                    line_s[w, pl.ds(first * steps + t, ROWS, stride=steps), :] = out[
                        :, w * LANES : (w + 1) * LANES
                    ]
        for w in range(WIDE):
            some = pl.ds(pl.multiple_of((chunk * WIDE + w) * LANES, LANES), LANES)
            dec_ref[:, :, some] = line_s[w].reshape(rb, steps, LANES).astype(BF16)
        return carry

    lax.fori_loop(0, chunks, own_chunk, 0)
    for copy in copies:
        copy.wait()


def on_device(
    prompt_ssm,
    prompt_conv,
    prompt_of,
    step_in,
    conv_weight,
    conv_bias,
    x_weight,
    dt_weight,
    dt_bias,
    a_log,
    skip,
    send_rows,
    child_slot,
):
    owners = lax.axis_size("branch")
    tensors = lax.axis_size("tensor")
    assert owners & (owners - 1) == 0 and tensors & (tensors - 1) == 0
    assert prompt_ssm.shape[0] == 1 and send_rows.shape[2] == 1
    rb, steps, _, channels = step_in.shape
    taps = conv_weight.shape[0]
    width = x_weight.shape[1]
    n_state = a_log.shape[0]
    rows = steps * (rb + owners)
    short = taps - 1 + steps + 1
    depth = short + n_state
    direct = owners == DIRECT
    owner = pinned(lax.axis_index("branch").astype(jnp.int32).reshape(1))

    if direct:
        msg_shapes = [(1, d, channels) for d in (short, depth, short, short)]
    else:
        msg_shapes = [(owners, depth, channels)]
    msgs = call(
        functools.partial(pack_kernel, direct),
        [shaped(s, BF16) for s in msg_shapes],
        [hbm()] * 6,
        [vmem()] * len(msg_shapes),
        [
            pltpu.SMEM((1,), jnp.int32),
            pltpu.SMEM((owners,), jnp.int32),
            pltpu.SMEM((rb,), jnp.int32),
            pltpu.VMEM(step_in.shape, BF16),
            pltpu.VMEM(prompt_conv.shape, BF16),
            pltpu.VMEM(prompt_ssm.shape, F32),
            pltpu.SemaphoreType.DMA((5 + STEP_PARTS,)),
        ],
        nbytes=owners * depth * channels * 2,
    )(
        owner,
        pinned(send_rows.reshape(owners)),
        pinned(prompt_of),
        pinned(step_in),
        pinned(prompt_conv),
        pinned(prompt_ssm),
    )
    if direct:
        own = msgs[0]
        msgs = [own] + [
            lax.ppermute(m, "branch", list(enumerate(to))) for m, to in zip(msgs[1:], SENDS)
        ]
        after = own
    else:
        msgs = [lax.all_to_all(msgs[0], "branch", split_axis=0, concat_axis=0, tiled=True)]
        after = msgs[0]
    n_msgs = len(msgs)
    near = call(
        functools.partial(prepare_kernel, direct),
        [
            shaped((steps, rb, channels), F32),
            shaped((steps, rb, channels), F32),
            shaped((rb, owners), F32),
            shaped((rb, owners), F32),
            shaped((1, owners), F32),
            shaped((taps, channels), F32),
            shaped((1, channels), F32),
            shaped((width, channels), BF16),
            shaped((n_state, channels), F32),
            shaped((n_state // 2, 2 * owners, channels), F32),
            shaped((1, channels), F32),
            shaped((1, channels), F32),
        ],
        [hbm()] * 3 + [vmem()] + [hbm()] * 6 + [anywhere()],
        [vmem()] * 12,
        [
            pltpu.SMEM((1,), jnp.int32),
            pltpu.SMEM((rb,), jnp.int32),
            pltpu.SMEM((rb,), jnp.int32),
            pltpu.VMEM((n_state, channels), F32),
            pltpu.SemaphoreType.DMA((8 + WEIGHT_PARTS,)),
        ],
        flops=10 * steps * rb * channels,
        nbytes=12 * steps * rb * channels,
        trans=steps * rb * channels,
    )(
        owner,
        pinned(prompt_of),
        pinned(child_slot),
        step_in,
        pinned(conv_weight),
        pinned(conv_bias[None]),
        pinned(x_weight.T),
        pinned(a_log),
        pinned(dt_bias[None]),
        pinned(skip[None]),
        after,
    )
    base, gate, pick, child_pick, sender, taps_near, bias_near, weight_near = near[:8]
    rate, twin, dtb_near, skip_near = near[8:]
    states = []
    if direct:
        pair = call(
            functools.partial(pair_kernel, short),
            shaped((1, 3 * n_state, channels), BF16),
            [vmem()] * 2 + [anywhere()],
            vmem(),
            nbytes=12 * n_state * channels,
        )(prompt_ssm, msgs[1], pick)
        states = [prompt_ssm, swap(pair, "branch", 1)]
    act, part, brief = call(
        functools.partial(project_kernel, n_msgs),
        [
            shaped((rows, channels), F32),
            shaped((rows, width), F32),
            shaped((rows, width), BF16),
        ],
        [vmem()] * (6 + n_msgs),
        [vmem()] * 3,
        flops=2 * rows * channels * width,
        nbytes=channels * width * 2 + rows * (channels + width) * 4,
        trans=rows * channels,
    )(pick, sender, base, taps_near, bias_near, weight_near, *msgs)
    other = swap(brief, "tensor", 1)
    distance = 2
    while distance < tensors:
        part, brief = call(
            add_kernel,
            [shaped((rows, width), F32), shaped((rows, width), BF16)],
            [vmem()] * 2,
            [vmem()] * 2,
            flops=rows * width,
            nbytes=rows * width * 14,
        )(part, other)
        other = swap(brief, "tensor", 2 * distance - 1)
        distance *= 2

    child_conv = call(
        functools.partial(windows_kernel, n_msgs, steps),
        shaped((taps - 1, rb, channels), BF16),
        [vmem(), anywhere()] + [vmem()] * n_msgs,
        vmem(),
        flops=2 * owners * taps * rb * channels,
        nbytes=4 * taps * rb * channels,
    )(child_pick, part, *msgs)
    own_start, slot_start = call(
        functools.partial(start_kernel, n_msgs, direct, short),
        [
            shaped((n_state, rb, channels), F32),
            shaped((n_state // 2, 2 * owners, channels), F32),
        ],
        [vmem()] * 2 + [anywhere()] + [vmem()] * (n_msgs + len(states)),
        [vmem()] * 2,
        [pltpu.VMEM((owners, n_state, channels), F32)],
        flops=2 * owners * n_state * (rb + owners) * channels,
        nbytes=4 * n_state * (rb + owners) * channels,
    )(pick, sender, part, *msgs, *states)

    decoded, child_ssm = call(
        functools.partial(decode_kernel, direct),
        [
            shaped((rb, steps, channels), BF16),
            shaped((rb, n_state, channels), F32),
        ],
        [hbm()] * 2 + [vmem()] * 11,
        [vmem(), anywhere()],
        [
            pltpu.SMEM((1,), jnp.int32),
            pltpu.SMEM((rb,), jnp.int32),
            pltpu.VMEM((steps * rb, channels), F32),
            pltpu.VMEM((steps * rb, channels), F32),
            pltpu.VMEM((steps, 2 * owners, channels), F32),
            pltpu.VMEM((steps, 2 * owners, channels), F32),
            pltpu.VMEM((n_state, steps * rb, LANES), F32),
            pltpu.VMEM((n_state, steps * rb, LANES), F32),
            pltpu.VMEM((n_state // 2, steps, 2 * owners, LANES), F32),
            pltpu.VMEM((owners, n_state, channels), F32),
            pltpu.VMEM((WIDE, steps * rb, LANES), F32),
            pltpu.SemaphoreType.DMA((2 + rb,)),
        ],
        flops=8 * rows * n_state * channels,
        nbytes=(rb + owners) * n_state * channels * 4,
        trans=rows * n_state * channels,
    )(
        owner,
        pinned(child_slot),
        act,
        gate,
        own_start,
        slot_start,
        rate,
        twin,
        dt_weight,
        dtb_near,
        skip_near,
        part,
        other,
    )
    return (decoded, child_ssm, jnp.transpose(child_conv, (1, 0, 2)))


def solution(mesh):
    placed = (
        P(("replica", "branch"), None, "tensor"),
        P(("replica", "branch"), None, "tensor"),
        P(("replica", "branch")),
        P(("replica", "branch"), None, None, "tensor"),
        P(None, "tensor"),
        P("tensor"),
        P("tensor", None),
        P(None, "tensor"),
        P("tensor"),
        P(None, "tensor"),
        P("tensor"),
        P(("replica", "branch"), None, None),
        P(("replica", "branch")),
    )
    return jax.shard_map(
        on_device,
        mesh=mesh,
        in_specs=placed,
        out_specs=(
            P(("replica", "branch"), None, "tensor"),
            P(("replica", "branch"), None, "tensor"),
            P(("replica", "branch"), None, "tensor"),
        ),
        check_vma=False,
    )
```

```python
import functools
import math

import jax
import jax.numpy as jnp
from jax import lax
from jax.experimental import pallas as pl
from jax.experimental.pallas import tpu as pltpu
from jax.sharding import PartitionSpec as P

F32 = jnp.float32
BF16 = jnp.bfloat16
LANES = 128
ROWS = 8
WIDE = 2
VMEM_LIMIT = 48 * 2**20
WEIGHT_PARTS = 6
STEP_PARTS = 4
DIRECT = 4
SENDS = ((2, 3, 1, 0), (3, 2, 0, 1), (1, 0, 3, 2))


def vmem():
    return pl.BlockSpec(memory_space=pltpu.VMEM)


def hbm():
    return pl.BlockSpec(memory_space=pltpu.HBM)


def anywhere():
    return pl.BlockSpec(memory_space=pl.ANY)


def pinned(array):
    return pltpu.with_memory_space_constraint(array, pltpu.HBM)


def shaped(shape, dtype):
    return jax.ShapeDtypeStruct(shape, dtype)


def call(kernel, outs, in_specs, out_specs, scratch=(), flops=0, nbytes=0, trans=0):
    return pl.pallas_call(
        kernel,
        out_shape=outs,
        in_specs=in_specs,
        out_specs=out_specs,
        scratch_shapes=list(scratch),
        compiler_params=pltpu.CompilerParams(vmem_limit_bytes=VMEM_LIMIT),
        cost_estimate=pl.CostEstimate(flops=flops, bytes_accessed=nbytes, transcendentals=trans),
    )


def swap(value, axis, distance):
    size = lax.axis_size(axis)
    return lax.ppermute(value, axis, [(i, i ^ distance) for i in range(size)])


def chosen(number, values):
    total = values[0]
    for i in range(1, len(values)):
        total = jnp.where(number == i, values[i], total)
    return total


def blocks_of(owner):
    table = [
        [0 if s == r else 1 + [to[s] for to in SENDS].index(r) for s in range(DIRECT)]
        for r in range(DIRECT)
    ]
    return [chosen(owner, [row[s] for row in table]) for s in range(DIRECT)]


def all_of(copies):
    for copy in copies:
        copy.start()
    for copy in copies:
        copy.wait()


def read_messages(refs):
    return [ref[i].astype(F32) for ref in refs for i in range(ref.shape[0])]


def in_parts(source, target, sems, first, count):
    rows = source.shape[0] // count
    at = [pl.ds(i * rows, rows) for i in range(count)]
    return [
        pltpu.make_async_copy(source.at[a], target.at[a], sems.at[first + i])
        for i, a in enumerate(at)
    ]


def scalar_onehot(senders_s, places, shape):
    row_of = lax.broadcasted_iota(jnp.int32, shape, 0)
    wanted = jnp.zeros(shape, jnp.int32)
    for b in range(shape[0]):
        wanted = jnp.where(row_of == b, senders_s[b], wanted)
    wanted = wanted if places is None else chosen(wanted, places)
    return (wanted == lax.broadcasted_iota(jnp.int32, shape, 1)).astype(F32)


def pick_rows(pick, rows):
    total = pick[:, 0:1] * rows[0]
    for k in range(1, len(rows)):
        total = total + pick[:, k : k + 1] * rows[k]
    return total


def pack_kernel(direct, owner_hbm, rows_hbm, prompt_hbm, step_hbm, conv_hbm, ssm_hbm, *rest):
    outs, (owner_s, rows_s, prompt_s, step, conv, ssm, sems) = rest[:-7], rest[-7:]
    owners = rows_hbm.shape[0]
    channels = step_hbm.shape[3]
    copies = [
        pltpu.make_async_copy(owner_hbm, owner_s, sems.at[4]),
        pltpu.make_async_copy(rows_hbm, rows_s, sems.at[0]),
        pltpu.make_async_copy(prompt_hbm, prompt_s, sems.at[1]),
        pltpu.make_async_copy(conv_hbm, conv, sems.at[2]),
        pltpu.make_async_copy(ssm_hbm, ssm, sems.at[3]),
    ]
    all_of(copies + in_parts(step_hbm, step, sems, 5, STEP_PARTS))
    owner = owner_s[0]
    window = conv[0].astype(F32)

    def write(ref, target):
        row = jnp.maximum(rows_s[target], 0)
        xs = step[row, :, 0, :].astype(F32)
        number = prompt_s[row].astype(F32)
        pieces = [xs, window, jnp.full((1, channels), number, F32)]
        if ref.shape[0] > sum(p.shape[0] for p in pieces):
            pieces.append(ssm[0])
        ref[...] = jnp.concatenate(pieces, axis=0).astype(BF16)

    if direct:
        write(outs[0].at[0], owner)
        for ref, to in zip(outs[1:], SENDS):
            write(ref.at[0], chosen(owner, to))
    else:
        for target in range(owners):
            write(outs[0].at[target], target)


def pair_kernel(text, ssm_ref, came_ref, after_ref, pair_ref):
    del after_ref
    state = ssm_ref[0]
    head = state.astype(BF16).astype(F32)
    came = came_ref[0].astype(F32)[text:, :]
    pair_ref[0] = jnp.concatenate([head, state - head, came], axis=0).astype(BF16)


def silu(v):
    return v / (1.0 + jnp.exp(-v))


def prepare_kernel(
    direct,
    owner_hbm,
    prompt_hbm,
    step_hbm,
    cw_hbm,
    cb_hbm,
    xwt_hbm,
    after_ref,
    base_ref,
    pick_ref,
    sender_ref,
    cw_ref,
    cb_ref,
    xwt_ref,
    step_ref,
    owner_s,
    prompt_s,
    sems,
):
    del after_ref
    small = [
        pltpu.make_async_copy(source, target, sems.at[i])
        for i, (source, target) in enumerate(
            ((cw_hbm, cw_ref), (cb_hbm, cb_ref), (owner_hbm, owner_s), (prompt_hbm, prompt_s))
        )
    ]
    inputs = in_parts(step_hbm, step_ref, sems, len(small), STEP_PARTS)
    large = in_parts(xwt_hbm, xwt_ref, sems, len(small) + STEP_PARTS, WEIGHT_PARTS)
    for copy in inputs + small + large:
        copy.start()
    for copy in inputs + small:
        copy.wait()
    steps = step_ref.shape[1]
    taps = cw_hbm.shape[0]
    xs = [step_ref[:, t, 0, :].astype(F32) for t in range(steps)]
    for t in range(steps):
        total = cw_ref[taps - 1 : taps, :] * xs[t] + cb_ref[...]
        for k in range(max(0, taps - 1 - t), taps - 1):
            total = total + cw_ref[k : k + 1, :] * xs[t + k - taps + 1]
        base_ref[t] = total
    places = blocks_of(owner_s[0]) if direct else None
    pick_ref[...] = scalar_onehot(prompt_s, places, pick_ref.shape)
    column = lax.broadcasted_iota(jnp.int32, sender_ref.shape, 1)
    sender = column
    for sent, place in enumerate(places or []):
        sender = jnp.where(column == place, sent, sender)
    sender_ref[...] = sender.astype(F32)
    for copy in large:
        copy.wait()


def slot_onehot(numbers, sender_ref):
    owners = sender_ref.shape[1]
    return (numbers[:, :owners] == sender_ref[...]).astype(F32)


def project_kernel(n_msgs, pick_ref, sender_ref, base_ref, cw_ref, cb_ref, xwt_ref, *rest):
    msgs, (act_ref, part_ref, short_ref) = rest[:n_msgs], rest[n_msgs:]
    taps = cw_ref.shape[0]
    steps, rb, _ = base_ref.shape
    past = taps - 1
    held = read_messages(msgs)
    owners = len(held)
    windows = [[h[steps + k : steps + k + 1, :] for h in held] for k in range(past)]
    own = pick_ref[...]
    own_windows = [pick_rows(own, w) for w in windows]
    for t in range(steps):
        conv = base_ref[t]
        for k in range(past - t):
            conv = conv + cw_ref[k : k + 1, :] * own_windows[t + k]
        act_ref[t * rb : (t + 1) * rb, :] = silu(conv)

    def line_of(row):
        return jnp.concatenate([h[row : row + 1, :] for h in held], axis=0)

    slot = slot_onehot(line_of(past + steps), sender_ref)
    line = [pick_rows(slot, w) for w in windows]
    line += [line_of(t) for t in range(steps)]
    row = steps * rb
    for t in range(steps):
        conv = cw_ref[past:taps, :] * line[t + past] + cb_ref[...]
        for k in range(past):
            conv = conv + cw_ref[k : k + 1, :] * line[t + k]
        act_ref[row : row + owners, :] = silu(conv)
        row += owners
    part = lax.dot_general(
        act_ref[...].astype(BF16),
        xwt_ref[...],
        (((1,), (1,)), ((), ())),
        preferred_element_type=F32,
    )
    part_ref[...] = part
    short_ref[...] = part.astype(BF16)


def add_kernel(a_ref, b_ref, sum_ref, short_ref):
    total = a_ref[...] + b_ref[...].astype(F32)
    sum_ref[...] = total
    short_ref[...] = total.astype(BF16)


def late_kernel(n_msgs, direct, *refs):
    sources, refs = refs[:6], refs[7:]
    owner_hbm, child_hbm, step_hbm, alog_hbm, dtb_hbm, skip_hbm = sources
    msgs, refs = refs[:n_msgs], refs[n_msgs:]
    conv_hbm, gate_ref, rate_ref, twin_ref, dtb_ref, skip_ref = refs[:6]
    owner_s, child_s, step_ref, alog, conv_s, sems = refs[6:]
    small = [
        pltpu.make_async_copy(source, target, sems.at[i])
        for i, (source, target) in enumerate(
            (
                (owner_hbm, owner_s),
                (child_hbm, child_s),
                (alog_hbm, alog),
                (dtb_hbm, dtb_ref),
                (skip_hbm, skip_ref),
            )
        )
    ]
    inputs = in_parts(step_hbm, step_ref, sems, len(small), STEP_PARTS)
    for copy in small + inputs:
        copy.start()
    held = read_messages(msgs)
    past, rb, _ = conv_s.shape
    steps = step_ref.shape[1]
    for copy in small:
        copy.wait()
    places = blocks_of(owner_s[0]) if direct else None
    child = scalar_onehot(child_s, places, (rb, len(held)))
    for k in range(past):
        at = steps - past + k
        conv_s[k] = pick_rows(child, [h[at : at + 1, :] for h in held]).astype(BF16)
    out = pltpu.make_async_copy(conv_s, conv_hbm, sems.at[len(small) + STEP_PARTS])
    out.start()
    rate = jnp.exp(alog[...]) * (-math.log2(math.e))
    rate_ref[...] = rate
    half = (twin_ref.shape[1] // 2, rate.shape[1])
    for m in range(rate.shape[0] // 2):
        two = [jnp.broadcast_to(rate[n : n + 1, :], half) for n in (2 * m, 2 * m + 1)]
        twin_ref[m] = jnp.concatenate(two, axis=0)
    for copy in inputs:
        copy.wait()
    for t in range(steps):
        gate_ref[t] = silu(step_ref[:, t, 1, :].astype(F32))
    out.wait()


def start_kernel(n_msgs, direct, text, pick_ref, sender_ref, after_ref, *rest):
    del after_ref
    msgs, rest = rest[:n_msgs], rest[n_msgs:]
    apart, (own_ref, slot_ref, state_s) = rest[:-3], rest[-3:]
    n_state = own_ref.shape[0]
    held = read_messages(msgs)
    owners = len(held)
    numbers = jnp.concatenate([h[text - 1 : text, :] for h in held], axis=0)
    states = [h[text:, :] for h in held]
    if direct:
        ssm_ref, pair_ref = apart
        head, low, came = [
            pair_ref[0].astype(F32)[i * n_state : (i + 1) * n_state, :] for i in range(3)
        ]
        states[0], states[2], states[3] = ssm_ref[0], came, head + low
    for k, state in enumerate(states):
        state_s[k] = state
    own = pick_ref[...]
    slot = slot_onehot(numbers, sender_ref)

    def two(m, carry):
        picked = []
        for n in (2 * m, 2 * m + 1):
            rows = [state_s[k, pl.ds(n, 1), :] for k in range(owners)]
            own_ref[n] = pick_rows(own, rows)
            picked.append(pick_rows(slot, rows))
        slot_ref[m] = jnp.concatenate(picked, axis=0)
        return carry

    lax.fori_loop(0, n_state // 2, two, 0, unroll=owners <= DIRECT)


def decode_kernel(
    direct,
    owner_hbm,
    child_hbm,
    act_ref,
    gate_ref,
    own_ref,
    slot_ref,
    rate_ref,
    twin_ref,
    dtw_ref,
    dtb_ref,
    skip_ref,
    part_ref,
    other_ref,
    dec_ref,
    child_ssm,
    owner_s,
    child_s,
    delta_s,
    gain_s,
    slot_delta_s,
    slot_gain_s,
    b_s,
    c_s,
    twin_b_s,
    slots_s,
    line_s,
    sems,
):
    scalars = [
        pltpu.make_async_copy(owner_hbm, owner_s, sems.at[0]),
        pltpu.make_async_copy(child_hbm, child_s, sems.at[1]),
    ]
    for copy in scalars:
        copy.start()
    rb, steps, channels = dec_ref.shape
    rank = dtw_ref.shape[0]
    n_state = rate_ref.shape[0]
    n_slots = slots_s.shape[0]
    own_rows = steps * rb
    chunks = channels // (WIDE * LANES)

    proj = part_ref[...] + other_ref[...].astype(F32)
    delta_in = proj[:, :rank].astype(BF16)
    delta = jnp.dot(delta_in, dtw_ref[...], preferred_element_type=F32) + dtb_ref[...]
    delta = jnp.maximum(delta, 0.0) + jnp.log(1.0 + jnp.exp(-jnp.abs(delta)))
    gain = delta * act_ref[...]
    delta_s[...] = delta[:own_rows, :]
    gain_s[...] = gain[:own_rows, :]

    def column(at, n, rows):
        return jnp.broadcast_to(at[:, n : n + 1], (rows, LANES))

    for t in range(steps):
        at = slice(own_rows + t * n_slots, own_rows + (t + 1) * n_slots)
        slot_delta_s[t] = jnp.concatenate([delta[at, :]] * 2, axis=0)
        slot_gain_s[t] = jnp.concatenate([gain[at, :]] * 2, axis=0)
        twice = jnp.concatenate([proj[at, rank:]] * 2, axis=0)
        upper = lax.broadcasted_iota(jnp.int32, (2 * n_slots, LANES), 0) < n_slots
        for m in range(n_state // 2):
            twin_b_s[m, t] = jnp.where(
                upper, column(twice, 2 * m, 2 * n_slots), column(twice, 2 * m + 1, 2 * n_slots)
            )
    for n in range(n_state):
        b_s[n] = column(proj[:own_rows, rank:], n, own_rows)
        c_s[n] = column(proj[:own_rows, rank:], n_state + n, own_rows)

    def wide(part):
        return jnp.concatenate([part] * WIDE, axis=1)

    def slot_chunk(chunk, carry):
        columns = pl.ds(pl.multiple_of(chunk * WIDE * LANES, WIDE * LANES), WIDE * LANES)
        delta = [slot_delta_s[t, :, columns] for t in range(steps)]
        gain = [slot_gain_s[t, :, columns] for t in range(steps)]
        for m in range(n_state // 2):
            rate = twin_ref[m, :, columns]
            state = slot_ref[m, :, columns]
            for t in range(steps):
                state = jnp.exp2(delta[t] * rate) * state + gain[t] * wide(twin_b_s[m, t])
            slots_s[:, 2 * m, columns] = state[:n_slots, :]
            slots_s[:, 2 * m + 1, columns] = state[n_slots:, :]
        return carry

    lax.fori_loop(0, chunks, slot_chunk, 0)
    for copy in scalars:
        copy.wait()
    places = blocks_of(owner_s[0]) if direct else None
    copies = []
    for j in range(rb):
        at = chosen(child_s[j], places) if direct else child_s[j]
        copy = pltpu.make_async_copy(slots_s.at[at], child_ssm.at[j], sems.at[2 + j])
        copy.start()
        copies.append(copy)

    def own_chunk(chunk, carry):
        columns = pl.ds(pl.multiple_of(chunk * WIDE * LANES, WIDE * LANES), WIDE * LANES)
        for first in range(0, rb, ROWS):
            at = [pl.ds(t * rb + first, ROWS) for t in range(steps)]
            delta = [delta_s[a, columns] for a in at]
            gain = [gain_s[a, columns] for a in at]
            sums = [skip_ref[:, columns] * act_ref[a, columns] for a in at]
            for n in range(n_state):
                rate = rate_ref[n : n + 1, columns]
                state = own_ref[n, pl.ds(first, ROWS), columns]
                for t in range(steps):
                    state = jnp.exp2(delta[t] * rate) * state + gain[t] * wide(b_s[n, at[t], :])
                    sums[t] = sums[t] + wide(c_s[n, at[t], :]) * state
            for t in range(steps):
                out = sums[t] * gate_ref[t, pl.ds(first, ROWS), columns]
                for w in range(WIDE):
                    line_s[w, pl.ds(first * steps + t, ROWS, stride=steps), :] = out[
                        :, w * LANES : (w + 1) * LANES
                    ]
        for w in range(WIDE):
            some = pl.ds(pl.multiple_of((chunk * WIDE + w) * LANES, LANES), LANES)
            dec_ref[:, :, some] = line_s[w].reshape(rb, steps, LANES).astype(BF16)
        return carry

    lax.fori_loop(0, chunks, own_chunk, 0)
    for copy in copies:
        copy.wait()


def on_device(
    prompt_ssm,
    prompt_conv,
    prompt_of,
    step_in,
    conv_weight,
    conv_bias,
    x_weight,
    dt_weight,
    dt_bias,
    a_log,
    skip,
    send_rows,
    child_slot,
):
    owners = lax.axis_size("branch")
    tensors = lax.axis_size("tensor")
    assert owners & (owners - 1) == 0 and tensors & (tensors - 1) == 0
    assert prompt_ssm.shape[0] == 1 and send_rows.shape[2] == 1
    rb, steps, _, channels = step_in.shape
    taps = conv_weight.shape[0]
    width = x_weight.shape[1]
    n_state = a_log.shape[0]
    rows = steps * (rb + owners)
    short = taps - 1 + steps + 1
    depth = short + n_state
    direct = owners == DIRECT
    owner = pinned(lax.axis_index("branch").astype(jnp.int32).reshape(1))

    if direct:
        msg_shapes = [(1, d, channels) for d in (short, depth, short, short)]
    else:
        msg_shapes = [(owners, depth, channels)]
    msgs = call(
        functools.partial(pack_kernel, direct),
        [shaped(s, BF16) for s in msg_shapes],
        [hbm()] * 6,
        [vmem()] * len(msg_shapes),
        [
            pltpu.SMEM((1,), jnp.int32),
            pltpu.SMEM((owners,), jnp.int32),
            pltpu.SMEM((rb,), jnp.int32),
            pltpu.VMEM(step_in.shape, BF16),
            pltpu.VMEM(prompt_conv.shape, BF16),
            pltpu.VMEM(prompt_ssm.shape, F32),
            pltpu.SemaphoreType.DMA((5 + STEP_PARTS,)),
        ],
        nbytes=owners * depth * channels * 2,
    )(
        owner,
        pinned(send_rows.reshape(owners)),
        pinned(prompt_of),
        pinned(step_in),
        pinned(prompt_conv),
        pinned(prompt_ssm),
    )
    if direct:
        own = msgs[0]
        msgs = [own] + [
            lax.ppermute(m, "branch", list(enumerate(to))) for m, to in zip(msgs[1:], SENDS)
        ]
        after = own
    else:
        msgs = [lax.all_to_all(msgs[0], "branch", split_axis=0, concat_axis=0, tiled=True)]
        after = msgs[0]
    n_msgs = len(msgs)
    base, pick, sender, taps_near, bias_near, weight_near = call(
        functools.partial(prepare_kernel, direct),
        [
            shaped((steps, rb, channels), F32),
            shaped((rb, owners), F32),
            shaped((1, owners), F32),
            shaped((taps, channels), F32),
            shaped((1, channels), F32),
            shaped((width, channels), BF16),
        ],
        [hbm()] * 6 + [anywhere()],
        [vmem()] * 6,
        [
            pltpu.VMEM(step_in.shape, BF16),
            pltpu.SMEM((1,), jnp.int32),
            pltpu.SMEM((rb,), jnp.int32),
            pltpu.SemaphoreType.DMA((4 + WEIGHT_PARTS + STEP_PARTS,)),
        ],
        flops=10 * steps * rb * channels,
        nbytes=12 * steps * rb * channels,
    )(
        owner,
        pinned(prompt_of),
        pinned(step_in),
        pinned(conv_weight),
        pinned(conv_bias[None]),
        pinned(x_weight.T),
        after,
    )
    states = []
    if direct:
        pair = call(
            functools.partial(pair_kernel, short),
            shaped((1, 3 * n_state, channels), BF16),
            [vmem()] * 2 + [anywhere()],
            vmem(),
            nbytes=12 * n_state * channels,
        )(prompt_ssm, msgs[1], pick)
        states = [prompt_ssm, swap(pair, "branch", 1)]
    act, part, brief = call(
        functools.partial(project_kernel, n_msgs),
        [
            shaped((rows, channels), F32),
            shaped((rows, width), F32),
            shaped((rows, width), BF16),
        ],
        [vmem()] * (6 + n_msgs),
        [vmem()] * 3,
        flops=2 * rows * channels * width,
        nbytes=channels * width * 2 + rows * (channels + width) * 4,
        trans=rows * channels,
    )(pick, sender, base, taps_near, bias_near, weight_near, *msgs)
    other = swap(brief, "tensor", 1)
    distance = 2
    while distance < tensors:
        part, brief = call(
            add_kernel,
            [shaped((rows, width), F32), shaped((rows, width), BF16)],
            [vmem()] * 2,
            [vmem()] * 2,
            flops=rows * width,
            nbytes=rows * width * 14,
        )(part, other)
        other = swap(brief, "tensor", 2 * distance - 1)
        distance *= 2

    child_conv, gate, rate, twin, dtb_near, skip_near = call(
        functools.partial(late_kernel, n_msgs, direct),
        [
            shaped((taps - 1, rb, channels), BF16),
            shaped((steps, rb, channels), F32),
            shaped((n_state, channels), F32),
            shaped((n_state // 2, 2 * owners, channels), F32),
            shaped((1, channels), F32),
            shaped((1, channels), F32),
        ],
        [hbm()] * 6 + [anywhere()] + [vmem()] * n_msgs,
        [anywhere()] + [vmem()] * 5,
        [
            pltpu.SMEM((1,), jnp.int32),
            pltpu.SMEM((rb,), jnp.int32),
            pltpu.VMEM(step_in.shape, BF16),
            pltpu.VMEM((n_state, channels), F32),
            pltpu.VMEM((taps - 1, rb, channels), BF16),
            pltpu.SemaphoreType.DMA((6 + STEP_PARTS,)),
        ],
        flops=10 * steps * rb * channels,
        nbytes=12 * steps * rb * channels,
        trans=steps * rb * channels,
    )(
        owner,
        pinned(child_slot),
        pinned(step_in),
        pinned(a_log),
        pinned(dt_bias[None]),
        pinned(skip[None]),
        part,
        *msgs,
    )
    own_start, slot_start = call(
        functools.partial(start_kernel, n_msgs, direct, short),
        [
            shaped((n_state, rb, channels), F32),
            shaped((n_state // 2, 2 * owners, channels), F32),
        ],
        [vmem()] * 2 + [anywhere()] + [vmem()] * (n_msgs + len(states)),
        [vmem()] * 2,
        [pltpu.VMEM((owners, n_state, channels), F32)],
        flops=2 * owners * n_state * (rb + owners) * channels,
        nbytes=4 * n_state * (rb + owners) * channels,
    )(pick, sender, part, *msgs, *states)

    decoded, child_ssm = call(
        functools.partial(decode_kernel, direct),
        [
            shaped((rb, steps, channels), BF16),
            shaped((rb, n_state, channels), F32),
        ],
        [hbm()] * 2 + [vmem()] * 11,
        [vmem(), anywhere()],
        [
            pltpu.SMEM((1,), jnp.int32),
            pltpu.SMEM((rb,), jnp.int32),
            pltpu.VMEM((steps * rb, channels), F32),
            pltpu.VMEM((steps * rb, channels), F32),
            pltpu.VMEM((steps, 2 * owners, channels), F32),
            pltpu.VMEM((steps, 2 * owners, channels), F32),
            pltpu.VMEM((n_state, steps * rb, LANES), F32),
            pltpu.VMEM((n_state, steps * rb, LANES), F32),
            pltpu.VMEM((n_state // 2, steps, 2 * owners, LANES), F32),
            pltpu.VMEM((owners, n_state, channels), F32),
            pltpu.VMEM((WIDE, steps * rb, LANES), F32),
            pltpu.SemaphoreType.DMA((2 + rb,)),
        ],
        flops=8 * rows * n_state * channels,
        nbytes=(rb + owners) * n_state * channels * 4,
        trans=rows * n_state * channels,
    )(
        owner,
        pinned(child_slot),
        act,
        gate,
        own_start,
        slot_start,
        rate,
        twin,
        dt_weight,
        dtb_near,
        skip_near,
        part,
        other,
    )
    return (decoded, child_ssm, jnp.transpose(child_conv, (1, 0, 2)))


def solution(mesh):
    placed = (
        P(("replica", "branch"), None, "tensor"),
        P(("replica", "branch"), None, "tensor"),
        P(("replica", "branch")),
        P(("replica", "branch"), None, None, "tensor"),
        P(None, "tensor"),
        P("tensor"),
        P("tensor", None),
        P(None, "tensor"),
        P("tensor"),
        P(None, "tensor"),
        P("tensor"),
        P(("replica", "branch"), None, None),
        P(("replica", "branch")),
    )
    return jax.shard_map(
        on_device,
        mesh=mesh,
        in_specs=placed,
        out_specs=(
            P(("replica", "branch"), None, "tensor"),
            P(("replica", "branch"), None, "tensor"),
            P(("replica", "branch"), None, "tensor"),
        ),
        check_vma=False,
    )
```

```python
import functools
import math

import jax
import jax.numpy as jnp
from jax import lax
from jax.experimental import pallas as pl
from jax.experimental.pallas import tpu as pltpu
from jax.sharding import PartitionSpec as P

F32 = jnp.float32
BF16 = jnp.bfloat16
LANES = 128
ROWS = 8
WIDE = 2
VMEM_LIMIT = 48 * 2**20
WEIGHT_PARTS = 6
STEP_PARTS = 4
DIRECT = 4
SENDS = ((2, 3, 1, 0), (3, 2, 0, 1), (1, 0, 3, 2))


def vmem():
    return pl.BlockSpec(memory_space=pltpu.VMEM)


def hbm():
    return pl.BlockSpec(memory_space=pltpu.HBM)


def anywhere():
    return pl.BlockSpec(memory_space=pl.ANY)


def pinned(array):
    return pltpu.with_memory_space_constraint(array, pltpu.HBM)


def shaped(shape, dtype):
    return jax.ShapeDtypeStruct(shape, dtype)


def call(kernel, outs, in_specs, out_specs, scratch=(), flops=0, nbytes=0, trans=0):
    return pl.pallas_call(
        kernel,
        out_shape=outs,
        in_specs=in_specs,
        out_specs=out_specs,
        scratch_shapes=list(scratch),
        compiler_params=pltpu.CompilerParams(vmem_limit_bytes=VMEM_LIMIT),
        cost_estimate=pl.CostEstimate(flops=flops, bytes_accessed=nbytes, transcendentals=trans),
    )


def swap(value, axis, distance):
    size = lax.axis_size(axis)
    return lax.ppermute(value, axis, [(i, i ^ distance) for i in range(size)])


def chosen(number, values):
    total = values[0]
    for i in range(1, len(values)):
        total = jnp.where(number == i, values[i], total)
    return total


def blocks_of(owner):
    table = [
        [0 if s == r else 1 + [to[s] for to in SENDS].index(r) for s in range(DIRECT)]
        for r in range(DIRECT)
    ]
    return [chosen(owner, [row[s] for row in table]) for s in range(DIRECT)]


def all_of(copies):
    for copy in copies:
        copy.start()
    for copy in copies:
        copy.wait()


def read_messages(refs):
    return [ref[i].astype(F32) for ref in refs for i in range(ref.shape[0])]


def in_parts(source, target, sems, first, count):
    rows = source.shape[0] // count
    at = [pl.ds(i * rows, rows) for i in range(count)]
    return [
        pltpu.make_async_copy(source.at[a], target.at[a], sems.at[first + i])
        for i, a in enumerate(at)
    ]


def scalar_onehot(senders_s, places, shape):
    row_of = lax.broadcasted_iota(jnp.int32, shape, 0)
    wanted = jnp.zeros(shape, jnp.int32)
    for b in range(shape[0]):
        wanted = jnp.where(row_of == b, senders_s[b], wanted)
    wanted = wanted if places is None else chosen(wanted, places)
    return (wanted == lax.broadcasted_iota(jnp.int32, shape, 1)).astype(F32)


def pick_rows(pick, rows):
    total = pick[:, 0:1] * rows[0]
    for k in range(1, len(rows)):
        total = total + pick[:, k : k + 1] * rows[k]
    return total


def pack_kernel(direct, owner_hbm, rows_hbm, prompt_hbm, step_hbm, conv_hbm, ssm_hbm, *rest):
    outs, (owner_s, rows_s, prompt_s, step, conv, ssm, sems) = rest[:-7], rest[-7:]
    owners = rows_hbm.shape[0]
    channels = step_hbm.shape[3]
    copies = [
        pltpu.make_async_copy(owner_hbm, owner_s, sems.at[4]),
        pltpu.make_async_copy(rows_hbm, rows_s, sems.at[0]),
        pltpu.make_async_copy(prompt_hbm, prompt_s, sems.at[1]),
        pltpu.make_async_copy(conv_hbm, conv, sems.at[2]),
        pltpu.make_async_copy(ssm_hbm, ssm, sems.at[3]),
    ]
    all_of(copies + in_parts(step_hbm, step, sems, 5, STEP_PARTS))
    owner = owner_s[0]
    window = conv[0].astype(F32)

    def write(ref, target):
        row = jnp.maximum(rows_s[target], 0)
        xs = step[row, :, 0, :].astype(F32)
        number = prompt_s[row].astype(F32)
        pieces = [xs, window, jnp.full((1, channels), number, F32)]
        if ref.shape[0] > sum(p.shape[0] for p in pieces):
            pieces.append(ssm[0])
        ref[...] = jnp.concatenate(pieces, axis=0).astype(BF16)

    if direct:
        write(outs[0].at[0], owner)
        for ref, to in zip(outs[1:], SENDS):
            write(ref.at[0], chosen(owner, to))
    else:
        for target in range(owners):
            write(outs[0].at[target], target)


def pair_kernel(text, ssm_ref, came_ref, after_ref, pair_ref):
    del after_ref
    state = ssm_ref[0]
    head = state.astype(BF16).astype(F32)
    came = came_ref[0].astype(F32)[text:, :]
    pair_ref[0] = jnp.concatenate([head, state - head, came], axis=0).astype(BF16)


def silu(v):
    return v / (1.0 + jnp.exp(-v))


def prepare_kernel(
    direct,
    owner_hbm,
    prompt_hbm,
    step_hbm,
    cw_hbm,
    cb_hbm,
    xwt_hbm,
    after_ref,
    base_ref,
    pick_ref,
    sender_ref,
    cw_ref,
    cb_ref,
    xwt_ref,
    step_ref,
    owner_s,
    prompt_s,
    sems,
):
    del after_ref
    small = [
        pltpu.make_async_copy(source, target, sems.at[i])
        for i, (source, target) in enumerate(
            ((cw_hbm, cw_ref), (cb_hbm, cb_ref), (owner_hbm, owner_s), (prompt_hbm, prompt_s))
        )
    ]
    inputs = in_parts(step_hbm, step_ref, sems, len(small), STEP_PARTS)
    large = in_parts(xwt_hbm, xwt_ref, sems, len(small) + STEP_PARTS, WEIGHT_PARTS)
    for copy in inputs + small + large:
        copy.start()
    for copy in inputs + small:
        copy.wait()
    steps = step_ref.shape[1]
    taps = cw_hbm.shape[0]
    xs = [step_ref[:, t, 0, :].astype(F32) for t in range(steps)]
    for t in range(steps):
        total = cw_ref[taps - 1 : taps, :] * xs[t] + cb_ref[...]
        for k in range(max(0, taps - 1 - t), taps - 1):
            total = total + cw_ref[k : k + 1, :] * xs[t + k - taps + 1]
        base_ref[t] = total
    places = blocks_of(owner_s[0]) if direct else None
    pick_ref[...] = scalar_onehot(prompt_s, places, pick_ref.shape)
    column = lax.broadcasted_iota(jnp.int32, sender_ref.shape, 1)
    sender = column
    for sent, place in enumerate(places or []):
        sender = jnp.where(column == place, sent, sender)
    sender_ref[...] = sender.astype(F32)
    for copy in large:
        copy.wait()


def softplus(v):
    return jnp.maximum(v, 0.0) + jnp.log(1.0 + jnp.exp(-jnp.abs(v)))


def slot_onehot(numbers, sender_ref):
    owners = sender_ref.shape[1]
    return (numbers[:, :owners] == sender_ref[...]).astype(F32)


def project_kernel(n_msgs, pick_ref, sender_ref, base_ref, cw_ref, cb_ref, xwt_ref, *rest):
    msgs, (act_ref, part_ref, short_ref) = rest[:n_msgs], rest[n_msgs:]
    taps = cw_ref.shape[0]
    steps, rb, _ = base_ref.shape
    past = taps - 1
    held = read_messages(msgs)
    owners = len(held)
    windows = [[h[steps + k : steps + k + 1, :] for h in held] for k in range(past)]
    own = pick_ref[...]
    own_windows = [pick_rows(own, w) for w in windows]
    for t in range(steps):
        conv = base_ref[t]
        for k in range(past - t):
            conv = conv + cw_ref[k : k + 1, :] * own_windows[t + k]
        act_ref[t * rb : (t + 1) * rb, :] = silu(conv)

    def line_of(row):
        return jnp.concatenate([h[row : row + 1, :] for h in held], axis=0)

    slot = slot_onehot(line_of(past + steps), sender_ref)
    line = [pick_rows(slot, w) for w in windows]
    line += [line_of(t) for t in range(steps)]
    row = steps * rb
    for t in range(steps):
        conv = cw_ref[past:taps, :] * line[t + past] + cb_ref[...]
        for k in range(past):
            conv = conv + cw_ref[k : k + 1, :] * line[t + k]
        act_ref[row : row + owners, :] = silu(conv)
        row += owners
    part = lax.dot_general(
        act_ref[...].astype(BF16),
        xwt_ref[...],
        (((1,), (1,)), ((), ())),
        preferred_element_type=F32,
    )
    part_ref[...] = part
    short_ref[...] = part.astype(BF16)


def add_kernel(a_ref, b_ref, sum_ref, short_ref):
    total = a_ref[...] + b_ref[...].astype(F32)
    sum_ref[...] = total
    short_ref[...] = total.astype(BF16)


def late_kernel(n_msgs, direct, *refs):
    sources, refs = refs[:6], refs[7:]
    owner_hbm, child_hbm, step_hbm, alog_hbm, dtb_hbm, skip_hbm = sources
    msgs, refs = refs[:n_msgs], refs[n_msgs:]
    conv_hbm, gate_ref, rate_ref, twin_ref, dtb_ref, skip_ref = refs[:6]
    owner_s, child_s, step_ref, alog, conv_s, sems = refs[6:]
    small = [
        pltpu.make_async_copy(source, target, sems.at[i])
        for i, (source, target) in enumerate(
            (
                (owner_hbm, owner_s),
                (child_hbm, child_s),
                (alog_hbm, alog),
                (dtb_hbm, dtb_ref),
                (skip_hbm, skip_ref),
            )
        )
    ]
    inputs = in_parts(step_hbm, step_ref, sems, len(small), STEP_PARTS)
    for copy in small + inputs:
        copy.start()
    held = read_messages(msgs)
    past, rb, _ = conv_s.shape
    steps = step_ref.shape[1]
    for copy in small:
        copy.wait()
    places = blocks_of(owner_s[0]) if direct else None
    child = scalar_onehot(child_s, places, (rb, len(held)))
    for k in range(past):
        at = steps - past + k
        conv_s[k] = pick_rows(child, [h[at : at + 1, :] for h in held]).astype(BF16)
    out = pltpu.make_async_copy(conv_s, conv_hbm, sems.at[len(small) + STEP_PARTS])
    out.start()
    rate = jnp.exp(alog[...]) * (-math.log2(math.e))
    rate_ref[...] = rate
    half = (twin_ref.shape[1] // 2, rate.shape[1])
    for m in range(rate.shape[0] // 2):
        two = [jnp.broadcast_to(rate[n : n + 1, :], half) for n in (2 * m, 2 * m + 1)]
        twin_ref[m] = jnp.concatenate(two, axis=0)
    for copy in inputs:
        copy.wait()
    for t in range(steps):
        gate_ref[t] = silu(step_ref[:, t, 1, :].astype(F32))
    out.wait()


def start_kernel(n_msgs, direct, text, pick_ref, sender_ref, after_ref, *rest):
    del after_ref
    msgs, rest = rest[:n_msgs], rest[n_msgs:]
    apart, (own_ref, slot_ref, state_s) = rest[:-3], rest[-3:]
    n_state = own_ref.shape[0]
    held = read_messages(msgs)
    owners = len(held)
    numbers = jnp.concatenate([h[text - 1 : text, :] for h in held], axis=0)
    states = [h[text:, :] for h in held]
    if direct:
        ssm_ref, pair_ref = apart
        head, low, came = [
            pair_ref[0].astype(F32)[i * n_state : (i + 1) * n_state, :] for i in range(3)
        ]
        states[0], states[2], states[3] = ssm_ref[0], came, head + low
    for k, state in enumerate(states):
        state_s[k] = state
    own = pick_ref[...]
    slot = slot_onehot(numbers, sender_ref)

    def two(m, carry):
        picked = []
        for n in (2 * m, 2 * m + 1):
            rows = [state_s[k, pl.ds(n, 1), :] for k in range(owners)]
            own_ref[n] = pick_rows(own, rows)
            picked.append(pick_rows(slot, rows))
        slot_ref[m] = jnp.concatenate(picked, axis=0)
        return carry

    lax.fori_loop(0, n_state // 2, two, 0, unroll=owners <= DIRECT)


def decode_kernel(
    direct,
    owner_hbm,
    child_hbm,
    act_ref,
    gate_ref,
    own_ref,
    slot_ref,
    rate_ref,
    twin_ref,
    dtw_ref,
    dtb_ref,
    skip_ref,
    part_ref,
    other_ref,
    dec_ref,
    child_ssm,
    owner_s,
    child_s,
    delta_s,
    gain_s,
    slot_delta_s,
    slot_gain_s,
    b_s,
    c_s,
    twin_b_s,
    slots_s,
    line_s,
    sems,
):
    scalars = [
        pltpu.make_async_copy(owner_hbm, owner_s, sems.at[0]),
        pltpu.make_async_copy(child_hbm, child_s, sems.at[1]),
    ]
    for copy in scalars:
        copy.start()
    rb, steps, channels = dec_ref.shape
    rank = dtw_ref.shape[0]
    n_state = rate_ref.shape[0]
    n_slots = slots_s.shape[0]
    own_rows = steps * rb
    chunks = channels // (WIDE * LANES)

    proj = part_ref[...] + other_ref[...].astype(F32)
    delta_in = proj[:, :rank].astype(BF16)
    raw = jnp.dot(delta_in, dtw_ref[...], preferred_element_type=F32) + dtb_ref[...]
    delta_s[...] = raw[:own_rows, :]
    delta = softplus(raw[own_rows:, :])
    gain = delta * act_ref[own_rows:, :]

    def column(at, n, rows):
        return jnp.broadcast_to(at[:, n : n + 1], (rows, LANES))

    for t in range(steps):
        at = slice(t * n_slots, (t + 1) * n_slots)
        slot_delta_s[t] = jnp.concatenate([delta[at, :]] * 2, axis=0)
        slot_gain_s[t] = jnp.concatenate([gain[at, :]] * 2, axis=0)
        twice = jnp.concatenate([proj[own_rows:, rank:][at, :]] * 2, axis=0)
        upper = lax.broadcasted_iota(jnp.int32, (2 * n_slots, LANES), 0) < n_slots
        for m in range(n_state // 2):
            twin_b_s[m, t] = jnp.where(
                upper, column(twice, 2 * m, 2 * n_slots), column(twice, 2 * m + 1, 2 * n_slots)
            )

    def wide(part):
        return jnp.concatenate([part] * WIDE, axis=1)

    def slot_chunk(chunk, carry):
        columns = pl.ds(pl.multiple_of(chunk * WIDE * LANES, WIDE * LANES), WIDE * LANES)
        delta = [slot_delta_s[t, :, columns] for t in range(steps)]
        gain = [slot_gain_s[t, :, columns] for t in range(steps)]
        for m in range(n_state // 2):
            rate = twin_ref[m, :, columns]
            state = slot_ref[m, :, columns]
            for t in range(steps):
                state = jnp.exp2(delta[t] * rate) * state + gain[t] * wide(twin_b_s[m, t])
            slots_s[:, 2 * m, columns] = state[:n_slots, :]
            slots_s[:, 2 * m + 1, columns] = state[n_slots:, :]
        return carry

    lax.fori_loop(0, chunks, slot_chunk, 0)
    for copy in scalars:
        copy.wait()
    places = blocks_of(owner_s[0]) if direct else None
    copies = []
    for j in range(rb):
        at = chosen(child_s[j], places) if direct else child_s[j]
        copy = pltpu.make_async_copy(slots_s.at[at], child_ssm.at[j], sems.at[2 + j])
        copy.start()
        copies.append(copy)

    delta = softplus(delta_s[...])
    delta_s[...] = delta
    gain_s[...] = delta * act_ref[:own_rows, :]
    proj = part_ref[:own_rows, rank:] + other_ref[:own_rows, rank:].astype(F32)
    for n in range(n_state):
        b_s[n] = column(proj, n, own_rows)
        c_s[n] = column(proj, n_state + n, own_rows)

    def own_chunk(chunk, carry):
        columns = pl.ds(pl.multiple_of(chunk * WIDE * LANES, WIDE * LANES), WIDE * LANES)
        for first in range(0, rb, ROWS):
            at = [pl.ds(t * rb + first, ROWS) for t in range(steps)]
            delta = [delta_s[a, columns] for a in at]
            gain = [gain_s[a, columns] for a in at]
            sums = [skip_ref[:, columns] * act_ref[a, columns] for a in at]
            for n in range(n_state):
                rate = rate_ref[n : n + 1, columns]
                state = own_ref[n, pl.ds(first, ROWS), columns]
                for t in range(steps):
                    state = jnp.exp2(delta[t] * rate) * state + gain[t] * wide(b_s[n, at[t], :])
                    sums[t] = sums[t] + wide(c_s[n, at[t], :]) * state
            for t in range(steps):
                out = sums[t] * gate_ref[t, pl.ds(first, ROWS), columns]
                for w in range(WIDE):
                    line_s[w, pl.ds(first * steps + t, ROWS, stride=steps), :] = out[
                        :, w * LANES : (w + 1) * LANES
                    ]
        for w in range(WIDE):
            some = pl.ds(pl.multiple_of((chunk * WIDE + w) * LANES, LANES), LANES)
            dec_ref[:, :, some] = line_s[w].reshape(rb, steps, LANES).astype(BF16)
        return carry

    lax.fori_loop(0, chunks, own_chunk, 0)
    for copy in copies:
        copy.wait()


def on_device(
    prompt_ssm,
    prompt_conv,
    prompt_of,
    step_in,
    conv_weight,
    conv_bias,
    x_weight,
    dt_weight,
    dt_bias,
    a_log,
    skip,
    send_rows,
    child_slot,
):
    owners = lax.axis_size("branch")
    tensors = lax.axis_size("tensor")
    assert owners & (owners - 1) == 0 and tensors & (tensors - 1) == 0
    assert prompt_ssm.shape[0] == 1 and send_rows.shape[2] == 1
    rb, steps, _, channels = step_in.shape
    taps = conv_weight.shape[0]
    width = x_weight.shape[1]
    n_state = a_log.shape[0]
    rows = steps * (rb + owners)
    short = taps - 1 + steps + 1
    depth = short + n_state
    direct = owners == DIRECT
    owner = pinned(lax.axis_index("branch").astype(jnp.int32).reshape(1))

    if direct:
        msg_shapes = [(1, d, channels) for d in (short, depth, short, short)]
    else:
        msg_shapes = [(owners, depth, channels)]
    msgs = call(
        functools.partial(pack_kernel, direct),
        [shaped(s, BF16) for s in msg_shapes],
        [hbm()] * 6,
        [vmem()] * len(msg_shapes),
        [
            pltpu.SMEM((1,), jnp.int32),
            pltpu.SMEM((owners,), jnp.int32),
            pltpu.SMEM((rb,), jnp.int32),
            pltpu.VMEM(step_in.shape, BF16),
            pltpu.VMEM(prompt_conv.shape, BF16),
            pltpu.VMEM(prompt_ssm.shape, F32),
            pltpu.SemaphoreType.DMA((5 + STEP_PARTS,)),
        ],
        nbytes=owners * depth * channels * 2,
    )(
        owner,
        pinned(send_rows.reshape(owners)),
        pinned(prompt_of),
        pinned(step_in),
        pinned(prompt_conv),
        pinned(prompt_ssm),
    )
    if direct:
        own = msgs[0]
        msgs = [own] + [
            lax.ppermute(m, "branch", list(enumerate(to))) for m, to in zip(msgs[1:], SENDS)
        ]
        after = own
    else:
        msgs = [lax.all_to_all(msgs[0], "branch", split_axis=0, concat_axis=0, tiled=True)]
        after = msgs[0]
    n_msgs = len(msgs)
    base, pick, sender, taps_near, bias_near, weight_near = call(
        functools.partial(prepare_kernel, direct),
        [
            shaped((steps, rb, channels), F32),
            shaped((rb, owners), F32),
            shaped((1, owners), F32),
            shaped((taps, channels), F32),
            shaped((1, channels), F32),
            shaped((width, channels), BF16),
        ],
        [hbm()] * 6 + [anywhere()],
        [vmem()] * 6,
        [
            pltpu.VMEM(step_in.shape, BF16),
            pltpu.SMEM((1,), jnp.int32),
            pltpu.SMEM((rb,), jnp.int32),
            pltpu.SemaphoreType.DMA((4 + WEIGHT_PARTS + STEP_PARTS,)),
        ],
        flops=10 * steps * rb * channels,
        nbytes=12 * steps * rb * channels,
    )(
        owner,
        pinned(prompt_of),
        pinned(step_in),
        pinned(conv_weight),
        pinned(conv_bias[None]),
        pinned(x_weight.T),
        after,
    )
    states = []
    if direct:
        pair = call(
            functools.partial(pair_kernel, short),
            shaped((1, 3 * n_state, channels), BF16),
            [vmem()] * 2 + [anywhere()],
            vmem(),
            nbytes=12 * n_state * channels,
        )(prompt_ssm, msgs[1], pick)
        states = [prompt_ssm, swap(pair, "branch", 1)]
    act, part, brief = call(
        functools.partial(project_kernel, n_msgs),
        [
            shaped((rows, channels), F32),
            shaped((rows, width), F32),
            shaped((rows, width), BF16),
        ],
        [vmem()] * (6 + n_msgs),
        [vmem()] * 3,
        flops=2 * rows * channels * width,
        nbytes=channels * width * 2 + rows * (channels + width) * 4,
        trans=rows * channels,
    )(pick, sender, base, taps_near, bias_near, weight_near, *msgs)
    other = swap(brief, "tensor", 1)
    distance = 2
    while distance < tensors:
        part, brief = call(
            add_kernel,
            [shaped((rows, width), F32), shaped((rows, width), BF16)],
            [vmem()] * 2,
            [vmem()] * 2,
            flops=rows * width,
            nbytes=rows * width * 14,
        )(part, other)
        other = swap(brief, "tensor", 2 * distance - 1)
        distance *= 2

    child_conv, gate, rate, twin, dtb_near, skip_near = call(
        functools.partial(late_kernel, n_msgs, direct),
        [
            shaped((taps - 1, rb, channels), BF16),
            shaped((steps, rb, channels), F32),
            shaped((n_state, channels), F32),
            shaped((n_state // 2, 2 * owners, channels), F32),
            shaped((1, channels), F32),
            shaped((1, channels), F32),
        ],
        [hbm()] * 6 + [anywhere()] + [vmem()] * n_msgs,
        [anywhere()] + [vmem()] * 5,
        [
            pltpu.SMEM((1,), jnp.int32),
            pltpu.SMEM((rb,), jnp.int32),
            pltpu.VMEM(step_in.shape, BF16),
            pltpu.VMEM((n_state, channels), F32),
            pltpu.VMEM((taps - 1, rb, channels), BF16),
            pltpu.SemaphoreType.DMA((6 + STEP_PARTS,)),
        ],
        flops=10 * steps * rb * channels,
        nbytes=12 * steps * rb * channels,
        trans=steps * rb * channels,
    )(
        owner,
        pinned(child_slot),
        pinned(step_in),
        pinned(a_log),
        pinned(dt_bias[None]),
        pinned(skip[None]),
        part,
        *msgs,
    )
    own_start, slot_start = call(
        functools.partial(start_kernel, n_msgs, direct, short),
        [
            shaped((n_state, rb, channels), F32),
            shaped((n_state // 2, 2 * owners, channels), F32),
        ],
        [vmem()] * 2 + [anywhere()] + [vmem()] * (n_msgs + len(states)),
        [vmem()] * 2,
        [pltpu.VMEM((owners, n_state, channels), F32)],
        flops=2 * owners * n_state * (rb + owners) * channels,
        nbytes=4 * n_state * (rb + owners) * channels,
    )(pick, sender, part, *msgs, *states)

    decoded, child_ssm = call(
        functools.partial(decode_kernel, direct),
        [
            shaped((rb, steps, channels), BF16),
            shaped((rb, n_state, channels), F32),
        ],
        [hbm()] * 2 + [vmem()] * 11,
        [vmem(), anywhere()],
        [
            pltpu.SMEM((1,), jnp.int32),
            pltpu.SMEM((rb,), jnp.int32),
            pltpu.VMEM((steps * rb, channels), F32),
            pltpu.VMEM((steps * rb, channels), F32),
            pltpu.VMEM((steps, 2 * owners, channels), F32),
            pltpu.VMEM((steps, 2 * owners, channels), F32),
            pltpu.VMEM((n_state, steps * rb, LANES), F32),
            pltpu.VMEM((n_state, steps * rb, LANES), F32),
            pltpu.VMEM((n_state // 2, steps, 2 * owners, LANES), F32),
            pltpu.VMEM((owners, n_state, channels), F32),
            pltpu.VMEM((WIDE, steps * rb, LANES), F32),
            pltpu.SemaphoreType.DMA((2 + rb,)),
        ],
        flops=8 * rows * n_state * channels,
        nbytes=(rb + owners) * n_state * channels * 4,
        trans=rows * n_state * channels,
    )(
        owner,
        pinned(child_slot),
        act,
        gate,
        own_start,
        slot_start,
        rate,
        twin,
        dt_weight,
        dtb_near,
        skip_near,
        part,
        other,
    )
    return (decoded, child_ssm, jnp.transpose(child_conv, (1, 0, 2)))


def solution(mesh):
    placed = (
        P(("replica", "branch"), None, "tensor"),
        P(("replica", "branch"), None, "tensor"),
        P(("replica", "branch")),
        P(("replica", "branch"), None, None, "tensor"),
        P(None, "tensor"),
        P("tensor"),
        P("tensor", None),
        P(None, "tensor"),
        P("tensor"),
        P(None, "tensor"),
        P("tensor"),
        P(("replica", "branch"), None, None),
        P(("replica", "branch")),
    )
    return jax.shard_map(
        on_device,
        mesh=mesh,
        in_specs=placed,
        out_specs=(
            P(("replica", "branch"), None, "tensor"),
            P(("replica", "branch"), None, "tensor"),
            P(("replica", "branch"), None, "tensor"),
        ),
        check_vma=False,
    )
```

```python
import functools
import math

import jax
import jax.numpy as jnp
from jax import lax
from jax.experimental import pallas as pl
from jax.experimental.pallas import tpu as pltpu
from jax.sharding import PartitionSpec as P

F32 = jnp.float32
BF16 = jnp.bfloat16
LANES = 128
ROWS = 8
WIDE = 2
SLOT_WIDE = 4
VMEM_LIMIT = 48 * 2**20
WEIGHT_PARTS = 6
STEP_PARTS = 4
DIRECT = 4
SENDS = ((2, 3, 1, 0), (3, 2, 0, 1), (1, 0, 3, 2))


def vmem():
    return pl.BlockSpec(memory_space=pltpu.VMEM)


def hbm():
    return pl.BlockSpec(memory_space=pltpu.HBM)


def anywhere():
    return pl.BlockSpec(memory_space=pl.ANY)


def pinned(array):
    return pltpu.with_memory_space_constraint(array, pltpu.HBM)


def shaped(shape, dtype):
    return jax.ShapeDtypeStruct(shape, dtype)


def call(kernel, outs, in_specs, out_specs, scratch=(), flops=0, nbytes=0, trans=0):
    return pl.pallas_call(
        kernel,
        out_shape=outs,
        in_specs=in_specs,
        out_specs=out_specs,
        scratch_shapes=list(scratch),
        compiler_params=pltpu.CompilerParams(vmem_limit_bytes=VMEM_LIMIT),
        cost_estimate=pl.CostEstimate(flops=flops, bytes_accessed=nbytes, transcendentals=trans),
    )


def swap(value, axis, distance):
    size = lax.axis_size(axis)
    return lax.ppermute(value, axis, [(i, i ^ distance) for i in range(size)])


def chosen(number, values):
    total = values[0]
    for i in range(1, len(values)):
        total = jnp.where(number == i, values[i], total)
    return total


def blocks_of(owner):
    table = [
        [0 if s == r else 1 + [to[s] for to in SENDS].index(r) for s in range(DIRECT)]
        for r in range(DIRECT)
    ]
    return [chosen(owner, [row[s] for row in table]) for s in range(DIRECT)]


def all_of(copies):
    for copy in copies:
        copy.start()
    for copy in copies:
        copy.wait()


def read_messages(refs):
    return [ref[i].astype(F32) for ref in refs for i in range(ref.shape[0])]


def in_parts(source, target, sems, first, count):
    rows = source.shape[0] // count
    at = [pl.ds(i * rows, rows) for i in range(count)]
    return [
        pltpu.make_async_copy(source.at[a], target.at[a], sems.at[first + i])
        for i, a in enumerate(at)
    ]


def scalar_onehot(senders_s, places, shape):
    row_of = lax.broadcasted_iota(jnp.int32, shape, 0)
    wanted = jnp.zeros(shape, jnp.int32)
    for b in range(shape[0]):
        wanted = jnp.where(row_of == b, senders_s[b], wanted)
    wanted = wanted if places is None else chosen(wanted, places)
    return (wanted == lax.broadcasted_iota(jnp.int32, shape, 1)).astype(F32)


def pick_rows(pick, rows):
    total = pick[:, 0:1] * rows[0]
    for k in range(1, len(rows)):
        total = total + pick[:, k : k + 1] * rows[k]
    return total


def message(target, rows_s, prompt_s, step, conv, state):
    row = jnp.maximum(rows_s[target], 0)
    xs = step[row, :, 0, :].astype(F32)
    number = jnp.full((1, xs.shape[1]), prompt_s[row].astype(F32), F32)
    pieces = [xs, conv[0].astype(F32), number] + ([] if state is None else [state])
    return jnp.concatenate(pieces, axis=0).astype(BF16)


def pack_kernel(direct, owner_hbm, rows_hbm, prompt_hbm, step_hbm, conv_hbm, ssm_hbm, *rest):
    outs, (owner_s, rows_s, prompt_s, step, conv, ssm, sems) = rest[:-7], rest[-7:]
    owners = rows_hbm.shape[0]
    copies = [
        pltpu.make_async_copy(owner_hbm, owner_s, sems.at[4]),
        pltpu.make_async_copy(rows_hbm, rows_s, sems.at[0]),
        pltpu.make_async_copy(prompt_hbm, prompt_s, sems.at[1]),
        pltpu.make_async_copy(conv_hbm, conv, sems.at[2]),
        pltpu.make_async_copy(ssm_hbm, ssm, sems.at[3]),
    ]
    all_of(copies + in_parts(step_hbm, step, sems, 5, STEP_PARTS))
    owner = owner_s[0]
    targets = [chosen(owner, to) for to in SENDS] if direct else range(owners)
    for i, target in enumerate(targets):
        ref = outs[i].at[0] if direct else outs[0].at[i]
        state = ssm[0] if ref.shape[0] > conv.shape[1] + step.shape[1] + 1 else None
        ref[...] = message(target, rows_s, prompt_s, step, conv, state)


def pair_kernel(text, ssm_ref, came_ref, after_ref, pair_ref):
    del after_ref
    state = ssm_ref[0]
    head = state.astype(BF16).astype(F32)
    came = came_ref[0].astype(F32)[text:, :]
    pair_ref[0] = jnp.concatenate([head, state - head, came], axis=0).astype(BF16)


def silu(v):
    return v / (1.0 + jnp.exp(-v))


def prepare_kernel(
    direct,
    owner_hbm,
    prompt_hbm,
    rows_hbm,
    conv_hbm,
    step_hbm,
    cw_hbm,
    cb_hbm,
    xwt_hbm,
    after_ref,
    own_ref,
    base_ref,
    pick_ref,
    sender_ref,
    cw_ref,
    cb_ref,
    xwt_ref,
    step_ref,
    owner_s,
    prompt_s,
    rows_s,
    conv,
    sems,
):
    del after_ref
    small = [
        pltpu.make_async_copy(source, target, sems.at[i])
        for i, (source, target) in enumerate(
            (
                (cw_hbm, cw_ref),
                (cb_hbm, cb_ref),
                (owner_hbm, owner_s),
                (prompt_hbm, prompt_s),
                (rows_hbm, rows_s),
                (conv_hbm, conv),
            )
        )
    ]
    inputs = in_parts(step_hbm, step_ref, sems, len(small), STEP_PARTS)
    large = in_parts(xwt_hbm, xwt_ref, sems, len(small) + STEP_PARTS, WEIGHT_PARTS)
    for copy in inputs + small + large:
        copy.start()
    for copy in inputs + small:
        copy.wait()
    own_ref[0] = message(owner_s[0], rows_s, prompt_s, step_ref, conv, None)
    steps = step_ref.shape[1]
    taps = cw_hbm.shape[0]
    xs = [step_ref[:, t, 0, :].astype(F32) for t in range(steps)]
    for t in range(steps):
        total = cw_ref[taps - 1 : taps, :] * xs[t] + cb_ref[...]
        for k in range(max(0, taps - 1 - t), taps - 1):
            total = total + cw_ref[k : k + 1, :] * xs[t + k - taps + 1]
        base_ref[t] = total
    places = blocks_of(owner_s[0]) if direct else None
    pick_ref[...] = scalar_onehot(prompt_s, places, pick_ref.shape)
    column = lax.broadcasted_iota(jnp.int32, sender_ref.shape, 1)
    sender = column
    for sent, place in enumerate(places or []):
        sender = jnp.where(column == place, sent, sender)
    sender_ref[...] = sender.astype(F32)
    for copy in large:
        copy.wait()


def slot_onehot(numbers, sender_ref):
    owners = sender_ref.shape[1]
    return (numbers[:, :owners] == sender_ref[...]).astype(F32)


def project_kernel(n_msgs, pick_ref, sender_ref, base_ref, cw_ref, cb_ref, xwt_ref, *rest):
    msgs, (act_ref, part_ref, short_ref) = rest[:n_msgs], rest[n_msgs:]
    taps = cw_ref.shape[0]
    steps, rb, _ = base_ref.shape
    past = taps - 1
    held = read_messages(msgs)
    owners = len(held)
    windows = [[h[steps + k : steps + k + 1, :] for h in held] for k in range(past)]
    own = pick_ref[...]
    own_windows = [pick_rows(own, w) for w in windows]
    for t in range(steps):
        conv = base_ref[t]
        for k in range(past - t):
            conv = conv + cw_ref[k : k + 1, :] * own_windows[t + k]
        act_ref[t * rb : (t + 1) * rb, :] = silu(conv)

    def line_of(row):
        return jnp.concatenate([h[row : row + 1, :] for h in held], axis=0)

    slot = slot_onehot(line_of(past + steps), sender_ref)
    line = [pick_rows(slot, w) for w in windows]
    line += [line_of(t) for t in range(steps)]
    row = steps * rb
    for t in range(steps):
        conv = cw_ref[past:taps, :] * line[t + past] + cb_ref[...]
        for k in range(past):
            conv = conv + cw_ref[k : k + 1, :] * line[t + k]
        act_ref[row : row + owners, :] = silu(conv)
        row += owners
    part = lax.dot_general(
        act_ref[...].astype(BF16),
        xwt_ref[...],
        (((1,), (1,)), ((), ())),
        preferred_element_type=F32,
    )
    part_ref[...] = part
    short_ref[...] = part.astype(BF16)


def add_kernel(a_ref, b_ref, sum_ref, short_ref):
    total = a_ref[...] + b_ref[...].astype(F32)
    sum_ref[...] = total
    short_ref[...] = total.astype(BF16)


def late_kernel(n_msgs, direct, *refs):
    sources, refs = refs[:6], refs[7:]
    owner_hbm, child_hbm, step_hbm, alog_hbm, dtb_hbm, skip_hbm = sources
    msgs, refs = refs[:n_msgs], refs[n_msgs:]
    conv_hbm, gate_ref, rate_ref, twin_ref, dtb_ref, skip_ref = refs[:6]
    owner_s, child_s, step_ref, alog, conv_s, sems = refs[6:]
    small = [
        pltpu.make_async_copy(source, target, sems.at[i])
        for i, (source, target) in enumerate(
            (
                (owner_hbm, owner_s),
                (child_hbm, child_s),
                (alog_hbm, alog),
                (dtb_hbm, dtb_ref),
                (skip_hbm, skip_ref),
            )
        )
    ]
    inputs = in_parts(step_hbm, step_ref, sems, len(small), STEP_PARTS)
    for copy in small + inputs:
        copy.start()
    held = read_messages(msgs)
    past, rb, _ = conv_s.shape
    steps = step_ref.shape[1]
    for copy in small:
        copy.wait()
    places = blocks_of(owner_s[0]) if direct else None
    child = scalar_onehot(child_s, places, (rb, len(held)))
    for k in range(past):
        at = steps - past + k
        conv_s[k] = pick_rows(child, [h[at : at + 1, :] for h in held]).astype(BF16)
    out = pltpu.make_async_copy(conv_s, conv_hbm, sems.at[len(small) + STEP_PARTS])
    out.start()
    rate = jnp.exp(alog[...]) * (-math.log2(math.e))
    rate_ref[...] = rate
    half = (twin_ref.shape[1] // 2, rate.shape[1])
    for m in range(rate.shape[0] // 2):
        two = [jnp.broadcast_to(rate[n : n + 1, :], half) for n in (2 * m, 2 * m + 1)]
        twin_ref[m] = jnp.concatenate(two, axis=0)
    for copy in inputs:
        copy.wait()
    for t in range(steps):
        gate_ref[t] = silu(step_ref[:, t, 1, :].astype(F32))
    out.wait()


def start_kernel(n_msgs, direct, text, pick_ref, sender_ref, after_ref, *rest):
    del after_ref
    msgs, rest = rest[:n_msgs], rest[n_msgs:]
    apart, (own_ref, slot_ref, state_s) = rest[:-3], rest[-3:]
    n_state = own_ref.shape[0]
    held = read_messages(msgs)
    owners = len(held)
    numbers = jnp.concatenate([h[text - 1 : text, :] for h in held], axis=0)
    states = [h[text:, :] for h in held]
    if direct:
        ssm_ref, pair_ref = apart
        head, low, came = [
            pair_ref[0].astype(F32)[i * n_state : (i + 1) * n_state, :] for i in range(3)
        ]
        states[0], states[2], states[3] = ssm_ref[0], came, head + low
    for k, state in enumerate(states):
        state_s[k] = state
    own = pick_ref[...]
    slot = slot_onehot(numbers, sender_ref)

    def two(m, carry):
        picked = []
        for n in (2 * m, 2 * m + 1):
            rows = [state_s[k, pl.ds(n, 1), :] for k in range(owners)]
            own_ref[n] = pick_rows(own, rows)
            picked.append(pick_rows(slot, rows))
        slot_ref[m] = jnp.concatenate(picked, axis=0)
        return carry

    lax.fori_loop(0, n_state // 2, two, 0, unroll=owners <= DIRECT)


def decode_kernel(
    direct,
    owner_hbm,
    child_hbm,
    act_ref,
    gate_ref,
    own_ref,
    slot_ref,
    rate_ref,
    twin_ref,
    dtw_ref,
    dtb_ref,
    skip_ref,
    part_ref,
    other_ref,
    dec_ref,
    child_ssm,
    owner_s,
    child_s,
    delta_s,
    gain_s,
    slot_delta_s,
    slot_gain_s,
    b_s,
    c_s,
    twin_b_s,
    slots_s,
    line_s,
    sems,
):
    scalars = [
        pltpu.make_async_copy(owner_hbm, owner_s, sems.at[0]),
        pltpu.make_async_copy(child_hbm, child_s, sems.at[1]),
    ]
    for copy in scalars:
        copy.start()
    rb, steps, channels = dec_ref.shape
    rank = dtw_ref.shape[0]
    n_state = rate_ref.shape[0]
    n_slots = slots_s.shape[0]
    own_rows = steps * rb
    chunks = channels // (WIDE * LANES)

    proj = part_ref[...] + other_ref[...].astype(F32)
    delta_in = proj[:, :rank].astype(BF16)
    delta = jnp.dot(delta_in, dtw_ref[...], preferred_element_type=F32) + dtb_ref[...]
    delta = jnp.maximum(delta, 0.0) + jnp.log(1.0 + jnp.exp(-jnp.abs(delta)))
    gain = delta * act_ref[...]
    delta_s[...] = delta[:own_rows, :]
    gain_s[...] = gain[:own_rows, :]

    def column(at, n, rows):
        return jnp.broadcast_to(at[:, n : n + 1], (rows, LANES))

    for t in range(steps):
        at = slice(own_rows + t * n_slots, own_rows + (t + 1) * n_slots)
        slot_delta_s[t] = jnp.concatenate([delta[at, :]] * 2, axis=0)
        slot_gain_s[t] = jnp.concatenate([gain[at, :]] * 2, axis=0)
        twice = jnp.concatenate([proj[at, rank:]] * 2, axis=0)
        upper = lax.broadcasted_iota(jnp.int32, (2 * n_slots, LANES), 0) < n_slots
        for m in range(n_state // 2):
            twin_b_s[m, t] = jnp.where(
                upper, column(twice, 2 * m, 2 * n_slots), column(twice, 2 * m + 1, 2 * n_slots)
            )
    for n in range(n_state):
        b_s[n] = column(proj[:own_rows, rank:], n, own_rows)
        c_s[n] = column(proj[:own_rows, rank:], n_state + n, own_rows)

    def wide(part, times=WIDE):
        return jnp.concatenate([part] * times, axis=1)

    def slot_chunk(chunk, carry):
        breadth = SLOT_WIDE * LANES
        columns = pl.ds(pl.multiple_of(chunk * breadth, breadth), breadth)
        delta = [slot_delta_s[t, :, columns] for t in range(steps)]
        gain = [slot_gain_s[t, :, columns] for t in range(steps)]
        for m in range(n_state // 2):
            rate = twin_ref[m, :, columns]
            state = slot_ref[m, :, columns]
            for t in range(steps):
                state = jnp.exp2(delta[t] * rate) * state + gain[t] * wide(twin_b_s[m, t], SLOT_WIDE)
            slots_s[:, 2 * m, columns] = state[:n_slots, :]
            slots_s[:, 2 * m + 1, columns] = state[n_slots:, :]
        return carry

    lax.fori_loop(0, channels // (SLOT_WIDE * LANES), slot_chunk, 0)
    for copy in scalars:
        copy.wait()
    places = blocks_of(owner_s[0]) if direct else None
    copies = []
    for j in range(rb):
        at = chosen(child_s[j], places) if direct else child_s[j]
        copy = pltpu.make_async_copy(slots_s.at[at], child_ssm.at[j], sems.at[2 + j])
        copy.start()
        copies.append(copy)

    def own_chunk(chunk, carry):
        columns = pl.ds(pl.multiple_of(chunk * WIDE * LANES, WIDE * LANES), WIDE * LANES)
        for first in range(0, rb, ROWS):
            at = [pl.ds(t * rb + first, ROWS) for t in range(steps)]
            delta = [delta_s[a, columns] for a in at]
            gain = [gain_s[a, columns] for a in at]
            sums = [skip_ref[:, columns] * act_ref[a, columns] for a in at]
            for n in range(n_state):
                rate = rate_ref[n : n + 1, columns]
                state = own_ref[n, pl.ds(first, ROWS), columns]
                for t in range(steps):
                    state = jnp.exp2(delta[t] * rate) * state + gain[t] * wide(b_s[n, at[t], :])
                    sums[t] = sums[t] + wide(c_s[n, at[t], :]) * state
            for t in range(steps):
                out = sums[t] * gate_ref[t, pl.ds(first, ROWS), columns]
                for w in range(WIDE):
                    line_s[w, pl.ds(first * steps + t, ROWS, stride=steps), :] = out[
                        :, w * LANES : (w + 1) * LANES
                    ]
        for w in range(WIDE):
            some = pl.ds(pl.multiple_of((chunk * WIDE + w) * LANES, LANES), LANES)
            dec_ref[:, :, some] = line_s[w].reshape(rb, steps, LANES).astype(BF16)
        return carry

    lax.fori_loop(0, chunks, own_chunk, 0)
    for copy in copies:
        copy.wait()


def on_device(
    prompt_ssm,
    prompt_conv,
    prompt_of,
    step_in,
    conv_weight,
    conv_bias,
    x_weight,
    dt_weight,
    dt_bias,
    a_log,
    skip,
    send_rows,
    child_slot,
):
    owners = lax.axis_size("branch")
    tensors = lax.axis_size("tensor")
    assert owners & (owners - 1) == 0 and tensors & (tensors - 1) == 0
    assert prompt_ssm.shape[0] == 1 and send_rows.shape[2] == 1
    rb, steps, _, channels = step_in.shape
    taps = conv_weight.shape[0]
    width = x_weight.shape[1]
    n_state = a_log.shape[0]
    rows = steps * (rb + owners)
    short = taps - 1 + steps + 1
    depth = short + n_state
    direct = owners == DIRECT
    owner = pinned(lax.axis_index("branch").astype(jnp.int32).reshape(1))

    if direct:
        msg_shapes = [(1, d, channels) for d in (depth, short, short)]
    else:
        msg_shapes = [(owners, depth, channels)]
    msgs = call(
        functools.partial(pack_kernel, direct),
        [shaped(s, BF16) for s in msg_shapes],
        [hbm()] * 6,
        [vmem()] * len(msg_shapes),
        [
            pltpu.SMEM((1,), jnp.int32),
            pltpu.SMEM((owners,), jnp.int32),
            pltpu.SMEM((rb,), jnp.int32),
            pltpu.VMEM(step_in.shape, BF16),
            pltpu.VMEM(prompt_conv.shape, BF16),
            pltpu.VMEM(prompt_ssm.shape, F32),
            pltpu.SemaphoreType.DMA((5 + STEP_PARTS,)),
        ],
        nbytes=owners * depth * channels * 2,
    )(
        owner,
        pinned(send_rows.reshape(owners)),
        pinned(prompt_of),
        pinned(step_in),
        pinned(prompt_conv),
        pinned(prompt_ssm),
    )
    after = msgs[0]
    if direct:
        msgs = [lax.ppermute(m, "branch", list(enumerate(to))) for m, to in zip(msgs, SENDS)]
    else:
        msgs = [lax.all_to_all(msgs[0], "branch", split_axis=0, concat_axis=0, tiled=True)]
    own, base, pick, sender, taps_near, bias_near, weight_near = call(
        functools.partial(prepare_kernel, direct),
        [
            shaped((1, short, channels), BF16),
            shaped((steps, rb, channels), F32),
            shaped((rb, owners), F32),
            shaped((1, owners), F32),
            shaped((taps, channels), F32),
            shaped((1, channels), F32),
            shaped((width, channels), BF16),
        ],
        [hbm()] * 8 + [anywhere()],
        [vmem()] * 7,
        [
            pltpu.VMEM(step_in.shape, BF16),
            pltpu.SMEM((1,), jnp.int32),
            pltpu.SMEM((rb,), jnp.int32),
            pltpu.SMEM((owners,), jnp.int32),
            pltpu.VMEM(prompt_conv.shape, BF16),
            pltpu.SemaphoreType.DMA((6 + WEIGHT_PARTS + STEP_PARTS,)),
        ],
        flops=10 * steps * rb * channels,
        nbytes=12 * steps * rb * channels,
    )(
        owner,
        pinned(prompt_of),
        pinned(send_rows.reshape(owners)),
        pinned(prompt_conv),
        pinned(step_in),
        pinned(conv_weight),
        pinned(conv_bias[None]),
        pinned(x_weight.T),
        after,
    )
    states = []
    if direct:
        msgs = [own] + msgs
        pair = call(
            functools.partial(pair_kernel, short),
            shaped((1, 3 * n_state, channels), BF16),
            [vmem()] * 2 + [anywhere()],
            vmem(),
            nbytes=12 * n_state * channels,
        )(prompt_ssm, msgs[1], pick)
        states = [prompt_ssm, swap(pair, "branch", 1)]
    n_msgs = len(msgs)
    act, part, brief = call(
        functools.partial(project_kernel, n_msgs),
        [
            shaped((rows, channels), F32),
            shaped((rows, width), F32),
            shaped((rows, width), BF16),
        ],
        [vmem()] * (6 + n_msgs),
        [vmem()] * 3,
        flops=2 * rows * channels * width,
        nbytes=channels * width * 2 + rows * (channels + width) * 4,
        trans=rows * channels,
    )(pick, sender, base, taps_near, bias_near, weight_near, *msgs)
    other = swap(brief, "tensor", 1)
    distance = 2
    while distance < tensors:
        part, brief = call(
            add_kernel,
            [shaped((rows, width), F32), shaped((rows, width), BF16)],
            [vmem()] * 2,
            [vmem()] * 2,
            flops=rows * width,
            nbytes=rows * width * 14,
        )(part, other)
        other = swap(brief, "tensor", 2 * distance - 1)
        distance *= 2

    child_conv, gate, rate, twin, dtb_near, skip_near = call(
        functools.partial(late_kernel, n_msgs, direct),
        [
            shaped((taps - 1, rb, channels), BF16),
            shaped((steps, rb, channels), F32),
            shaped((n_state, channels), F32),
            shaped((n_state // 2, 2 * owners, channels), F32),
            shaped((1, channels), F32),
            shaped((1, channels), F32),
        ],
        [hbm()] * 6 + [anywhere()] + [vmem()] * n_msgs,
        [anywhere()] + [vmem()] * 5,
        [
            pltpu.SMEM((1,), jnp.int32),
            pltpu.SMEM((rb,), jnp.int32),
            pltpu.VMEM(step_in.shape, BF16),
            pltpu.VMEM((n_state, channels), F32),
            pltpu.VMEM((taps - 1, rb, channels), BF16),
            pltpu.SemaphoreType.DMA((6 + STEP_PARTS,)),
        ],
        flops=10 * steps * rb * channels,
        nbytes=12 * steps * rb * channels,
        trans=steps * rb * channels,
    )(
        owner,
        pinned(child_slot),
        pinned(step_in),
        pinned(a_log),
        pinned(dt_bias[None]),
        pinned(skip[None]),
        part,
        *msgs,
    )
    own_start, slot_start = call(
        functools.partial(start_kernel, n_msgs, direct, short),
        [
            shaped((n_state, rb, channels), F32),
            shaped((n_state // 2, 2 * owners, channels), F32),
        ],
        [vmem()] * 2 + [anywhere()] + [vmem()] * (n_msgs + len(states)),
        [vmem()] * 2,
        [pltpu.VMEM((owners, n_state, channels), F32)],
        flops=2 * owners * n_state * (rb + owners) * channels,
        nbytes=4 * n_state * (rb + owners) * channels,
    )(pick, sender, part, *msgs, *states)

    decoded, child_ssm = call(
        functools.partial(decode_kernel, direct),
        [
            shaped((rb, steps, channels), BF16),
            shaped((rb, n_state, channels), F32),
        ],
        [hbm()] * 2 + [vmem()] * 11,
        [vmem(), anywhere()],
        [
            pltpu.SMEM((1,), jnp.int32),
            pltpu.SMEM((rb,), jnp.int32),
            pltpu.VMEM((steps * rb, channels), F32),
            pltpu.VMEM((steps * rb, channels), F32),
            pltpu.VMEM((steps, 2 * owners, channels), F32),
            pltpu.VMEM((steps, 2 * owners, channels), F32),
            pltpu.VMEM((n_state, steps * rb, LANES), F32),
            pltpu.VMEM((n_state, steps * rb, LANES), F32),
            pltpu.VMEM((n_state // 2, steps, 2 * owners, LANES), F32),
            pltpu.VMEM((owners, n_state, channels), F32),
            pltpu.VMEM((WIDE, steps * rb, LANES), F32),
            pltpu.SemaphoreType.DMA((2 + rb,)),
        ],
        flops=8 * rows * n_state * channels,
        nbytes=(rb + owners) * n_state * channels * 4,
        trans=rows * n_state * channels,
    )(
        owner,
        pinned(child_slot),
        act,
        gate,
        own_start,
        slot_start,
        rate,
        twin,
        dt_weight,
        dtb_near,
        skip_near,
        part,
        other,
    )
    return (decoded, child_ssm, jnp.transpose(child_conv, (1, 0, 2)))


def solution(mesh):
    placed = (
        P(("replica", "branch"), None, "tensor"),
        P(("replica", "branch"), None, "tensor"),
        P(("replica", "branch")),
        P(("replica", "branch"), None, None, "tensor"),
        P(None, "tensor"),
        P("tensor"),
        P("tensor", None),
        P(None, "tensor"),
        P("tensor"),
        P(None, "tensor"),
        P("tensor"),
        P(("replica", "branch"), None, None),
        P(("replica", "branch")),
    )
    return jax.shard_map(
        on_device,
        mesh=mesh,
        in_specs=placed,
        out_specs=(
            P(("replica", "branch"), None, "tensor"),
            P(("replica", "branch"), None, "tensor"),
            P(("replica", "branch"), None, "tensor"),
        ),
        check_vma=False,
    )
```

```python
import functools
import math

import jax
import jax.numpy as jnp
from jax import lax
from jax.experimental import pallas as pl
from jax.experimental.pallas import tpu as pltpu
from jax.sharding import PartitionSpec as P

F32 = jnp.float32
BF16 = jnp.bfloat16
LANES = 128
ROWS = 8
WIDE = 4
SLOT_WIDE = 4
VMEM_LIMIT = 48 * 2**20
WEIGHT_PARTS = 6
STEP_PARTS = 4
DIRECT = 4
SENDS = ((2, 3, 1, 0), (3, 2, 0, 1), (1, 0, 3, 2))


def vmem():
    return pl.BlockSpec(memory_space=pltpu.VMEM)


def hbm():
    return pl.BlockSpec(memory_space=pltpu.HBM)


def anywhere():
    return pl.BlockSpec(memory_space=pl.ANY)


def pinned(array):
    return pltpu.with_memory_space_constraint(array, pltpu.HBM)


def shaped(shape, dtype):
    return jax.ShapeDtypeStruct(shape, dtype)


def call(kernel, outs, in_specs, out_specs, scratch=(), flops=0, nbytes=0, trans=0):
    return pl.pallas_call(
        kernel,
        out_shape=outs,
        in_specs=in_specs,
        out_specs=out_specs,
        scratch_shapes=list(scratch),
        compiler_params=pltpu.CompilerParams(vmem_limit_bytes=VMEM_LIMIT),
        cost_estimate=pl.CostEstimate(flops=flops, bytes_accessed=nbytes, transcendentals=trans),
    )


def swap(value, axis, distance):
    size = lax.axis_size(axis)
    return lax.ppermute(value, axis, [(i, i ^ distance) for i in range(size)])


def chosen(number, values):
    total = values[0]
    for i in range(1, len(values)):
        total = jnp.where(number == i, values[i], total)
    return total


def blocks_of(owner):
    table = [
        [0 if s == r else 1 + [to[s] for to in SENDS].index(r) for s in range(DIRECT)]
        for r in range(DIRECT)
    ]
    return [chosen(owner, [row[s] for row in table]) for s in range(DIRECT)]


def all_of(copies):
    for copy in copies:
        copy.start()
    for copy in copies:
        copy.wait()


def read_messages(refs):
    return [ref[i].astype(F32) for ref in refs for i in range(ref.shape[0])]


def in_parts(source, target, sems, first, count):
    rows = source.shape[0] // count
    at = [pl.ds(i * rows, rows) for i in range(count)]
    return [
        pltpu.make_async_copy(source.at[a], target.at[a], sems.at[first + i])
        for i, a in enumerate(at)
    ]


def scalar_onehot(senders_s, places, shape):
    row_of = lax.broadcasted_iota(jnp.int32, shape, 0)
    wanted = jnp.zeros(shape, jnp.int32)
    for b in range(shape[0]):
        wanted = jnp.where(row_of == b, senders_s[b], wanted)
    wanted = wanted if places is None else chosen(wanted, places)
    return (wanted == lax.broadcasted_iota(jnp.int32, shape, 1)).astype(F32)


def pick_rows(pick, rows):
    total = pick[:, 0:1] * rows[0]
    for k in range(1, len(rows)):
        total = total + pick[:, k : k + 1] * rows[k]
    return total


def message(target, rows_s, prompt_s, step, conv, state):
    row = jnp.maximum(rows_s[target], 0)
    xs = step[row, :, 0, :].astype(F32)
    number = jnp.full((1, xs.shape[1]), prompt_s[row].astype(F32), F32)
    pieces = [xs, conv[0].astype(F32), number] + ([] if state is None else [state])
    return jnp.concatenate(pieces, axis=0).astype(BF16)


def pack_kernel(direct, owner_hbm, rows_hbm, prompt_hbm, step_hbm, conv_hbm, ssm_hbm, *rest):
    outs, (owner_s, rows_s, prompt_s, step, conv, ssm, sems) = rest[:-7], rest[-7:]
    owners = rows_hbm.shape[0]
    copies = [
        pltpu.make_async_copy(owner_hbm, owner_s, sems.at[4]),
        pltpu.make_async_copy(rows_hbm, rows_s, sems.at[0]),
        pltpu.make_async_copy(prompt_hbm, prompt_s, sems.at[1]),
        pltpu.make_async_copy(conv_hbm, conv, sems.at[2]),
        pltpu.make_async_copy(ssm_hbm, ssm, sems.at[3]),
    ]
    all_of(copies + in_parts(step_hbm, step, sems, 5, STEP_PARTS))
    owner = owner_s[0]
    targets = [chosen(owner, to) for to in SENDS] if direct else range(owners)
    for i, target in enumerate(targets):
        ref = outs[i].at[0] if direct else outs[0].at[i]
        state = ssm[0] if ref.shape[0] > conv.shape[1] + step.shape[1] + 1 else None
        ref[...] = message(target, rows_s, prompt_s, step, conv, state)


def pair_kernel(text, ssm_ref, came_ref, after_ref, pair_ref):
    del after_ref
    state = ssm_ref[0]
    head = state.astype(BF16).astype(F32)
    came = came_ref[0].astype(F32)[text:, :]
    pair_ref[0] = jnp.concatenate([head, state - head, came], axis=0).astype(BF16)


def silu(v):
    return v / (1.0 + jnp.exp(-v))


def prepare_kernel(
    direct,
    owner_hbm,
    prompt_hbm,
    rows_hbm,
    conv_hbm,
    step_hbm,
    cw_hbm,
    cb_hbm,
    xwt_hbm,
    after_ref,
    own_ref,
    base_ref,
    pick_ref,
    sender_ref,
    cw_ref,
    cb_ref,
    xwt_ref,
    step_ref,
    owner_s,
    prompt_s,
    rows_s,
    conv,
    sems,
):
    del after_ref
    small = [
        pltpu.make_async_copy(source, target, sems.at[i])
        for i, (source, target) in enumerate(
            (
                (cw_hbm, cw_ref),
                (cb_hbm, cb_ref),
                (owner_hbm, owner_s),
                (prompt_hbm, prompt_s),
                (rows_hbm, rows_s),
                (conv_hbm, conv),
            )
        )
    ]
    inputs = in_parts(step_hbm, step_ref, sems, len(small), STEP_PARTS)
    large = in_parts(xwt_hbm, xwt_ref, sems, len(small) + STEP_PARTS, WEIGHT_PARTS)
    for copy in inputs + small + large:
        copy.start()
    for copy in inputs + small:
        copy.wait()
    own_ref[0] = message(owner_s[0], rows_s, prompt_s, step_ref, conv, None)
    steps = step_ref.shape[1]
    taps = cw_hbm.shape[0]
    xs = [step_ref[:, t, 0, :].astype(F32) for t in range(steps)]
    for t in range(steps):
        total = cw_ref[taps - 1 : taps, :] * xs[t] + cb_ref[...]
        for k in range(max(0, taps - 1 - t), taps - 1):
            total = total + cw_ref[k : k + 1, :] * xs[t + k - taps + 1]
        base_ref[t] = total
    places = blocks_of(owner_s[0]) if direct else None
    pick_ref[...] = scalar_onehot(prompt_s, places, pick_ref.shape)
    column = lax.broadcasted_iota(jnp.int32, sender_ref.shape, 1)
    sender = column
    for sent, place in enumerate(places or []):
        sender = jnp.where(column == place, sent, sender)
    sender_ref[...] = sender.astype(F32)
    for copy in large:
        copy.wait()


def slot_onehot(numbers, sender_ref):
    owners = sender_ref.shape[1]
    return (numbers[:, :owners] == sender_ref[...]).astype(F32)


def project_kernel(n_msgs, pick_ref, sender_ref, base_ref, cw_ref, cb_ref, xwt_ref, *rest):
    msgs, (act_ref, part_ref, short_ref) = rest[:n_msgs], rest[n_msgs:]
    taps = cw_ref.shape[0]
    steps, rb, _ = base_ref.shape
    past = taps - 1
    held = read_messages(msgs)
    owners = len(held)
    windows = [[h[steps + k : steps + k + 1, :] for h in held] for k in range(past)]
    own = pick_ref[...]
    own_windows = [pick_rows(own, w) for w in windows]
    for t in range(steps):
        conv = base_ref[t]
        for k in range(past - t):
            conv = conv + cw_ref[k : k + 1, :] * own_windows[t + k]
        act_ref[t * rb : (t + 1) * rb, :] = silu(conv)

    def line_of(row):
        return jnp.concatenate([h[row : row + 1, :] for h in held], axis=0)

    slot = slot_onehot(line_of(past + steps), sender_ref)
    line = [pick_rows(slot, w) for w in windows]
    line += [line_of(t) for t in range(steps)]
    row = steps * rb
    for t in range(steps):
        conv = cw_ref[past:taps, :] * line[t + past] + cb_ref[...]
        for k in range(past):
            conv = conv + cw_ref[k : k + 1, :] * line[t + k]
        act_ref[row : row + owners, :] = silu(conv)
        row += owners
    part = lax.dot_general(
        act_ref[...].astype(BF16),
        xwt_ref[...],
        (((1,), (1,)), ((), ())),
        preferred_element_type=F32,
    )
    part_ref[...] = part
    short_ref[...] = part.astype(BF16)


def add_kernel(a_ref, b_ref, sum_ref, short_ref):
    total = a_ref[...] + b_ref[...].astype(F32)
    sum_ref[...] = total
    short_ref[...] = total.astype(BF16)


def late_kernel(n_msgs, direct, *refs):
    sources, refs = refs[:6], refs[7:]
    owner_hbm, child_hbm, step_hbm, alog_hbm, dtb_hbm, skip_hbm = sources
    msgs, refs = refs[:n_msgs], refs[n_msgs:]
    conv_hbm, gate_ref, rate_ref, twin_ref, dtb_ref, skip_ref = refs[:6]
    owner_s, child_s, step_ref, alog, conv_s, sems = refs[6:]
    small = [
        pltpu.make_async_copy(source, target, sems.at[i])
        for i, (source, target) in enumerate(
            (
                (owner_hbm, owner_s),
                (child_hbm, child_s),
                (alog_hbm, alog),
                (dtb_hbm, dtb_ref),
                (skip_hbm, skip_ref),
            )
        )
    ]
    inputs = in_parts(step_hbm, step_ref, sems, len(small), STEP_PARTS)
    for copy in small + inputs:
        copy.start()
    held = read_messages(msgs)
    past, rb, _ = conv_s.shape
    steps = step_ref.shape[1]
    for copy in small:
        copy.wait()
    places = blocks_of(owner_s[0]) if direct else None
    child = scalar_onehot(child_s, places, (rb, len(held)))
    for k in range(past):
        at = steps - past + k
        conv_s[k] = pick_rows(child, [h[at : at + 1, :] for h in held]).astype(BF16)
    out = pltpu.make_async_copy(conv_s, conv_hbm, sems.at[len(small) + STEP_PARTS])
    out.start()
    rate = jnp.exp(alog[...]) * (-math.log2(math.e))
    rate_ref[...] = rate
    half = (twin_ref.shape[1] // 2, rate.shape[1])
    for m in range(rate.shape[0] // 2):
        two = [jnp.broadcast_to(rate[n : n + 1, :], half) for n in (2 * m, 2 * m + 1)]
        twin_ref[m] = jnp.concatenate(two, axis=0)
    for copy in inputs:
        copy.wait()
    for t in range(steps):
        gate_ref[t] = silu(step_ref[:, t, 1, :].astype(F32))
    out.wait()


def start_kernel(n_msgs, direct, text, pick_ref, sender_ref, after_ref, *rest):
    del after_ref
    msgs, rest = rest[:n_msgs], rest[n_msgs:]
    apart, (own_ref, slot_ref, state_s) = rest[:-3], rest[-3:]
    n_state = own_ref.shape[0]
    held = read_messages(msgs)
    owners = len(held)
    numbers = jnp.concatenate([h[text - 1 : text, :] for h in held], axis=0)
    states = [h[text:, :] for h in held]
    if direct:
        ssm_ref, pair_ref = apart
        head, low, came = [
            pair_ref[0].astype(F32)[i * n_state : (i + 1) * n_state, :] for i in range(3)
        ]
        states[0], states[2], states[3] = ssm_ref[0], came, head + low
    for k, state in enumerate(states):
        state_s[k] = state
    own = pick_ref[...]
    slot = slot_onehot(numbers, sender_ref)

    def two(m, carry):
        picked = []
        for n in (2 * m, 2 * m + 1):
            rows = [state_s[k, pl.ds(n, 1), :] for k in range(owners)]
            own_ref[n] = pick_rows(own, rows)
            picked.append(pick_rows(slot, rows))
        slot_ref[m] = jnp.concatenate(picked, axis=0)
        return carry

    lax.fori_loop(0, n_state // 2, two, 0, unroll=owners <= DIRECT)


def decode_kernel(
    direct,
    owner_hbm,
    child_hbm,
    act_ref,
    gate_ref,
    own_ref,
    slot_ref,
    rate_ref,
    twin_ref,
    dtw_ref,
    dtb_ref,
    skip_ref,
    part_ref,
    other_ref,
    dec_ref,
    child_ssm,
    owner_s,
    child_s,
    delta_s,
    gain_s,
    slot_delta_s,
    slot_gain_s,
    b_s,
    c_s,
    twin_b_s,
    slots_s,
    line_s,
    sems,
):
    scalars = [
        pltpu.make_async_copy(owner_hbm, owner_s, sems.at[0]),
        pltpu.make_async_copy(child_hbm, child_s, sems.at[1]),
    ]
    for copy in scalars:
        copy.start()
    rb, steps, channels = dec_ref.shape
    rank = dtw_ref.shape[0]
    n_state = rate_ref.shape[0]
    n_slots = slots_s.shape[0]
    own_rows = steps * rb
    chunks = channels // (WIDE * LANES)

    proj = part_ref[...] + other_ref[...].astype(F32)
    delta_in = proj[:, :rank].astype(BF16)
    delta = jnp.dot(delta_in, dtw_ref[...], preferred_element_type=F32) + dtb_ref[...]
    delta = jnp.maximum(delta, 0.0) + jnp.log(1.0 + jnp.exp(-jnp.abs(delta)))
    gain = delta * act_ref[...]
    delta_s[...] = delta[:own_rows, :]
    gain_s[...] = gain[:own_rows, :]

    def column(at, n, rows):
        return jnp.broadcast_to(at[:, n : n + 1], (rows, LANES))

    for t in range(steps):
        at = slice(own_rows + t * n_slots, own_rows + (t + 1) * n_slots)
        slot_delta_s[t] = jnp.concatenate([delta[at, :]] * 2, axis=0)
        slot_gain_s[t] = jnp.concatenate([gain[at, :]] * 2, axis=0)
        twice = jnp.concatenate([proj[at, rank:]] * 2, axis=0)
        upper = lax.broadcasted_iota(jnp.int32, (2 * n_slots, LANES), 0) < n_slots
        for m in range(n_state // 2):
            twin_b_s[m, t] = jnp.where(
                upper, column(twice, 2 * m, 2 * n_slots), column(twice, 2 * m + 1, 2 * n_slots)
            )
    for n in range(n_state):
        b_s[n] = column(proj[:own_rows, rank:], n, own_rows)
        c_s[n] = column(proj[:own_rows, rank:], n_state + n, own_rows)

    def wide(part, times=WIDE):
        return jnp.concatenate([part] * times, axis=1)

    def slot_chunk(chunk, carry):
        breadth = SLOT_WIDE * LANES
        columns = pl.ds(pl.multiple_of(chunk * breadth, breadth), breadth)
        delta = [slot_delta_s[t, :, columns] for t in range(steps)]
        gain = [slot_gain_s[t, :, columns] for t in range(steps)]
        for m in range(n_state // 2):
            rate = twin_ref[m, :, columns]
            state = slot_ref[m, :, columns]
            for t in range(steps):
                state = jnp.exp2(delta[t] * rate) * state + gain[t] * wide(twin_b_s[m, t], SLOT_WIDE)
            slots_s[:, 2 * m, columns] = state[:n_slots, :]
            slots_s[:, 2 * m + 1, columns] = state[n_slots:, :]
        return carry

    lax.fori_loop(0, channels // (SLOT_WIDE * LANES), slot_chunk, 0)
    for copy in scalars:
        copy.wait()
    places = blocks_of(owner_s[0]) if direct else None
    copies = []
    for j in range(rb):
        at = chosen(child_s[j], places) if direct else child_s[j]
        copy = pltpu.make_async_copy(slots_s.at[at], child_ssm.at[j], sems.at[2 + j])
        copy.start()
        copies.append(copy)

    def own_chunk(chunk, carry):
        columns = pl.ds(pl.multiple_of(chunk * WIDE * LANES, WIDE * LANES), WIDE * LANES)
        for first in range(0, rb, ROWS):
            at = [pl.ds(t * rb + first, ROWS) for t in range(steps)]
            delta = [delta_s[a, columns] for a in at]
            gain = [gain_s[a, columns] for a in at]
            sums = [skip_ref[:, columns] * act_ref[a, columns] for a in at]
            for n in range(n_state):
                rate = rate_ref[n : n + 1, columns]
                state = own_ref[n, pl.ds(first, ROWS), columns]
                for t in range(steps):
                    state = jnp.exp2(delta[t] * rate) * state + gain[t] * wide(b_s[n, at[t], :])
                    sums[t] = sums[t] + wide(c_s[n, at[t], :]) * state
            for t in range(steps):
                out = sums[t] * gate_ref[t, pl.ds(first, ROWS), columns]
                for w in range(WIDE):
                    line_s[w, pl.ds(first * steps + t, ROWS, stride=steps), :] = out[
                        :, w * LANES : (w + 1) * LANES
                    ]
        for w in range(WIDE):
            some = pl.ds(pl.multiple_of((chunk * WIDE + w) * LANES, LANES), LANES)
            dec_ref[:, :, some] = line_s[w].reshape(rb, steps, LANES).astype(BF16)
        return carry

    lax.fori_loop(0, chunks, own_chunk, 0)
    for copy in copies:
        copy.wait()


def on_device(
    prompt_ssm,
    prompt_conv,
    prompt_of,
    step_in,
    conv_weight,
    conv_bias,
    x_weight,
    dt_weight,
    dt_bias,
    a_log,
    skip,
    send_rows,
    child_slot,
):
    owners = lax.axis_size("branch")
    tensors = lax.axis_size("tensor")
    assert owners & (owners - 1) == 0 and tensors & (tensors - 1) == 0
    assert prompt_ssm.shape[0] == 1 and send_rows.shape[2] == 1
    rb, steps, _, channels = step_in.shape
    taps = conv_weight.shape[0]
    width = x_weight.shape[1]
    n_state = a_log.shape[0]
    rows = steps * (rb + owners)
    short = taps - 1 + steps + 1
    depth = short + n_state
    direct = owners == DIRECT
    owner = pinned(lax.axis_index("branch").astype(jnp.int32).reshape(1))

    if direct:
        msg_shapes = [(1, d, channels) for d in (depth, short, short)]
    else:
        msg_shapes = [(owners, depth, channels)]
    msgs = call(
        functools.partial(pack_kernel, direct),
        [shaped(s, BF16) for s in msg_shapes],
        [hbm()] * 6,
        [vmem()] * len(msg_shapes),
        [
            pltpu.SMEM((1,), jnp.int32),
            pltpu.SMEM((owners,), jnp.int32),
            pltpu.SMEM((rb,), jnp.int32),
            pltpu.VMEM(step_in.shape, BF16),
            pltpu.VMEM(prompt_conv.shape, BF16),
            pltpu.VMEM(prompt_ssm.shape, F32),
            pltpu.SemaphoreType.DMA((5 + STEP_PARTS,)),
        ],
        nbytes=owners * depth * channels * 2,
    )(
        owner,
        pinned(send_rows.reshape(owners)),
        pinned(prompt_of),
        pinned(step_in),
        pinned(prompt_conv),
        pinned(prompt_ssm),
    )
    after = msgs[0]
    if direct:
        msgs = [lax.ppermute(m, "branch", list(enumerate(to))) for m, to in zip(msgs, SENDS)]
    else:
        msgs = [lax.all_to_all(msgs[0], "branch", split_axis=0, concat_axis=0, tiled=True)]
    own, base, pick, sender, taps_near, bias_near, weight_near = call(
        functools.partial(prepare_kernel, direct),
        [
            shaped((1, short, channels), BF16),
            shaped((steps, rb, channels), F32),
            shaped((rb, owners), F32),
            shaped((1, owners), F32),
            shaped((taps, channels), F32),
            shaped((1, channels), F32),
            shaped((width, channels), BF16),
        ],
        [hbm()] * 8 + [anywhere()],
        [vmem()] * 7,
        [
            pltpu.VMEM(step_in.shape, BF16),
            pltpu.SMEM((1,), jnp.int32),
            pltpu.SMEM((rb,), jnp.int32),
            pltpu.SMEM((owners,), jnp.int32),
            pltpu.VMEM(prompt_conv.shape, BF16),
            pltpu.SemaphoreType.DMA((6 + WEIGHT_PARTS + STEP_PARTS,)),
        ],
        flops=10 * steps * rb * channels,
        nbytes=12 * steps * rb * channels,
    )(
        owner,
        pinned(prompt_of),
        pinned(send_rows.reshape(owners)),
        pinned(prompt_conv),
        pinned(step_in),
        pinned(conv_weight),
        pinned(conv_bias[None]),
        pinned(x_weight.T),
        after,
    )
    states = []
    if direct:
        msgs = [own] + msgs
        pair = call(
            functools.partial(pair_kernel, short),
            shaped((1, 3 * n_state, channels), BF16),
            [vmem()] * 2 + [anywhere()],
            vmem(),
            nbytes=12 * n_state * channels,
        )(prompt_ssm, msgs[1], pick)
        states = [prompt_ssm, swap(pair, "branch", 1)]
    n_msgs = len(msgs)
    act, part, brief = call(
        functools.partial(project_kernel, n_msgs),
        [
            shaped((rows, channels), F32),
            shaped((rows, width), F32),
            shaped((rows, width), BF16),
        ],
        [vmem()] * (6 + n_msgs),
        [vmem()] * 3,
        flops=2 * rows * channels * width,
        nbytes=channels * width * 2 + rows * (channels + width) * 4,
        trans=rows * channels,
    )(pick, sender, base, taps_near, bias_near, weight_near, *msgs)
    other = swap(brief, "tensor", 1)
    distance = 2
    while distance < tensors:
        part, brief = call(
            add_kernel,
            [shaped((rows, width), F32), shaped((rows, width), BF16)],
            [vmem()] * 2,
            [vmem()] * 2,
            flops=rows * width,
            nbytes=rows * width * 14,
        )(part, other)
        other = swap(brief, "tensor", 2 * distance - 1)
        distance *= 2

    child_conv, gate, rate, twin, dtb_near, skip_near = call(
        functools.partial(late_kernel, n_msgs, direct),
        [
            shaped((taps - 1, rb, channels), BF16),
            shaped((steps, rb, channels), F32),
            shaped((n_state, channels), F32),
            shaped((n_state // 2, 2 * owners, channels), F32),
            shaped((1, channels), F32),
            shaped((1, channels), F32),
        ],
        [hbm()] * 6 + [anywhere()] + [vmem()] * n_msgs,
        [anywhere()] + [vmem()] * 5,
        [
            pltpu.SMEM((1,), jnp.int32),
            pltpu.SMEM((rb,), jnp.int32),
            pltpu.VMEM(step_in.shape, BF16),
            pltpu.VMEM((n_state, channels), F32),
            pltpu.VMEM((taps - 1, rb, channels), BF16),
            pltpu.SemaphoreType.DMA((6 + STEP_PARTS,)),
        ],
        flops=10 * steps * rb * channels,
        nbytes=12 * steps * rb * channels,
        trans=steps * rb * channels,
    )(
        owner,
        pinned(child_slot),
        pinned(step_in),
        pinned(a_log),
        pinned(dt_bias[None]),
        pinned(skip[None]),
        part,
        *msgs,
    )
    own_start, slot_start = call(
        functools.partial(start_kernel, n_msgs, direct, short),
        [
            shaped((n_state, rb, channels), F32),
            shaped((n_state // 2, 2 * owners, channels), F32),
        ],
        [vmem()] * 2 + [anywhere()] + [vmem()] * (n_msgs + len(states)),
        [vmem()] * 2,
        [pltpu.VMEM((owners, n_state, channels), F32)],
        flops=2 * owners * n_state * (rb + owners) * channels,
        nbytes=4 * n_state * (rb + owners) * channels,
    )(pick, sender, part, *msgs, *states)

    decoded, child_ssm = call(
        functools.partial(decode_kernel, direct),
        [
            shaped((rb, steps, channels), BF16),
            shaped((rb, n_state, channels), F32),
        ],
        [hbm()] * 2 + [vmem()] * 11,
        [vmem(), anywhere()],
        [
            pltpu.SMEM((1,), jnp.int32),
            pltpu.SMEM((rb,), jnp.int32),
            pltpu.VMEM((steps * rb, channels), F32),
            pltpu.VMEM((steps * rb, channels), F32),
            pltpu.VMEM((steps, 2 * owners, channels), F32),
            pltpu.VMEM((steps, 2 * owners, channels), F32),
            pltpu.VMEM((n_state, steps * rb, LANES), F32),
            pltpu.VMEM((n_state, steps * rb, LANES), F32),
            pltpu.VMEM((n_state // 2, steps, 2 * owners, LANES), F32),
            pltpu.VMEM((owners, n_state, channels), F32),
            pltpu.VMEM((WIDE, steps * rb, LANES), F32),
            pltpu.SemaphoreType.DMA((2 + rb,)),
        ],
        flops=8 * rows * n_state * channels,
        nbytes=(rb + owners) * n_state * channels * 4,
        trans=rows * n_state * channels,
    )(
        owner,
        pinned(child_slot),
        act,
        gate,
        own_start,
        slot_start,
        rate,
        twin,
        dt_weight,
        dtb_near,
        skip_near,
        part,
        other,
    )
    return (decoded, child_ssm, jnp.transpose(child_conv, (1, 0, 2)))


def solution(mesh):
    placed = (
        P(("replica", "branch"), None, "tensor"),
        P(("replica", "branch"), None, "tensor"),
        P(("replica", "branch")),
        P(("replica", "branch"), None, None, "tensor"),
        P(None, "tensor"),
        P("tensor"),
        P("tensor", None),
        P(None, "tensor"),
        P("tensor"),
        P(None, "tensor"),
        P("tensor"),
        P(("replica", "branch"), None, None),
        P(("replica", "branch")),
    )
    return jax.shard_map(
        on_device,
        mesh=mesh,
        in_specs=placed,
        out_specs=(
            P(("replica", "branch"), None, "tensor"),
            P(("replica", "branch"), None, "tensor"),
            P(("replica", "branch"), None, "tensor"),
        ),
        check_vma=False,
    )
```

```python
import functools
import math

import jax
import jax.numpy as jnp
from jax import lax
from jax.experimental import pallas as pl
from jax.experimental.pallas import tpu as pltpu
from jax.sharding import PartitionSpec as P

F32 = jnp.float32
BF16 = jnp.bfloat16
LANES = 128
ROWS = 8
WIDE = 4
SLOT_WIDE = 4
VMEM_LIMIT = 48 * 2**20
WEIGHT_PARTS = 6
STEP_PARTS = 4
DIRECT = 4
SENDS = ((2, 3, 1, 0), (3, 2, 0, 1), (1, 0, 3, 2))


def vmem():
    return pl.BlockSpec(memory_space=pltpu.VMEM)


def hbm():
    return pl.BlockSpec(memory_space=pltpu.HBM)


def anywhere():
    return pl.BlockSpec(memory_space=pl.ANY)


def pinned(array):
    return pltpu.with_memory_space_constraint(array, pltpu.HBM)


def shaped(shape, dtype):
    return jax.ShapeDtypeStruct(shape, dtype)


def call(kernel, outs, in_specs, out_specs, scratch=(), flops=0, nbytes=0, trans=0):
    return pl.pallas_call(
        kernel,
        out_shape=outs,
        in_specs=in_specs,
        out_specs=out_specs,
        scratch_shapes=list(scratch),
        compiler_params=pltpu.CompilerParams(vmem_limit_bytes=VMEM_LIMIT),
        cost_estimate=pl.CostEstimate(flops=flops, bytes_accessed=nbytes, transcendentals=trans),
    )


def swap(value, axis, distance):
    size = lax.axis_size(axis)
    return lax.ppermute(value, axis, [(i, i ^ distance) for i in range(size)])


def chosen(number, values):
    total = values[0]
    for i in range(1, len(values)):
        total = jnp.where(number == i, values[i], total)
    return total


def blocks_of(owner):
    table = [
        [0 if s == r else 1 + [to[s] for to in SENDS].index(r) for s in range(DIRECT)]
        for r in range(DIRECT)
    ]
    return [chosen(owner, [row[s] for row in table]) for s in range(DIRECT)]


def all_of(copies):
    for copy in copies:
        copy.start()
    for copy in copies:
        copy.wait()


def read_messages(refs):
    return [ref[i].astype(F32) for ref in refs for i in range(ref.shape[0])]


def in_parts(source, target, sems, first, count):
    rows = source.shape[0] // count
    at = [pl.ds(i * rows, rows) for i in range(count)]
    return [
        pltpu.make_async_copy(source.at[a], target.at[a], sems.at[first + i])
        for i, a in enumerate(at)
    ]


def scalar_onehot(senders_s, places, shape):
    row_of = lax.broadcasted_iota(jnp.int32, shape, 0)
    wanted = jnp.zeros(shape, jnp.int32)
    for b in range(shape[0]):
        wanted = jnp.where(row_of == b, senders_s[b], wanted)
    wanted = wanted if places is None else chosen(wanted, places)
    return (wanted == lax.broadcasted_iota(jnp.int32, shape, 1)).astype(F32)


def pick_rows(pick, rows):
    total = pick[:, 0:1] * rows[0]
    for k in range(1, len(rows)):
        total = total + pick[:, k : k + 1] * rows[k]
    return total


def message(target, rows_s, prompt_s, step, conv, state):
    row = jnp.maximum(rows_s[target], 0)
    xs = step[row, :, 0, :].astype(F32)
    number = jnp.full((1, xs.shape[1]), prompt_s[row].astype(F32), F32)
    pieces = [xs, conv[0].astype(F32), number] + ([] if state is None else [state])
    return jnp.concatenate(pieces, axis=0).astype(BF16)


def pack_kernel(direct, owner_hbm, rows_hbm, prompt_hbm, step_hbm, conv_hbm, ssm_hbm, *rest):
    outs, (owner_s, rows_s, prompt_s, step, conv, ssm, sems) = rest[:-7], rest[-7:]
    owners = rows_hbm.shape[0]
    copies = [
        pltpu.make_async_copy(owner_hbm, owner_s, sems.at[4]),
        pltpu.make_async_copy(rows_hbm, rows_s, sems.at[0]),
        pltpu.make_async_copy(prompt_hbm, prompt_s, sems.at[1]),
        pltpu.make_async_copy(conv_hbm, conv, sems.at[2]),
        pltpu.make_async_copy(ssm_hbm, ssm, sems.at[3]),
    ]
    all_of(copies + in_parts(step_hbm, step, sems, 5, STEP_PARTS))
    owner = owner_s[0]
    targets = [chosen(owner, to) for to in SENDS] if direct else range(owners)
    for i, target in enumerate(targets):
        ref = outs[i].at[0] if direct else outs[0].at[i]
        state = ssm[0] if ref.shape[0] > conv.shape[1] + step.shape[1] + 1 else None
        ref[...] = message(target, rows_s, prompt_s, step, conv, state)


def pair_kernel(text, ssm_ref, came_ref, after_ref, pair_ref):
    del after_ref
    state = ssm_ref[0]
    head = state.astype(BF16).astype(F32)
    came = came_ref[0].astype(F32)[text:, :]
    pair_ref[0] = jnp.concatenate([head, state - head, came], axis=0).astype(BF16)


def silu(v):
    return v / (1.0 + jnp.exp(-v))


def prepare_kernel(
    direct,
    owner_hbm,
    prompt_hbm,
    rows_hbm,
    conv_hbm,
    step_hbm,
    cw_hbm,
    cb_hbm,
    xwt_hbm,
    after_ref,
    own_ref,
    base_ref,
    pick_ref,
    sender_ref,
    cw_ref,
    cb_ref,
    xwt_ref,
    step_ref,
    owner_s,
    prompt_s,
    rows_s,
    conv,
    sems,
):
    del after_ref
    small = [
        pltpu.make_async_copy(source, target, sems.at[i])
        for i, (source, target) in enumerate(
            (
                (cw_hbm, cw_ref),
                (cb_hbm, cb_ref),
                (owner_hbm, owner_s),
                (prompt_hbm, prompt_s),
                (rows_hbm, rows_s),
                (conv_hbm, conv),
            )
        )
    ]
    inputs = in_parts(step_hbm, step_ref, sems, len(small), STEP_PARTS)
    large = in_parts(xwt_hbm, xwt_ref, sems, len(small) + STEP_PARTS, WEIGHT_PARTS)
    for copy in inputs + small + large:
        copy.start()
    for copy in inputs + small:
        copy.wait()
    own_ref[0] = message(owner_s[0], rows_s, prompt_s, step_ref, conv, None)
    steps = step_ref.shape[1]
    taps = cw_hbm.shape[0]
    xs = [step_ref[:, t, 0, :].astype(F32) for t in range(steps)]
    for t in range(steps):
        total = cw_ref[taps - 1 : taps, :] * xs[t] + cb_ref[...]
        for k in range(max(0, taps - 1 - t), taps - 1):
            total = total + cw_ref[k : k + 1, :] * xs[t + k - taps + 1]
        base_ref[t] = total
    places = blocks_of(owner_s[0]) if direct else None
    pick_ref[...] = scalar_onehot(prompt_s, places, pick_ref.shape)
    column = lax.broadcasted_iota(jnp.int32, sender_ref.shape, 1)
    sender = column
    for sent, place in enumerate(places or []):
        sender = jnp.where(column == place, sent, sender)
    sender_ref[...] = sender.astype(F32)
    for copy in large:
        copy.wait()


def slot_onehot(numbers, sender_ref):
    owners = sender_ref.shape[1]
    return (numbers[:, :owners] == sender_ref[...]).astype(F32)


def project_kernel(n_msgs, pick_ref, sender_ref, base_ref, cw_ref, cb_ref, xwt_ref, *rest):
    msgs, (act_ref, part_ref, short_ref) = rest[:n_msgs], rest[n_msgs:]
    taps = cw_ref.shape[0]
    steps, rb, _ = base_ref.shape
    past = taps - 1
    held = read_messages(msgs)
    owners = len(held)
    windows = [[h[steps + k : steps + k + 1, :] for h in held] for k in range(past)]
    own = pick_ref[...]
    own_windows = [pick_rows(own, w) for w in windows]
    for t in range(steps):
        conv = base_ref[t]
        for k in range(past - t):
            conv = conv + cw_ref[k : k + 1, :] * own_windows[t + k]
        act_ref[t * rb : (t + 1) * rb, :] = silu(conv)

    def line_of(row):
        return jnp.concatenate([h[row : row + 1, :] for h in held], axis=0)

    slot = slot_onehot(line_of(past + steps), sender_ref)
    line = [pick_rows(slot, w) for w in windows]
    line += [line_of(t) for t in range(steps)]
    row = steps * rb
    for t in range(steps):
        conv = cw_ref[past:taps, :] * line[t + past] + cb_ref[...]
        for k in range(past):
            conv = conv + cw_ref[k : k + 1, :] * line[t + k]
        act_ref[row : row + owners, :] = silu(conv)
        row += owners
    part = lax.dot_general(
        act_ref[...].astype(BF16),
        xwt_ref[...],
        (((1,), (1,)), ((), ())),
        preferred_element_type=F32,
    )
    part_ref[...] = part
    short_ref[...] = part.astype(BF16)


def add_kernel(a_ref, b_ref, sum_ref, short_ref):
    total = a_ref[...] + b_ref[...].astype(F32)
    sum_ref[...] = total
    short_ref[...] = total.astype(BF16)


def late_kernel(n_msgs, direct, *refs):
    sources, refs = refs[:6], refs[7:]
    owner_hbm, child_hbm, step_hbm, alog_hbm, dtb_hbm, skip_hbm = sources
    msgs, refs = refs[:n_msgs], refs[n_msgs:]
    conv_hbm, gate_ref, rate_ref, twin_ref, dtb_ref, skip_ref = refs[:6]
    owner_s, child_s, step_ref, alog, conv_s, sems = refs[6:]
    small = [
        pltpu.make_async_copy(source, target, sems.at[i])
        for i, (source, target) in enumerate(
            (
                (owner_hbm, owner_s),
                (child_hbm, child_s),
                (alog_hbm, alog),
                (dtb_hbm, dtb_ref),
                (skip_hbm, skip_ref),
            )
        )
    ]
    inputs = in_parts(step_hbm, step_ref, sems, len(small), STEP_PARTS)
    for copy in small + inputs:
        copy.start()
    held = read_messages(msgs)
    past, rb, _ = conv_s.shape
    steps = step_ref.shape[1]
    for copy in small:
        copy.wait()
    places = blocks_of(owner_s[0]) if direct else None
    child = scalar_onehot(child_s, places, (rb, len(held)))
    for k in range(past):
        at = steps - past + k
        conv_s[k] = pick_rows(child, [h[at : at + 1, :] for h in held]).astype(BF16)
    out = pltpu.make_async_copy(conv_s, conv_hbm, sems.at[len(small) + STEP_PARTS])
    out.start()
    rate = jnp.exp(alog[...]) * (-math.log2(math.e))
    rate_ref[...] = rate
    half = (twin_ref.shape[1] // 2, rate.shape[1])
    for m in range(rate.shape[0] // 2):
        two = [jnp.broadcast_to(rate[n : n + 1, :], half) for n in (2 * m, 2 * m + 1)]
        twin_ref[m] = jnp.concatenate(two, axis=0)
    for copy in inputs:
        copy.wait()
    for t in range(steps):
        gate_ref[t] = silu(step_ref[:, t, 1, :].astype(F32))
    out.wait()


def start_kernel(n_msgs, direct, text, pick_ref, sender_ref, after_ref, *rest):
    del after_ref
    msgs, rest = rest[:n_msgs], rest[n_msgs:]
    apart, (own_ref, slot_ref, state_s) = rest[:-3], rest[-3:]
    n_state = own_ref.shape[0]
    held = read_messages(msgs)
    owners = len(held)
    numbers = jnp.concatenate([h[text - 1 : text, :] for h in held], axis=0)
    states = [h[text:, :] for h in held]
    if direct:
        ssm_ref, pair_ref = apart
        head, low, came = [
            pair_ref[0].astype(F32)[i * n_state : (i + 1) * n_state, :] for i in range(3)
        ]
        states[0], states[2], states[3] = ssm_ref[0], came, head + low
    for k, state in enumerate(states):
        state_s[k] = state
    own = pick_ref[...]
    slot = slot_onehot(numbers, sender_ref)

    def two(m, carry):
        picked = []
        for n in (2 * m, 2 * m + 1):
            rows = [state_s[k, pl.ds(n, 1), :] for k in range(owners)]
            own_ref[n] = pick_rows(own, rows)
            picked.append(pick_rows(slot, rows))
        slot_ref[m] = jnp.concatenate(picked, axis=0)
        return carry

    lax.fori_loop(0, n_state // 2, two, 0, unroll=owners <= DIRECT)


def decode_kernel(
    direct,
    owner_hbm,
    child_hbm,
    act_ref,
    gate_ref,
    own_ref,
    slot_ref,
    rate_ref,
    twin_ref,
    dtw_ref,
    dtb_ref,
    skip_ref,
    part_ref,
    other_ref,
    dec_ref,
    child_ssm,
    owner_s,
    child_s,
    delta_s,
    gain_s,
    slot_delta_s,
    slot_gain_s,
    b_s,
    c_s,
    twin_b_s,
    slots_s,
    rows_s,
    line_s,
    sems,
):
    scalars = [
        pltpu.make_async_copy(owner_hbm, owner_s, sems.at[0]),
        pltpu.make_async_copy(child_hbm, child_s, sems.at[1]),
    ]
    for copy in scalars:
        copy.start()
    rb, steps, channels = dec_ref.shape
    rank = dtw_ref.shape[0]
    n_state = rate_ref.shape[0]
    n_slots = slots_s.shape[0]
    own_rows = steps * rb
    chunks = channels // (WIDE * LANES)

    proj = part_ref[...] + other_ref[...].astype(F32)
    delta_in = proj[:, :rank].astype(BF16)
    delta = jnp.dot(delta_in, dtw_ref[...], preferred_element_type=F32) + dtb_ref[...]
    delta = jnp.maximum(delta, 0.0) + jnp.log(1.0 + jnp.exp(-jnp.abs(delta)))
    gain = delta * act_ref[...]
    delta_s[...] = delta[:own_rows, :]
    gain_s[...] = gain[:own_rows, :]

    def column(at, n, rows):
        return jnp.broadcast_to(at[:, n : n + 1], (rows, LANES))

    for t in range(steps):
        at = slice(own_rows + t * n_slots, own_rows + (t + 1) * n_slots)
        slot_delta_s[t] = jnp.concatenate([delta[at, :]] * 2, axis=0)
        slot_gain_s[t] = jnp.concatenate([gain[at, :]] * 2, axis=0)
        twice = jnp.concatenate([proj[at, rank:]] * 2, axis=0)
        upper = lax.broadcasted_iota(jnp.int32, (2 * n_slots, LANES), 0) < n_slots
        for m in range(n_state // 2):
            twin_b_s[m, t] = jnp.where(
                upper, column(twice, 2 * m, 2 * n_slots), column(twice, 2 * m + 1, 2 * n_slots)
            )
    for n in range(n_state):
        b_s[n] = column(proj[:own_rows, rank:], n, own_rows)
        c_s[n] = column(proj[:own_rows, rank:], n_state + n, own_rows)

    def wide(part, times=WIDE):
        return jnp.concatenate([part] * times, axis=1)

    def slot_chunk(chunk, carry):
        breadth = SLOT_WIDE * LANES
        columns = pl.ds(pl.multiple_of(chunk * breadth, breadth), breadth)
        delta = [slot_delta_s[t, :, columns] for t in range(steps)]
        gain = [slot_gain_s[t, :, columns] for t in range(steps)]
        for m in range(n_state // 2):
            rate = twin_ref[m, :, columns]
            state = slot_ref[m, :, columns]
            for t in range(steps):
                state = jnp.exp2(delta[t] * rate) * state + gain[t] * wide(twin_b_s[m, t], SLOT_WIDE)
            for w in range(SLOT_WIDE):
                rows = pl.ds(2 * m * n_slots, 2 * n_slots)
                lanes = slice(w * LANES, (w + 1) * LANES)
                rows_s[chunk * SLOT_WIDE + w, rows, :] = state[:, lanes]
        return carry

    lax.fori_loop(0, channels // (SLOT_WIDE * LANES), slot_chunk, 0)
    for slot in range(n_slots):
        for i in range(channels // LANES):
            rows = rows_s[i, pl.ds(slot, n_state, stride=n_slots), :]
            slots_s[slot, :, i * LANES : (i + 1) * LANES] = rows
    for copy in scalars:
        copy.wait()
    places = blocks_of(owner_s[0]) if direct else None
    copies = []
    for j in range(rb):
        at = chosen(child_s[j], places) if direct else child_s[j]
        copy = pltpu.make_async_copy(slots_s.at[at], child_ssm.at[j], sems.at[2 + j])
        copy.start()
        copies.append(copy)

    def own_chunk(chunk, carry):
        columns = pl.ds(pl.multiple_of(chunk * WIDE * LANES, WIDE * LANES), WIDE * LANES)
        for first in range(0, rb, ROWS):
            at = [pl.ds(t * rb + first, ROWS) for t in range(steps)]
            delta = [delta_s[a, columns] for a in at]
            gain = [gain_s[a, columns] for a in at]
            sums = [skip_ref[:, columns] * act_ref[a, columns] for a in at]
            for n in range(n_state):
                rate = rate_ref[n : n + 1, columns]
                state = own_ref[n, pl.ds(first, ROWS), columns]
                for t in range(steps):
                    state = jnp.exp2(delta[t] * rate) * state + gain[t] * wide(b_s[n, at[t], :])
                    sums[t] = sums[t] + wide(c_s[n, at[t], :]) * state
            for t in range(steps):
                out = sums[t] * gate_ref[t, pl.ds(first, ROWS), columns]
                for w in range(WIDE):
                    line_s[w, pl.ds(first * steps + t, ROWS, stride=steps), :] = out[
                        :, w * LANES : (w + 1) * LANES
                    ]
        for w in range(WIDE):
            some = pl.ds(pl.multiple_of((chunk * WIDE + w) * LANES, LANES), LANES)
            dec_ref[:, :, some] = line_s[w].reshape(rb, steps, LANES).astype(BF16)
        return carry

    lax.fori_loop(0, chunks, own_chunk, 0)
    for copy in copies:
        copy.wait()


def on_device(
    prompt_ssm,
    prompt_conv,
    prompt_of,
    step_in,
    conv_weight,
    conv_bias,
    x_weight,
    dt_weight,
    dt_bias,
    a_log,
    skip,
    send_rows,
    child_slot,
):
    owners = lax.axis_size("branch")
    tensors = lax.axis_size("tensor")
    assert owners & (owners - 1) == 0 and tensors & (tensors - 1) == 0
    assert prompt_ssm.shape[0] == 1 and send_rows.shape[2] == 1
    rb, steps, _, channels = step_in.shape
    taps = conv_weight.shape[0]
    width = x_weight.shape[1]
    n_state = a_log.shape[0]
    rows = steps * (rb + owners)
    short = taps - 1 + steps + 1
    depth = short + n_state
    direct = owners == DIRECT
    owner = pinned(lax.axis_index("branch").astype(jnp.int32).reshape(1))

    if direct:
        msg_shapes = [(1, d, channels) for d in (depth, short, short)]
    else:
        msg_shapes = [(owners, depth, channels)]
    msgs = call(
        functools.partial(pack_kernel, direct),
        [shaped(s, BF16) for s in msg_shapes],
        [hbm()] * 6,
        [vmem()] * len(msg_shapes),
        [
            pltpu.SMEM((1,), jnp.int32),
            pltpu.SMEM((owners,), jnp.int32),
            pltpu.SMEM((rb,), jnp.int32),
            pltpu.VMEM(step_in.shape, BF16),
            pltpu.VMEM(prompt_conv.shape, BF16),
            pltpu.VMEM(prompt_ssm.shape, F32),
            pltpu.SemaphoreType.DMA((5 + STEP_PARTS,)),
        ],
        nbytes=owners * depth * channels * 2,
    )(
        owner,
        pinned(send_rows.reshape(owners)),
        pinned(prompt_of),
        pinned(step_in),
        pinned(prompt_conv),
        pinned(prompt_ssm),
    )
    after = msgs[0]
    if direct:
        msgs = [lax.ppermute(m, "branch", list(enumerate(to))) for m, to in zip(msgs, SENDS)]
    else:
        msgs = [lax.all_to_all(msgs[0], "branch", split_axis=0, concat_axis=0, tiled=True)]
    own, base, pick, sender, taps_near, bias_near, weight_near = call(
        functools.partial(prepare_kernel, direct),
        [
            shaped((1, short, channels), BF16),
            shaped((steps, rb, channels), F32),
            shaped((rb, owners), F32),
            shaped((1, owners), F32),
            shaped((taps, channels), F32),
            shaped((1, channels), F32),
            shaped((width, channels), BF16),
        ],
        [hbm()] * 8 + [anywhere()],
        [vmem()] * 7,
        [
            pltpu.VMEM(step_in.shape, BF16),
            pltpu.SMEM((1,), jnp.int32),
            pltpu.SMEM((rb,), jnp.int32),
            pltpu.SMEM((owners,), jnp.int32),
            pltpu.VMEM(prompt_conv.shape, BF16),
            pltpu.SemaphoreType.DMA((6 + WEIGHT_PARTS + STEP_PARTS,)),
        ],
        flops=10 * steps * rb * channels,
        nbytes=12 * steps * rb * channels,
    )(
        owner,
        pinned(prompt_of),
        pinned(send_rows.reshape(owners)),
        pinned(prompt_conv),
        pinned(step_in),
        pinned(conv_weight),
        pinned(conv_bias[None]),
        pinned(x_weight.T),
        after,
    )
    states = []
    if direct:
        msgs = [own] + msgs
        pair = call(
            functools.partial(pair_kernel, short),
            shaped((1, 3 * n_state, channels), BF16),
            [vmem()] * 2 + [anywhere()],
            vmem(),
            nbytes=12 * n_state * channels,
        )(prompt_ssm, msgs[1], pick)
        states = [prompt_ssm, swap(pair, "branch", 1)]
    n_msgs = len(msgs)
    act, part, brief = call(
        functools.partial(project_kernel, n_msgs),
        [
            shaped((rows, channels), F32),
            shaped((rows, width), F32),
            shaped((rows, width), BF16),
        ],
        [vmem()] * (6 + n_msgs),
        [vmem()] * 3,
        flops=2 * rows * channels * width,
        nbytes=channels * width * 2 + rows * (channels + width) * 4,
        trans=rows * channels,
    )(pick, sender, base, taps_near, bias_near, weight_near, *msgs)
    other = swap(brief, "tensor", 1)
    distance = 2
    while distance < tensors:
        part, brief = call(
            add_kernel,
            [shaped((rows, width), F32), shaped((rows, width), BF16)],
            [vmem()] * 2,
            [vmem()] * 2,
            flops=rows * width,
            nbytes=rows * width * 14,
        )(part, other)
        other = swap(brief, "tensor", 2 * distance - 1)
        distance *= 2

    child_conv, gate, rate, twin, dtb_near, skip_near = call(
        functools.partial(late_kernel, n_msgs, direct),
        [
            shaped((taps - 1, rb, channels), BF16),
            shaped((steps, rb, channels), F32),
            shaped((n_state, channels), F32),
            shaped((n_state // 2, 2 * owners, channels), F32),
            shaped((1, channels), F32),
            shaped((1, channels), F32),
        ],
        [hbm()] * 6 + [anywhere()] + [vmem()] * n_msgs,
        [anywhere()] + [vmem()] * 5,
        [
            pltpu.SMEM((1,), jnp.int32),
            pltpu.SMEM((rb,), jnp.int32),
            pltpu.VMEM(step_in.shape, BF16),
            pltpu.VMEM((n_state, channels), F32),
            pltpu.VMEM((taps - 1, rb, channels), BF16),
            pltpu.SemaphoreType.DMA((6 + STEP_PARTS,)),
        ],
        flops=10 * steps * rb * channels,
        nbytes=12 * steps * rb * channels,
        trans=steps * rb * channels,
    )(
        owner,
        pinned(child_slot),
        pinned(step_in),
        pinned(a_log),
        pinned(dt_bias[None]),
        pinned(skip[None]),
        part,
        *msgs,
    )
    own_start, slot_start = call(
        functools.partial(start_kernel, n_msgs, direct, short),
        [
            shaped((n_state, rb, channels), F32),
            shaped((n_state // 2, 2 * owners, channels), F32),
        ],
        [vmem()] * 2 + [anywhere()] + [vmem()] * (n_msgs + len(states)),
        [vmem()] * 2,
        [pltpu.VMEM((owners, n_state, channels), F32)],
        flops=2 * owners * n_state * (rb + owners) * channels,
        nbytes=4 * n_state * (rb + owners) * channels,
    )(pick, sender, part, *msgs, *states)

    decoded, child_ssm = call(
        functools.partial(decode_kernel, direct),
        [
            shaped((rb, steps, channels), BF16),
            shaped((rb, n_state, channels), F32),
        ],
        [hbm()] * 2 + [vmem()] * 11,
        [vmem(), anywhere()],
        [
            pltpu.SMEM((1,), jnp.int32),
            pltpu.SMEM((rb,), jnp.int32),
            pltpu.VMEM((steps * rb, channels), F32),
            pltpu.VMEM((steps * rb, channels), F32),
            pltpu.VMEM((steps, 2 * owners, channels), F32),
            pltpu.VMEM((steps, 2 * owners, channels), F32),
            pltpu.VMEM((n_state, steps * rb, LANES), F32),
            pltpu.VMEM((n_state, steps * rb, LANES), F32),
            pltpu.VMEM((n_state // 2, steps, 2 * owners, LANES), F32),
            pltpu.VMEM((owners, n_state, channels), F32),
            pltpu.VMEM((channels // LANES, n_state * owners, LANES), F32),
            pltpu.VMEM((WIDE, steps * rb, LANES), F32),
            pltpu.SemaphoreType.DMA((2 + rb,)),
        ],
        flops=8 * rows * n_state * channels,
        nbytes=(rb + owners) * n_state * channels * 4,
        trans=rows * n_state * channels,
    )(
        owner,
        pinned(child_slot),
        act,
        gate,
        own_start,
        slot_start,
        rate,
        twin,
        dt_weight,
        dtb_near,
        skip_near,
        part,
        other,
    )
    return (decoded, child_ssm, jnp.transpose(child_conv, (1, 0, 2)))


def solution(mesh):
    placed = (
        P(("replica", "branch"), None, "tensor"),
        P(("replica", "branch"), None, "tensor"),
        P(("replica", "branch")),
        P(("replica", "branch"), None, None, "tensor"),
        P(None, "tensor"),
        P("tensor"),
        P("tensor", None),
        P(None, "tensor"),
        P("tensor"),
        P(None, "tensor"),
        P("tensor"),
        P(("replica", "branch"), None, None),
        P(("replica", "branch")),
    )
    return jax.shard_map(
        on_device,
        mesh=mesh,
        in_specs=placed,
        out_specs=(
            P(("replica", "branch"), None, "tensor"),
            P(("replica", "branch"), None, "tensor"),
            P(("replica", "branch"), None, "tensor"),
        ),
        check_vma=False,
    )
```

```python
import functools
import math

import jax
import jax.numpy as jnp
from jax import lax
from jax.experimental import pallas as pl
from jax.experimental.pallas import tpu as pltpu
from jax.sharding import PartitionSpec as P

F32 = jnp.float32
BF16 = jnp.bfloat16
LANES = 128
ROWS = 8
WIDE = 4
SLOT_WIDE = 4
VMEM_LIMIT = 48 * 2**20
WEIGHT_PARTS = 6
STEP_PARTS = 4
DIRECT = 4
SENDS = ((2, 3, 1, 0), (3, 2, 0, 1), (1, 0, 3, 2))


def vmem():
    return pl.BlockSpec(memory_space=pltpu.VMEM)


def hbm():
    return pl.BlockSpec(memory_space=pltpu.HBM)


def anywhere():
    return pl.BlockSpec(memory_space=pl.ANY)


def pinned(array):
    return pltpu.with_memory_space_constraint(array, pltpu.HBM)


def shaped(shape, dtype):
    return jax.ShapeDtypeStruct(shape, dtype)


def call(kernel, outs, in_specs, out_specs, scratch=(), flops=0, nbytes=0, trans=0):
    return pl.pallas_call(
        kernel,
        out_shape=outs,
        in_specs=in_specs,
        out_specs=out_specs,
        scratch_shapes=list(scratch),
        compiler_params=pltpu.CompilerParams(vmem_limit_bytes=VMEM_LIMIT),
        cost_estimate=pl.CostEstimate(flops=flops, bytes_accessed=nbytes, transcendentals=trans),
    )


def swap(value, axis, distance):
    size = lax.axis_size(axis)
    return lax.ppermute(value, axis, [(i, i ^ distance) for i in range(size)])


def chosen(number, values):
    total = values[0]
    for i in range(1, len(values)):
        total = jnp.where(number == i, values[i], total)
    return total


def blocks_of(owner):
    table = [
        [0 if s == r else 1 + [to[s] for to in SENDS].index(r) for s in range(DIRECT)]
        for r in range(DIRECT)
    ]
    return [chosen(owner, [row[s] for row in table]) for s in range(DIRECT)]


def all_of(copies):
    for copy in copies:
        copy.start()
    for copy in copies:
        copy.wait()


def read_messages(refs):
    return [ref[i].astype(F32) for ref in refs for i in range(ref.shape[0])]


def in_parts(source, target, sems, first, count):
    rows = source.shape[0] // count
    at = [pl.ds(i * rows, rows) for i in range(count)]
    return [
        pltpu.make_async_copy(source.at[a], target.at[a], sems.at[first + i])
        for i, a in enumerate(at)
    ]


def scalar_onehot(senders_s, places, shape):
    row_of = lax.broadcasted_iota(jnp.int32, shape, 0)
    wanted = jnp.zeros(shape, jnp.int32)
    for b in range(shape[0]):
        wanted = jnp.where(row_of == b, senders_s[b], wanted)
    wanted = wanted if places is None else chosen(wanted, places)
    return (wanted == lax.broadcasted_iota(jnp.int32, shape, 1)).astype(F32)


def pick_rows(pick, rows):
    total = pick[:, 0:1] * rows[0]
    for k in range(1, len(rows)):
        total = total + pick[:, k : k + 1] * rows[k]
    return total


def message(target, rows_s, prompt_s, step, conv, state):
    row = jnp.maximum(rows_s[target], 0)
    xs = step[row, :, 0, :].astype(F32)
    number = jnp.full((1, xs.shape[1]), prompt_s[row].astype(F32), F32)
    pieces = [xs, conv[0].astype(F32), number] + ([] if state is None else [state])
    return jnp.concatenate(pieces, axis=0).astype(BF16)


def pack_kernel(direct, owner_hbm, rows_hbm, prompt_hbm, step_hbm, conv_hbm, ssm_hbm, *rest):
    outs, (owner_s, rows_s, prompt_s, step, conv, ssm, sems) = rest[:-7], rest[-7:]
    owners = rows_hbm.shape[0]
    copies = [
        pltpu.make_async_copy(owner_hbm, owner_s, sems.at[4]),
        pltpu.make_async_copy(rows_hbm, rows_s, sems.at[0]),
        pltpu.make_async_copy(prompt_hbm, prompt_s, sems.at[1]),
        pltpu.make_async_copy(conv_hbm, conv, sems.at[2]),
        pltpu.make_async_copy(ssm_hbm, ssm, sems.at[3]),
    ]
    all_of(copies + in_parts(step_hbm, step, sems, 5, STEP_PARTS))
    owner = owner_s[0]
    targets = [chosen(owner, to) for to in SENDS] if direct else range(owners)
    for i, target in enumerate(targets):
        ref = outs[i].at[0] if direct else outs[0].at[i]
        state = ssm[0] if ref.shape[0] > conv.shape[1] + step.shape[1] + 1 else None
        ref[...] = message(target, rows_s, prompt_s, step, conv, state)


def pair_kernel(text, ssm_ref, came_ref, after_ref, pair_ref):
    del after_ref
    state = ssm_ref[0]
    head = state.astype(BF16).astype(F32)
    came = came_ref[0].astype(F32)[text:, :]
    pair_ref[0] = jnp.concatenate([head, state - head, came], axis=0).astype(BF16)


def silu(v):
    return v / (1.0 + jnp.exp(-v))


def prepare_kernel(
    direct,
    owner_hbm,
    prompt_hbm,
    rows_hbm,
    conv_hbm,
    step_hbm,
    cw_hbm,
    cb_hbm,
    xwt_hbm,
    after_ref,
    own_ref,
    base_ref,
    pick_ref,
    sender_ref,
    cw_ref,
    cb_ref,
    xwt_ref,
    step_ref,
    owner_s,
    prompt_s,
    rows_s,
    conv,
    sems,
):
    del after_ref
    small = [
        pltpu.make_async_copy(source, target, sems.at[i])
        for i, (source, target) in enumerate(
            (
                (cw_hbm, cw_ref),
                (cb_hbm, cb_ref),
                (owner_hbm, owner_s),
                (prompt_hbm, prompt_s),
                (rows_hbm, rows_s),
                (conv_hbm, conv),
            )
        )
    ]
    inputs = in_parts(step_hbm, step_ref, sems, len(small), STEP_PARTS)
    large = in_parts(xwt_hbm, xwt_ref, sems, len(small) + STEP_PARTS, WEIGHT_PARTS)
    for copy in inputs + small + large:
        copy.start()
    for copy in inputs + small:
        copy.wait()
    own_ref[0] = message(owner_s[0], rows_s, prompt_s, step_ref, conv, None)
    steps = step_ref.shape[1]
    taps = cw_hbm.shape[0]
    xs = [step_ref[:, t, 0, :].astype(F32) for t in range(steps)]
    for t in range(steps):
        total = cw_ref[taps - 1 : taps, :] * xs[t] + cb_ref[...]
        for k in range(max(0, taps - 1 - t), taps - 1):
            total = total + cw_ref[k : k + 1, :] * xs[t + k - taps + 1]
        base_ref[t] = total
    places = blocks_of(owner_s[0]) if direct else None
    pick_ref[...] = scalar_onehot(prompt_s, places, pick_ref.shape)
    column = lax.broadcasted_iota(jnp.int32, sender_ref.shape, 1)
    sender = column
    for sent, place in enumerate(places or []):
        sender = jnp.where(column == place, sent, sender)
    sender_ref[...] = sender.astype(F32)
    for copy in large:
        copy.wait()


def slot_onehot(numbers, sender_ref):
    owners = sender_ref.shape[1]
    return (numbers[:, :owners] == sender_ref[...]).astype(F32)


def project_kernel(n_msgs, pick_ref, sender_ref, base_ref, cw_ref, cb_ref, xwt_ref, *rest):
    msgs, (act_ref, part_ref, short_ref) = rest[:n_msgs], rest[n_msgs:]
    taps = cw_ref.shape[0]
    steps, rb, _ = base_ref.shape
    past = taps - 1
    held = read_messages(msgs)
    owners = len(held)
    windows = [[h[steps + k : steps + k + 1, :] for h in held] for k in range(past)]
    own = pick_ref[...]
    own_windows = [pick_rows(own, w) for w in windows]
    for t in range(steps):
        conv = base_ref[t]
        for k in range(past - t):
            conv = conv + cw_ref[k : k + 1, :] * own_windows[t + k]
        act_ref[t * rb : (t + 1) * rb, :] = silu(conv)

    def line_of(row):
        return jnp.concatenate([h[row : row + 1, :] for h in held], axis=0)

    slot = slot_onehot(line_of(past + steps), sender_ref)
    line = [pick_rows(slot, w) for w in windows]
    line += [line_of(t) for t in range(steps)]
    row = steps * rb
    for t in range(steps):
        conv = cw_ref[past:taps, :] * line[t + past] + cb_ref[...]
        for k in range(past):
            conv = conv + cw_ref[k : k + 1, :] * line[t + k]
        act_ref[row : row + owners, :] = silu(conv)
        row += owners
    part = lax.dot_general(
        act_ref[...].astype(BF16),
        xwt_ref[...],
        (((1,), (1,)), ((), ())),
        preferred_element_type=F32,
    )
    part_ref[...] = part
    short_ref[...] = part.astype(BF16)


def add_kernel(a_ref, b_ref, sum_ref, short_ref):
    total = a_ref[...] + b_ref[...].astype(F32)
    sum_ref[...] = total
    short_ref[...] = total.astype(BF16)


def late_kernel(n_msgs, direct, *refs):
    sources, refs = refs[:6], refs[7:]
    owner_hbm, child_hbm, step_hbm, alog_hbm, dtb_hbm, skip_hbm = sources
    msgs, refs = refs[:n_msgs], refs[n_msgs:]
    conv_hbm, gate_ref, rate_ref, twin_ref, dtb_ref, skip_ref = refs[:6]
    owner_s, child_s, step_ref, alog, conv_s, sems = refs[6:]
    small = [
        pltpu.make_async_copy(source, target, sems.at[i])
        for i, (source, target) in enumerate(
            (
                (owner_hbm, owner_s),
                (child_hbm, child_s),
                (alog_hbm, alog),
                (dtb_hbm, dtb_ref),
                (skip_hbm, skip_ref),
            )
        )
    ]
    inputs = in_parts(step_hbm, step_ref, sems, len(small), STEP_PARTS)
    for copy in small + inputs:
        copy.start()
    held = read_messages(msgs)
    past, rb, _ = conv_s.shape
    steps = step_ref.shape[1]
    for copy in small:
        copy.wait()
    places = blocks_of(owner_s[0]) if direct else None
    child = scalar_onehot(child_s, places, (rb, len(held)))
    for k in range(past):
        at = steps - past + k
        conv_s[k] = pick_rows(child, [h[at : at + 1, :] for h in held]).astype(BF16)
    out = pltpu.make_async_copy(conv_s, conv_hbm, sems.at[len(small) + STEP_PARTS])
    out.start()
    rate = jnp.exp(alog[...]) * (-math.log2(math.e))
    rate_ref[...] = rate
    half = (twin_ref.shape[1] // 2, rate.shape[1])
    for m in range(rate.shape[0] // 2):
        two = [jnp.broadcast_to(rate[n : n + 1, :], half) for n in (2 * m, 2 * m + 1)]
        twin_ref[m] = jnp.concatenate(two, axis=0)
    for copy in inputs:
        copy.wait()
    for t in range(steps):
        gate_ref[t] = silu(step_ref[:, t, 1, :].astype(F32))
    out.wait()


def start_kernel(n_msgs, direct, text, pick_ref, sender_ref, after_ref, *rest):
    del after_ref
    msgs, rest = rest[:n_msgs], rest[n_msgs:]
    apart, (own_ref, slot_ref, state_s) = rest[:-3], rest[-3:]
    n_state = own_ref.shape[0]
    held = read_messages(msgs)
    owners = len(held)
    numbers = jnp.concatenate([h[text - 1 : text, :] for h in held], axis=0)
    states = [h[text:, :] for h in held]
    if direct:
        ssm_ref, pair_ref = apart
        head, low, came = [
            pair_ref[0].astype(F32)[i * n_state : (i + 1) * n_state, :] for i in range(3)
        ]
        states[0], states[2], states[3] = ssm_ref[0], came, head + low
    for k, state in enumerate(states):
        state_s[k] = state
    own = pick_ref[...]
    slot = slot_onehot(numbers, sender_ref)

    def two(m, carry):
        picked = []
        for n in (2 * m, 2 * m + 1):
            rows = [state_s[k, pl.ds(n, 1), :] for k in range(owners)]
            own_ref[n] = pick_rows(own, rows)
            picked.append(pick_rows(slot, rows))
        slot_ref[m] = jnp.concatenate(picked, axis=0)
        return carry

    lax.fori_loop(0, n_state // 2, two, 0, unroll=owners <= DIRECT)


def decode_kernel(
    direct,
    owner_hbm,
    child_hbm,
    act_ref,
    gate_ref,
    own_ref,
    slot_ref,
    rate_ref,
    twin_ref,
    dtw_ref,
    dtb_ref,
    skip_ref,
    part_ref,
    other_ref,
    dec_ref,
    child_ssm,
    owner_s,
    child_s,
    delta_s,
    gain_s,
    slot_delta_s,
    slot_gain_s,
    b_s,
    c_s,
    twin_b_s,
    slots_s,
    rows_s,
    line_s,
    sems,
):
    scalars = [
        pltpu.make_async_copy(owner_hbm, owner_s, sems.at[0]),
        pltpu.make_async_copy(child_hbm, child_s, sems.at[1]),
    ]
    for copy in scalars:
        copy.start()
    rb, steps, channels = dec_ref.shape
    rank = dtw_ref.shape[0]
    n_state = rate_ref.shape[0]
    n_slots = slots_s.shape[0]
    own_rows = steps * rb
    chunks = channels // (WIDE * LANES)

    proj = part_ref[...] + other_ref[...].astype(F32)
    delta_in = proj[:, :rank].astype(BF16)
    delta = jnp.dot(delta_in, dtw_ref[...], preferred_element_type=F32) + dtb_ref[...]
    delta = jnp.maximum(delta, 0.0) + jnp.log(1.0 + jnp.exp(-jnp.abs(delta)))
    gain = delta * act_ref[...]
    delta_s[...] = delta[:own_rows, :]
    gain_s[...] = gain[:own_rows, :]

    def column(at, n, rows):
        return jnp.broadcast_to(at[:, n : n + 1], (rows, LANES))

    for t in range(steps):
        at = slice(own_rows + t * n_slots, own_rows + (t + 1) * n_slots)
        slot_delta_s[t] = jnp.concatenate([delta[at, :]] * 2, axis=0)
        slot_gain_s[t] = jnp.concatenate([gain[at, :]] * 2, axis=0)
        twice = jnp.concatenate([proj[at, rank:]] * 2, axis=0)
        upper = lax.broadcasted_iota(jnp.int32, (2 * n_slots, LANES), 0) < n_slots
        for m in range(n_state // 2):
            twin_b_s[m, t] = jnp.where(
                upper, column(twice, 2 * m, 2 * n_slots), column(twice, 2 * m + 1, 2 * n_slots)
            )
    for n in range(n_state):
        b_s[n] = column(proj[:own_rows, rank:], n, own_rows)
        c_s[n] = column(proj[:own_rows, rank:], n_state + n, own_rows)

    def wide(part, times=WIDE):
        return jnp.concatenate([part] * times, axis=1)

    def slot_chunk(chunk, carry):
        breadth = SLOT_WIDE * LANES
        columns = pl.ds(pl.multiple_of(chunk * breadth, breadth), breadth)
        delta = [slot_delta_s[t, :, columns] for t in range(steps)]
        gain = [slot_gain_s[t, :, columns] for t in range(steps)]
        for m in range(n_state // 2):
            rate = twin_ref[m, :, columns]
            state = slot_ref[m, :, columns]
            for t in range(steps):
                state = jnp.exp2(delta[t] * rate) * state + gain[t] * wide(twin_b_s[m, t], SLOT_WIDE)
            for w in range(SLOT_WIDE):
                rows = pl.ds(2 * m * n_slots, 2 * n_slots)
                lanes = slice(w * LANES, (w + 1) * LANES)
                rows_s[chunk * SLOT_WIDE + w, rows, :] = state[:, lanes]
        return carry

    lax.fori_loop(0, channels // (SLOT_WIDE * LANES), slot_chunk, 0)
    for slot in range(n_slots):
        for i in range(channels // LANES):
            rows = rows_s[i, pl.ds(slot, n_state, stride=n_slots), :]
            slots_s[slot, :, i * LANES : (i + 1) * LANES] = rows
    for copy in scalars:
        copy.wait()
    places = blocks_of(owner_s[0]) if direct else None
    copies = []
    for j in range(rb):
        at = chosen(child_s[j], places) if direct else child_s[j]
        copy = pltpu.make_async_copy(slots_s.at[at], child_ssm.at[j], sems.at[2 + j])
        copy.start()
        copies.append(copy)

    def own_chunk(chunk, carry):
        columns = pl.ds(pl.multiple_of(chunk * WIDE * LANES, WIDE * LANES), WIDE * LANES)
        for first in range(0, rb, ROWS):
            at = [pl.ds(t * rb + first, ROWS) for t in range(steps)]
            delta = [delta_s[a, columns] for a in at]
            gain = [gain_s[a, columns] for a in at]
            sums = [skip_ref[:, columns] * act_ref[a, columns] for a in at]
            for n in range(n_state):
                rate = rate_ref[n : n + 1, columns]
                state = own_ref[n, pl.ds(first, ROWS), columns]
                for t in range(steps):
                    state = jnp.exp2(delta[t] * rate) * state + gain[t] * wide(b_s[n, at[t], :])
                    sums[t] = sums[t] + wide(c_s[n, at[t], :]) * state
            for t in range(steps):
                out = sums[t] * gate_ref[t, pl.ds(first, ROWS), columns]
                for w in range(WIDE):
                    line_s[w, pl.ds(first * steps + t, ROWS, stride=steps), :] = out[
                        :, w * LANES : (w + 1) * LANES
                    ]
        for w in range(WIDE):
            some = pl.ds(pl.multiple_of((chunk * WIDE + w) * LANES, LANES), LANES)
            dec_ref[:, :, some] = line_s[w, : steps * rb, :].reshape(rb, steps, LANES).astype(BF16)
        return carry

    lax.fori_loop(0, chunks, own_chunk, 0)
    for copy in copies:
        copy.wait()


def on_device(
    prompt_ssm,
    prompt_conv,
    prompt_of,
    step_in,
    conv_weight,
    conv_bias,
    x_weight,
    dt_weight,
    dt_bias,
    a_log,
    skip,
    send_rows,
    child_slot,
):
    owners = lax.axis_size("branch")
    tensors = lax.axis_size("tensor")
    assert owners & (owners - 1) == 0 and tensors & (tensors - 1) == 0
    assert prompt_ssm.shape[0] == 1 and send_rows.shape[2] == 1
    rb, steps, _, channels = step_in.shape
    taps = conv_weight.shape[0]
    width = x_weight.shape[1]
    n_state = a_log.shape[0]
    rows = steps * (rb + owners)
    short = taps - 1 + steps + 1
    depth = short + n_state
    direct = owners == DIRECT
    owner = pinned(lax.axis_index("branch").astype(jnp.int32).reshape(1))

    if direct:
        msg_shapes = [(1, d, channels) for d in (depth, short, short)]
    else:
        msg_shapes = [(owners, depth, channels)]
    msgs = call(
        functools.partial(pack_kernel, direct),
        [shaped(s, BF16) for s in msg_shapes],
        [hbm()] * 6,
        [vmem()] * len(msg_shapes),
        [
            pltpu.SMEM((1,), jnp.int32),
            pltpu.SMEM((owners,), jnp.int32),
            pltpu.SMEM((rb,), jnp.int32),
            pltpu.VMEM(step_in.shape, BF16),
            pltpu.VMEM(prompt_conv.shape, BF16),
            pltpu.VMEM(prompt_ssm.shape, F32),
            pltpu.SemaphoreType.DMA((5 + STEP_PARTS,)),
        ],
        nbytes=owners * depth * channels * 2,
    )(
        owner,
        pinned(send_rows.reshape(owners)),
        pinned(prompt_of),
        pinned(step_in),
        pinned(prompt_conv),
        pinned(prompt_ssm),
    )
    after = msgs[0]
    if direct:
        msgs = [lax.ppermute(m, "branch", list(enumerate(to))) for m, to in zip(msgs, SENDS)]
    else:
        msgs = [lax.all_to_all(msgs[0], "branch", split_axis=0, concat_axis=0, tiled=True)]
    own, base, pick, sender, taps_near, bias_near, weight_near = call(
        functools.partial(prepare_kernel, direct),
        [
            shaped((1, short, channels), BF16),
            shaped((steps, rb, channels), F32),
            shaped((rb, owners), F32),
            shaped((1, owners), F32),
            shaped((taps, channels), F32),
            shaped((1, channels), F32),
            shaped((width, channels), BF16),
        ],
        [hbm()] * 8 + [anywhere()],
        [vmem()] * 7,
        [
            pltpu.VMEM(step_in.shape, BF16),
            pltpu.SMEM((1,), jnp.int32),
            pltpu.SMEM((rb,), jnp.int32),
            pltpu.SMEM((owners,), jnp.int32),
            pltpu.VMEM(prompt_conv.shape, BF16),
            pltpu.SemaphoreType.DMA((6 + WEIGHT_PARTS + STEP_PARTS,)),
        ],
        flops=10 * steps * rb * channels,
        nbytes=12 * steps * rb * channels,
    )(
        owner,
        pinned(prompt_of),
        pinned(send_rows.reshape(owners)),
        pinned(prompt_conv),
        pinned(step_in),
        pinned(conv_weight),
        pinned(conv_bias[None]),
        pinned(x_weight.T),
        after,
    )
    states = []
    if direct:
        msgs = [own] + msgs
        pair = call(
            functools.partial(pair_kernel, short),
            shaped((1, 3 * n_state, channels), BF16),
            [vmem()] * 2 + [anywhere()],
            vmem(),
            nbytes=12 * n_state * channels,
        )(prompt_ssm, msgs[1], pick)
        states = [prompt_ssm, swap(pair, "branch", 1)]
    n_msgs = len(msgs)
    act, part, brief = call(
        functools.partial(project_kernel, n_msgs),
        [
            shaped((rows, channels), F32),
            shaped((rows, width), F32),
            shaped((rows, width), BF16),
        ],
        [vmem()] * (6 + n_msgs),
        [vmem()] * 3,
        flops=2 * rows * channels * width,
        nbytes=channels * width * 2 + rows * (channels + width) * 4,
        trans=rows * channels,
    )(pick, sender, base, taps_near, bias_near, weight_near, *msgs)
    other = swap(brief, "tensor", 1)
    distance = 2
    while distance < tensors:
        part, brief = call(
            add_kernel,
            [shaped((rows, width), F32), shaped((rows, width), BF16)],
            [vmem()] * 2,
            [vmem()] * 2,
            flops=rows * width,
            nbytes=rows * width * 14,
        )(part, other)
        other = swap(brief, "tensor", 2 * distance - 1)
        distance *= 2

    child_conv, gate, rate, twin, dtb_near, skip_near = call(
        functools.partial(late_kernel, n_msgs, direct),
        [
            shaped((taps - 1, rb, channels), BF16),
            shaped((steps, rb, channels), F32),
            shaped((n_state, channels), F32),
            shaped((n_state // 2, 2 * owners, channels), F32),
            shaped((1, channels), F32),
            shaped((1, channels), F32),
        ],
        [hbm()] * 6 + [anywhere()] + [vmem()] * n_msgs,
        [anywhere()] + [vmem()] * 5,
        [
            pltpu.SMEM((1,), jnp.int32),
            pltpu.SMEM((rb,), jnp.int32),
            pltpu.VMEM(step_in.shape, BF16),
            pltpu.VMEM((n_state, channels), F32),
            pltpu.VMEM((taps - 1, rb, channels), BF16),
            pltpu.SemaphoreType.DMA((6 + STEP_PARTS,)),
        ],
        flops=10 * steps * rb * channels,
        nbytes=12 * steps * rb * channels,
        trans=steps * rb * channels,
    )(
        owner,
        pinned(child_slot),
        pinned(step_in),
        pinned(a_log),
        pinned(dt_bias[None]),
        pinned(skip[None]),
        part,
        *msgs,
    )
    own_start, slot_start = call(
        functools.partial(start_kernel, n_msgs, direct, short),
        [
            shaped((n_state, rb, channels), F32),
            shaped((n_state // 2, 2 * owners, channels), F32),
        ],
        [vmem()] * 2 + [anywhere()] + [vmem()] * (n_msgs + len(states)),
        [vmem()] * 2,
        [pltpu.VMEM((owners, n_state, channels), F32)],
        flops=2 * owners * n_state * (rb + owners) * channels,
        nbytes=4 * n_state * (rb + owners) * channels,
    )(pick, sender, part, *msgs, *states)

    decoded, child_ssm = call(
        functools.partial(decode_kernel, direct),
        [
            shaped((rb, steps, channels), BF16),
            shaped((rb, n_state, channels), F32),
        ],
        [hbm()] * 2 + [vmem()] * 11,
        [vmem(), anywhere()],
        [
            pltpu.SMEM((1,), jnp.int32),
            pltpu.SMEM((rb,), jnp.int32),
            pltpu.VMEM((steps * rb, channels), F32),
            pltpu.VMEM((steps * rb, channels), F32),
            pltpu.VMEM((steps, 2 * owners, channels), F32),
            pltpu.VMEM((steps, 2 * owners, channels), F32),
            pltpu.VMEM((n_state, steps * rb, LANES), F32),
            pltpu.VMEM((n_state, steps * rb, LANES), F32),
            pltpu.VMEM((n_state // 2, steps, 2 * owners, LANES), F32),
            pltpu.VMEM((owners, n_state, channels), F32),
            pltpu.VMEM((channels // LANES, (n_state + 1) * owners + 4, LANES), F32),
            pltpu.VMEM((WIDE, steps * rb + 8, LANES), F32),
            pltpu.SemaphoreType.DMA((2 + rb,)),
        ],
        flops=8 * rows * n_state * channels,
        nbytes=(rb + owners) * n_state * channels * 4,
        trans=rows * n_state * channels,
    )(
        owner,
        pinned(child_slot),
        act,
        gate,
        own_start,
        slot_start,
        rate,
        twin,
        dt_weight,
        dtb_near,
        skip_near,
        part,
        other,
    )
    return (decoded, child_ssm, jnp.transpose(child_conv, (1, 0, 2)))


def solution(mesh):
    placed = (
        P(("replica", "branch"), None, "tensor"),
        P(("replica", "branch"), None, "tensor"),
        P(("replica", "branch")),
        P(("replica", "branch"), None, None, "tensor"),
        P(None, "tensor"),
        P("tensor"),
        P("tensor", None),
        P(None, "tensor"),
        P("tensor"),
        P(None, "tensor"),
        P("tensor"),
        P(("replica", "branch"), None, None),
        P(("replica", "branch")),
    )
    return jax.shard_map(
        on_device,
        mesh=mesh,
        in_specs=placed,
        out_specs=(
            P(("replica", "branch"), None, "tensor"),
            P(("replica", "branch"), None, "tensor"),
            P(("replica", "branch"), None, "tensor"),
        ),
        check_vma=False,
    )
```

```python
import functools
import math

import jax
import jax.numpy as jnp
from jax import lax
from jax.experimental import pallas as pl
from jax.experimental.pallas import tpu as pltpu
from jax.sharding import PartitionSpec as P

F32 = jnp.float32
BF16 = jnp.bfloat16
LANES = 128
ROWS = 8
WIDE = 4
SLOT_WIDE = 4
VMEM_LIMIT = 48 * 2**20
WEIGHT_PARTS = 6
STEP_PARTS = 4
DIRECT = 4
SENDS = ((2, 3, 1, 0), (3, 2, 0, 1), (1, 0, 3, 2))


def vmem():
    return pl.BlockSpec(memory_space=pltpu.VMEM)


def hbm():
    return pl.BlockSpec(memory_space=pltpu.HBM)


def anywhere():
    return pl.BlockSpec(memory_space=pl.ANY)


def pinned(array):
    return pltpu.with_memory_space_constraint(array, pltpu.HBM)


def shaped(shape, dtype):
    return jax.ShapeDtypeStruct(shape, dtype)


def call(kernel, outs, in_specs, out_specs, scratch=(), flops=0, nbytes=0, trans=0):
    return pl.pallas_call(
        kernel,
        out_shape=outs,
        in_specs=in_specs,
        out_specs=out_specs,
        scratch_shapes=list(scratch),
        compiler_params=pltpu.CompilerParams(vmem_limit_bytes=VMEM_LIMIT),
        cost_estimate=pl.CostEstimate(flops=flops, bytes_accessed=nbytes, transcendentals=trans),
    )


def swap(value, axis, distance):
    size = lax.axis_size(axis)
    return lax.ppermute(value, axis, [(i, i ^ distance) for i in range(size)])


def chosen(number, values):
    total = values[0]
    for i in range(1, len(values)):
        total = jnp.where(number == i, values[i], total)
    return total


def blocks_of(owner):
    table = [
        [0 if s == r else 1 + [to[s] for to in SENDS].index(r) for s in range(DIRECT)]
        for r in range(DIRECT)
    ]
    return [chosen(owner, [row[s] for row in table]) for s in range(DIRECT)]


def all_of(copies):
    for copy in copies:
        copy.start()
    for copy in copies:
        copy.wait()


def read_messages(refs):
    return [ref[i].astype(F32) for ref in refs for i in range(ref.shape[0])]


def in_parts(source, target, sems, first, count):
    rows = source.shape[0] // count
    at = [pl.ds(i * rows, rows) for i in range(count)]
    return [
        pltpu.make_async_copy(source.at[a], target.at[a], sems.at[first + i])
        for i, a in enumerate(at)
    ]


def scalar_onehot(senders_s, places, shape):
    row_of = lax.broadcasted_iota(jnp.int32, shape, 0)
    wanted = jnp.zeros(shape, jnp.int32)
    for b in range(shape[0]):
        wanted = jnp.where(row_of == b, senders_s[b], wanted)
    wanted = wanted if places is None else chosen(wanted, places)
    return (wanted == lax.broadcasted_iota(jnp.int32, shape, 1)).astype(F32)


def pick_rows(pick, rows):
    total = pick[:, 0:1] * rows[0]
    for k in range(1, len(rows)):
        total = total + pick[:, k : k + 1] * rows[k]
    return total


def message(target, rows_s, prompt_s, step, conv, state):
    row = jnp.maximum(rows_s[target], 0)
    xs = step[row, :, 0, :].astype(F32)
    number = jnp.full((1, xs.shape[1]), prompt_s[row].astype(F32), F32)
    pieces = [xs, conv[0].astype(F32), number] + ([] if state is None else [state])
    return jnp.concatenate(pieces, axis=0).astype(BF16)


def pack_kernel(direct, owner_hbm, rows_hbm, prompt_hbm, step_hbm, conv_hbm, ssm_hbm, *rest):
    outs, (owner_s, rows_s, prompt_s, step, conv, ssm, sems) = rest[:-7], rest[-7:]
    owners = rows_hbm.shape[0]
    copies = [
        pltpu.make_async_copy(owner_hbm, owner_s, sems.at[4]),
        pltpu.make_async_copy(rows_hbm, rows_s, sems.at[0]),
        pltpu.make_async_copy(prompt_hbm, prompt_s, sems.at[1]),
        pltpu.make_async_copy(conv_hbm, conv, sems.at[2]),
        pltpu.make_async_copy(ssm_hbm, ssm, sems.at[3]),
    ]
    all_of(copies + in_parts(step_hbm, step, sems, 5, STEP_PARTS))
    owner = owner_s[0]
    targets = [chosen(owner, to) for to in SENDS] if direct else range(owners)
    for i, target in enumerate(targets):
        ref = outs[i].at[0] if direct else outs[0].at[i]
        state = ssm[0] if ref.shape[0] > conv.shape[1] + step.shape[1] + 1 else None
        ref[...] = message(target, rows_s, prompt_s, step, conv, state)


def pair_kernel(text, ssm_ref, came_ref, after_ref, pair_ref):
    del after_ref
    state = ssm_ref[0]
    head = state.astype(BF16).astype(F32)
    came = came_ref[0].astype(F32)[text:, :]
    pair_ref[0] = jnp.concatenate([head, state - head, came], axis=0).astype(BF16)


def silu(v):
    below = 1.0 + jnp.exp(-v)
    estimate = pl.reciprocal(below, approx=True)
    return v * (estimate * (2.0 - below * estimate))


def prepare_kernel(
    direct,
    owner_hbm,
    prompt_hbm,
    rows_hbm,
    conv_hbm,
    step_hbm,
    cw_hbm,
    cb_hbm,
    xwt_hbm,
    after_ref,
    own_ref,
    base_ref,
    pick_ref,
    sender_ref,
    cw_ref,
    cb_ref,
    xwt_ref,
    step_ref,
    owner_s,
    prompt_s,
    rows_s,
    conv,
    sems,
):
    del after_ref
    small = [
        pltpu.make_async_copy(source, target, sems.at[i])
        for i, (source, target) in enumerate(
            (
                (cw_hbm, cw_ref),
                (cb_hbm, cb_ref),
                (owner_hbm, owner_s),
                (prompt_hbm, prompt_s),
                (rows_hbm, rows_s),
                (conv_hbm, conv),
            )
        )
    ]
    inputs = in_parts(step_hbm, step_ref, sems, len(small), STEP_PARTS)
    large = in_parts(xwt_hbm, xwt_ref, sems, len(small) + STEP_PARTS, WEIGHT_PARTS)
    for copy in inputs + small + large:
        copy.start()
    for copy in inputs + small:
        copy.wait()
    own_ref[0] = message(owner_s[0], rows_s, prompt_s, step_ref, conv, None)
    steps = step_ref.shape[1]
    taps = cw_hbm.shape[0]
    xs = [step_ref[:, t, 0, :].astype(F32) for t in range(steps)]
    for t in range(steps):
        total = cw_ref[taps - 1 : taps, :] * xs[t] + cb_ref[...]
        for k in range(max(0, taps - 1 - t), taps - 1):
            total = total + cw_ref[k : k + 1, :] * xs[t + k - taps + 1]
        base_ref[t] = total
    places = blocks_of(owner_s[0]) if direct else None
    pick_ref[...] = scalar_onehot(prompt_s, places, pick_ref.shape)
    column = lax.broadcasted_iota(jnp.int32, sender_ref.shape, 1)
    sender = column
    for sent, place in enumerate(places or []):
        sender = jnp.where(column == place, sent, sender)
    sender_ref[...] = sender.astype(F32)
    for copy in large:
        copy.wait()


def slot_onehot(numbers, sender_ref):
    owners = sender_ref.shape[1]
    return (numbers[:, :owners] == sender_ref[...]).astype(F32)


def project_kernel(n_msgs, pick_ref, sender_ref, base_ref, cw_ref, cb_ref, xwt_ref, *rest):
    msgs, (act_ref, part_ref, short_ref) = rest[:n_msgs], rest[n_msgs:]
    taps = cw_ref.shape[0]
    steps, rb, _ = base_ref.shape
    past = taps - 1
    held = read_messages(msgs)
    owners = len(held)
    windows = [[h[steps + k : steps + k + 1, :] for h in held] for k in range(past)]
    own = pick_ref[...]
    own_windows = [pick_rows(own, w) for w in windows]
    for t in range(steps):
        conv = base_ref[t]
        for k in range(past - t):
            conv = conv + cw_ref[k : k + 1, :] * own_windows[t + k]
        act_ref[t * rb : (t + 1) * rb, :] = silu(conv)

    def line_of(row):
        return jnp.concatenate([h[row : row + 1, :] for h in held], axis=0)

    slot = slot_onehot(line_of(past + steps), sender_ref)
    line = [pick_rows(slot, w) for w in windows]
    line += [line_of(t) for t in range(steps)]
    row = steps * rb
    for t in range(steps):
        conv = cw_ref[past:taps, :] * line[t + past] + cb_ref[...]
        for k in range(past):
            conv = conv + cw_ref[k : k + 1, :] * line[t + k]
        act_ref[row : row + owners, :] = silu(conv)
        row += owners
    part = lax.dot_general(
        act_ref[...].astype(BF16),
        xwt_ref[...],
        (((1,), (1,)), ((), ())),
        preferred_element_type=F32,
    )
    part_ref[...] = part
    short_ref[...] = part.astype(BF16)


def add_kernel(a_ref, b_ref, sum_ref, short_ref):
    total = a_ref[...] + b_ref[...].astype(F32)
    sum_ref[...] = total
    short_ref[...] = total.astype(BF16)


def late_kernel(n_msgs, direct, *refs):
    sources, refs = refs[:6], refs[7:]
    owner_hbm, child_hbm, step_hbm, alog_hbm, dtb_hbm, skip_hbm = sources
    msgs, refs = refs[:n_msgs], refs[n_msgs:]
    conv_hbm, gate_ref, rate_ref, twin_ref, dtb_ref, skip_ref = refs[:6]
    owner_s, child_s, step_ref, alog, conv_s, sems = refs[6:]
    small = [
        pltpu.make_async_copy(source, target, sems.at[i])
        for i, (source, target) in enumerate(
            (
                (owner_hbm, owner_s),
                (child_hbm, child_s),
                (alog_hbm, alog),
                (dtb_hbm, dtb_ref),
                (skip_hbm, skip_ref),
            )
        )
    ]
    inputs = in_parts(step_hbm, step_ref, sems, len(small), STEP_PARTS)
    for copy in small + inputs:
        copy.start()
    held = read_messages(msgs)
    past, rb, _ = conv_s.shape
    steps = step_ref.shape[1]
    for copy in small:
        copy.wait()
    places = blocks_of(owner_s[0]) if direct else None
    child = scalar_onehot(child_s, places, (rb, len(held)))
    for k in range(past):
        at = steps - past + k
        conv_s[k] = pick_rows(child, [h[at : at + 1, :] for h in held]).astype(BF16)
    out = pltpu.make_async_copy(conv_s, conv_hbm, sems.at[len(small) + STEP_PARTS])
    out.start()
    rate = jnp.exp(alog[...]) * (-math.log2(math.e))
    rate_ref[...] = rate
    half = (twin_ref.shape[1] // 2, rate.shape[1])
    for m in range(rate.shape[0] // 2):
        two = [jnp.broadcast_to(rate[n : n + 1, :], half) for n in (2 * m, 2 * m + 1)]
        twin_ref[m] = jnp.concatenate(two, axis=0)
    for copy in inputs:
        copy.wait()
    for t in range(steps):
        gate_ref[t] = silu(step_ref[:, t, 1, :].astype(F32))
    out.wait()


def start_kernel(n_msgs, direct, text, pick_ref, sender_ref, after_ref, *rest):
    del after_ref
    msgs, rest = rest[:n_msgs], rest[n_msgs:]
    apart, (own_ref, slot_ref, state_s) = rest[:-3], rest[-3:]
    n_state = own_ref.shape[0]
    held = read_messages(msgs)
    owners = len(held)
    numbers = jnp.concatenate([h[text - 1 : text, :] for h in held], axis=0)
    states = [h[text:, :] for h in held]
    if direct:
        ssm_ref, pair_ref = apart
        head, low, came = [
            pair_ref[0].astype(F32)[i * n_state : (i + 1) * n_state, :] for i in range(3)
        ]
        states[0], states[2], states[3] = ssm_ref[0], came, head + low
    for k, state in enumerate(states):
        state_s[k] = state
    own = pick_ref[...]
    slot = slot_onehot(numbers, sender_ref)

    def two(m, carry):
        picked = []
        for n in (2 * m, 2 * m + 1):
            rows = [state_s[k, pl.ds(n, 1), :] for k in range(owners)]
            own_ref[n] = pick_rows(own, rows)
            picked.append(pick_rows(slot, rows))
        slot_ref[m] = jnp.concatenate(picked, axis=0)
        return carry

    lax.fori_loop(0, n_state // 2, two, 0, unroll=owners <= DIRECT)


def decode_kernel(
    direct,
    owner_hbm,
    child_hbm,
    act_ref,
    gate_ref,
    own_ref,
    slot_ref,
    rate_ref,
    twin_ref,
    dtw_ref,
    dtb_ref,
    skip_ref,
    part_ref,
    other_ref,
    dec_ref,
    child_ssm,
    owner_s,
    child_s,
    delta_s,
    gain_s,
    slot_delta_s,
    slot_gain_s,
    b_s,
    c_s,
    twin_b_s,
    slots_s,
    rows_s,
    line_s,
    sems,
):
    scalars = [
        pltpu.make_async_copy(owner_hbm, owner_s, sems.at[0]),
        pltpu.make_async_copy(child_hbm, child_s, sems.at[1]),
    ]
    for copy in scalars:
        copy.start()
    rb, steps, channels = dec_ref.shape
    rank = dtw_ref.shape[0]
    n_state = rate_ref.shape[0]
    n_slots = slots_s.shape[0]
    own_rows = steps * rb
    chunks = channels // (WIDE * LANES)

    proj = part_ref[...] + other_ref[...].astype(F32)
    delta_in = proj[:, :rank].astype(BF16)
    delta = jnp.dot(delta_in, dtw_ref[...], preferred_element_type=F32) + dtb_ref[...]
    delta = jnp.maximum(delta, 0.0) + jnp.log(1.0 + jnp.exp(-jnp.abs(delta)))
    gain = delta * act_ref[...]
    delta_s[...] = delta[:own_rows, :]
    gain_s[...] = gain[:own_rows, :]

    def column(at, n, rows):
        return jnp.broadcast_to(at[:, n : n + 1], (rows, LANES))

    for t in range(steps):
        at = slice(own_rows + t * n_slots, own_rows + (t + 1) * n_slots)
        slot_delta_s[t] = jnp.concatenate([delta[at, :]] * 2, axis=0)
        slot_gain_s[t] = jnp.concatenate([gain[at, :]] * 2, axis=0)
        twice = jnp.concatenate([proj[at, rank:]] * 2, axis=0)
        upper = lax.broadcasted_iota(jnp.int32, (2 * n_slots, LANES), 0) < n_slots
        for m in range(n_state // 2):
            twin_b_s[m, t] = jnp.where(
                upper, column(twice, 2 * m, 2 * n_slots), column(twice, 2 * m + 1, 2 * n_slots)
            )
    for n in range(n_state):
        b_s[n] = column(proj[:own_rows, rank:], n, own_rows)
        c_s[n] = column(proj[:own_rows, rank:], n_state + n, own_rows)

    def wide(part, times=WIDE):
        return jnp.concatenate([part] * times, axis=1)

    def slot_chunk(chunk, carry):
        breadth = SLOT_WIDE * LANES
        columns = pl.ds(pl.multiple_of(chunk * breadth, breadth), breadth)
        delta = [slot_delta_s[t, :, columns] for t in range(steps)]
        gain = [slot_gain_s[t, :, columns] for t in range(steps)]
        for m in range(n_state // 2):
            rate = twin_ref[m, :, columns]
            state = slot_ref[m, :, columns]
            for t in range(steps):
                state = jnp.exp2(delta[t] * rate) * state + gain[t] * wide(twin_b_s[m, t], SLOT_WIDE)
            for w in range(SLOT_WIDE):
                rows = pl.ds(2 * m * n_slots, 2 * n_slots)
                lanes = slice(w * LANES, (w + 1) * LANES)
                rows_s[chunk * SLOT_WIDE + w, rows, :] = state[:, lanes]
        return carry

    lax.fori_loop(0, channels // (SLOT_WIDE * LANES), slot_chunk, 0)
    for slot in range(n_slots):
        for i in range(channels // LANES):
            rows = rows_s[i, pl.ds(slot, n_state, stride=n_slots), :]
            slots_s[slot, :, i * LANES : (i + 1) * LANES] = rows
    for copy in scalars:
        copy.wait()
    places = blocks_of(owner_s[0]) if direct else None
    copies = []
    for j in range(rb):
        at = chosen(child_s[j], places) if direct else child_s[j]
        copy = pltpu.make_async_copy(slots_s.at[at], child_ssm.at[j], sems.at[2 + j])
        copy.start()
        copies.append(copy)

    def own_chunk(chunk, carry):
        columns = pl.ds(pl.multiple_of(chunk * WIDE * LANES, WIDE * LANES), WIDE * LANES)
        for first in range(0, rb, ROWS):
            at = [pl.ds(t * rb + first, ROWS) for t in range(steps)]
            delta = [delta_s[a, columns] for a in at]
            gain = [gain_s[a, columns] for a in at]
            sums = [skip_ref[:, columns] * act_ref[a, columns] for a in at]
            for n in range(n_state):
                rate = rate_ref[n : n + 1, columns]
                state = own_ref[n, pl.ds(first, ROWS), columns]
                for t in range(steps):
                    state = jnp.exp2(delta[t] * rate) * state + gain[t] * wide(b_s[n, at[t], :])
                    sums[t] = sums[t] + wide(c_s[n, at[t], :]) * state
            for t in range(steps):
                out = sums[t] * gate_ref[t, pl.ds(first, ROWS), columns]
                for w in range(WIDE):
                    line_s[w, pl.ds(first * steps + t, ROWS, stride=steps), :] = out[
                        :, w * LANES : (w + 1) * LANES
                    ]
        for w in range(WIDE):
            some = pl.ds(pl.multiple_of((chunk * WIDE + w) * LANES, LANES), LANES)
            dec_ref[:, :, some] = line_s[w, : steps * rb, :].reshape(rb, steps, LANES).astype(BF16)
        return carry

    lax.fori_loop(0, chunks, own_chunk, 0)
    for copy in copies:
        copy.wait()


def on_device(
    prompt_ssm,
    prompt_conv,
    prompt_of,
    step_in,
    conv_weight,
    conv_bias,
    x_weight,
    dt_weight,
    dt_bias,
    a_log,
    skip,
    send_rows,
    child_slot,
):
    owners = lax.axis_size("branch")
    tensors = lax.axis_size("tensor")
    assert owners & (owners - 1) == 0 and tensors & (tensors - 1) == 0
    assert prompt_ssm.shape[0] == 1 and send_rows.shape[2] == 1
    rb, steps, _, channels = step_in.shape
    taps = conv_weight.shape[0]
    width = x_weight.shape[1]
    n_state = a_log.shape[0]
    rows = steps * (rb + owners)
    short = taps - 1 + steps + 1
    depth = short + n_state
    direct = owners == DIRECT
    owner = pinned(lax.axis_index("branch").astype(jnp.int32).reshape(1))

    if direct:
        msg_shapes = [(1, d, channels) for d in (depth, short, short)]
    else:
        msg_shapes = [(owners, depth, channels)]
    msgs = call(
        functools.partial(pack_kernel, direct),
        [shaped(s, BF16) for s in msg_shapes],
        [hbm()] * 6,
        [vmem()] * len(msg_shapes),
        [
            pltpu.SMEM((1,), jnp.int32),
            pltpu.SMEM((owners,), jnp.int32),
            pltpu.SMEM((rb,), jnp.int32),
            pltpu.VMEM(step_in.shape, BF16),
            pltpu.VMEM(prompt_conv.shape, BF16),
            pltpu.VMEM(prompt_ssm.shape, F32),
            pltpu.SemaphoreType.DMA((5 + STEP_PARTS,)),
        ],
        nbytes=owners * depth * channels * 2,
    )(
        owner,
        pinned(send_rows.reshape(owners)),
        pinned(prompt_of),
        pinned(step_in),
        pinned(prompt_conv),
        pinned(prompt_ssm),
    )
    after = msgs[0]
    if direct:
        msgs = [lax.ppermute(m, "branch", list(enumerate(to))) for m, to in zip(msgs, SENDS)]
    else:
        msgs = [lax.all_to_all(msgs[0], "branch", split_axis=0, concat_axis=0, tiled=True)]
    own, base, pick, sender, taps_near, bias_near, weight_near = call(
        functools.partial(prepare_kernel, direct),
        [
            shaped((1, short, channels), BF16),
            shaped((steps, rb, channels), F32),
            shaped((rb, owners), F32),
            shaped((1, owners), F32),
            shaped((taps, channels), F32),
            shaped((1, channels), F32),
            shaped((width, channels), BF16),
        ],
        [hbm()] * 8 + [anywhere()],
        [vmem()] * 7,
        [
            pltpu.VMEM(step_in.shape, BF16),
            pltpu.SMEM((1,), jnp.int32),
            pltpu.SMEM((rb,), jnp.int32),
            pltpu.SMEM((owners,), jnp.int32),
            pltpu.VMEM(prompt_conv.shape, BF16),
            pltpu.SemaphoreType.DMA((6 + WEIGHT_PARTS + STEP_PARTS,)),
        ],
        flops=10 * steps * rb * channels,
        nbytes=12 * steps * rb * channels,
    )(
        owner,
        pinned(prompt_of),
        pinned(send_rows.reshape(owners)),
        pinned(prompt_conv),
        pinned(step_in),
        pinned(conv_weight),
        pinned(conv_bias[None]),
        pinned(x_weight.T),
        after,
    )
    states = []
    if direct:
        msgs = [own] + msgs
        pair = call(
            functools.partial(pair_kernel, short),
            shaped((1, 3 * n_state, channels), BF16),
            [vmem()] * 2 + [anywhere()],
            vmem(),
            nbytes=12 * n_state * channels,
        )(prompt_ssm, msgs[1], pick)
        states = [prompt_ssm, swap(pair, "branch", 1)]
    n_msgs = len(msgs)
    act, part, brief = call(
        functools.partial(project_kernel, n_msgs),
        [
            shaped((rows, channels), F32),
            shaped((rows, width), F32),
            shaped((rows, width), BF16),
        ],
        [vmem()] * (6 + n_msgs),
        [vmem()] * 3,
        flops=2 * rows * channels * width,
        nbytes=channels * width * 2 + rows * (channels + width) * 4,
        trans=rows * channels,
    )(pick, sender, base, taps_near, bias_near, weight_near, *msgs)
    other = swap(brief, "tensor", 1)
    distance = 2
    while distance < tensors:
        part, brief = call(
            add_kernel,
            [shaped((rows, width), F32), shaped((rows, width), BF16)],
            [vmem()] * 2,
            [vmem()] * 2,
            flops=rows * width,
            nbytes=rows * width * 14,
        )(part, other)
        other = swap(brief, "tensor", 2 * distance - 1)
        distance *= 2

    child_conv, gate, rate, twin, dtb_near, skip_near = call(
        functools.partial(late_kernel, n_msgs, direct),
        [
            shaped((taps - 1, rb, channels), BF16),
            shaped((steps, rb, channels), F32),
            shaped((n_state, channels), F32),
            shaped((n_state // 2, 2 * owners, channels), F32),
            shaped((1, channels), F32),
            shaped((1, channels), F32),
        ],
        [hbm()] * 6 + [anywhere()] + [vmem()] * n_msgs,
        [anywhere()] + [vmem()] * 5,
        [
            pltpu.SMEM((1,), jnp.int32),
            pltpu.SMEM((rb,), jnp.int32),
            pltpu.VMEM(step_in.shape, BF16),
            pltpu.VMEM((n_state, channels), F32),
            pltpu.VMEM((taps - 1, rb, channels), BF16),
            pltpu.SemaphoreType.DMA((6 + STEP_PARTS,)),
        ],
        flops=10 * steps * rb * channels,
        nbytes=12 * steps * rb * channels,
        trans=steps * rb * channels,
    )(
        owner,
        pinned(child_slot),
        pinned(step_in),
        pinned(a_log),
        pinned(dt_bias[None]),
        pinned(skip[None]),
        part,
        *msgs,
    )
    own_start, slot_start = call(
        functools.partial(start_kernel, n_msgs, direct, short),
        [
            shaped((n_state, rb, channels), F32),
            shaped((n_state // 2, 2 * owners, channels), F32),
        ],
        [vmem()] * 2 + [anywhere()] + [vmem()] * (n_msgs + len(states)),
        [vmem()] * 2,
        [pltpu.VMEM((owners, n_state, channels), F32)],
        flops=2 * owners * n_state * (rb + owners) * channels,
        nbytes=4 * n_state * (rb + owners) * channels,
    )(pick, sender, part, *msgs, *states)

    decoded, child_ssm = call(
        functools.partial(decode_kernel, direct),
        [
            shaped((rb, steps, channels), BF16),
            shaped((rb, n_state, channels), F32),
        ],
        [hbm()] * 2 + [vmem()] * 11,
        [vmem(), anywhere()],
        [
            pltpu.SMEM((1,), jnp.int32),
            pltpu.SMEM((rb,), jnp.int32),
            pltpu.VMEM((steps * rb, channels), F32),
            pltpu.VMEM((steps * rb, channels), F32),
            pltpu.VMEM((steps, 2 * owners, channels), F32),
            pltpu.VMEM((steps, 2 * owners, channels), F32),
            pltpu.VMEM((n_state, steps * rb, LANES), F32),
            pltpu.VMEM((n_state, steps * rb, LANES), F32),
            pltpu.VMEM((n_state // 2, steps, 2 * owners, LANES), F32),
            pltpu.VMEM((owners, n_state, channels), F32),
            pltpu.VMEM((channels // LANES, (n_state + 1) * owners + 4, LANES), F32),
            pltpu.VMEM((WIDE, steps * rb + 8, LANES), F32),
            pltpu.SemaphoreType.DMA((2 + rb,)),
        ],
        flops=8 * rows * n_state * channels,
        nbytes=(rb + owners) * n_state * channels * 4,
        trans=rows * n_state * channels,
    )(
        owner,
        pinned(child_slot),
        act,
        gate,
        own_start,
        slot_start,
        rate,
        twin,
        dt_weight,
        dtb_near,
        skip_near,
        part,
        other,
    )
    return (decoded, child_ssm, jnp.transpose(child_conv, (1, 0, 2)))


def solution(mesh):
    placed = (
        P(("replica", "branch"), None, "tensor"),
        P(("replica", "branch"), None, "tensor"),
        P(("replica", "branch")),
        P(("replica", "branch"), None, None, "tensor"),
        P(None, "tensor"),
        P("tensor"),
        P("tensor", None),
        P(None, "tensor"),
        P("tensor"),
        P(None, "tensor"),
        P("tensor"),
        P(("replica", "branch"), None, None),
        P(("replica", "branch")),
    )
    return jax.shard_map(
        on_device,
        mesh=mesh,
        in_specs=placed,
        out_specs=(
            P(("replica", "branch"), None, "tensor"),
            P(("replica", "branch"), None, "tensor"),
            P(("replica", "branch"), None, "tensor"),
        ),
        check_vma=False,
    )
```
